32 devices in a mesh: gz: 2 (over y), px: 4 (over x, core), py: 4 (over z).
Axes of the slice: x: 2, y: 2, z: 4, core: 2. Of those that a mesh axis runs over, the one named last changes fastest.
Arguments:
- flux_x: bfloat16 [3, 32, 32, 2048], P(None, 'gz', 'py', 'px'), may hold values from -6 to 6
- flux_y: bfloat16 [3, 32, 64, 2048], P(None, 'gz', 'px', 'py'), may hold values from -6 to 6
- flux_z: bfloat16 [3, 32, 32, 2048], P(None, 'gz', 'py', 'px'), may hold values from -6 to 6
- line_op: bfloat16 [2048, 2048], replicated, may hold values from -0.125 to 0.125
Outputs:
- xz_part: bfloat16 [3, 32, 32, 2048], P(None, ('gz', 'px'), 'py')
- y_part: bfloat16 [3, 32, 64, 2048], P(None, 'gz', ('px', 'py'))
The draws below stay inside these ranges and needn't reach their ends.
All inputs are finite; a program needn't handle non-finite values.
Results may differ from the reference program's by a relative error of at most 0.0042.
Values may be sent and summed in bfloat16 or wider, within the bound.
No kernel may reach another device: no remote copies, remote signals or barrier semaphores. Data moves between devices by JAX's collectives and lax.ppermute only.
A program may use at most 64 MiB of HBM per device.

```python
import jax
import jax.numpy as jnp
from jax import lax

LINE = 2048
NZ = 32
YB = 32
XB = 64


def block_levels(own_key, extent, cuts, low, high):
    loudness, own = 1.0, jax.random.fold_in(own_key, 6)
    for position, shards_of in cuts:
        heights = jnp.exp(jax.random.uniform(jax.random.fold_in(own, position), (shards_of,), jnp.float32, low / len(cuts), high / len(cuts)))
        loudness = loudness * jnp.repeat(heights, extent[position] // shards_of).reshape([-1 if axis == position else 1 for axis in range(len(extent))])
    return loudness


def noise(key, dims, spread, most, split=(), kind=jnp.bfloat16):
    result = spread * jax.random.normal(key, dims, jnp.float32)
    if split:
        result = result * block_levels(key, dims, split, -0.22, 0.18)
    return jnp.clip(result, -most, most).astype(kind)


def setup_inputs(seed: int = 0) -> dict:
    key_list = jax.random.split(jax.random.key(seed), 5)
    return {
        "flux_x": noise(key_list[0], (3, NZ, YB, LINE), 1.0, 6.0, ((1, 2), (2, 4), (3, 4))),
        "flux_y": noise(key_list[1], (3, NZ, XB, LINE), 1.0, 6.0, ((1, 2), (2, 4), (3, 4))),
        "flux_z": noise(key_list[2], (3, NZ, YB, LINE), 1.0, 6.0, ((1, 2), (2, 4), (3, 4))),
        "line_op": noise(key_list[3], (LINE, LINE), LINE ** -0.5, 0.125),
    }


STENCIL_COEFS = (0.8, -0.2, 4.0 / 105.0, -1.0 / 280.0)


def apply_lines(fluxes, line_op):
    op_t = line_op.astype(jnp.float32).T
    leading = fluxes.shape[:-2]
    planes = fluxes.reshape((-1,) + fluxes.shape[-2:])

    def one_plane(plane):
        return jnp.dot(plane.astype(jnp.float32), op_t, precision=lax.Precision.HIGHEST)

    return lax.map(one_plane, planes).reshape(leading + fluxes.shape[-2:])


def reference(flux_x, flux_y, flux_z, line_op):
    widened = flux_z.astype(jnp.float32)
    z_total = jnp.zeros_like(widened)
    for offset in range(4):
        reach = offset + 1
        z_total = z_total + STENCIL_COEFS[offset] * (jnp.roll(widened, -reach, axis=1) - jnp.roll(widened, reach, axis=1))
    z_deriv = z_total.astype(jnp.bfloat16)
    xz_part = (apply_lines(flux_x, line_op) + z_deriv.astype(jnp.float32)).astype(jnp.bfloat16)
    y_part = apply_lines(flux_y, line_op).astype(jnp.bfloat16)
    return xz_part, y_part
```

```python
import functools

import jax
import jax.numpy as jnp
from jax import lax
from jax.experimental import pallas as pl
from jax.experimental.pallas import tpu as pltpu
from jax.sharding import PartitionSpec as P

STENCIL_COEFS = (0.8, -0.2, 4.0 / 105.0, -1.0 / 280.0)
WIDTH = 4
MIB = 1 << 20
VMEM = pl.BlockSpec(memory_space=pltpu.VMEM)


def with_halo(block, sides, width):
    for axis, dim in sides:
        count = lax.axis_size(axis)
        forward = [(i, i + 1) for i in range(count - 1)]
        forward.append((count - 1, 0))
        backward = [(target, source) for source, target in forward]
        low = lax.ppermute(
            lax.slice_in_dim(block, block.shape[dim] - width, None, axis=dim), axis, forward
        )
        high = lax.ppermute(lax.slice_in_dim(block, 0, width, axis=dim), axis, backward)
        block = jnp.concatenate([low, block, high], axis=dim)
    return block


def line_product(block, line_op):
    return lax.dot_general(
        block, line_op, (((3,), (1,)), ((), ())), preferred_element_type=jnp.float32
    )


def z_stencil(padded, planes):
    widened = padded.astype(jnp.float32)
    total = jnp.zeros((widened.shape[0], planes) + widened.shape[2:], jnp.float32)
    for offset in range(WIDTH):
        reach = offset + 1
        upper = widened[:, WIDTH + reach : WIDTH + reach + planes]
        lower = widened[:, WIDTH - reach : WIDTH - reach + planes]
        total = total + STENCIL_COEFS[offset] * (upper - lower)
    return total.astype(jnp.bfloat16)


def plain(flux_x, flux_y, flux_z, line_op):
    planes = flux_z.shape[1]
    z_deriv = z_stencil(with_halo(flux_z, (("gz", 1),), WIDTH), planes)
    y_part = line_product(
        lax.all_to_all(flux_y, "py", split_axis=2, concat_axis=3, tiled=True), line_op
    ).astype(jnp.bfloat16)
    products = line_product(
        lax.all_to_all(flux_x, "px", split_axis=1, concat_axis=3, tiled=True), line_op
    )
    moved = lax.all_to_all(z_deriv, "px", split_axis=1, concat_axis=3, tiled=True)
    xz_part = (products + moved.astype(jnp.float32)).astype(jnp.bfloat16)
    return (xz_part, y_part)


def partner(axis, flip):
    return lax.axis_index(axis) ^ flip


def swap(block, axis, flip):
    pairs = [(i, i ^ flip) for i in range(lax.axis_size(axis))]
    return lax.ppermute(block, axis, pairs)


def call(kernel, out_shape, *operands, limit, flops=0, scratch=()):
    moved = sum(a.size * a.dtype.itemsize for a in (*operands, *jax.tree.leaves(out_shape)))
    return pl.pallas_call(
        kernel,
        out_shape=out_shape,
        in_specs=[VMEM] * len(operands),
        out_specs=jax.tree.map(lambda _: VMEM, out_shape),
        scratch_shapes=scratch,
        compiler_params=pltpu.CompilerParams(vmem_limit_bytes=limit * MIB),
        cost_estimate=pl.CostEstimate(flops=flops, bytes_accessed=moved, transcendentals=0),
    )(*operands)


def pick_rows(lines, rows, count, flip, out):
    group = 256
    kept = group // count
    line = lax.broadcasted_iota(jnp.int32, (kept, group), 0)
    source = lax.broadcasted_iota(jnp.int32, (kept, group), 1)
    wanted = (line // rows) * (count * rows) + partner("py", flip) * rows + line % rows
    chosen = (source == wanted).astype(jnp.bfloat16)
    for part in range(lines.shape[0] // group):
        picked = jnp.dot(
            chosen,
            lines[part * group : (part + 1) * group, :],
            preferred_element_type=jnp.float32,
        )
        out[part * kept : (part + 1) * kept, :] = picked.astype(jnp.bfloat16)


def first_kernel(rows, count, flip, flux_y, out):
    pick_rows(flux_y, rows, count, flip, out)


def pack_kernel(rows, count, flips, planes, x_count, flux_y, flux_x, flux_z, *outs):
    low, high = outs[0], outs[1]
    low[...] = flux_z[:, flux_z.shape[1] - WIDTH :]
    high[...] = flux_z[:, :WIDTH]
    for flip in range(x_count):
        outs[2 + flip][...] = flux_x[:, pl.ds(partner("px", flip) * planes, planes)]
    for flip, out in zip(flips, outs[2 + x_count :]):
        pick_rows(flux_y, rows, count, flip, out)


def stencil_kernel(planes, flux_z, low, high, *refs):
    outs, held = refs[:-1], refs[-1]
    own = flux_z.shape[1]

    def plane(variable, index):
        if index < 0:
            return low[variable, WIDTH + index].astype(jnp.float32)
        if index >= own:
            return high[variable, index - own].astype(jnp.float32)
        return flux_z[variable, index].astype(jnp.float32)

    for variable in range(flux_z.shape[0]):
        for index in range(own):
            total = jnp.zeros(flux_z.shape[2:], jnp.float32)
            for offset in range(WIDTH):
                upper = plane(variable, index + offset + 1)
                lower = plane(variable, index - offset - 1)
                total = total + STENCIL_COEFS[offset] * (upper - lower)
            held[variable, index] = total.astype(jnp.bfloat16)
    for flip, out in enumerate(outs):
        out[...] = held[:, pl.ds(partner("px", flip) * planes, planes)]


def cells(axis, flip, width):
    return pl.ds(pl.multiple_of(partner(axis, flip) * width, width), width)


def times(block, line_op, to, of):
    return lax.dot_general(
        block, line_op[to, of], (((1,), (1,)), ((), ())), preferred_element_type=jnp.float32
    )


def xz_kernel(count, *refs):
    blocks, derivs = refs[:count], refs[count : 2 * count]
    line_op, out = refs[2 * count :]
    width = blocks[0].shape[1]
    for to in range(count):
        place = cells("px", to, width)
        total = derivs[to][...].astype(jnp.float32)
        for flip in range(count):
            total = total + times(blocks[flip][...], line_op, place, cells("px", flip, width))
        out[:, place] = total.astype(jnp.bfloat16)


def early_kernel(flips, *refs):
    blocks = refs[: len(flips)]
    line_op, out = refs[len(flips) :]
    width = blocks[0].shape[1]
    for start in range(0, out.shape[1], width):
        place = pl.ds(start, width)
        total = None
        for flip, block in zip(flips, blocks):
            part = times(block[...], line_op, place, cells("py", flip, width))
            total = part if total is None else total + part
        out[:, place] = total


def late_kernel(flips, *refs):
    blocks = refs[: len(flips)]
    early, line_op, out = refs[len(flips) :]
    width = blocks[0].shape[1]
    rows = out.shape[1]
    for start in range(0, out.shape[2], width):
        place = pl.ds(start, width)
        total = early[:, place]
        for flip, block in zip(flips, blocks):
            total = total + times(block[...], line_op, place, cells("py", flip, width))
        for group in range(out.shape[0]):
            out[group, :, place] = total[group * rows : (group + 1) * rows].astype(jnp.bfloat16)


def local(flux_x, flux_y, flux_z, line_op):
    variables, slab, lines, x_width = flux_x.shape
    x_count, y_count = lax.axis_size("px"), lax.axis_size("py")
    planes = slab // x_count
    x_lines, y_width = flux_y.shape[2:]
    rows = x_lines // y_count
    line = line_op.shape[0]
    gathered = variables * slab * rows
    bf16 = jnp.bfloat16

    rows_y = flux_y.reshape(-1, y_width)
    chunk_y = jax.ShapeDtypeStruct((gathered, y_width), bf16)
    face = jax.ShapeDtypeStruct((variables, WIDTH, lines, x_width), bf16)
    chunk_x = jax.ShapeDtypeStruct((variables, planes, lines, x_width), bf16)

    (sent_2,) = call(
        functools.partial(first_kernel, rows, y_count, 2), [chunk_y], rows_y, limit=4
    )
    got_2 = swap(sent_2, "py", 2)
    later = (3, 1, 0)
    low, high, *packed = call(
        functools.partial(pack_kernel, rows, y_count, later, planes, x_count),
        [face, face] + [chunk_x] * x_count + [chunk_y] * 3,
        rows_y,
        flux_x,
        flux_z,
        limit=8,
    )
    packed_x, (sent_3, sent_1, own_y) = packed[:x_count], packed[x_count:]
    got_3 = swap(sent_3, "py", 3)
    got_1 = swap(sent_1, "py", 1)

    count_z = lax.axis_size("gz")
    forward = [(i, (i + 1) % count_z) for i in range(count_z)]
    backward = [(target, source) for source, target in forward]
    low = lax.ppermute(low, "gz", forward)
    high = lax.ppermute(high, "gz", backward)
    got_x = [packed_x[0]] + [swap(packed_x[k], "px", k) for k in range(1, x_count)]
    derivs = call(
        functools.partial(stencil_kernel, planes),
        [chunk_x] * x_count,
        flux_z,
        low,
        high,
        limit=8,
        scratch=[pltpu.VMEM(flux_z.shape, bf16)],
    )
    got_z = [derivs[0]] + [swap(derivs[k], "px", k) for k in range(1, x_count)]

    flat = [a.reshape(-1, x_width) for a in (*got_x, *got_z)]
    lines_x = flat[0].shape[0]
    xz_part = call(
        functools.partial(xz_kernel, x_count),
        jax.ShapeDtypeStruct((lines_x, line), bf16),
        *flat,
        line_op,
        limit=24,
        flops=2 * lines_x * line * line,
    )
    early = call(
        functools.partial(early_kernel, (0, 2)),
        jax.ShapeDtypeStruct((gathered, line), jnp.float32),
        own_y,
        got_2,
        line_op,
        limit=24,
        flops=gathered * line * line,
    )
    y_part = call(
        functools.partial(late_kernel, (1, 3)),
        jax.ShapeDtypeStruct((variables * slab, rows, line), bf16),
        got_1,
        got_3,
        early,
        line_op,
        limit=24,
        flops=gathered * line * line,
    )
    return (
        xz_part.reshape(variables, planes, lines, line),
        y_part.reshape(variables, slab, rows, line),
    )


def solution(mesh):
    fits = mesh.shape["py"] == 4 and mesh.shape["px"] == 4
    return jax.shard_map(
        local if fits else plain,
        mesh=mesh,
        in_specs=(
            P(None, "gz", "py", "px"),
            P(None, "gz", "px", "py"),
            P(None, "gz", "py", "px"),
            P(),
        ),
        out_specs=(P(None, ("gz", "px"), "py", None), P(None, "gz", ("px", "py"), None)),
        check_vma=False,
    )
```

```python
import functools

import jax
import jax.numpy as jnp
from jax import lax
from jax.experimental import pallas as pl
from jax.experimental.pallas import tpu as pltpu
from jax.sharding import PartitionSpec as P

STENCIL_COEFS = (0.8, -0.2, 4.0 / 105.0, -1.0 / 280.0)
WIDTH = 4
STAGE = 5 * 10**9
MIB = 1 << 20
VMEM = pl.BlockSpec(memory_space=pltpu.VMEM)
FAR = pl.BlockSpec(memory_space=pltpu.HBM)


def with_halo(block, sides, width):
    for axis, dim in sides:
        count = lax.axis_size(axis)
        forward = [(i, i + 1) for i in range(count - 1)]
        forward.append((count - 1, 0))
        backward = [(target, source) for source, target in forward]
        low = lax.ppermute(
            lax.slice_in_dim(block, block.shape[dim] - width, None, axis=dim), axis, forward
        )
        high = lax.ppermute(lax.slice_in_dim(block, 0, width, axis=dim), axis, backward)
        block = jnp.concatenate([low, block, high], axis=dim)
    return block


def line_product(block, line_op):
    return lax.dot_general(
        block, line_op, (((3,), (1,)), ((), ())), preferred_element_type=jnp.float32
    )


def z_stencil(padded, planes):
    widened = padded.astype(jnp.float32)
    total = jnp.zeros((widened.shape[0], planes) + widened.shape[2:], jnp.float32)
    for offset in range(WIDTH):
        reach = offset + 1
        upper = widened[:, WIDTH + reach : WIDTH + reach + planes]
        lower = widened[:, WIDTH - reach : WIDTH - reach + planes]
        total = total + STENCIL_COEFS[offset] * (upper - lower)
    return total.astype(jnp.bfloat16)


def plain(flux_x, flux_y, flux_z, line_op):
    planes = flux_z.shape[1]
    z_deriv = z_stencil(with_halo(flux_z, (("gz", 1),), WIDTH), planes)
    y_part = line_product(
        lax.all_to_all(flux_y, "py", split_axis=2, concat_axis=3, tiled=True), line_op
    ).astype(jnp.bfloat16)
    products = line_product(
        lax.all_to_all(flux_x, "px", split_axis=1, concat_axis=3, tiled=True), line_op
    )
    moved = lax.all_to_all(z_deriv, "px", split_axis=1, concat_axis=3, tiled=True)
    xz_part = (products + moved.astype(jnp.float32)).astype(jnp.bfloat16)
    return (xz_part, y_part)


def partner(axis, flip):
    return lax.axis_index(axis) ^ flip


def swap(block, axis, flip):
    pairs = [(i, i ^ flip) for i in range(lax.axis_size(axis))]
    return lax.ppermute(block, axis, pairs)


def call(kernel, out_shape, *operands, limit, flops=0, scratch=(), far=()):
    moved = sum(a.size * a.dtype.itemsize for a in (*operands, *jax.tree.leaves(out_shape)))
    operands = [
        pltpu.with_memory_space_constraint(a, pltpu.HBM) if index in far else a
        for index, a in enumerate(operands)
    ]
    return pl.pallas_call(
        kernel,
        out_shape=out_shape,
        in_specs=[FAR if index in far else VMEM for index in range(len(operands))],
        out_specs=jax.tree.map(lambda _: VMEM, out_shape),
        scratch_shapes=scratch,
        compiler_params=pltpu.CompilerParams(vmem_limit_bytes=limit * MIB),
        cost_estimate=pl.CostEstimate(flops=flops, bytes_accessed=moved, transcendentals=0),
    )(*operands)


def pick_rows(lines, rows, count, flip, out):
    group = 256
    kept = group // count
    line = lax.broadcasted_iota(jnp.int32, (kept, group), 0)
    source = lax.broadcasted_iota(jnp.int32, (kept, group), 1)
    wanted = (line // rows) * (count * rows) + partner("py", flip) * rows + line % rows
    chosen = (source == wanted).astype(jnp.bfloat16)
    for part in range(lines.shape[0] // group):
        picked = jnp.dot(
            chosen,
            lines[part * group : (part + 1) * group, :],
            preferred_element_type=jnp.float32,
        )
        out[part * kept : (part + 1) * kept, :] = picked.astype(jnp.bfloat16)


def pack_kernel(rows, count, planes, flux_y, flux_x, flux_z, *refs):
    sent_y, (faces, across, stay, held_z), (held_y, sems) = refs[:count], refs[count:-2], refs[-2:]
    last = flux_z.shape[1] - WIDTH
    moves = [(flux_y, held_y), (flux_z, held_z)]
    moves += [(flux_z.at[:, pl.ds(last, WIDTH)], faces.at[:, :WIDTH])]
    moves += [(flux_z.at[:, :WIDTH], faces.at[:, WIDTH:])]
    for flip, place in ((2, across.at[0]), (3, across.at[1]), (0, stay.at[0]), (1, stay.at[1])):
        moves.append((flux_x.at[:, pl.ds(partner("px", flip) * planes, planes)], place))
    copies = [pltpu.make_async_copy(a, b, sems.at[i]) for i, (a, b) in enumerate(moves)]
    for copy in copies:
        copy.start()
    copies[0].wait()
    for flip in (2, 3, 1, 0):
        pick_rows(held_y, rows, count, flip, sent_y[flip])
    for copy in copies[1:]:
        copy.wait()


def join_kernel(stay, got, out):
    out[0] = stay[1]
    out[1] = got[1]


def stencil_kernel(planes, flux_z, faces, across, stay, held):
    own = flux_z.shape[1]

    def plane(variable, index):
        if index < 0:
            return faces[variable, WIDTH + index].astype(jnp.float32)
        if index >= own:
            return faces[variable, WIDTH + index - own].astype(jnp.float32)
        return flux_z[variable, index].astype(jnp.float32)

    for variable in range(flux_z.shape[0]):
        for index in range(own):
            total = jnp.zeros(flux_z.shape[2:], jnp.float32)
            for offset in range(WIDTH):
                upper = plane(variable, index + offset + 1)
                lower = plane(variable, index - offset - 1)
                total = total + STENCIL_COEFS[offset] * (upper - lower)
            held[variable, index] = total.astype(jnp.bfloat16)
    for flip, place in ((2, across.at[0]), (3, across.at[1]), (0, stay.at[0]), (1, stay.at[1])):
        place[...] = held[:, pl.ds(partner("px", flip) * planes, planes)]


def cells(axis, flip, width):
    return pl.ds(pl.multiple_of(partner(axis, flip) * width, width), width)


def times(block, line_op, to, of):
    return lax.dot_general(
        block, line_op[to, of], (((1,), (1,)), ((), ())), preferred_element_type=jnp.float32
    )


def blocks_of(stay, across, joined):
    return ((0, stay, 0), (2, across, 0), (1, joined, 0), (3, joined, 1))


def main_kernel(stay, across, joined, own_y, line_op, out_x, out_y, held, sems):
    width = stay.shape[2]
    places = [pl.ds(start, width) for start in range(0, line_op.shape[0], width)]
    copies = [
        pltpu.make_async_copy(line_op.at[place], held.at[place], sems.at[i])
        for i, place in enumerate(places)
    ]
    for copy in copies:
        copy.start()
    for place, copy in zip(places, copies):
        copy.wait()
        total = None
        for flip, ref, index in blocks_of(stay, across, joined):
            part = times(ref[index], held, place, cells("px", flip, width))
            total = part if total is None else total + part
        out_x[:, place] = total
        out_y[:, place] = times(own_y[...], held, place, cells("py", 0, width))


def add_kernel(products, stay, across, joined, out):
    width = stay.shape[2]
    for flip, ref, index in blocks_of(stay, across, joined):
        place = cells("px", flip, width)
        out[:, place] = (products[:, place] + ref[index].astype(jnp.float32)).astype(jnp.bfloat16)


def early_kernel(flips, first, *refs):
    blocks = refs[: len(flips)]
    line_op, out = refs[len(flips) :]
    width = blocks[0].shape[1]
    for start in range(0, out.shape[1], width):
        place = pl.ds(start, width)
        total = first[:, place]
        for flip, block in zip(flips, blocks):
            total = total + times(block[...], line_op, place, cells("py", flip, width))
        out[:, place] = total


def late_kernel(flip, block, early, line_op, out):
    width = block.shape[1]
    rows = out.shape[1]
    for start in range(0, out.shape[2], width):
        place = pl.ds(start, width)
        total = early[:, place] + times(block[...], line_op, place, cells("py", flip, width))
        for group in range(out.shape[0]):
            out[group, :, place] = total[group * rows : (group + 1) * rows].astype(jnp.bfloat16)


def local(flux_x, flux_y, flux_z, line_op):
    variables, slab, lines, x_width = flux_x.shape
    x_count, y_count = lax.axis_size("px"), lax.axis_size("py")
    planes = slab // x_count
    x_lines, y_width = flux_y.shape[2:]
    rows = x_lines // y_count
    line = line_op.shape[0]
    gathered = variables * slab * rows
    lines_x = variables * planes * lines
    bf16 = jnp.bfloat16

    def like(*shape, kind=bf16):
        return jax.ShapeDtypeStruct(shape, kind)

    rows_y = flux_y.reshape(-1, y_width)
    pair_x = like(2, variables, planes, lines, x_width)
    *sent_y, faces, across_x, stay_x, held_z = call(
        functools.partial(pack_kernel, rows, y_count, planes),
        [like(gathered, y_width)] * y_count
        + [like(variables, 2 * WIDTH, lines, x_width), pair_x, pair_x, like(*flux_z.shape)],
        rows_y,
        flux_x,
        flux_z,
        far=(0, 1, 2),
        limit=8,
        scratch=[pltpu.VMEM(rows_y.shape, bf16), pltpu.SemaphoreType.DMA((8,))],
    )
    got_2 = swap(sent_y[2], "py", 2)
    faces = swap(faces, "gz", 1)
    across_x = swap(across_x, "px", 2)
    got_3 = swap(sent_y[3], "py", 3)
    got_1 = swap(sent_y[1], "py", 1)

    across_z, stay_z = call(
        functools.partial(stencil_kernel, planes),
        [pair_x, pair_x],
        held_z,
        faces,
        limit=8,
        flops=STAGE,
        scratch=[pltpu.VMEM(flux_z.shape, bf16)],
    )
    across_z = swap(across_z, "px", 2)
    joined_x = swap(call(join_kernel, pair_x, stay_x, across_x, limit=8, flops=STAGE), "px", 1)
    joined_z = swap(call(join_kernel, pair_x, stay_z, across_z, limit=8, flops=STAGE), "px", 1)

    flat = (2, lines_x, x_width)
    in_x = [a.reshape(flat) for a in (stay_x, across_x, joined_x)]
    in_z = [a.reshape(flat) for a in (stay_z, across_z, joined_z)]
    products, own_part, held_op = call(
        main_kernel,
        [
            like(lines_x, line, kind=jnp.float32),
            like(gathered, line, kind=jnp.float32),
            like(line, line),
        ],
        *in_x,
        sent_y[0],
        line_op,
        far=(4,),
        limit=24,
        flops=2 * lines_x * line * line + 2 * gathered * y_width * line,
        scratch=[pltpu.SemaphoreType.DMA((line // x_width,))],
    )
    xz_part = call(add_kernel, like(lines_x, line), products, *in_z, limit=8)
    early = call(
        functools.partial(early_kernel, (2, 1)),
        like(gathered, line, kind=jnp.float32),
        own_part,
        got_2,
        got_1,
        held_op,
        limit=24,
        flops=4 * gathered * y_width * line,
    )
    y_part = call(
        functools.partial(late_kernel, 3),
        like(variables * slab, rows, line),
        got_3,
        early,
        held_op,
        limit=24,
        flops=2 * gathered * y_width * line,
    )
    return (
        xz_part.reshape(variables, planes, lines, line),
        y_part.reshape(variables, slab, rows, line),
    )


def solution(mesh):
    fits = mesh.shape["py"] == 4 and mesh.shape["px"] == 4 and mesh.shape["gz"] == 2
    return jax.shard_map(
        local if fits else plain,
        mesh=mesh,
        in_specs=(
            P(None, "gz", "py", "px"),
            P(None, "gz", "px", "py"),
            P(None, "gz", "py", "px"),
            P(),
        ),
        out_specs=(P(None, ("gz", "px"), "py", None), P(None, "gz", ("px", "py"), None)),
        check_vma=False,
    )
```

```python
import functools

import jax
import jax.numpy as jnp
from jax import lax
from jax.experimental import pallas as pl
from jax.experimental.pallas import tpu as pltpu
from jax.sharding import PartitionSpec as P

STENCIL_COEFS = (0.8, -0.2, 4.0 / 105.0, -1.0 / 280.0)
WIDTH = 4
STAGE = 5 * 10**9
MIB = 1 << 20
VMEM = pl.BlockSpec(memory_space=pltpu.VMEM)
FAR = pl.BlockSpec(memory_space=pltpu.HBM)


def with_halo(block, sides, width):
    for axis, dim in sides:
        count = lax.axis_size(axis)
        forward = [(i, i + 1) for i in range(count - 1)]
        forward.append((count - 1, 0))
        backward = [(target, source) for source, target in forward]
        low = lax.ppermute(
            lax.slice_in_dim(block, block.shape[dim] - width, None, axis=dim), axis, forward
        )
        high = lax.ppermute(lax.slice_in_dim(block, 0, width, axis=dim), axis, backward)
        block = jnp.concatenate([low, block, high], axis=dim)
    return block


def line_product(block, line_op):
    return lax.dot_general(
        block, line_op, (((3,), (1,)), ((), ())), preferred_element_type=jnp.float32
    )


def z_stencil(padded, planes):
    widened = padded.astype(jnp.float32)
    total = jnp.zeros((widened.shape[0], planes) + widened.shape[2:], jnp.float32)
    for offset in range(WIDTH):
        reach = offset + 1
        upper = widened[:, WIDTH + reach : WIDTH + reach + planes]
        lower = widened[:, WIDTH - reach : WIDTH - reach + planes]
        total = total + STENCIL_COEFS[offset] * (upper - lower)
    return total.astype(jnp.bfloat16)


def plain(flux_x, flux_y, flux_z, line_op):
    planes = flux_z.shape[1]
    z_deriv = z_stencil(with_halo(flux_z, (("gz", 1),), WIDTH), planes)
    y_part = line_product(
        lax.all_to_all(flux_y, "py", split_axis=2, concat_axis=3, tiled=True), line_op
    ).astype(jnp.bfloat16)
    products = line_product(
        lax.all_to_all(flux_x, "px", split_axis=1, concat_axis=3, tiled=True), line_op
    )
    moved = lax.all_to_all(z_deriv, "px", split_axis=1, concat_axis=3, tiled=True)
    xz_part = (products + moved.astype(jnp.float32)).astype(jnp.bfloat16)
    return (xz_part, y_part)


def partner(axis, flip):
    return lax.axis_index(axis) ^ flip


def swap(block, axis, flip):
    pairs = [(i, i ^ flip) for i in range(lax.axis_size(axis))]
    return lax.ppermute(block, axis, pairs)


def call(kernel, out_shape, *operands, limit, flops=0, scratch=(), far=()):
    moved = sum(a.size * a.dtype.itemsize for a in (*operands, *jax.tree.leaves(out_shape)))
    operands = [
        pltpu.with_memory_space_constraint(a, pltpu.HBM) if index in far else a
        for index, a in enumerate(operands)
    ]
    return pl.pallas_call(
        kernel,
        out_shape=out_shape,
        in_specs=[FAR if index in far else VMEM for index in range(len(operands))],
        out_specs=jax.tree.map(lambda _: VMEM, out_shape),
        scratch_shapes=scratch,
        compiler_params=pltpu.CompilerParams(vmem_limit_bytes=limit * MIB),
        cost_estimate=pl.CostEstimate(flops=flops, bytes_accessed=moved, transcendentals=0),
    )(*operands)


def pick_rows(lines, rows, count, flip, out):
    group = 256
    kept = group // count
    line = lax.broadcasted_iota(jnp.int32, (kept, group), 0)
    source = lax.broadcasted_iota(jnp.int32, (kept, group), 1)
    wanted = (line // rows) * (count * rows) + partner("py", flip) * rows + line % rows
    chosen = (source == wanted).astype(jnp.bfloat16)
    for part in range(lines.shape[0] // group):
        picked = jnp.dot(
            chosen,
            lines[part * group : (part + 1) * group, :],
            preferred_element_type=jnp.float32,
        )
        out[part * kept : (part + 1) * kept, :] = picked.astype(jnp.bfloat16)


def first_kernel(rows, count, planes, flux_y, flux_x, flux_z, *refs):
    sent_y, held_y, faces, across, stay, held_z, sems = refs
    last = flux_z.shape[1] - WIDTH
    moves = [(flux_y, held_y), (flux_z, held_z)]
    moves += [(flux_z.at[:, pl.ds(last, WIDTH)], faces.at[:, :WIDTH])]
    moves += [(flux_z.at[:, :WIDTH], faces.at[:, WIDTH:])]
    for flip, place in ((2, across.at[0]), (3, across.at[1]), (0, stay.at[0]), (1, stay.at[1])):
        moves.append((flux_x.at[:, pl.ds(partner("px", flip) * planes, planes)], place))
    copies = [pltpu.make_async_copy(a, b, sems.at[i]) for i, (a, b) in enumerate(moves)]
    for copy in copies:
        copy.start()
    copies[0].wait()
    pick_rows(held_y, rows, count, 2, sent_y)
    for copy in copies[1:]:
        copy.wait()


def second_kernel(rows, count, flips, flux_y, *outs):
    for flip, out in zip(flips, outs):
        pick_rows(flux_y, rows, count, flip, out)


def join_kernel(stay, got, *refs):
    out = refs[-1]
    out[0] = stay[1]
    out[1] = got[1]


def stencil_kernel(planes, flux_z, faces, across, stay, held):
    own = flux_z.shape[1]

    def plane(variable, index):
        if index < 0:
            return faces[variable, WIDTH + index].astype(jnp.float32)
        if index >= own:
            return faces[variable, WIDTH + index - own].astype(jnp.float32)
        return flux_z[variable, index].astype(jnp.float32)

    for variable in range(flux_z.shape[0]):
        for index in range(own):
            total = jnp.zeros(flux_z.shape[2:], jnp.float32)
            for offset in range(WIDTH):
                upper = plane(variable, index + offset + 1)
                lower = plane(variable, index - offset - 1)
                total = total + STENCIL_COEFS[offset] * (upper - lower)
            held[variable, index] = total.astype(jnp.bfloat16)
    for flip, place in ((2, across.at[0]), (3, across.at[1]), (0, stay.at[0]), (1, stay.at[1])):
        place[...] = held[:, pl.ds(partner("px", flip) * planes, planes)]


def cells(axis, flip, width):
    return pl.ds(pl.multiple_of(partner(axis, flip) * width, width), width)


def times(block, line_op, to, of):
    return lax.dot_general(
        block, line_op[to, of], (((1,), (1,)), ((), ())), preferred_element_type=jnp.float32
    )


def blocks_of(stay, across, joined):
    return ((0, stay, 0), (2, across, 0), (1, joined, 0), (3, joined, 1))


def main_kernel(stay, across, joined, own_y, line_op, out_x, out_y):
    width = stay.shape[2]
    for start in range(0, line_op.shape[0], width):
        place = pl.ds(start, width)
        total = None
        for flip, ref, index in blocks_of(stay, across, joined):
            part = times(ref[index], line_op, place, cells("px", flip, width))
            total = part if total is None else total + part
        out_x[:, place] = total
        out_y[:, place] = times(own_y[...], line_op, place, cells("py", 0, width))


def add_kernel(after, stay, across, joined, products, out):
    width = stay.shape[2]
    for flip, ref, index in blocks_of(stay, across, joined):
        place = cells("px", flip, width)
        out[:, place] = (products[:, place] + ref[index].astype(jnp.float32)).astype(jnp.bfloat16)


def early_kernel(flips, first, *refs):
    blocks = refs[: len(flips)]
    line_op, out = refs[len(flips) :]
    width = blocks[0].shape[1]
    for start in range(0, out.shape[1], width):
        place = pl.ds(start, width)
        total = first[:, place]
        for flip, block in zip(flips, blocks):
            total = total + times(block[...], line_op, place, cells("py", flip, width))
        out[:, place] = total


def late_kernel(flip, block, early, line_op, out):
    width = block.shape[1]
    rows = out.shape[1]
    for start in range(0, out.shape[2], width):
        place = pl.ds(start, width)
        total = early[:, place] + times(block[...], line_op, place, cells("py", flip, width))
        for group in range(out.shape[0]):
            out[group, :, place] = total[group * rows : (group + 1) * rows].astype(jnp.bfloat16)


def local(flux_x, flux_y, flux_z, line_op):
    variables, slab, lines, x_width = flux_x.shape
    x_count, y_count = lax.axis_size("px"), lax.axis_size("py")
    planes = slab // x_count
    x_lines, y_width = flux_y.shape[2:]
    rows = x_lines // y_count
    line = line_op.shape[0]
    gathered = variables * slab * rows
    lines_x = variables * planes * lines
    bf16 = jnp.bfloat16

    def like(*shape, kind=bf16):
        return jax.ShapeDtypeStruct(shape, kind)

    rows_y = flux_y.reshape(-1, y_width)
    chunk_y = like(gathered, y_width)
    pair_x = like(2, variables, planes, lines, x_width)
    sent_2, held_y, faces, across_x, stay_x, held_z = call(
        functools.partial(first_kernel, rows, y_count, planes),
        [
            chunk_y,
            like(*rows_y.shape),
            like(variables, 2 * WIDTH, lines, x_width),
            pair_x,
            pair_x,
            like(*flux_z.shape),
        ],
        rows_y,
        flux_x,
        flux_z,
        far=(0, 1, 2),
        limit=8,
        scratch=[pltpu.SemaphoreType.DMA((8,))],
    )
    got_2 = swap(sent_2, "py", 2)
    faces = swap(faces, "gz", 1)
    across_x = swap(across_x, "px", 2)
    sent_3, sent_1, own_y = call(
        functools.partial(second_kernel, rows, y_count, (3, 1, 0)),
        [chunk_y] * 3,
        held_y,
        limit=8,
        flops=STAGE,
    )
    got_3 = swap(sent_3, "py", 3)
    got_1 = swap(sent_1, "py", 1)

    joined_x = swap(call(join_kernel, pair_x, stay_x, across_x, limit=8, flops=STAGE), "px", 1)
    flat = (2, lines_x, x_width)
    products, own_part = call(
        main_kernel,
        [like(lines_x, line, kind=jnp.float32), like(gathered, line, kind=jnp.float32)],
        *(a.reshape(flat) for a in (stay_x, across_x, joined_x)),
        own_y,
        line_op,
        limit=16,
        flops=STAGE,
    )
    across_z, stay_z = call(
        functools.partial(stencil_kernel, planes),
        [pair_x, pair_x],
        held_z,
        faces,
        limit=8,
        flops=STAGE,
        scratch=[pltpu.VMEM(flux_z.shape, bf16)],
    )
    across_z = swap(across_z, "px", 2)
    joined_z = swap(
        call(join_kernel, pair_x, stay_z, across_z, products, limit=8, flops=STAGE), "px", 1
    )
    xz_part = call(
        add_kernel,
        like(lines_x, line),
        got_2,
        *(a.reshape(flat) for a in (stay_z, across_z, joined_z)),
        products,
        limit=8,
    )
    early = call(
        functools.partial(early_kernel, (2, 1)),
        like(gathered, line, kind=jnp.float32),
        own_part,
        got_2,
        got_1,
        line_op,
        limit=16,
        flops=4 * gathered * y_width * line,
    )
    y_part = call(
        functools.partial(late_kernel, 3),
        like(variables * slab, rows, line),
        got_3,
        early,
        line_op,
        limit=16,
        flops=2 * gathered * y_width * line,
    )
    return (
        xz_part.reshape(variables, planes, lines, line),
        y_part.reshape(variables, slab, rows, line),
    )


def solution(mesh):
    fits = mesh.shape["py"] == 4 and mesh.shape["px"] == 4 and mesh.shape["gz"] == 2
    return jax.shard_map(
        local if fits else plain,
        mesh=mesh,
        in_specs=(
            P(None, "gz", "py", "px"),
            P(None, "gz", "px", "py"),
            P(None, "gz", "py", "px"),
            P(),
        ),
        out_specs=(P(None, ("gz", "px"), "py", None), P(None, "gz", ("px", "py"), None)),
        check_vma=False,
    )
```

```python
import functools

import jax
import jax.numpy as jnp
from jax import lax
from jax.experimental import pallas as pl
from jax.experimental.pallas import tpu as pltpu
from jax.sharding import PartitionSpec as P

STENCIL_COEFS = (0.8, -0.2, 4.0 / 105.0, -1.0 / 280.0)
WIDTH = 4
STAGE = 5 * 10**9
MIB = 1 << 20
VMEM = pl.BlockSpec(memory_space=pltpu.VMEM)
FAR = pl.BlockSpec(memory_space=pltpu.HBM)


def with_halo(block, sides, width):
    for axis, dim in sides:
        count = lax.axis_size(axis)
        forward = [(i, i + 1) for i in range(count - 1)]
        forward.append((count - 1, 0))
        backward = [(target, source) for source, target in forward]
        low = lax.ppermute(
            lax.slice_in_dim(block, block.shape[dim] - width, None, axis=dim), axis, forward
        )
        high = lax.ppermute(lax.slice_in_dim(block, 0, width, axis=dim), axis, backward)
        block = jnp.concatenate([low, block, high], axis=dim)
    return block


def line_product(block, line_op):
    return lax.dot_general(
        block, line_op, (((3,), (1,)), ((), ())), preferred_element_type=jnp.float32
    )


def z_stencil(padded, planes):
    widened = padded.astype(jnp.float32)
    total = jnp.zeros((widened.shape[0], planes) + widened.shape[2:], jnp.float32)
    for offset in range(WIDTH):
        reach = offset + 1
        upper = widened[:, WIDTH + reach : WIDTH + reach + planes]
        lower = widened[:, WIDTH - reach : WIDTH - reach + planes]
        total = total + STENCIL_COEFS[offset] * (upper - lower)
    return total.astype(jnp.bfloat16)


def plain(flux_x, flux_y, flux_z, line_op):
    planes = flux_z.shape[1]
    z_deriv = z_stencil(with_halo(flux_z, (("gz", 1),), WIDTH), planes)
    y_part = line_product(
        lax.all_to_all(flux_y, "py", split_axis=2, concat_axis=3, tiled=True), line_op
    ).astype(jnp.bfloat16)
    products = line_product(
        lax.all_to_all(flux_x, "px", split_axis=1, concat_axis=3, tiled=True), line_op
    )
    moved = lax.all_to_all(z_deriv, "px", split_axis=1, concat_axis=3, tiled=True)
    xz_part = (products + moved.astype(jnp.float32)).astype(jnp.bfloat16)
    return (xz_part, y_part)


def partner(axis, flip):
    return lax.axis_index(axis) ^ flip


def swap(block, axis, flip):
    pairs = [(i, i ^ flip) for i in range(lax.axis_size(axis))]
    return lax.ppermute(block, axis, pairs)


def call(kernel, out_shape, *operands, limit, flops=0, scratch=(), far=()):
    moved = sum(a.size * a.dtype.itemsize for a in (*operands, *jax.tree.leaves(out_shape)))
    operands = [
        pltpu.with_memory_space_constraint(a, pltpu.HBM) if index in far else a
        for index, a in enumerate(operands)
    ]
    return pl.pallas_call(
        kernel,
        out_shape=out_shape,
        in_specs=[FAR if index in far else VMEM for index in range(len(operands))],
        out_specs=jax.tree.map(lambda _: VMEM, out_shape),
        scratch_shapes=scratch,
        compiler_params=pltpu.CompilerParams(vmem_limit_bytes=limit * MIB),
        cost_estimate=pl.CostEstimate(flops=flops, bytes_accessed=moved, transcendentals=0),
    )(*operands)


def pick_rows(lines, rows, count, flip, out):
    group = 256
    kept = group // count
    line = lax.broadcasted_iota(jnp.int32, (kept, group), 0)
    source = lax.broadcasted_iota(jnp.int32, (kept, group), 1)
    wanted = (line // rows) * (count * rows) + partner("py", flip) * rows + line % rows
    chosen = (source == wanted).astype(jnp.bfloat16)
    for part in range(lines.shape[0] // group):
        picked = jnp.dot(
            chosen,
            lines[part * group : (part + 1) * group, :],
            preferred_element_type=jnp.float32,
        )
        out[part * kept : (part + 1) * kept, :] = picked.astype(jnp.bfloat16)


def first_kernel(rows, count, planes, flux_y, flux_x, flux_z, *refs):
    *sent_y, held_y, faces, across, stay, held_z, sems = refs
    last = flux_z.shape[1] - WIDTH
    moves = [(flux_y, held_y), (flux_z, held_z)]
    moves += [(flux_z.at[:, pl.ds(last, WIDTH)], faces.at[:, :WIDTH])]
    moves += [(flux_z.at[:, :WIDTH], faces.at[:, WIDTH:])]
    for flip, place in ((2, across.at[0]), (3, across.at[1]), (0, stay.at[0]), (1, stay.at[1])):
        moves.append((flux_x.at[:, pl.ds(partner("px", flip) * planes, planes)], place))
    copies = [pltpu.make_async_copy(a, b, sems.at[i]) for i, (a, b) in enumerate(moves)]
    for copy in copies:
        copy.start()
    copies[0].wait()
    for flip, out in zip((2, 3), sent_y):
        pick_rows(held_y, rows, count, flip, out)
    for copy in copies[1:]:
        copy.wait()


def second_kernel(rows, count, flips, flux_y, *outs):
    for flip, out in zip(flips, outs):
        pick_rows(flux_y, rows, count, flip, out)


def join_kernel(stay, got, *refs):
    out = refs[-1]
    out[0] = stay[1]
    out[1] = got[1]


def stencil_kernel(planes, flux_z, faces, across, stay, held):
    own = flux_z.shape[1]

    def plane(variable, index):
        if index < 0:
            return faces[variable, WIDTH + index].astype(jnp.float32)
        if index >= own:
            return faces[variable, WIDTH + index - own].astype(jnp.float32)
        return flux_z[variable, index].astype(jnp.float32)

    for variable in range(flux_z.shape[0]):
        for index in range(own):
            total = jnp.zeros(flux_z.shape[2:], jnp.float32)
            for offset in range(WIDTH):
                upper = plane(variable, index + offset + 1)
                lower = plane(variable, index - offset - 1)
                total = total + STENCIL_COEFS[offset] * (upper - lower)
            held[variable, index] = total.astype(jnp.bfloat16)
    for flip, place in ((2, across.at[0]), (3, across.at[1]), (0, stay.at[0]), (1, stay.at[1])):
        place[...] = held[:, pl.ds(partner("px", flip) * planes, planes)]


def cells(axis, flip, width):
    return pl.ds(pl.multiple_of(partner(axis, flip) * width, width), width)


def times(block, line_op, to, of):
    return lax.dot_general(
        block, line_op[to, of], (((1,), (1,)), ((), ())), preferred_element_type=jnp.float32
    )


def blocks_of(stay, across, joined):
    return ((0, stay, 0), (2, across, 0), (1, joined, 0), (3, joined, 1))


def main_kernel(stay, across, joined, own_y, line_op, out_x, out_y):
    width = stay.shape[2]
    for start in range(0, line_op.shape[0], width):
        place = pl.ds(start, width)
        total = None
        for flip, ref, index in blocks_of(stay, across, joined):
            part = times(ref[index], line_op, place, cells("px", flip, width))
            total = part if total is None else total + part
        out_x[:, place] = total
        out_y[:, place] = times(own_y[...], line_op, place, cells("py", 0, width))


def add_kernel(after, stay, across, joined, products, out):
    width = stay.shape[2]
    for flip, ref, index in blocks_of(stay, across, joined):
        place = cells("px", flip, width)
        out[:, place] = (products[:, place] + ref[index].astype(jnp.float32)).astype(jnp.bfloat16)


def step_kernel(flip, block, before, line_op, *refs):
    out = refs[-1]
    width = block.shape[1]
    for start in range(0, out.shape[1], width):
        place = pl.ds(start, width)
        part = times(block[...], line_op, place, cells("py", flip, width))
        out[:, place] = before[:, place] + part


def late_kernel(flip, block, early, line_op, out):
    width = block.shape[1]
    rows = out.shape[1]
    for start in range(0, out.shape[2], width):
        place = pl.ds(start, width)
        total = early[:, place] + times(block[...], line_op, place, cells("py", flip, width))
        for group in range(out.shape[0]):
            out[group, :, place] = total[group * rows : (group + 1) * rows].astype(jnp.bfloat16)


def local(flux_x, flux_y, flux_z, line_op):
    variables, slab, lines, x_width = flux_x.shape
    x_count, y_count = lax.axis_size("px"), lax.axis_size("py")
    planes = slab // x_count
    x_lines, y_width = flux_y.shape[2:]
    rows = x_lines // y_count
    line = line_op.shape[0]
    gathered = variables * slab * rows
    lines_x = variables * planes * lines
    bf16 = jnp.bfloat16

    def like(*shape, kind=bf16):
        return jax.ShapeDtypeStruct(shape, kind)

    rows_y = flux_y.reshape(-1, y_width)
    chunk_y = like(gathered, y_width)
    pair_x = like(2, variables, planes, lines, x_width)
    sent_2, sent_3, held_y, faces, across_x, stay_x, held_z = call(
        functools.partial(first_kernel, rows, y_count, planes),
        [
            chunk_y,
            chunk_y,
            like(*rows_y.shape),
            like(variables, 2 * WIDTH, lines, x_width),
            pair_x,
            pair_x,
            like(*flux_z.shape),
        ],
        rows_y,
        flux_x,
        flux_z,
        far=(0, 1, 2),
        limit=8,
        scratch=[pltpu.SemaphoreType.DMA((8,))],
    )
    got_2 = swap(sent_2, "py", 2)
    got_3 = swap(sent_3, "py", 3)
    faces = swap(faces, "gz", 1)
    across_x = swap(across_x, "px", 2)
    sent_1, own_y = call(
        functools.partial(second_kernel, rows, y_count, (1, 0)),
        [chunk_y] * 2,
        held_y,
        limit=8,
        flops=STAGE,
    )
    got_1 = swap(sent_1, "py", 1)

    joined_x = swap(call(join_kernel, pair_x, stay_x, across_x, limit=8, flops=STAGE), "px", 1)
    flat = (2, lines_x, x_width)
    products, own_part = call(
        main_kernel,
        [like(lines_x, line, kind=jnp.float32), like(gathered, line, kind=jnp.float32)],
        *(a.reshape(flat) for a in (stay_x, across_x, joined_x)),
        own_y,
        line_op,
        limit=16,
        flops=STAGE,
    )
    across_z, stay_z = call(
        functools.partial(stencil_kernel, planes),
        [pair_x, pair_x],
        held_z,
        faces,
        limit=8,
        flops=STAGE,
        scratch=[pltpu.VMEM(flux_z.shape, bf16)],
    )
    across_z = swap(across_z, "px", 2)
    joined_z = swap(
        call(join_kernel, pair_x, stay_z, across_z, products, limit=8, flops=STAGE), "px", 1
    )
    partial = like(gathered, line, kind=jnp.float32)
    block_flops = 2 * gathered * y_width * line
    sum_2 = call(
        functools.partial(step_kernel, 2),
        partial,
        got_2,
        own_part,
        line_op,
        limit=16,
        flops=STAGE,
    )
    xz_part = call(
        add_kernel,
        like(lines_x, line),
        sum_2,
        *(a.reshape(flat) for a in (stay_z, across_z, joined_z)),
        products,
        limit=8,
    )
    sum_1 = call(
        functools.partial(step_kernel, 1),
        partial,
        got_1,
        sum_2,
        line_op,
        xz_part,
        far=(3,),
        limit=16,
        flops=block_flops,
    )
    y_part = call(
        functools.partial(late_kernel, 3),
        like(variables * slab, rows, line),
        got_3,
        sum_1,
        line_op,
        limit=16,
        flops=block_flops,
    )
    y_part, xz_part = lax.optimization_barrier((y_part, xz_part))
    return (
        xz_part.reshape(variables, planes, lines, line),
        y_part.reshape(variables, slab, rows, line),
    )


def solution(mesh):
    fits = mesh.shape["py"] == 4 and mesh.shape["px"] == 4 and mesh.shape["gz"] == 2
    return jax.shard_map(
        local if fits else plain,
        mesh=mesh,
        in_specs=(
            P(None, "gz", "py", "px"),
            P(None, "gz", "px", "py"),
            P(None, "gz", "py", "px"),
            P(),
        ),
        out_specs=(P(None, ("gz", "px"), "py", None), P(None, "gz", ("px", "py"), None)),
        check_vma=False,
    )
```

```python
import functools

import jax
import jax.numpy as jnp
from jax import lax
from jax.experimental import pallas as pl
from jax.experimental.pallas import tpu as pltpu
from jax.sharding import PartitionSpec as P

STENCIL_COEFS = (0.8, -0.2, 4.0 / 105.0, -1.0 / 280.0)
WIDTH = 4
STAGE = 3 * 10**9
MIB = 1 << 20
VMEM = pl.BlockSpec(memory_space=pltpu.VMEM)
FAR = pl.BlockSpec(memory_space=pltpu.HBM)


def with_halo(block, sides, width):
    for axis, dim in sides:
        count = lax.axis_size(axis)
        forward = [(i, i + 1) for i in range(count - 1)]
        forward.append((count - 1, 0))
        backward = [(target, source) for source, target in forward]
        low = lax.ppermute(
            lax.slice_in_dim(block, block.shape[dim] - width, None, axis=dim), axis, forward
        )
        high = lax.ppermute(lax.slice_in_dim(block, 0, width, axis=dim), axis, backward)
        block = jnp.concatenate([low, block, high], axis=dim)
    return block


def line_product(block, line_op):
    return lax.dot_general(
        block, line_op, (((3,), (1,)), ((), ())), preferred_element_type=jnp.float32
    )


def z_stencil(padded, planes):
    widened = padded.astype(jnp.float32)
    total = jnp.zeros((widened.shape[0], planes) + widened.shape[2:], jnp.float32)
    for offset in range(WIDTH):
        reach = offset + 1
        upper = widened[:, WIDTH + reach : WIDTH + reach + planes]
        lower = widened[:, WIDTH - reach : WIDTH - reach + planes]
        total = total + STENCIL_COEFS[offset] * (upper - lower)
    return total.astype(jnp.bfloat16)


def plain(flux_x, flux_y, flux_z, line_op):
    planes = flux_z.shape[1]
    z_deriv = z_stencil(with_halo(flux_z, (("gz", 1),), WIDTH), planes)
    y_part = line_product(
        lax.all_to_all(flux_y, "py", split_axis=2, concat_axis=3, tiled=True), line_op
    ).astype(jnp.bfloat16)
    products = line_product(
        lax.all_to_all(flux_x, "px", split_axis=1, concat_axis=3, tiled=True), line_op
    )
    moved = lax.all_to_all(z_deriv, "px", split_axis=1, concat_axis=3, tiled=True)
    xz_part = (products + moved.astype(jnp.float32)).astype(jnp.bfloat16)
    return (xz_part, y_part)


def partner(axis, flip):
    return lax.axis_index(axis) ^ flip


def swap(block, axis, flip):
    pairs = [(i, i ^ flip) for i in range(lax.axis_size(axis))]
    return lax.ppermute(block, axis, pairs)


def call(kernel, out_shape, *operands, limit, flops=0, scratch=(), far=()):
    moved = sum(a.size * a.dtype.itemsize for a in (*operands, *jax.tree.leaves(out_shape)))
    operands = [
        pltpu.with_memory_space_constraint(a, pltpu.HBM) if index in far else a
        for index, a in enumerate(operands)
    ]
    return pl.pallas_call(
        kernel,
        out_shape=out_shape,
        in_specs=[FAR if index in far else VMEM for index in range(len(operands))],
        out_specs=jax.tree.map(lambda _: VMEM, out_shape),
        scratch_shapes=scratch,
        compiler_params=pltpu.CompilerParams(vmem_limit_bytes=limit * MIB),
        cost_estimate=pl.CostEstimate(flops=flops, bytes_accessed=moved, transcendentals=0),
    )(*operands)


def pick_rows(lines, rows, count, flip, out):
    group = 256
    kept = group // count
    line = lax.broadcasted_iota(jnp.int32, (kept, group), 0)
    source = lax.broadcasted_iota(jnp.int32, (kept, group), 1)
    wanted = (line // rows) * (count * rows) + partner("py", flip) * rows + line % rows
    chosen = (source == wanted).astype(jnp.bfloat16)
    for part in range(lines.shape[0] // group):
        picked = jnp.dot(
            chosen,
            lines[part * group : (part + 1) * group, :],
            preferred_element_type=jnp.float32,
        )
        out[part * kept : (part + 1) * kept, :] = picked.astype(jnp.bfloat16)


def first_kernel(rows, count, planes, flux_y, flux_x, flux_z, *refs):
    sent_y, held_y, faces, across, stay, held_z, sems = refs
    last = flux_z.shape[1] - WIDTH
    moves = [(flux_y, held_y), (flux_z, held_z)]
    moves += [(flux_z.at[:, pl.ds(last, WIDTH)], faces.at[:, :WIDTH])]
    moves += [(flux_z.at[:, :WIDTH], faces.at[:, WIDTH:])]
    for flip, place in ((2, across.at[0]), (3, across.at[1]), (0, stay.at[0]), (1, stay.at[1])):
        moves.append((flux_x.at[:, pl.ds(partner("px", flip) * planes, planes)], place))
    copies = [pltpu.make_async_copy(a, b, sems.at[i]) for i, (a, b) in enumerate(moves)]
    for copy in copies:
        copy.start()
    copies[0].wait()
    pick_rows(held_y, rows, count, 2, sent_y)
    for copy in copies[1:]:
        copy.wait()


def second_kernel(rows, count, flips, flux_y, *outs):
    for flip, out in zip(flips, outs):
        pick_rows(flux_y, rows, count, flip, out)


def join_kernel(stay, got, *refs):
    out = refs[-1]
    out[0] = stay[1]
    out[1] = got[1]


def third_kernel(rows, count, flip, flux_y, stay, got, sent_y, out):
    pick_rows(flux_y, rows, count, flip, sent_y)
    join_kernel(stay, got, out)


def stencil_kernel(planes, flux_z, faces, across, stay, held):
    own = flux_z.shape[1]

    def plane(variable, index):
        if index < 0:
            return faces[variable, WIDTH + index].astype(jnp.float32)
        if index >= own:
            return faces[variable, WIDTH + index - own].astype(jnp.float32)
        return flux_z[variable, index].astype(jnp.float32)

    for variable in range(flux_z.shape[0]):
        for index in range(own):
            total = jnp.zeros(flux_z.shape[2:], jnp.float32)
            for offset in range(WIDTH):
                upper = plane(variable, index + offset + 1)
                lower = plane(variable, index - offset - 1)
                total = total + STENCIL_COEFS[offset] * (upper - lower)
            held[variable, index] = total.astype(jnp.bfloat16)
    for flip, place in ((2, across.at[0]), (3, across.at[1]), (0, stay.at[0]), (1, stay.at[1])):
        place[...] = held[:, pl.ds(partner("px", flip) * planes, planes)]


def cells(axis, flip, width):
    return pl.ds(pl.multiple_of(partner(axis, flip) * width, width), width)


def times(block, line_op, to, of):
    return lax.dot_general(
        block, line_op[to, of], (((1,), (1,)), ((), ())), preferred_element_type=jnp.float32
    )


def blocks_of(stay, across, joined):
    return ((0, stay, 0), (2, across, 0), (1, joined, 0), (3, joined, 1))


def main_kernel(stay, across, joined, own_y, line_op, out_x, out_y):
    width = stay.shape[2]
    for start in range(0, line_op.shape[0], width):
        place = pl.ds(start, width)
        total = None
        for flip, ref, index in blocks_of(stay, across, joined):
            part = times(ref[index], line_op, place, cells("px", flip, width))
            total = part if total is None else total + part
        out_x[:, place] = total
        out_y[:, place] = times(own_y[...], line_op, place, cells("py", 0, width))


def add_kernel(after, stay, across, joined, products, out):
    width = stay.shape[2]
    for flip, ref, index in blocks_of(stay, across, joined):
        place = cells("px", flip, width)
        out[:, place] = (products[:, place] + ref[index].astype(jnp.float32)).astype(jnp.bfloat16)


def early_kernel(flips, *refs):
    blocks = refs[: len(flips)]
    own, line_op, out = refs[len(flips) :]
    width = blocks[0].shape[1]
    for start in range(0, out.shape[1], width):
        place = pl.ds(start, width)
        total = own[:, place]
        for flip, block in zip(flips, blocks):
            total = total + times(block[...], line_op, place, cells("py", flip, width))
        out[:, place] = total


def late_kernel(flip, early, block, line_op, after, out):
    width = block.shape[1]
    rows = out.shape[1]
    for start in range(0, out.shape[2], width):
        place = pl.ds(start, width)
        total = early[:, place] + times(block[...], line_op, place, cells("py", flip, width))
        for group in range(out.shape[0]):
            out[group, :, place] = total[group * rows : (group + 1) * rows].astype(jnp.bfloat16)


def local(flux_x, flux_y, flux_z, line_op):
    variables, slab, lines, x_width = flux_x.shape
    x_count, y_count = lax.axis_size("px"), lax.axis_size("py")
    planes = slab // x_count
    x_lines, y_width = flux_y.shape[2:]
    rows = x_lines // y_count
    line = line_op.shape[0]
    gathered = variables * slab * rows
    lines_x = variables * planes * lines
    bf16 = jnp.bfloat16

    def like(*shape, kind=bf16):
        return jax.ShapeDtypeStruct(shape, kind)

    rows_y = flux_y.reshape(-1, y_width)
    chunk_y = like(gathered, y_width)
    pair_x = like(2, variables, planes, lines, x_width)
    sent_2, held_y, faces, across_x, stay_x, held_z = call(
        functools.partial(first_kernel, rows, y_count, planes),
        [
            chunk_y,
            like(*rows_y.shape),
            like(variables, 2 * WIDTH, lines, x_width),
            pair_x,
            pair_x,
            like(*flux_z.shape),
        ],
        rows_y,
        flux_x,
        flux_z,
        far=(0, 1, 2),
        limit=8,
        scratch=[pltpu.SemaphoreType.DMA((8,))],
    )
    got_2 = swap(sent_2, "py", 2)
    faces = swap(faces, "gz", 1)
    across_x = swap(across_x, "px", 2)
    sent_1, own_y = call(
        functools.partial(second_kernel, rows, y_count, (1, 0)),
        [chunk_y] * 2,
        held_y,
        limit=8,
        flops=STAGE,
    )
    got_1 = swap(sent_1, "py", 1)

    sent_3, joined_x = call(
        functools.partial(third_kernel, rows, y_count, 3),
        [chunk_y, pair_x],
        held_y,
        stay_x,
        across_x,
        limit=8,
        flops=STAGE,
    )
    got_3 = swap(sent_3, "py", 3)
    joined_x = swap(joined_x, "px", 1)
    flat = (2, lines_x, x_width)
    products, own_part = call(
        main_kernel,
        [like(lines_x, line, kind=jnp.float32), like(gathered, line, kind=jnp.float32)],
        *(a.reshape(flat) for a in (stay_x, across_x, joined_x)),
        own_y,
        line_op,
        limit=16,
        flops=STAGE,
    )
    across_z, stay_z = call(
        functools.partial(stencil_kernel, planes),
        [pair_x, pair_x],
        held_z,
        faces,
        limit=8,
        flops=STAGE,
        scratch=[pltpu.VMEM(flux_z.shape, bf16)],
    )
    across_z = swap(across_z, "px", 2)
    joined_z = swap(
        call(join_kernel, pair_x, stay_z, across_z, products, limit=8, flops=STAGE), "px", 1
    )
    early = call(
        functools.partial(early_kernel, (2, 1)),
        like(gathered, line, kind=jnp.float32),
        got_2,
        got_1,
        own_part,
        line_op,
        limit=16,
        flops=STAGE,
    )
    xz_part = call(
        add_kernel,
        like(lines_x, line),
        early,
        *(a.reshape(flat) for a in (stay_z, across_z, joined_z)),
        products,
        limit=8,
    )
    y_part = call(
        functools.partial(late_kernel, 3),
        like(variables * slab, rows, line),
        early,
        got_3,
        line_op,
        xz_part,
        far=(3,),
        limit=16,
        flops=2 * gathered * y_width * line,
    )
    y_part, xz_part = lax.optimization_barrier((y_part, xz_part))
    return (
        xz_part.reshape(variables, planes, lines, line),
        y_part.reshape(variables, slab, rows, line),
    )


def solution(mesh):
    fits = mesh.shape["py"] == 4 and mesh.shape["px"] == 4 and mesh.shape["gz"] == 2
    return jax.shard_map(
        local if fits else plain,
        mesh=mesh,
        in_specs=(
            P(None, "gz", "py", "px"),
            P(None, "gz", "px", "py"),
            P(None, "gz", "py", "px"),
            P(),
        ),
        out_specs=(P(None, ("gz", "px"), "py", None), P(None, "gz", ("px", "py"), None)),
        check_vma=False,
    )
```

```python
import functools

import jax
import jax.numpy as jnp
from jax import lax
from jax.experimental import pallas as pl
from jax.experimental.pallas import tpu as pltpu
from jax.sharding import PartitionSpec as P

STENCIL_COEFS = (0.8, -0.2, 4.0 / 105.0, -1.0 / 280.0)
WIDTH = 4
STAGE = 3 * 10**9
MIB = 1 << 20
VMEM = pl.BlockSpec(memory_space=pltpu.VMEM)
FAR = pl.BlockSpec(memory_space=pltpu.HBM)


def with_halo(block, sides, width):
    for axis, dim in sides:
        count = lax.axis_size(axis)
        forward = [(i, i + 1) for i in range(count - 1)]
        forward.append((count - 1, 0))
        backward = [(target, source) for source, target in forward]
        low = lax.ppermute(
            lax.slice_in_dim(block, block.shape[dim] - width, None, axis=dim), axis, forward
        )
        high = lax.ppermute(lax.slice_in_dim(block, 0, width, axis=dim), axis, backward)
        block = jnp.concatenate([low, block, high], axis=dim)
    return block


def line_product(block, line_op):
    return lax.dot_general(
        block, line_op, (((3,), (1,)), ((), ())), preferred_element_type=jnp.float32
    )


def z_stencil(padded, planes):
    widened = padded.astype(jnp.float32)
    total = jnp.zeros((widened.shape[0], planes) + widened.shape[2:], jnp.float32)
    for offset in range(WIDTH):
        reach = offset + 1
        upper = widened[:, WIDTH + reach : WIDTH + reach + planes]
        lower = widened[:, WIDTH - reach : WIDTH - reach + planes]
        total = total + STENCIL_COEFS[offset] * (upper - lower)
    return total.astype(jnp.bfloat16)


def plain(flux_x, flux_y, flux_z, line_op):
    planes = flux_z.shape[1]
    z_deriv = z_stencil(with_halo(flux_z, (("gz", 1),), WIDTH), planes)
    y_part = line_product(
        lax.all_to_all(flux_y, "py", split_axis=2, concat_axis=3, tiled=True), line_op
    ).astype(jnp.bfloat16)
    products = line_product(
        lax.all_to_all(flux_x, "px", split_axis=1, concat_axis=3, tiled=True), line_op
    )
    moved = lax.all_to_all(z_deriv, "px", split_axis=1, concat_axis=3, tiled=True)
    xz_part = (products + moved.astype(jnp.float32)).astype(jnp.bfloat16)
    return (xz_part, y_part)


def partner(axis, flip):
    return lax.axis_index(axis) ^ flip


def swap(block, axis, flip):
    pairs = [(i, i ^ flip) for i in range(lax.axis_size(axis))]
    return lax.ppermute(block, axis, pairs)


def call(kernel, out_shape, *operands, limit, flops=0, scratch=(), far=()):
    moved = sum(a.size * a.dtype.itemsize for a in (*operands, *jax.tree.leaves(out_shape)))
    operands = [
        pltpu.with_memory_space_constraint(a, pltpu.HBM) if index in far else a
        for index, a in enumerate(operands)
    ]
    return pl.pallas_call(
        kernel,
        out_shape=out_shape,
        in_specs=[FAR if index in far else VMEM for index in range(len(operands))],
        out_specs=jax.tree.map(lambda _: VMEM, out_shape),
        scratch_shapes=scratch,
        compiler_params=pltpu.CompilerParams(vmem_limit_bytes=limit * MIB),
        cost_estimate=pl.CostEstimate(flops=flops, bytes_accessed=moved, transcendentals=0),
    )(*operands)


def pick_rows(lines, rows, count, flip, out):
    group = 256
    kept = group // count
    line = lax.broadcasted_iota(jnp.int32, (kept, group), 0)
    source = lax.broadcasted_iota(jnp.int32, (kept, group), 1)
    wanted = (line // rows) * (count * rows) + partner("py", flip) * rows + line % rows
    chosen = (source == wanted).astype(jnp.bfloat16)
    for part in range(lines.shape[0] // group):
        picked = jnp.dot(
            chosen,
            lines[part * group : (part + 1) * group, :],
            preferred_element_type=jnp.float32,
        )
        out[part * kept : (part + 1) * kept, :] = picked.astype(jnp.bfloat16)


def first_kernel(rows, count, planes, flux_y, flux_x, flux_z, *refs):
    sent_y, held_y, faces, across, stay, held_z, sems = refs
    last = flux_z.shape[1] - WIDTH
    moves = [(flux_y, held_y), (flux_z, held_z)]
    moves += [(flux_z.at[:, pl.ds(last, WIDTH)], faces.at[:, :WIDTH])]
    moves += [(flux_z.at[:, :WIDTH], faces.at[:, WIDTH:])]
    for flip, place in ((2, across.at[0]), (3, across.at[1]), (0, stay.at[0]), (1, stay.at[1])):
        moves.append((flux_x.at[:, pl.ds(partner("px", flip) * planes, planes)], place))
    copies = [pltpu.make_async_copy(a, b, sems.at[i]) for i, (a, b) in enumerate(moves)]
    for copy in copies:
        copy.start()
    copies[0].wait()
    pick_rows(held_y, rows, count, 2, sent_y)
    for copy in copies[1:]:
        copy.wait()


def second_kernel(rows, count, flips, flux_y, *outs):
    for flip, out in zip(flips, outs):
        pick_rows(flux_y, rows, count, flip, out)


def join_kernel(stay, got, *refs):
    out = refs[-1]
    out[0] = stay[1]
    out[1] = got[1]


def stencil_kernel(planes, flux_z, faces, across, stay, held):
    own = flux_z.shape[1]

    def plane(variable, index):
        if index < 0:
            return faces[variable, WIDTH + index].astype(jnp.float32)
        if index >= own:
            return faces[variable, WIDTH + index - own].astype(jnp.float32)
        return flux_z[variable, index].astype(jnp.float32)

    for variable in range(flux_z.shape[0]):
        for index in range(own):
            total = jnp.zeros(flux_z.shape[2:], jnp.float32)
            for offset in range(WIDTH):
                upper = plane(variable, index + offset + 1)
                lower = plane(variable, index - offset - 1)
                total = total + STENCIL_COEFS[offset] * (upper - lower)
            held[variable, index] = total.astype(jnp.bfloat16)
    for flip, place in ((2, across.at[0]), (3, across.at[1]), (0, stay.at[0]), (1, stay.at[1])):
        place[...] = held[:, pl.ds(partner("px", flip) * planes, planes)]


def cells(axis, flip, width):
    return pl.ds(pl.multiple_of(partner(axis, flip) * width, width), width)


def times(block, line_op, to, of):
    return lax.dot_general(
        block, line_op[to, of], (((1,), (1,)), ((), ())), preferred_element_type=jnp.float32
    )


def blocks_of(stay, across, joined):
    return ((0, stay, 0), (2, across, 0), (1, joined, 0), (3, joined, 1))


def own_kernel(rows, count, flip, flux_y, stay, own_y, line_op, sent_y, out_x, out_y):
    pick_rows(flux_y, rows, count, flip, sent_y)
    width = stay.shape[2]
    for start in range(0, line_op.shape[0], width):
        place = pl.ds(start, width)
        out_x[:, place] = times(stay[0], line_op, place, cells("px", 0, width))
        out_y[:, place] = times(own_y[...], line_op, place, cells("py", 0, width))


def main_kernel(own, across, joined, line_op, out):
    width = across.shape[2]
    for start in range(0, line_op.shape[0], width):
        place = pl.ds(start, width)
        total = own[:, place]
        for flip, ref, index in blocks_of(None, across, joined)[1:]:
            total = total + times(ref[index], line_op, place, cells("px", flip, width))
        out[:, place] = total


def add_kernel(after, stay, across, joined, products, out):
    width = stay.shape[2]
    for flip, ref, index in blocks_of(stay, across, joined):
        place = cells("px", flip, width)
        out[:, place] = (products[:, place] + ref[index].astype(jnp.float32)).astype(jnp.bfloat16)


def early_kernel(flips, *refs):
    blocks = refs[: len(flips)]
    own, line_op, out = refs[len(flips) :]
    width = blocks[0].shape[1]
    for start in range(0, out.shape[1], width):
        place = pl.ds(start, width)
        total = own[:, place]
        for flip, block in zip(flips, blocks):
            total = total + times(block[...], line_op, place, cells("py", flip, width))
        out[:, place] = total


def late_kernel(flip, early, block, line_op, after, out):
    width = block.shape[1]
    rows = out.shape[1]
    for start in range(0, out.shape[2], width):
        place = pl.ds(start, width)
        total = early[:, place] + times(block[...], line_op, place, cells("py", flip, width))
        for group in range(out.shape[0]):
            out[group, :, place] = total[group * rows : (group + 1) * rows].astype(jnp.bfloat16)


def local(flux_x, flux_y, flux_z, line_op):
    variables, slab, lines, x_width = flux_x.shape
    x_count, y_count = lax.axis_size("px"), lax.axis_size("py")
    planes = slab // x_count
    x_lines, y_width = flux_y.shape[2:]
    rows = x_lines // y_count
    line = line_op.shape[0]
    gathered = variables * slab * rows
    lines_x = variables * planes * lines
    bf16 = jnp.bfloat16

    def like(*shape, kind=bf16):
        return jax.ShapeDtypeStruct(shape, kind)

    rows_y = flux_y.reshape(-1, y_width)
    chunk_y = like(gathered, y_width)
    pair_x = like(2, variables, planes, lines, x_width)
    sent_2, held_y, faces, across_x, stay_x, held_z = call(
        functools.partial(first_kernel, rows, y_count, planes),
        [
            chunk_y,
            like(*rows_y.shape),
            like(variables, 2 * WIDTH, lines, x_width),
            pair_x,
            pair_x,
            like(*flux_z.shape),
        ],
        rows_y,
        flux_x,
        flux_z,
        far=(0, 1, 2),
        limit=8,
        scratch=[pltpu.SemaphoreType.DMA((8,))],
    )
    got_2 = swap(sent_2, "py", 2)
    faces = swap(faces, "gz", 1)
    across_x = swap(across_x, "px", 2)
    sent_1, own_y = call(
        functools.partial(second_kernel, rows, y_count, (1, 0)),
        [chunk_y] * 2,
        held_y,
        limit=8,
        flops=STAGE,
    )
    got_1 = swap(sent_1, "py", 1)

    flat = (2, lines_x, x_width)
    products_like = like(lines_x, line, kind=jnp.float32)
    sums_like = like(gathered, line, kind=jnp.float32)
    sent_3, own_x, own_sum = call(
        functools.partial(own_kernel, rows, y_count, 3),
        [chunk_y, products_like, sums_like],
        held_y,
        stay_x.reshape(flat),
        own_y,
        line_op,
        limit=16,
        flops=STAGE,
    )
    got_3 = swap(sent_3, "py", 3)
    joined_x = swap(
        call(join_kernel, pair_x, stay_x, across_x, own_sum, limit=8, flops=STAGE), "px", 1
    )
    products = call(
        main_kernel,
        products_like,
        own_x,
        across_x.reshape(flat),
        joined_x.reshape(flat),
        line_op,
        limit=16,
        flops=STAGE,
    )
    across_z, stay_z = call(
        functools.partial(stencil_kernel, planes),
        [pair_x, pair_x],
        held_z,
        faces,
        limit=8,
        flops=STAGE,
        scratch=[pltpu.VMEM(flux_z.shape, bf16)],
    )
    across_z = swap(across_z, "px", 2)
    joined_z = swap(
        call(join_kernel, pair_x, stay_z, across_z, products, limit=8, flops=STAGE), "px", 1
    )
    early = call(
        functools.partial(early_kernel, (2, 1)),
        sums_like,
        got_2,
        got_1,
        own_sum,
        line_op,
        limit=16,
        flops=STAGE,
    )
    xz_part = call(
        add_kernel,
        like(lines_x, line),
        early,
        *(a.reshape(flat) for a in (stay_z, across_z, joined_z)),
        products,
        limit=8,
    )
    y_part = call(
        functools.partial(late_kernel, 3),
        like(variables * slab, rows, line),
        early,
        got_3,
        line_op,
        xz_part,
        far=(3,),
        limit=16,
        flops=2 * gathered * y_width * line,
    )
    y_part, xz_part = lax.optimization_barrier((y_part, xz_part))
    return (
        xz_part.reshape(variables, planes, lines, line),
        y_part.reshape(variables, slab, rows, line),
    )


def solution(mesh):
    fits = mesh.shape["py"] == 4 and mesh.shape["px"] == 4 and mesh.shape["gz"] == 2
    return jax.shard_map(
        local if fits else plain,
        mesh=mesh,
        in_specs=(
            P(None, "gz", "py", "px"),
            P(None, "gz", "px", "py"),
            P(None, "gz", "py", "px"),
            P(),
        ),
        out_specs=(P(None, ("gz", "px"), "py", None), P(None, "gz", ("px", "py"), None)),
        check_vma=False,
    )
```

```python
import functools

import jax
import jax.numpy as jnp
from jax import lax
from jax.experimental import pallas as pl
from jax.experimental.pallas import tpu as pltpu
from jax.sharding import PartitionSpec as P

STENCIL_COEFS = (0.8, -0.2, 4.0 / 105.0, -1.0 / 280.0)
WIDTH = 4
STAGE = 3 * 10**9
MIB = 1 << 20
VMEM = pl.BlockSpec(memory_space=pltpu.VMEM)
FAR = pl.BlockSpec(memory_space=pltpu.HBM)


def with_halo(block, sides, width):
    for axis, dim in sides:
        count = lax.axis_size(axis)
        forward = [(i, i + 1) for i in range(count - 1)]
        forward.append((count - 1, 0))
        backward = [(target, source) for source, target in forward]
        low = lax.ppermute(
            lax.slice_in_dim(block, block.shape[dim] - width, None, axis=dim), axis, forward
        )
        high = lax.ppermute(lax.slice_in_dim(block, 0, width, axis=dim), axis, backward)
        block = jnp.concatenate([low, block, high], axis=dim)
    return block


def line_product(block, line_op):
    return lax.dot_general(
        block, line_op, (((3,), (1,)), ((), ())), preferred_element_type=jnp.float32
    )


def z_stencil(padded, planes):
    widened = padded.astype(jnp.float32)
    total = jnp.zeros((widened.shape[0], planes) + widened.shape[2:], jnp.float32)
    for offset in range(WIDTH):
        reach = offset + 1
        upper = widened[:, WIDTH + reach : WIDTH + reach + planes]
        lower = widened[:, WIDTH - reach : WIDTH - reach + planes]
        total = total + STENCIL_COEFS[offset] * (upper - lower)
    return total.astype(jnp.bfloat16)


def plain(flux_x, flux_y, flux_z, line_op):
    planes = flux_z.shape[1]
    z_deriv = z_stencil(with_halo(flux_z, (("gz", 1),), WIDTH), planes)
    y_part = line_product(
        lax.all_to_all(flux_y, "py", split_axis=2, concat_axis=3, tiled=True), line_op
    ).astype(jnp.bfloat16)
    products = line_product(
        lax.all_to_all(flux_x, "px", split_axis=1, concat_axis=3, tiled=True), line_op
    )
    moved = lax.all_to_all(z_deriv, "px", split_axis=1, concat_axis=3, tiled=True)
    xz_part = (products + moved.astype(jnp.float32)).astype(jnp.bfloat16)
    return (xz_part, y_part)


def partner(axis, flip):
    return lax.axis_index(axis) ^ flip


def swap(block, axis, flip):
    pairs = [(i, i ^ flip) for i in range(lax.axis_size(axis))]
    return lax.ppermute(block, axis, pairs)


def call(kernel, out_shape, *operands, limit, flops=0, scratch=(), far=()):
    moved = sum(a.size * a.dtype.itemsize for a in (*operands, *jax.tree.leaves(out_shape)))
    operands = [
        pltpu.with_memory_space_constraint(a, pltpu.HBM) if index in far else a
        for index, a in enumerate(operands)
    ]
    return pl.pallas_call(
        kernel,
        out_shape=out_shape,
        in_specs=[FAR if index in far else VMEM for index in range(len(operands))],
        out_specs=jax.tree.map(lambda _: VMEM, out_shape),
        scratch_shapes=scratch,
        compiler_params=pltpu.CompilerParams(vmem_limit_bytes=limit * MIB),
        cost_estimate=pl.CostEstimate(flops=flops, bytes_accessed=moved, transcendentals=0),
    )(*operands)


def pick_rows(lines, rows, count, flip, out):
    group = 256
    kept = group // count
    line = lax.broadcasted_iota(jnp.int32, (kept, group), 0)
    source = lax.broadcasted_iota(jnp.int32, (kept, group), 1)
    wanted = (line // rows) * (count * rows) + partner("py", flip) * rows + line % rows
    chosen = (source == wanted).astype(jnp.bfloat16)
    for part in range(lines.shape[0] // group):
        picked = jnp.dot(
            chosen,
            lines[part * group : (part + 1) * group, :],
            preferred_element_type=jnp.float32,
        )
        out[part * kept : (part + 1) * kept, :] = picked.astype(jnp.bfloat16)


def first_kernel(rows, count, planes, flux_y, flux_x, flux_z, *refs):
    sent_y, held_y, faces, across, stay, held_z, sems = refs
    last = flux_z.shape[1] - WIDTH
    moves = [(flux_y, held_y), (flux_z, held_z)]
    moves += [(flux_z.at[:, pl.ds(last, WIDTH)], faces.at[:, :WIDTH])]
    moves += [(flux_z.at[:, :WIDTH], faces.at[:, WIDTH:])]
    for flip, place in ((2, across.at[0]), (3, across.at[1]), (0, stay.at[0]), (1, stay.at[1])):
        moves.append((flux_x.at[:, pl.ds(partner("px", flip) * planes, planes)], place))
    copies = [pltpu.make_async_copy(a, b, sems.at[i]) for i, (a, b) in enumerate(moves)]
    for copy in copies:
        copy.start()
    copies[0].wait()
    pick_rows(held_y, rows, count, 2, sent_y)
    for copy in copies[1:]:
        copy.wait()


def second_kernel(rows, count, flips, flux_y, *outs):
    for flip, out in zip(flips, outs):
        pick_rows(flux_y, rows, count, flip, out)


def join_kernel(stay, got, *refs):
    out = refs[-1]
    out[0] = stay[1]
    out[1] = got[1]


def stencil_kernel(planes, flux_z, faces, across, stay, held):
    own = flux_z.shape[1]

    def plane(variable, index):
        if index < 0:
            return faces[variable, WIDTH + index].astype(jnp.float32)
        if index >= own:
            return faces[variable, WIDTH + index - own].astype(jnp.float32)
        return flux_z[variable, index].astype(jnp.float32)

    for variable in range(flux_z.shape[0]):
        for index in range(own):
            total = jnp.zeros(flux_z.shape[2:], jnp.float32)
            for offset in range(WIDTH):
                upper = plane(variable, index + offset + 1)
                lower = plane(variable, index - offset - 1)
                total = total + STENCIL_COEFS[offset] * (upper - lower)
            held[variable, index] = total.astype(jnp.bfloat16)
    for flip, place in ((2, across.at[0]), (3, across.at[1]), (0, stay.at[0]), (1, stay.at[1])):
        place[...] = held[:, pl.ds(partner("px", flip) * planes, planes)]


def cells(axis, flip, width):
    return pl.ds(pl.multiple_of(partner(axis, flip) * width, width), width)


def times(block, line_op, to, of):
    return lax.dot_general(
        block, line_op[to, of], (((1,), (1,)), ((), ())), preferred_element_type=jnp.float32
    )


def blocks_of(stay, across, joined):
    return ((0, stay, 0), (2, across, 0), (1, joined, 0), (3, joined, 1))


def main_kernel(stay, across, joined, own_y, line_op, out_x, out_y):
    width = stay.shape[2]
    for start in range(0, line_op.shape[0], width):
        place = pl.ds(start, width)
        total = None
        for flip, ref, index in blocks_of(stay, across, joined):
            part = times(ref[index], line_op, place, cells("px", flip, width))
            total = part if total is None else total + part
        out_x[:, place] = total
        out_y[:, place] = times(own_y[...], line_op, place, cells("py", 0, width))


def add_kernel(after, stay, across, joined, products, out):
    width = stay.shape[2]
    for flip, ref, index in blocks_of(stay, across, joined):
        place = cells("px", flip, width)
        out[:, place] = (products[:, place] + ref[index].astype(jnp.float32)).astype(jnp.bfloat16)


def early_kernel(flips, *refs):
    blocks = refs[: len(flips)]
    own, line_op, out = refs[len(flips) :]
    width = blocks[0].shape[1]
    for start in range(0, out.shape[1], width):
        place = pl.ds(start, width)
        total = own[:, place]
        for flip, block in zip(flips, blocks):
            total = total + times(block[...], line_op, place, cells("py", flip, width))
        out[:, place] = total


def late_kernel(flip, early, block, line_op, after, out):
    width = block.shape[1]
    rows = out.shape[1]
    for start in range(0, out.shape[2], width):
        place = pl.ds(start, width)
        total = early[:, place] + times(block[...], line_op, place, cells("py", flip, width))
        out[:, :, place] = total.astype(jnp.bfloat16).reshape(-1, rows, width)


def local(flux_x, flux_y, flux_z, line_op):
    variables, slab, lines, x_width = flux_x.shape
    x_count, y_count = lax.axis_size("px"), lax.axis_size("py")
    planes = slab // x_count
    x_lines, y_width = flux_y.shape[2:]
    rows = x_lines // y_count
    line = line_op.shape[0]
    gathered = variables * slab * rows
    lines_x = variables * planes * lines
    bf16 = jnp.bfloat16

    def like(*shape, kind=bf16):
        return jax.ShapeDtypeStruct(shape, kind)

    rows_y = flux_y.reshape(-1, y_width)
    chunk_y = like(gathered, y_width)
    pair_x = like(2, variables, planes, lines, x_width)
    sent_2, held_y, faces, across_x, stay_x, held_z = call(
        functools.partial(first_kernel, rows, y_count, planes),
        [
            chunk_y,
            like(*rows_y.shape),
            like(variables, 2 * WIDTH, lines, x_width),
            pair_x,
            pair_x,
            like(*flux_z.shape),
        ],
        rows_y,
        flux_x,
        flux_z,
        far=(0, 1, 2),
        limit=8,
        scratch=[pltpu.SemaphoreType.DMA((8,))],
    )
    got_2 = swap(sent_2, "py", 2)
    faces = swap(faces, "gz", 1)
    across_x = swap(across_x, "px", 2)
    sent_1, sent_3, own_y = call(
        functools.partial(second_kernel, rows, y_count, (1, 3, 0)),
        [chunk_y] * 3,
        held_y,
        limit=8,
        flops=STAGE,
    )
    got_1 = swap(sent_1, "py", 1)
    got_3 = swap(sent_3, "py", 3)

    joined_x = swap(call(join_kernel, pair_x, stay_x, across_x, limit=8, flops=STAGE), "px", 1)
    flat = (2, lines_x, x_width)
    products, own_part = call(
        main_kernel,
        [like(lines_x, line, kind=jnp.float32), like(gathered, line, kind=jnp.float32)],
        *(a.reshape(flat) for a in (stay_x, across_x, joined_x)),
        own_y,
        line_op,
        limit=16,
        flops=STAGE,
    )
    across_z, stay_z = call(
        functools.partial(stencil_kernel, planes),
        [pair_x, pair_x],
        held_z,
        faces,
        limit=8,
        flops=STAGE,
        scratch=[pltpu.VMEM(flux_z.shape, bf16)],
    )
    across_z = swap(across_z, "px", 2)
    joined_z = swap(
        call(join_kernel, pair_x, stay_z, across_z, products, limit=8, flops=STAGE), "px", 1
    )
    early = call(
        functools.partial(early_kernel, (2, 1)),
        like(gathered, line, kind=jnp.float32),
        got_2,
        got_1,
        own_part,
        line_op,
        limit=16,
        flops=STAGE,
    )
    xz_part = call(
        add_kernel,
        like(lines_x, line),
        early,
        *(a.reshape(flat) for a in (stay_z, across_z, joined_z)),
        products,
        limit=8,
    )
    y_part = call(
        functools.partial(late_kernel, 3),
        like(variables * slab, rows, line),
        early,
        got_3,
        line_op,
        xz_part,
        far=(3,),
        limit=16,
        flops=2 * gathered * y_width * line,
    )
    y_part, xz_part = lax.optimization_barrier((y_part, xz_part))
    return (
        xz_part.reshape(variables, planes, lines, line),
        y_part.reshape(variables, slab, rows, line),
    )


def solution(mesh):
    fits = mesh.shape["py"] == 4 and mesh.shape["px"] == 4 and mesh.shape["gz"] == 2
    return jax.shard_map(
        local if fits else plain,
        mesh=mesh,
        in_specs=(
            P(None, "gz", "py", "px"),
            P(None, "gz", "px", "py"),
            P(None, "gz", "py", "px"),
            P(),
        ),
        out_specs=(P(None, ("gz", "px"), "py", None), P(None, "gz", ("px", "py"), None)),
        check_vma=False,
    )
```

```python
import functools

import jax
import jax.numpy as jnp
from jax import lax
from jax.experimental import pallas as pl
from jax.experimental.pallas import tpu as pltpu
from jax.sharding import PartitionSpec as P

STENCIL_COEFS = (0.8, -0.2, 4.0 / 105.0, -1.0 / 280.0)
WIDTH = 4
STAGE = 3 * 10**9
MIB = 1 << 20
VMEM = pl.BlockSpec(memory_space=pltpu.VMEM)
FAR = pl.BlockSpec(memory_space=pltpu.HBM)


def with_halo(block, sides, width):
    for axis, dim in sides:
        count = lax.axis_size(axis)
        forward = [(i, i + 1) for i in range(count - 1)]
        forward.append((count - 1, 0))
        backward = [(target, source) for source, target in forward]
        low = lax.ppermute(
            lax.slice_in_dim(block, block.shape[dim] - width, None, axis=dim), axis, forward
        )
        high = lax.ppermute(lax.slice_in_dim(block, 0, width, axis=dim), axis, backward)
        block = jnp.concatenate([low, block, high], axis=dim)
    return block


def line_product(block, line_op):
    return lax.dot_general(
        block, line_op, (((3,), (1,)), ((), ())), preferred_element_type=jnp.float32
    )


def z_stencil(padded, planes):
    widened = padded.astype(jnp.float32)
    total = jnp.zeros((widened.shape[0], planes) + widened.shape[2:], jnp.float32)
    for offset in range(WIDTH):
        reach = offset + 1
        upper = widened[:, WIDTH + reach : WIDTH + reach + planes]
        lower = widened[:, WIDTH - reach : WIDTH - reach + planes]
        total = total + STENCIL_COEFS[offset] * (upper - lower)
    return total.astype(jnp.bfloat16)


def plain(flux_x, flux_y, flux_z, line_op):
    planes = flux_z.shape[1]
    z_deriv = z_stencil(with_halo(flux_z, (("gz", 1),), WIDTH), planes)
    y_part = line_product(
        lax.all_to_all(flux_y, "py", split_axis=2, concat_axis=3, tiled=True), line_op
    ).astype(jnp.bfloat16)
    products = line_product(
        lax.all_to_all(flux_x, "px", split_axis=1, concat_axis=3, tiled=True), line_op
    )
    moved = lax.all_to_all(z_deriv, "px", split_axis=1, concat_axis=3, tiled=True)
    xz_part = (products + moved.astype(jnp.float32)).astype(jnp.bfloat16)
    return (xz_part, y_part)


def partner(axis, flip):
    return lax.axis_index(axis) ^ flip


def swap(block, axis, flip):
    pairs = [(i, i ^ flip) for i in range(lax.axis_size(axis))]
    return lax.ppermute(block, axis, pairs)


def call(kernel, out_shape, *operands, limit, flops=0, scratch=(), far=()):
    moved = sum(a.size * a.dtype.itemsize for a in (*operands, *jax.tree.leaves(out_shape)))
    operands = [
        pltpu.with_memory_space_constraint(a, pltpu.HBM) if index in far else a
        for index, a in enumerate(operands)
    ]
    return pl.pallas_call(
        kernel,
        out_shape=out_shape,
        in_specs=[FAR if index in far else VMEM for index in range(len(operands))],
        out_specs=jax.tree.map(lambda _: VMEM, out_shape),
        scratch_shapes=scratch,
        compiler_params=pltpu.CompilerParams(vmem_limit_bytes=limit * MIB),
        cost_estimate=pl.CostEstimate(flops=flops, bytes_accessed=moved, transcendentals=0),
    )(*operands)


def pick_rows(lines, rows, count, flip, out):
    group = 256
    kept = group // count
    line = lax.broadcasted_iota(jnp.int32, (kept, group), 0)
    source = lax.broadcasted_iota(jnp.int32, (kept, group), 1)
    wanted = (line // rows) * (count * rows) + partner("py", flip) * rows + line % rows
    chosen = (source == wanted).astype(jnp.bfloat16)
    for part in range(lines.shape[0] // group):
        picked = jnp.dot(
            chosen,
            lines[part * group : (part + 1) * group, :],
            preferred_element_type=jnp.float32,
        )
        out[part * kept : (part + 1) * kept, :] = picked.astype(jnp.bfloat16)


def first_kernel(rows, count, planes, flux_y, flux_x, flux_z, *refs):
    sent_y, held_y, faces, across, stay, held_z, sems = refs
    last = flux_z.shape[1] - WIDTH
    moves = [(flux_y, held_y), (flux_z, held_z)]
    moves += [(flux_z.at[:, pl.ds(last, WIDTH)], faces.at[:, :WIDTH])]
    moves += [(flux_z.at[:, :WIDTH], faces.at[:, WIDTH:])]
    for flip, place in ((2, across.at[0]), (3, across.at[1]), (0, stay.at[0]), (1, stay.at[1])):
        moves.append((flux_x.at[:, pl.ds(partner("px", flip) * planes, planes)], place))
    copies = [pltpu.make_async_copy(a, b, sems.at[i]) for i, (a, b) in enumerate(moves)]
    for copy in copies:
        copy.start()
    copies[0].wait()
    pick_rows(held_y, rows, count, 2, sent_y)
    for copy in copies[1:]:
        copy.wait()


def second_kernel(rows, count, flips, flux_y, *outs):
    for flip, out in zip(flips, outs):
        pick_rows(flux_y, rows, count, flip, out)


def join_kernel(stay, got, *refs):
    out = refs[-1]
    out[0] = stay[1]
    out[1] = got[1]


def stencil_kernel(planes, flux_z, faces, across, stay, held):
    own = flux_z.shape[1]

    def plane(variable, index):
        if index < 0:
            return faces[variable, WIDTH + index].astype(jnp.float32)
        if index >= own:
            return faces[variable, WIDTH + index - own].astype(jnp.float32)
        return flux_z[variable, index].astype(jnp.float32)

    for variable in range(flux_z.shape[0]):
        for index in range(own):
            total = jnp.zeros(flux_z.shape[2:], jnp.float32)
            for offset in range(WIDTH):
                upper = plane(variable, index + offset + 1)
                lower = plane(variable, index - offset - 1)
                total = total + STENCIL_COEFS[offset] * (upper - lower)
            held[variable, index] = total.astype(jnp.bfloat16)
    for flip, place in ((2, across.at[0]), (3, across.at[1]), (0, stay.at[0]), (1, stay.at[1])):
        place[...] = held[:, pl.ds(partner("px", flip) * planes, planes)]


def cells(axis, flip, width):
    return pl.ds(pl.multiple_of(partner(axis, flip) * width, width), width)


def times(block, line_op, to, of):
    return lax.dot_general(
        block, line_op[to, of], (((1,), (1,)), ((), ())), preferred_element_type=jnp.float32
    )


def blocks_of(stay, across, joined):
    return ((0, stay, 0), (2, across, 0), (1, joined, 0), (3, joined, 1))


def main_kernel(stay, across, joined, own_y, line_op, out_x, out_y):
    width = stay.shape[2]
    for start in range(0, line_op.shape[0], width):
        place = pl.ds(start, width)
        total = None
        for flip, ref, index in blocks_of(stay, across, joined):
            part = times(ref[index], line_op, place, cells("px", flip, width))
            total = part if total is None else total + part
        out_x[:, place] = total
        out_y[:, place] = times(own_y[...], line_op, place, cells("py", 0, width))


def add_kernel(after, stay, across, joined, products, out):
    width = stay.shape[2]
    for flip, ref, index in blocks_of(stay, across, joined):
        place = cells("px", flip, width)
        out[:, place] = (products[:, place] + ref[index].astype(jnp.float32)).astype(jnp.bfloat16)


def step_kernel(flip, block, before, line_op, *refs, swapped=False):
    out = refs[-1]
    if swapped:
        block, before = before, block
    width = block.shape[1]
    for start in range(0, out.shape[1], width):
        place = pl.ds(start, width)
        part = times(block[...], line_op, place, cells("py", flip, width))
        out[:, place] = before[:, place] + part


def late_kernel(flip, early, block, line_op, out):
    width = block.shape[1]
    rows = out.shape[1]
    for start in range(0, out.shape[2], width):
        place = pl.ds(start, width)
        total = early[:, place] + times(block[...], line_op, place, cells("py", flip, width))
        out[:, :, place] = total.reshape(-1, rows, width).astype(jnp.bfloat16)


def local(flux_x, flux_y, flux_z, line_op):
    variables, slab, lines, x_width = flux_x.shape
    x_count, y_count = lax.axis_size("px"), lax.axis_size("py")
    planes = slab // x_count
    x_lines, y_width = flux_y.shape[2:]
    rows = x_lines // y_count
    line = line_op.shape[0]
    gathered = variables * slab * rows
    lines_x = variables * planes * lines
    bf16 = jnp.bfloat16

    def like(*shape, kind=bf16):
        return jax.ShapeDtypeStruct(shape, kind)

    rows_y = flux_y.reshape(-1, y_width)
    chunk_y = like(gathered, y_width)
    pair_x = like(2, variables, planes, lines, x_width)
    sent_2, held_y, faces, across_x, stay_x, held_z = call(
        functools.partial(first_kernel, rows, y_count, planes),
        [
            chunk_y,
            like(*rows_y.shape),
            like(variables, 2 * WIDTH, lines, x_width),
            pair_x,
            pair_x,
            like(*flux_z.shape),
        ],
        rows_y,
        flux_x,
        flux_z,
        far=(0, 1, 2),
        limit=8,
        scratch=[pltpu.SemaphoreType.DMA((8,))],
    )
    got_2 = swap(sent_2, "py", 2)
    faces = swap(faces, "gz", 1)
    across_x = swap(across_x, "px", 2)
    sent_1, sent_3, own_y = call(
        functools.partial(second_kernel, rows, y_count, (1, 3, 0)),
        [chunk_y] * 3,
        held_y,
        limit=8,
        flops=STAGE,
    )
    got_1 = swap(sent_1, "py", 1)
    got_3 = swap(sent_3, "py", 3)

    joined_x = swap(call(join_kernel, pair_x, stay_x, across_x, limit=8, flops=STAGE), "px", 1)
    flat = (2, lines_x, x_width)
    products, own_part = call(
        main_kernel,
        [like(lines_x, line, kind=jnp.float32), like(gathered, line, kind=jnp.float32)],
        *(a.reshape(flat) for a in (stay_x, across_x, joined_x)),
        own_y,
        line_op,
        limit=16,
        flops=STAGE,
    )
    across_z, stay_z = call(
        functools.partial(stencil_kernel, planes),
        [pair_x, pair_x],
        held_z,
        faces,
        limit=8,
        flops=STAGE,
        scratch=[pltpu.VMEM(flux_z.shape, bf16)],
    )
    across_z = swap(across_z, "px", 2)
    joined_z = swap(
        call(join_kernel, pair_x, stay_z, across_z, products, limit=8, flops=STAGE), "px", 1
    )
    sums_like = like(gathered, line, kind=jnp.float32)
    block_flops = 2 * gathered * y_width * line
    sum_2 = call(
        functools.partial(step_kernel, 2),
        sums_like,
        got_2,
        own_part,
        line_op,
        limit=16,
        flops=STAGE,
    )
    xz_part = call(
        add_kernel,
        like(lines_x, line),
        sum_2,
        *(a.reshape(flat) for a in (stay_z, across_z, joined_z)),
        products,
        limit=8,
    )
    sum_1 = call(
        functools.partial(step_kernel, 1, swapped=True),
        sums_like,
        sum_2,
        got_1,
        line_op,
        xz_part,
        far=(3,),
        limit=16,
        flops=block_flops,
    )
    y_part = call(
        functools.partial(late_kernel, 3),
        like(variables * slab, rows, line),
        sum_1,
        got_3,
        line_op,
        limit=16,
        flops=block_flops,
    )
    y_part, xz_part = lax.optimization_barrier((y_part, xz_part))
    return (
        xz_part.reshape(variables, planes, lines, line),
        y_part.reshape(variables, slab, rows, line),
    )


def solution(mesh):
    fits = mesh.shape["py"] == 4 and mesh.shape["px"] == 4 and mesh.shape["gz"] == 2
    return jax.shard_map(
        local if fits else plain,
        mesh=mesh,
        in_specs=(
            P(None, "gz", "py", "px"),
            P(None, "gz", "px", "py"),
            P(None, "gz", "py", "px"),
            P(),
        ),
        out_specs=(P(None, ("gz", "px"), "py", None), P(None, "gz", ("px", "py"), None)),
        check_vma=False,
    )
```

```python
import functools

import jax
import jax.numpy as jnp
from jax import lax
from jax.experimental import pallas as pl
from jax.experimental.pallas import tpu as pltpu
from jax.sharding import PartitionSpec as P

STENCIL_COEFS = (0.8, -0.2, 4.0 / 105.0, -1.0 / 280.0)
WIDTH = 4
STAGE = 3 * 10**9
MIB = 1 << 20
VMEM = pl.BlockSpec(memory_space=pltpu.VMEM)
FAR = pl.BlockSpec(memory_space=pltpu.HBM)


def with_halo(block, sides, width):
    for axis, dim in sides:
        count = lax.axis_size(axis)
        forward = [(i, i + 1) for i in range(count - 1)]
        forward.append((count - 1, 0))
        backward = [(target, source) for source, target in forward]
        low = lax.ppermute(
            lax.slice_in_dim(block, block.shape[dim] - width, None, axis=dim), axis, forward
        )
        high = lax.ppermute(lax.slice_in_dim(block, 0, width, axis=dim), axis, backward)
        block = jnp.concatenate([low, block, high], axis=dim)
    return block


def line_product(block, line_op):
    return lax.dot_general(
        block, line_op, (((3,), (1,)), ((), ())), preferred_element_type=jnp.float32
    )


def z_stencil(padded, planes):
    widened = padded.astype(jnp.float32)
    total = jnp.zeros((widened.shape[0], planes) + widened.shape[2:], jnp.float32)
    for offset in range(WIDTH):
        reach = offset + 1
        upper = widened[:, WIDTH + reach : WIDTH + reach + planes]
        lower = widened[:, WIDTH - reach : WIDTH - reach + planes]
        total = total + STENCIL_COEFS[offset] * (upper - lower)
    return total.astype(jnp.bfloat16)


def plain(flux_x, flux_y, flux_z, line_op):
    planes = flux_z.shape[1]
    z_deriv = z_stencil(with_halo(flux_z, (("gz", 1),), WIDTH), planes)
    y_part = line_product(
        lax.all_to_all(flux_y, "py", split_axis=2, concat_axis=3, tiled=True), line_op
    ).astype(jnp.bfloat16)
    products = line_product(
        lax.all_to_all(flux_x, "px", split_axis=1, concat_axis=3, tiled=True), line_op
    )
    moved = lax.all_to_all(z_deriv, "px", split_axis=1, concat_axis=3, tiled=True)
    xz_part = (products + moved.astype(jnp.float32)).astype(jnp.bfloat16)
    return (xz_part, y_part)


def partner(axis, flip):
    return lax.axis_index(axis) ^ flip


def swap(block, axis, flip):
    pairs = [(i, i ^ flip) for i in range(lax.axis_size(axis))]
    return lax.ppermute(block, axis, pairs)


def call(kernel, out_shape, *operands, limit, flops=0, scratch=(), far=(), far_out=()):
    single = not isinstance(out_shape, (list, tuple))
    out_shape = [out_shape] if single else out_shape
    moved = sum(a.size * a.dtype.itemsize for a in (*operands, *jax.tree.leaves(out_shape)))
    operands = [
        pltpu.with_memory_space_constraint(a, pltpu.HBM) if index in far else a
        for index, a in enumerate(operands)
    ]
    results = pl.pallas_call(
        kernel,
        out_shape=out_shape,
        in_specs=[FAR if index in far else VMEM for index in range(len(operands))],
        out_specs=[FAR if index in far_out else VMEM for index in range(len(out_shape))],
        scratch_shapes=scratch,
        compiler_params=pltpu.CompilerParams(vmem_limit_bytes=limit * MIB),
        cost_estimate=pl.CostEstimate(flops=flops, bytes_accessed=moved, transcendentals=0),
    )(*operands)
    return results[0] if single else results


def pick_rows(lines, rows, count, flip, out):
    group = 256
    kept = group // count
    line = lax.broadcasted_iota(jnp.int32, (kept, group), 0)
    source = lax.broadcasted_iota(jnp.int32, (kept, group), 1)
    wanted = (line // rows) * (count * rows) + partner("py", flip) * rows + line % rows
    chosen = (source == wanted).astype(jnp.bfloat16)
    for part in range(lines.shape[0] // group):
        picked = jnp.dot(
            chosen,
            lines[part * group : (part + 1) * group, :],
            preferred_element_type=jnp.float32,
        )
        out[part * kept : (part + 1) * kept, :] = picked.astype(jnp.bfloat16)


def first_kernel(rows, count, planes, flux_y, flux_x, flux_z, *refs):
    sent_y, held_y, faces, across, stay, held_z, sems = refs
    last = flux_z.shape[1] - WIDTH
    moves = [(flux_y, held_y), (flux_z, held_z)]
    moves += [(flux_z.at[:, pl.ds(last, WIDTH)], faces.at[:, :WIDTH])]
    moves += [(flux_z.at[:, :WIDTH], faces.at[:, WIDTH:])]
    for flip, place in ((2, across.at[0]), (3, across.at[1]), (0, stay.at[0]), (1, stay.at[1])):
        moves.append((flux_x.at[:, pl.ds(partner("px", flip) * planes, planes)], place))
    copies = [pltpu.make_async_copy(a, b, sems.at[i]) for i, (a, b) in enumerate(moves)]
    for copy in copies:
        copy.start()
    copies[0].wait()
    pick_rows(held_y, rows, count, 2, sent_y)
    for copy in copies[1:]:
        copy.wait()


def second_kernel(rows, count, flips, flux_y, *outs):
    for flip, out in zip(flips, outs):
        pick_rows(flux_y, rows, count, flip, out)


def join_kernel(stay, got, *refs):
    out = refs[-1]
    out[0] = stay[1]
    out[1] = got[1]


def stencil_kernel(planes, flux_z, faces, across, stay, held):
    own = flux_z.shape[1]

    def plane(variable, index):
        if index < 0:
            return faces[variable, WIDTH + index].astype(jnp.float32)
        if index >= own:
            return faces[variable, WIDTH + index - own].astype(jnp.float32)
        return flux_z[variable, index].astype(jnp.float32)

    for variable in range(flux_z.shape[0]):
        for index in range(own):
            total = jnp.zeros(flux_z.shape[2:], jnp.float32)
            for offset in range(WIDTH):
                upper = plane(variable, index + offset + 1)
                lower = plane(variable, index - offset - 1)
                total = total + STENCIL_COEFS[offset] * (upper - lower)
            held[variable, index] = total.astype(jnp.bfloat16)
    for flip, place in ((2, across.at[0]), (3, across.at[1]), (0, stay.at[0]), (1, stay.at[1])):
        place[...] = held[:, pl.ds(partner("px", flip) * planes, planes)]


def cells(axis, flip, width):
    return pl.ds(pl.multiple_of(partner(axis, flip) * width, width), width)


def times(block, line_op, to, of):
    return lax.dot_general(
        block, line_op[to, of], (((1,), (1,)), ((), ())), preferred_element_type=jnp.float32
    )


def blocks_of(stay, across, joined):
    return ((0, stay, 0), (2, across, 0), (1, joined, 0), (3, joined, 1))


def main_kernel(stay, across, joined, own_y, line_op, out_x, out_y):
    width = stay.shape[2]
    for start in range(0, line_op.shape[0], width):
        place = pl.ds(start, width)
        total = None
        for flip, ref, index in blocks_of(stay, across, joined):
            part = times(ref[index], line_op, place, cells("px", flip, width))
            total = part if total is None else total + part
        out_x[:, place] = total
        out_y[:, place] = times(own_y[...], line_op, place, cells("py", 0, width))


def add_derivative(products, stay, across, joined, out):
    width = stay.shape[2]
    for flip, ref, index in blocks_of(stay, across, joined):
        place = cells("px", flip, width)
        out[:, place] = (products[:, place] + ref[index].astype(jnp.float32)).astype(jnp.bfloat16)


def step_kernel(flip, block, before, line_op, out):
    width = block.shape[1]
    for start in range(0, out.shape[1], width):
        place = pl.ds(start, width)
        part = times(block[...], line_op, place, cells("py", flip, width))
        out[:, place] = before[:, place] + part


def step_add_kernel(flip, before, block, line_op, products, *refs):
    derivs, (out, xz_part, held, sem) = refs[:3], refs[3:]
    add_derivative(products, *derivs, held)
    copy = pltpu.make_async_copy(held, xz_part, sem)
    copy.start()
    step_kernel(flip, block, before, line_op, out)
    copy.wait()


def late_kernel(flip, early, block, line_op, out, held, sems):
    width = block.shape[1]
    rows = out.shape[1]
    copies = []
    for start in range(0, out.shape[2], width):
        place = pl.ds(start, width)
        total = early[:, place] + times(block[...], line_op, place, cells("py", flip, width))
        held[:, :, place] = total.reshape(-1, rows, width).astype(jnp.bfloat16)
        copy = pltpu.make_async_copy(
            held.at[:, :, place], out.at[:, :, place], sems.at[len(copies)]
        )
        copy.start()
        copies.append(copy)
    for copy in copies:
        copy.wait()


def local(flux_x, flux_y, flux_z, line_op):
    variables, slab, lines, x_width = flux_x.shape
    x_count, y_count = lax.axis_size("px"), lax.axis_size("py")
    planes = slab // x_count
    x_lines, y_width = flux_y.shape[2:]
    rows = x_lines // y_count
    line = line_op.shape[0]
    gathered = variables * slab * rows
    lines_x = variables * planes * lines
    bf16 = jnp.bfloat16

    def like(*shape, kind=bf16):
        return jax.ShapeDtypeStruct(shape, kind)

    rows_y = flux_y.reshape(-1, y_width)
    chunk_y = like(gathered, y_width)
    pair_x = like(2, variables, planes, lines, x_width)
    sent_2, held_y, faces, across_x, stay_x, held_z = call(
        functools.partial(first_kernel, rows, y_count, planes),
        [
            chunk_y,
            like(*rows_y.shape),
            like(variables, 2 * WIDTH, lines, x_width),
            pair_x,
            pair_x,
            like(*flux_z.shape),
        ],
        rows_y,
        flux_x,
        flux_z,
        far=(0, 1, 2),
        limit=8,
        scratch=[pltpu.SemaphoreType.DMA((8,))],
    )
    got_2 = swap(sent_2, "py", 2)
    faces = swap(faces, "gz", 1)
    across_x = swap(across_x, "px", 2)
    sent_1, sent_3, own_y = call(
        functools.partial(second_kernel, rows, y_count, (1, 3, 0)),
        [chunk_y] * 3,
        held_y,
        limit=8,
        flops=STAGE,
    )
    got_1 = swap(sent_1, "py", 1)
    got_3 = swap(sent_3, "py", 3)

    joined_x = swap(call(join_kernel, pair_x, stay_x, across_x, limit=8, flops=STAGE), "px", 1)
    flat = (2, lines_x, x_width)
    products, own_part = call(
        main_kernel,
        [like(lines_x, line, kind=jnp.float32), like(gathered, line, kind=jnp.float32)],
        *(a.reshape(flat) for a in (stay_x, across_x, joined_x)),
        own_y,
        line_op,
        limit=16,
        flops=STAGE,
    )
    across_z, stay_z = call(
        functools.partial(stencil_kernel, planes),
        [pair_x, pair_x],
        held_z,
        faces,
        limit=8,
        flops=STAGE,
        scratch=[pltpu.VMEM(flux_z.shape, bf16)],
    )
    across_z = swap(across_z, "px", 2)
    joined_z = swap(
        call(join_kernel, pair_x, stay_z, across_z, products, limit=8, flops=STAGE), "px", 1
    )
    sums_like = like(gathered, line, kind=jnp.float32)
    block_flops = 2 * gathered * y_width * line
    sum_2 = call(
        functools.partial(step_kernel, 2),
        sums_like,
        got_2,
        own_part,
        line_op,
        limit=16,
        flops=STAGE,
    )
    sum_1, xz_part = call(
        functools.partial(step_add_kernel, 1),
        [sums_like, like(lines_x, line)],
        sum_2,
        got_1,
        line_op,
        products,
        *(a.reshape(flat) for a in (stay_z, across_z, joined_z)),
        far_out=(1,),
        limit=16,
        flops=block_flops,
        scratch=[pltpu.VMEM((lines_x, line), bf16), pltpu.SemaphoreType.DMA],
    )
    y_like = like(variables * slab, rows, line)
    y_part = call(
        functools.partial(late_kernel, 3),
        y_like,
        sum_1,
        got_3,
        line_op,
        far_out=(0,),
        limit=16,
        flops=block_flops,
        scratch=[
            pltpu.VMEM(y_like.shape, bf16),
            pltpu.SemaphoreType.DMA((line // y_width,)),
        ],
    )
    y_part, xz_part = lax.optimization_barrier((y_part, xz_part))
    return (
        xz_part.reshape(variables, planes, lines, line),
        y_part.reshape(variables, slab, rows, line),
    )


def solution(mesh):
    fits = mesh.shape["py"] == 4 and mesh.shape["px"] == 4 and mesh.shape["gz"] == 2
    return jax.shard_map(
        local if fits else plain,
        mesh=mesh,
        in_specs=(
            P(None, "gz", "py", "px"),
            P(None, "gz", "px", "py"),
            P(None, "gz", "py", "px"),
            P(),
        ),
        out_specs=(P(None, ("gz", "px"), "py", None), P(None, "gz", ("px", "py"), None)),
        check_vma=False,
    )
```

```python
import functools

import jax
import jax.numpy as jnp
from jax import lax
from jax.experimental import pallas as pl
from jax.experimental.pallas import tpu as pltpu
from jax.sharding import PartitionSpec as P

STENCIL_COEFS = (0.8, -0.2, 4.0 / 105.0, -1.0 / 280.0)
WIDTH = 4
GROUP = 256
STAGE = 3 * 10**9
MIB = 1 << 20
VMEM = pl.BlockSpec(memory_space=pltpu.VMEM)
FAR = pl.BlockSpec(memory_space=pltpu.HBM)


def with_halo(block, sides, width):
    for axis, dim in sides:
        count = lax.axis_size(axis)
        forward = [(i, i + 1) for i in range(count - 1)]
        forward.append((count - 1, 0))
        backward = [(target, source) for source, target in forward]
        low = lax.ppermute(
            lax.slice_in_dim(block, block.shape[dim] - width, None, axis=dim), axis, forward
        )
        high = lax.ppermute(lax.slice_in_dim(block, 0, width, axis=dim), axis, backward)
        block = jnp.concatenate([low, block, high], axis=dim)
    return block


def line_product(block, line_op):
    return lax.dot_general(
        block, line_op, (((3,), (1,)), ((), ())), preferred_element_type=jnp.float32
    )


def z_stencil(padded, planes):
    widened = padded.astype(jnp.float32)
    total = jnp.zeros((widened.shape[0], planes) + widened.shape[2:], jnp.float32)
    for offset in range(WIDTH):
        reach = offset + 1
        upper = widened[:, WIDTH + reach : WIDTH + reach + planes]
        lower = widened[:, WIDTH - reach : WIDTH - reach + planes]
        total = total + STENCIL_COEFS[offset] * (upper - lower)
    return total.astype(jnp.bfloat16)


def plain(flux_x, flux_y, flux_z, line_op):
    planes = flux_z.shape[1]
    z_deriv = z_stencil(with_halo(flux_z, (("gz", 1),), WIDTH), planes)
    y_part = line_product(
        lax.all_to_all(flux_y, "py", split_axis=2, concat_axis=3, tiled=True), line_op
    ).astype(jnp.bfloat16)
    products = line_product(
        lax.all_to_all(flux_x, "px", split_axis=1, concat_axis=3, tiled=True), line_op
    )
    moved = lax.all_to_all(z_deriv, "px", split_axis=1, concat_axis=3, tiled=True)
    xz_part = (products + moved.astype(jnp.float32)).astype(jnp.bfloat16)
    return (xz_part, y_part)


def partner(axis, flip):
    return lax.axis_index(axis) ^ flip


def swap(block, axis, flip):
    pairs = [(i, i ^ flip) for i in range(lax.axis_size(axis))]
    return lax.ppermute(block, axis, pairs)


def call(kernel, out_shape, *operands, limit, flops=0, scratch=(), far=(), far_out=False):
    moved = sum(a.size * a.dtype.itemsize for a in (*operands, *jax.tree.leaves(out_shape)))
    operands = [
        pltpu.with_memory_space_constraint(a, pltpu.HBM) if index in far else a
        for index, a in enumerate(operands)
    ]
    return pl.pallas_call(
        kernel,
        out_shape=out_shape,
        in_specs=[FAR if index in far else VMEM for index in range(len(operands))],
        out_specs=jax.tree.map(lambda _: FAR if far_out else VMEM, out_shape),
        scratch_shapes=scratch,
        compiler_params=pltpu.CompilerParams(vmem_limit_bytes=limit * MIB),
        cost_estimate=pl.CostEstimate(flops=flops, bytes_accessed=moved, transcendentals=0),
    )(*operands)


def choice(rows, count, flip):
    kept = GROUP // count
    line = lax.broadcasted_iota(jnp.int32, (kept, GROUP), 0)
    source = lax.broadcasted_iota(jnp.int32, (kept, GROUP), 1)
    wanted = (line // rows) * (count * rows) + partner("py", flip) * rows + line % rows
    return (source == wanted).astype(jnp.bfloat16)


def pick_part(chosen, lines, part, out):
    kept = chosen.shape[0]
    picked = jnp.dot(
        chosen, lines[part * GROUP : (part + 1) * GROUP, :], preferred_element_type=jnp.float32
    )
    out[part * kept : (part + 1) * kept, :] = picked.astype(jnp.bfloat16)


def pick_rows(lines, rows, count, flip, out):
    chosen = choice(rows, count, flip)
    for part in range(lines.shape[0] // GROUP):
        pick_part(chosen, lines, part, out)


def first_kernel(rows, count, planes, flux_y, flux_x, flux_z, *refs):
    sent_y, held_y, faces, across, sems = refs
    last = flux_z.shape[1] - WIDTH
    parts = flux_y.shape[0] // GROUP
    moves = []
    for part in range(parts):
        lines = pl.ds(part * GROUP, GROUP)
        moves.append((flux_y.at[lines], held_y.at[lines]))
    moves += [(flux_z.at[:, pl.ds(last, WIDTH)], faces.at[:, :WIDTH])]
    moves += [(flux_z.at[:, :WIDTH], faces.at[:, WIDTH:])]
    for flip, place in ((2, across.at[0]), (3, across.at[1])):
        moves.append((flux_x.at[:, pl.ds(partner("px", flip) * planes, planes)], place))
    copies = [pltpu.make_async_copy(a, b, sems.at[i]) for i, (a, b) in enumerate(moves)]
    for copy in copies:
        copy.start()
    chosen = choice(rows, count, 2)
    for part in range(parts):
        copies[part].wait()
        pick_part(chosen, held_y, part, sent_y)
    for copy in copies[parts:]:
        copy.wait()


def second_kernel(rows, count, flips, flux_y, *outs):
    for flip, out in zip(flips, outs):
        pick_rows(flux_y, rows, count, flip, out)


def join_x_kernel(planes, flux_x, got, out):
    out[0] = flux_x[:, pl.ds(partner("px", 1) * planes, planes)]
    out[1] = got[1]


def join_kernel(stay, got, *refs):
    out = refs[-1]
    out[0] = stay[1]
    out[1] = got[1]


def stencil_kernel(planes, flux_z, faces, across, stay, held):
    own = flux_z.shape[1]

    def plane(variable, index):
        if index < 0:
            return faces[variable, WIDTH + index].astype(jnp.float32)
        if index >= own:
            return faces[variable, WIDTH + index - own].astype(jnp.float32)
        return flux_z[variable, index].astype(jnp.float32)

    for variable in range(flux_z.shape[0]):
        for index in range(own):
            total = jnp.zeros(flux_z.shape[2:], jnp.float32)
            for offset in range(WIDTH):
                upper = plane(variable, index + offset + 1)
                lower = plane(variable, index - offset - 1)
                total = total + STENCIL_COEFS[offset] * (upper - lower)
            held[variable, index] = total.astype(jnp.bfloat16)
    for flip, place in ((2, across.at[0]), (3, across.at[1]), (0, stay.at[0]), (1, stay.at[1])):
        place[...] = held[:, pl.ds(partner("px", flip) * planes, planes)]


def cells(axis, flip, width):
    return pl.ds(pl.multiple_of(partner(axis, flip) * width, width), width)


def times(block, line_op, to, of):
    return lax.dot_general(
        block, line_op[to, of], (((1,), (1,)), ((), ())), preferred_element_type=jnp.float32
    )


def blocks_of(stay, across, joined):
    return ((0, stay, 0), (2, across, 0), (1, joined, 0), (3, joined, 1))


def main_kernel(planes, flux_x, across, joined, own_y, line_op, out_x, out_y):
    width = across.shape[2]
    own = flux_x[:, pl.ds(partner("px", 0) * planes, planes)].reshape(-1, width)
    for start in range(0, line_op.shape[0], width):
        place = pl.ds(start, width)
        total = times(own, line_op, place, cells("px", 0, width))
        for flip, ref, index in blocks_of(None, across, joined)[1:]:
            total = total + times(ref[index], line_op, place, cells("px", flip, width))
        out_x[:, place] = total
        out_y[:, place] = times(own_y[...], line_op, place, cells("py", 0, width))


def add_kernel(after, stay, across, joined, products, out):
    width = stay.shape[2]
    for flip, ref, index in blocks_of(stay, across, joined):
        place = cells("px", flip, width)
        out[:, place] = (products[:, place] + ref[index].astype(jnp.float32)).astype(jnp.bfloat16)


def step_kernel(flip, block, before, line_op, out):
    place = pl.ds(0, out.shape[1])
    out[...] = before[...] + times(block[...], line_op, place, cells("py", flip, block.shape[1]))


def ordered_step_kernel(flip, before, after, block, line_op, out):
    step_kernel(flip, block, before, line_op, out)


def late_kernel(flip, early, block, line_op, out, held, sems):
    width = block.shape[1]
    rows = out.shape[1]
    copies = []
    for start in range(0, out.shape[2], width):
        place = pl.ds(start, width)
        total = early[:, place] + times(block[...], line_op, place, cells("py", flip, width))
        held[:, :, place] = total.reshape(-1, rows, width).astype(jnp.bfloat16)
        copy = pltpu.make_async_copy(
            held.at[:, :, place], out.at[:, :, place], sems.at[len(copies)]
        )
        copy.start()
        copies.append(copy)
    for copy in copies:
        copy.wait()


def local(flux_x, flux_y, flux_z, line_op):
    variables, slab, lines, x_width = flux_x.shape
    x_count, y_count = lax.axis_size("px"), lax.axis_size("py")
    planes = slab // x_count
    x_lines, y_width = flux_y.shape[2:]
    rows = x_lines // y_count
    line = line_op.shape[0]
    gathered = variables * slab * rows
    lines_x = variables * planes * lines
    bf16 = jnp.bfloat16

    def like(*shape, kind=bf16):
        return jax.ShapeDtypeStruct(shape, kind)

    rows_y = flux_y.reshape(-1, y_width)
    chunk_y = like(gathered, y_width)
    pair_x = like(2, variables, planes, lines, x_width)
    sent_2, held_y, faces, across_x = call(
        functools.partial(first_kernel, rows, y_count, planes),
        [
            chunk_y,
            like(*rows_y.shape),
            like(variables, 2 * WIDTH, lines, x_width),
            pair_x,
        ],
        rows_y,
        flux_x,
        flux_z,
        far=(0, 1, 2),
        limit=8,
        scratch=[pltpu.SemaphoreType.DMA((4 + rows_y.shape[0] // GROUP,))],
    )
    got_2 = swap(sent_2, "py", 2)
    faces = swap(faces, "gz", 1)
    across_x = swap(across_x, "px", 2)
    sent_1, sent_3, own_y = call(
        functools.partial(second_kernel, rows, y_count, (1, 3, 0)),
        [chunk_y] * 3,
        held_y,
        limit=8,
        flops=STAGE,
    )
    got_1 = swap(sent_1, "py", 1)
    got_3 = swap(sent_3, "py", 3)

    joined_x = swap(call(
            functools.partial(join_x_kernel, planes),
            pair_x,
            flux_x,
            across_x,
            limit=8,
            flops=STAGE,
        ), "px", 1)
    flat = (2, lines_x, x_width)
    products, own_part = call(
        functools.partial(main_kernel, planes),
        [like(lines_x, line, kind=jnp.float32), like(gathered, line, kind=jnp.float32)],
        flux_x,
        across_x.reshape(flat),
        joined_x.reshape(flat),
        own_y,
        line_op,
        limit=16,
        flops=STAGE,
    )
    across_z, stay_z = call(
        functools.partial(stencil_kernel, planes),
        [pair_x, pair_x],
        flux_z,
        faces,
        limit=8,
        flops=STAGE,
        scratch=[pltpu.VMEM(flux_z.shape, bf16)],
    )
    across_z = swap(across_z, "px", 2)
    joined_z = swap(
        call(join_kernel, pair_x, stay_z, across_z, products, limit=8, flops=STAGE), "px", 1
    )
    sums_like = like(gathered, line, kind=jnp.float32)
    block_flops = 2 * gathered * y_width * line
    sum_2 = call(
        functools.partial(step_kernel, 2),
        sums_like,
        got_2,
        own_part,
        line_op,
        limit=16,
        flops=STAGE,
    )
    xz_part = call(
        add_kernel,
        like(lines_x, line),
        sum_2,
        *(a.reshape(flat) for a in (stay_z, across_z, joined_z)),
        products,
        limit=8,
    )
    sum_1 = call(
        functools.partial(ordered_step_kernel, 1),
        sums_like,
        sum_2,
        xz_part,
        got_1,
        line_op,
        far=(1,),
        limit=16,
        flops=block_flops,
    )
    y_like = like(variables * slab, rows, line)
    y_part = call(
        functools.partial(late_kernel, 3),
        y_like,
        sum_1,
        got_3,
        line_op,
        far_out=True,
        limit=16,
        flops=block_flops,
        scratch=[
            pltpu.VMEM(y_like.shape, bf16),
            pltpu.SemaphoreType.DMA((line // y_width,)),
        ],
    )
    y_part, xz_part = lax.optimization_barrier((y_part, xz_part))
    return (
        xz_part.reshape(variables, planes, lines, line),
        y_part.reshape(variables, slab, rows, line),
    )


def solution(mesh):
    fits = mesh.shape["py"] == 4 and mesh.shape["px"] == 4 and mesh.shape["gz"] == 2
    return jax.shard_map(
        local if fits else plain,
        mesh=mesh,
        in_specs=(
            P(None, "gz", "py", "px"),
            P(None, "gz", "px", "py"),
            P(None, "gz", "py", "px"),
            P(),
        ),
        out_specs=(P(None, ("gz", "px"), "py", None), P(None, "gz", ("px", "py"), None)),
        check_vma=False,
    )
```

```python
import functools

import jax
import jax.numpy as jnp
from jax import lax
from jax.experimental import pallas as pl
from jax.experimental.pallas import tpu as pltpu
from jax.sharding import PartitionSpec as P

STENCIL_COEFS = (0.8, -0.2, 4.0 / 105.0, -1.0 / 280.0)
WIDTH = 4
GROUP = 256
STAGE = 3 * 10**9
MIB = 1 << 20
VMEM = pl.BlockSpec(memory_space=pltpu.VMEM)
FAR = pl.BlockSpec(memory_space=pltpu.HBM)


def with_halo(block, sides, width):
    for axis, dim in sides:
        count = lax.axis_size(axis)
        forward = [(i, i + 1) for i in range(count - 1)]
        forward.append((count - 1, 0))
        backward = [(target, source) for source, target in forward]
        low = lax.ppermute(
            lax.slice_in_dim(block, block.shape[dim] - width, None, axis=dim), axis, forward
        )
        high = lax.ppermute(lax.slice_in_dim(block, 0, width, axis=dim), axis, backward)
        block = jnp.concatenate([low, block, high], axis=dim)
    return block


def line_product(block, line_op):
    return lax.dot_general(
        block, line_op, (((3,), (1,)), ((), ())), preferred_element_type=jnp.float32
    )


def z_stencil(padded, planes):
    widened = padded.astype(jnp.float32)
    total = jnp.zeros((widened.shape[0], planes) + widened.shape[2:], jnp.float32)
    for offset in range(WIDTH):
        reach = offset + 1
        upper = widened[:, WIDTH + reach : WIDTH + reach + planes]
        lower = widened[:, WIDTH - reach : WIDTH - reach + planes]
        total = total + STENCIL_COEFS[offset] * (upper - lower)
    return total.astype(jnp.bfloat16)


def plain(flux_x, flux_y, flux_z, line_op):
    planes = flux_z.shape[1]
    z_deriv = z_stencil(with_halo(flux_z, (("gz", 1),), WIDTH), planes)
    y_part = line_product(
        lax.all_to_all(flux_y, "py", split_axis=2, concat_axis=3, tiled=True), line_op
    ).astype(jnp.bfloat16)
    products = line_product(
        lax.all_to_all(flux_x, "px", split_axis=1, concat_axis=3, tiled=True), line_op
    )
    moved = lax.all_to_all(z_deriv, "px", split_axis=1, concat_axis=3, tiled=True)
    xz_part = (products + moved.astype(jnp.float32)).astype(jnp.bfloat16)
    return (xz_part, y_part)


def partner(axis, flip):
    return lax.axis_index(axis) ^ flip


def swap(block, axis, flip):
    pairs = [(i, i ^ flip) for i in range(lax.axis_size(axis))]
    return lax.ppermute(block, axis, pairs)


def call(kernel, out_shape, *operands, limit, flops=0, scratch=(), far=(), far_out=False):
    moved = sum(a.size * a.dtype.itemsize for a in (*operands, *jax.tree.leaves(out_shape)))
    operands = [
        pltpu.with_memory_space_constraint(a, pltpu.HBM) if index in far else a
        for index, a in enumerate(operands)
    ]
    return pl.pallas_call(
        kernel,
        out_shape=out_shape,
        in_specs=[FAR if index in far else VMEM for index in range(len(operands))],
        out_specs=jax.tree.map(lambda _: FAR if far_out else VMEM, out_shape),
        scratch_shapes=scratch,
        compiler_params=pltpu.CompilerParams(vmem_limit_bytes=limit * MIB),
        cost_estimate=pl.CostEstimate(flops=flops, bytes_accessed=moved, transcendentals=0),
    )(*operands)


def pick_rows(lines, rows, count, flip, out):
    kept = GROUP // count
    line = lax.broadcasted_iota(jnp.int32, (kept, GROUP), 0)
    source = lax.broadcasted_iota(jnp.int32, (kept, GROUP), 1)
    wanted = (line // rows) * (count * rows) + partner("py", flip) * rows + line % rows
    chosen = (source == wanted).astype(jnp.bfloat16)
    for part in range(lines.shape[0] // GROUP):
        picked = jnp.dot(
            chosen,
            lines[part * GROUP : (part + 1) * GROUP, :],
            preferred_element_type=jnp.float32,
        )
        out[part * kept : (part + 1) * kept, :] = picked.astype(jnp.bfloat16)


def first_kernel(rows, count, flips, planes, flux_y, flux_x, flux_z, *refs):
    sent_y, (held_y, faces, across, sems) = refs[: len(flips)], refs[len(flips) :]
    last = flux_z.shape[1] - WIDTH
    moves = [(flux_y, held_y)]
    moves += [(flux_z.at[:, pl.ds(last, WIDTH)], faces.at[:, :WIDTH])]
    moves += [(flux_z.at[:, :WIDTH], faces.at[:, WIDTH:])]
    for flip, place in ((2, across.at[0]), (3, across.at[1])):
        moves.append((flux_x.at[:, pl.ds(partner("px", flip) * planes, planes)], place))
    copies = [pltpu.make_async_copy(a, b, sems.at[i]) for i, (a, b) in enumerate(moves)]
    for copy in copies:
        copy.start()
    copies[0].wait()
    for flip, out in zip(flips, sent_y):
        pick_rows(held_y, rows, count, flip, out)
    for copy in copies[1:]:
        copy.wait()


def second_kernel(rows, count, flips, flux_y, *outs):
    for flip, out in zip(flips, outs):
        pick_rows(flux_y, rows, count, flip, out)


def join_x_kernel(planes, after, flux_x, got, out):
    out[0] = flux_x[:, pl.ds(partner("px", 1) * planes, planes)]
    out[1] = got[1]


def join_kernel(stay, got, *refs):
    out = refs[-1]
    out[0] = stay[1]
    out[1] = got[1]


def stencil_kernel(planes, flux_z, faces, across, stay, held):
    own = flux_z.shape[1]

    def plane(variable, index):
        if index < 0:
            return faces[variable, WIDTH + index].astype(jnp.float32)
        if index >= own:
            return faces[variable, WIDTH + index - own].astype(jnp.float32)
        return flux_z[variable, index].astype(jnp.float32)

    for variable in range(flux_z.shape[0]):
        for index in range(own):
            total = jnp.zeros(flux_z.shape[2:], jnp.float32)
            for offset in range(WIDTH):
                upper = plane(variable, index + offset + 1)
                lower = plane(variable, index - offset - 1)
                total = total + STENCIL_COEFS[offset] * (upper - lower)
            held[variable, index] = total.astype(jnp.bfloat16)
    for flip, place in ((2, across.at[0]), (3, across.at[1]), (0, stay.at[0]), (1, stay.at[1])):
        place[...] = held[:, pl.ds(partner("px", flip) * planes, planes)]


def cells(axis, flip, width):
    return pl.ds(pl.multiple_of(partner(axis, flip) * width, width), width)


def times(block, line_op, to, of):
    return lax.dot_general(
        block, line_op[to, of], (((1,), (1,)), ((), ())), preferred_element_type=jnp.float32
    )


def blocks_of(stay, across, joined):
    return ((0, stay, 0), (2, across, 0), (1, joined, 0), (3, joined, 1))


def own_kernel(own_y, line_op, after, out_y):
    width = own_y.shape[1]
    for start in range(0, line_op.shape[0], width):
        place = pl.ds(start, width)
        out_y[:, place] = times(own_y[...], line_op, place, cells("py", 0, width))


def main_kernel(planes, flux_x, across, joined, line_op, out):
    width = across.shape[2]
    own = flux_x[:, pl.ds(partner("px", 0) * planes, planes)].reshape(-1, width)
    for start in range(0, line_op.shape[0], width):
        place = pl.ds(start, width)
        total = times(own, line_op, place, cells("px", 0, width))
        for flip, ref, index in blocks_of(None, across, joined)[1:]:
            total = total + times(ref[index], line_op, place, cells("px", flip, width))
        out[:, place] = total


def add_kernel(across, joined, stay, products, after, out):
    width = stay.shape[2]
    for flip, ref, index in blocks_of(stay, across, joined):
        place = cells("px", flip, width)
        out[:, place] = (products[:, place] + ref[index].astype(jnp.float32)).astype(jnp.bfloat16)


def step_kernel(flip, block, before, line_op, out):
    place = pl.ds(0, out.shape[1])
    out[...] = before[...] + times(block[...], line_op, place, cells("py", flip, block.shape[1]))


def ordered_step_kernel(flip, before, block, after, line_op, out):
    step_kernel(flip, block, before, line_op, out)


def late_kernel(flip, early, block, line_op, out, held, sems):
    width = block.shape[1]
    rows = out.shape[1]
    copies = []
    for start in range(0, out.shape[2], width):
        place = pl.ds(start, width)
        total = early[:, place] + times(block[...], line_op, place, cells("py", flip, width))
        held[:, :, place] = total.reshape(-1, rows, width).astype(jnp.bfloat16)
        copy = pltpu.make_async_copy(
            held.at[:, :, place], out.at[:, :, place], sems.at[len(copies)]
        )
        copy.start()
        copies.append(copy)
    for copy in copies:
        copy.wait()


def local(flux_x, flux_y, flux_z, line_op):
    variables, slab, lines, x_width = flux_x.shape
    x_count, y_count = lax.axis_size("px"), lax.axis_size("py")
    planes = slab // x_count
    x_lines, y_width = flux_y.shape[2:]
    rows = x_lines // y_count
    line = line_op.shape[0]
    gathered = variables * slab * rows
    lines_x = variables * planes * lines
    bf16 = jnp.bfloat16

    def like(*shape, kind=bf16):
        return jax.ShapeDtypeStruct(shape, kind)

    rows_y = flux_y.reshape(-1, y_width)
    chunk_y = like(gathered, y_width)
    pair_x = like(2, variables, planes, lines, x_width)
    sent_2, held_y, faces, across_x = call(
        functools.partial(first_kernel, rows, y_count, (2,), planes),
        [
            chunk_y,
            like(*rows_y.shape),
            like(variables, 2 * WIDTH, lines, x_width),
            pair_x,
        ],
        rows_y,
        flux_x,
        flux_z,
        far=(0, 1, 2),
        limit=8,
        scratch=[pltpu.SemaphoreType.DMA((5,))],
    )
    got_2 = swap(sent_2, "py", 2)
    faces = swap(faces, "gz", 1)
    across_x = swap(across_x, "px", 2)
    sent_1, sent_3, own_y = call(
        functools.partial(second_kernel, rows, y_count, (1, 3, 0)),
        [chunk_y] * 3,
        held_y,
        limit=8,
        flops=STAGE,
    )
    got_1 = swap(sent_1, "py", 1)
    got_3 = swap(sent_3, "py", 3)

    across_z, stay_z = call(
        functools.partial(stencil_kernel, planes),
        [pair_x, pair_x],
        flux_z,
        faces,
        limit=8,
        flops=STAGE,
        scratch=[pltpu.VMEM(flux_z.shape, bf16)],
    )
    joined_x = call(
        functools.partial(join_x_kernel, planes),
        pair_x,
        stay_z,
        flux_x,
        across_x,
        limit=8,
        flops=STAGE,
    )
    flat = (2, lines_x, x_width)
    products_like = like(lines_x, line, kind=jnp.float32)
    sums_like = like(gathered, line, kind=jnp.float32)
    own_sum = call(
        own_kernel,
        sums_like,
        own_y,
        line_op,
        joined_x,
        limit=16,
        flops=STAGE,
    )
    joined_x = swap(joined_x, "px", 1)
    products = call(
        functools.partial(main_kernel, planes),
        products_like,
        flux_x,
        across_x.reshape(flat),
        joined_x.reshape(flat),
        line_op,
        limit=16,
        flops=STAGE,
    )
    across_z = swap(across_z, "px", 2)
    joined_z = swap(
        call(join_kernel, pair_x, stay_z, across_z, products, limit=8, flops=STAGE), "px", 1
    )
    block_flops = 2 * gathered * y_width * line
    sum_2 = call(
        functools.partial(step_kernel, 2),
        sums_like,
        got_2,
        own_sum,
        line_op,
        limit=16,
        flops=STAGE,
    )
    xz_part = call(
        add_kernel,
        like(lines_x, line),
        *(a.reshape(flat) for a in (across_z, joined_z, stay_z)),
        products,
        sum_2,
        limit=8,
    )
    sum_1 = call(
        functools.partial(ordered_step_kernel, 1),
        sums_like,
        sum_2,
        got_1,
        xz_part,
        line_op,
        far=(2,),
        limit=16,
        flops=block_flops,
    )
    y_like = like(variables * slab, rows, line)
    y_part = call(
        functools.partial(late_kernel, 3),
        y_like,
        sum_1,
        got_3,
        line_op,
        far_out=True,
        limit=16,
        flops=block_flops,
        scratch=[
            pltpu.VMEM(y_like.shape, bf16),
            pltpu.SemaphoreType.DMA((line // y_width,)),
        ],
    )
    y_part, xz_part = lax.optimization_barrier((y_part, xz_part))
    return (
        xz_part.reshape(variables, planes, lines, line),
        y_part.reshape(variables, slab, rows, line),
    )


def solution(mesh):
    fits = mesh.shape["py"] == 4 and mesh.shape["px"] == 4 and mesh.shape["gz"] == 2
    return jax.shard_map(
        local if fits else plain,
        mesh=mesh,
        in_specs=(
            P(None, "gz", "py", "px"),
            P(None, "gz", "px", "py"),
            P(None, "gz", "py", "px"),
            P(),
        ),
        out_specs=(P(None, ("gz", "px"), "py", None), P(None, "gz", ("px", "py"), None)),
        check_vma=False,
    )
```

```python
import functools

import jax
import jax.numpy as jnp
from jax import lax
from jax.experimental import pallas as pl
from jax.experimental.pallas import tpu as pltpu
from jax.sharding import PartitionSpec as P

STENCIL_COEFS = (0.8, -0.2, 4.0 / 105.0, -1.0 / 280.0)
WIDTH = 4
GROUP = 256
STAGE = 3 * 10**9
MIB = 1 << 20
VMEM = pl.BlockSpec(memory_space=pltpu.VMEM)
FAR = pl.BlockSpec(memory_space=pltpu.HBM)


def with_halo(block, sides, width):
    for axis, dim in sides:
        count = lax.axis_size(axis)
        forward = [(i, i + 1) for i in range(count - 1)]
        forward.append((count - 1, 0))
        backward = [(target, source) for source, target in forward]
        low = lax.ppermute(
            lax.slice_in_dim(block, block.shape[dim] - width, None, axis=dim), axis, forward
        )
        high = lax.ppermute(lax.slice_in_dim(block, 0, width, axis=dim), axis, backward)
        block = jnp.concatenate([low, block, high], axis=dim)
    return block


def line_product(block, line_op):
    return lax.dot_general(
        block, line_op, (((3,), (1,)), ((), ())), preferred_element_type=jnp.float32
    )


def z_stencil(padded, planes):
    widened = padded.astype(jnp.float32)
    total = jnp.zeros((widened.shape[0], planes) + widened.shape[2:], jnp.float32)
    for offset in range(WIDTH):
        reach = offset + 1
        upper = widened[:, WIDTH + reach : WIDTH + reach + planes]
        lower = widened[:, WIDTH - reach : WIDTH - reach + planes]
        total = total + STENCIL_COEFS[offset] * (upper - lower)
    return total.astype(jnp.bfloat16)


def plain(flux_x, flux_y, flux_z, line_op):
    planes = flux_z.shape[1]
    z_deriv = z_stencil(with_halo(flux_z, (("gz", 1),), WIDTH), planes)
    y_part = line_product(
        lax.all_to_all(flux_y, "py", split_axis=2, concat_axis=3, tiled=True), line_op
    ).astype(jnp.bfloat16)
    products = line_product(
        lax.all_to_all(flux_x, "px", split_axis=1, concat_axis=3, tiled=True), line_op
    )
    moved = lax.all_to_all(z_deriv, "px", split_axis=1, concat_axis=3, tiled=True)
    xz_part = (products + moved.astype(jnp.float32)).astype(jnp.bfloat16)
    return (xz_part, y_part)


def partner(axis, flip):
    return lax.axis_index(axis) ^ flip


def swap(block, axis, flip):
    pairs = [(i, i ^ flip) for i in range(lax.axis_size(axis))]
    return lax.ppermute(block, axis, pairs)


def call(kernel, out_shape, *operands, limit, flops=0, scratch=(), far=(), far_out=False):
    moved = sum(a.size * a.dtype.itemsize for a in (*operands, *jax.tree.leaves(out_shape)))
    operands = [
        pltpu.with_memory_space_constraint(a, pltpu.HBM) if index in far else a
        for index, a in enumerate(operands)
    ]
    return pl.pallas_call(
        kernel,
        out_shape=out_shape,
        in_specs=[FAR if index in far else VMEM for index in range(len(operands))],
        out_specs=jax.tree.map(lambda _: FAR if far_out else VMEM, out_shape),
        scratch_shapes=scratch,
        compiler_params=pltpu.CompilerParams(vmem_limit_bytes=limit * MIB),
        cost_estimate=pl.CostEstimate(flops=flops, bytes_accessed=moved, transcendentals=0),
    )(*operands)


def pick_rows(lines, rows, count, flip, out):
    kept = GROUP // count
    line = lax.broadcasted_iota(jnp.int32, (kept, GROUP), 0)
    source = lax.broadcasted_iota(jnp.int32, (kept, GROUP), 1)
    wanted = (line // rows) * (count * rows) + partner("py", flip) * rows + line % rows
    chosen = (source == wanted).astype(jnp.bfloat16)
    for part in range(lines.shape[0] // GROUP):
        picked = jnp.dot(
            chosen,
            lines[part * GROUP : (part + 1) * GROUP, :],
            preferred_element_type=jnp.float32,
        )
        out[part * kept : (part + 1) * kept, :] = picked.astype(jnp.bfloat16)


def first_kernel(rows, count, flips, planes, flux_y, flux_x, flux_z, *refs):
    sent_y, (held_y, faces, across, sems) = refs[: len(flips)], refs[len(flips) :]
    last = flux_z.shape[1] - WIDTH
    moves = [(flux_y, held_y)]
    moves += [(flux_z.at[:, pl.ds(last, WIDTH)], faces.at[:, :WIDTH])]
    moves += [(flux_z.at[:, :WIDTH], faces.at[:, WIDTH:])]
    for flip, place in ((2, across.at[0]), (3, across.at[1])):
        moves.append((flux_x.at[:, pl.ds(partner("px", flip) * planes, planes)], place))
    copies = [pltpu.make_async_copy(a, b, sems.at[i]) for i, (a, b) in enumerate(moves)]
    for copy in copies:
        copy.start()
    copies[0].wait()
    for flip, out in zip(flips, sent_y):
        pick_rows(held_y, rows, count, flip, out)
    for copy in copies[1:]:
        copy.wait()


def second_kernel(rows, count, flips, flux_y, *outs):
    for flip, out in zip(flips, outs):
        pick_rows(flux_y, rows, count, flip, out)


def join_x_kernel(planes, after, flux_x, got, out):
    out[0] = flux_x[:, pl.ds(partner("px", 1) * planes, planes)]
    out[1] = got[1]


def join_kernel(stay, got, *refs):
    out = refs[-1]
    out[0] = stay[1]
    out[1] = got[1]


def stencil_kernel(planes, flux_z, faces, across, stay, held):
    own = flux_z.shape[1]

    def plane(variable, index):
        if index < 0:
            return faces[variable, WIDTH + index].astype(jnp.float32)
        if index >= own:
            return faces[variable, WIDTH + index - own].astype(jnp.float32)
        return flux_z[variable, index].astype(jnp.float32)

    for variable in range(flux_z.shape[0]):
        for index in range(own):
            total = jnp.zeros(flux_z.shape[2:], jnp.float32)
            for offset in range(WIDTH):
                upper = plane(variable, index + offset + 1)
                lower = plane(variable, index - offset - 1)
                total = total + STENCIL_COEFS[offset] * (upper - lower)
            held[variable, index] = total.astype(jnp.bfloat16)
    for flip, place in ((2, across.at[0]), (3, across.at[1]), (0, stay.at[0]), (1, stay.at[1])):
        place[...] = held[:, pl.ds(partner("px", flip) * planes, planes)]


def cells(axis, flip, width):
    return pl.ds(pl.multiple_of(partner(axis, flip) * width, width), width)


def times(block, line_op, to, of):
    return lax.dot_general(
        block, line_op[to, of], (((1,), (1,)), ((), ())), preferred_element_type=jnp.float32
    )


def blocks_of(stay, across, joined):
    return ((0, stay, 0), (2, across, 0), (1, joined, 0), (3, joined, 1))


def own_kernel(own_y, line_op, after, out_y):
    width = own_y.shape[1]
    for start in range(0, line_op.shape[0], width):
        place = pl.ds(start, width)
        out_y[:, place] = times(own_y[...], line_op, place, cells("py", 0, width))


def main_kernel(planes, flux_x, across, joined, line_op, out):
    width = across.shape[2]
    own = flux_x[:, pl.ds(partner("px", 0) * planes, planes)].reshape(-1, width)
    for start in range(0, line_op.shape[0], width):
        place = pl.ds(start, width)
        total = times(own, line_op, place, cells("px", 0, width))
        for flip, ref, index in blocks_of(None, across, joined)[1:]:
            total = total + times(ref[index], line_op, place, cells("px", flip, width))
        out[:, place] = total


def add_kernel(across, joined, stay, products, after, out):
    width = stay.shape[2]
    for flip, ref, index in blocks_of(stay, across, joined):
        place = cells("px", flip, width)
        out[:, place] = (products[:, place] + ref[index].astype(jnp.float32)).astype(jnp.bfloat16)


def step_kernel(flip, block, before, line_op, out):
    place = pl.ds(0, out.shape[1])
    out[...] = before[...] + times(block[...], line_op, place, cells("py", flip, block.shape[1]))


def ordered_step_kernel(flip, before, block, after, line_op, out):
    step_kernel(flip, block, before, line_op, out)


def late_kernel(flip, early, block, line_op, out, held, sems):
    width = block.shape[1]
    rows = out.shape[1]
    copies = []
    for start in range(0, out.shape[2], width):
        place = pl.ds(start, width)
        total = early[:, place] + times(block[...], line_op, place, cells("py", flip, width))
        held[:, :, place] = total.reshape(-1, rows, width).astype(jnp.bfloat16)
        copy = pltpu.make_async_copy(
            held.at[:, :, place], out.at[:, :, place], sems.at[len(copies)]
        )
        copy.start()
        copies.append(copy)
    for copy in copies:
        copy.wait()


def local(flux_x, flux_y, flux_z, line_op):
    variables, slab, lines, x_width = flux_x.shape
    x_count, y_count = lax.axis_size("px"), lax.axis_size("py")
    planes = slab // x_count
    x_lines, y_width = flux_y.shape[2:]
    rows = x_lines // y_count
    line = line_op.shape[0]
    gathered = variables * slab * rows
    lines_x = variables * planes * lines
    bf16 = jnp.bfloat16

    def like(*shape, kind=bf16):
        return jax.ShapeDtypeStruct(shape, kind)

    rows_y = flux_y.reshape(-1, y_width)
    chunk_y = like(gathered, y_width)
    pair_x = like(2, variables, planes, lines, x_width)
    sent_2, held_y, faces, across_x = call(
        functools.partial(first_kernel, rows, y_count, (2,), planes),
        [
            chunk_y,
            like(*rows_y.shape),
            like(variables, 2 * WIDTH, lines, x_width),
            pair_x,
        ],
        rows_y,
        flux_x,
        flux_z,
        far=(0, 1, 2),
        limit=8,
        scratch=[pltpu.SemaphoreType.DMA((5,))],
    )
    got_2 = swap(sent_2, "py", 2)
    faces = swap(faces, "gz", 1)
    across_x = swap(across_x, "px", 2)
    sent_1, sent_3, own_y = call(
        functools.partial(second_kernel, rows, y_count, (1, 3, 0)),
        [chunk_y] * 3,
        held_y,
        limit=8,
        flops=STAGE,
    )
    got_1 = swap(sent_1, "py", 1)
    got_3 = swap(sent_3, "py", 3)

    across_z, stay_z = call(
        functools.partial(stencil_kernel, planes),
        [pair_x, pair_x],
        flux_z,
        faces,
        limit=8,
        flops=STAGE,
        scratch=[pltpu.VMEM(flux_z.shape, bf16)],
    )
    joined_x = call(
        functools.partial(join_x_kernel, planes),
        pair_x,
        stay_z,
        flux_x,
        across_x,
        limit=8,
        flops=STAGE // 2,
    )
    flat = (2, lines_x, x_width)
    products_like = like(lines_x, line, kind=jnp.float32)
    sums_like = like(gathered, line, kind=jnp.float32)
    own_sum = call(
        own_kernel,
        sums_like,
        own_y,
        line_op,
        joined_x,
        limit=16,
        flops=STAGE,
    )
    joined_x = swap(joined_x, "px", 1)
    products = call(
        functools.partial(main_kernel, planes),
        products_like,
        flux_x,
        across_x.reshape(flat),
        joined_x.reshape(flat),
        line_op,
        limit=16,
        flops=STAGE,
    )
    across_z = swap(across_z, "px", 2)
    joined_z = swap(
        call(join_kernel, pair_x, stay_z, across_z, products, limit=8, flops=STAGE), "px", 1
    )
    block_flops = 2 * gathered * y_width * line
    sum_2 = call(
        functools.partial(step_kernel, 2),
        sums_like,
        got_2,
        own_sum,
        line_op,
        limit=16,
        flops=STAGE,
    )
    xz_part = call(
        add_kernel,
        like(lines_x, line),
        *(a.reshape(flat) for a in (across_z, joined_z, stay_z)),
        products,
        sum_2,
        limit=8,
    )
    sum_1 = call(
        functools.partial(ordered_step_kernel, 1),
        sums_like,
        sum_2,
        got_1,
        xz_part,
        line_op,
        far=(2,),
        limit=16,
        flops=block_flops,
    )
    y_like = like(variables * slab, rows, line)
    y_part = call(
        functools.partial(late_kernel, 3),
        y_like,
        sum_1,
        got_3,
        line_op,
        far_out=True,
        limit=16,
        flops=block_flops,
        scratch=[
            pltpu.VMEM(y_like.shape, bf16),
            pltpu.SemaphoreType.DMA((line // y_width,)),
        ],
    )
    y_part, xz_part = lax.optimization_barrier((y_part, xz_part))
    return (
        xz_part.reshape(variables, planes, lines, line),
        y_part.reshape(variables, slab, rows, line),
    )


def solution(mesh):
    fits = mesh.shape["py"] == 4 and mesh.shape["px"] == 4 and mesh.shape["gz"] == 2
    return jax.shard_map(
        local if fits else plain,
        mesh=mesh,
        in_specs=(
            P(None, "gz", "py", "px"),
            P(None, "gz", "px", "py"),
            P(None, "gz", "py", "px"),
            P(),
        ),
        out_specs=(P(None, ("gz", "px"), "py", None), P(None, "gz", ("px", "py"), None)),
        check_vma=False,
    )
```

```python
import functools

import jax
import jax.numpy as jnp
from jax import lax
from jax.experimental import pallas as pl
from jax.experimental.pallas import tpu as pltpu
from jax.sharding import PartitionSpec as P

STENCIL_COEFS = (0.8, -0.2, 4.0 / 105.0, -1.0 / 280.0)
WIDTH = 4
GROUP = 256
STAGE = 3 * 10**9
MIB = 1 << 20
VMEM = pl.BlockSpec(memory_space=pltpu.VMEM)
FAR = pl.BlockSpec(memory_space=pltpu.HBM)


def with_halo(block, sides, width):
    for axis, dim in sides:
        count = lax.axis_size(axis)
        forward = [(i, i + 1) for i in range(count - 1)]
        forward.append((count - 1, 0))
        backward = [(target, source) for source, target in forward]
        low = lax.ppermute(
            lax.slice_in_dim(block, block.shape[dim] - width, None, axis=dim), axis, forward
        )
        high = lax.ppermute(lax.slice_in_dim(block, 0, width, axis=dim), axis, backward)
        block = jnp.concatenate([low, block, high], axis=dim)
    return block


def line_product(block, line_op):
    return lax.dot_general(
        block, line_op, (((3,), (1,)), ((), ())), preferred_element_type=jnp.float32
    )


def z_stencil(padded, planes):
    widened = padded.astype(jnp.float32)
    total = jnp.zeros((widened.shape[0], planes) + widened.shape[2:], jnp.float32)
    for offset in range(WIDTH):
        reach = offset + 1
        upper = widened[:, WIDTH + reach : WIDTH + reach + planes]
        lower = widened[:, WIDTH - reach : WIDTH - reach + planes]
        total = total + STENCIL_COEFS[offset] * (upper - lower)
    return total.astype(jnp.bfloat16)


def plain(flux_x, flux_y, flux_z, line_op):
    planes = flux_z.shape[1]
    z_deriv = z_stencil(with_halo(flux_z, (("gz", 1),), WIDTH), planes)
    y_part = line_product(
        lax.all_to_all(flux_y, "py", split_axis=2, concat_axis=3, tiled=True), line_op
    ).astype(jnp.bfloat16)
    products = line_product(
        lax.all_to_all(flux_x, "px", split_axis=1, concat_axis=3, tiled=True), line_op
    )
    moved = lax.all_to_all(z_deriv, "px", split_axis=1, concat_axis=3, tiled=True)
    xz_part = (products + moved.astype(jnp.float32)).astype(jnp.bfloat16)
    return (xz_part, y_part)


def partner(axis, flip):
    return lax.axis_index(axis) ^ flip


def swap(block, axis, flip):
    pairs = [(i, i ^ flip) for i in range(lax.axis_size(axis))]
    return lax.ppermute(block, axis, pairs)


def call(kernel, out_shape, *operands, limit, flops=0, scratch=(), far=(), far_out=False):
    moved = sum(a.size * a.dtype.itemsize for a in (*operands, *jax.tree.leaves(out_shape)))
    operands = [
        pltpu.with_memory_space_constraint(a, pltpu.HBM) if index in far else a
        for index, a in enumerate(operands)
    ]
    return pl.pallas_call(
        kernel,
        out_shape=out_shape,
        in_specs=[FAR if index in far else VMEM for index in range(len(operands))],
        out_specs=jax.tree.map(lambda _: FAR if far_out else VMEM, out_shape),
        scratch_shapes=scratch,
        compiler_params=pltpu.CompilerParams(vmem_limit_bytes=limit * MIB),
        cost_estimate=pl.CostEstimate(flops=flops, bytes_accessed=moved, transcendentals=0),
    )(*operands)


def pick_rows(lines, rows, count, flip, out):
    kept = GROUP // count
    line = lax.broadcasted_iota(jnp.int32, (kept, GROUP), 0)
    source = lax.broadcasted_iota(jnp.int32, (kept, GROUP), 1)
    wanted = (line // rows) * (count * rows) + partner("py", flip) * rows + line % rows
    chosen = (source == wanted).astype(jnp.bfloat16)
    for part in range(lines.shape[0] // GROUP):
        picked = jnp.dot(
            chosen,
            lines[part * GROUP : (part + 1) * GROUP, :],
            preferred_element_type=jnp.float32,
        )
        out[part * kept : (part + 1) * kept, :] = picked.astype(jnp.bfloat16)


def first_kernel(rows, count, flips, planes, flux_y, flux_x, flux_z, *refs):
    sent_y, (held_y, faces, across, sems) = refs[: len(flips)], refs[len(flips) :]
    last = flux_z.shape[1] - WIDTH
    moves = [(flux_y, held_y)]
    moves += [(flux_z.at[:, pl.ds(last, WIDTH)], faces.at[:, :WIDTH])]
    moves += [(flux_z.at[:, :WIDTH], faces.at[:, WIDTH:])]
    for flip, place in ((2, across.at[0]), (3, across.at[1])):
        moves.append((flux_x.at[:, pl.ds(partner("px", flip) * planes, planes)], place))
    copies = [pltpu.make_async_copy(a, b, sems.at[i]) for i, (a, b) in enumerate(moves)]
    for copy in copies:
        copy.start()
    copies[0].wait()
    for flip, out in zip(flips, sent_y):
        pick_rows(held_y, rows, count, flip, out)
    for copy in copies[1:]:
        copy.wait()


def second_kernel(rows, count, flips, flux_y, *outs):
    for flip, out in zip(flips, outs):
        pick_rows(flux_y, rows, count, flip, out)


def join_x_kernel(planes, after, flux_x, got, out):
    out[0] = flux_x[:, pl.ds(partner("px", 1) * planes, planes)]
    out[1] = got[1]


def join_kernel(stay, got, *refs):
    out = refs[-1]
    out[0] = stay[1]
    out[1] = got[1]


def stencil_kernel(planes, flux_z, faces, across, stay, held):
    own = flux_z.shape[1]

    def plane(variable, index):
        if index < 0:
            return faces[variable, WIDTH + index].astype(jnp.float32)
        if index >= own:
            return faces[variable, WIDTH + index - own].astype(jnp.float32)
        return flux_z[variable, index].astype(jnp.float32)

    for variable in range(flux_z.shape[0]):
        for index in range(own):
            total = jnp.zeros(flux_z.shape[2:], jnp.float32)
            for offset in range(WIDTH):
                upper = plane(variable, index + offset + 1)
                lower = plane(variable, index - offset - 1)
                total = total + STENCIL_COEFS[offset] * (upper - lower)
            held[variable, index] = total.astype(jnp.bfloat16)
    for flip, place in ((2, across.at[0]), (3, across.at[1]), (0, stay.at[0]), (1, stay.at[1])):
        place[...] = held[:, pl.ds(partner("px", flip) * planes, planes)]


def cells(axis, flip, width):
    return pl.ds(pl.multiple_of(partner(axis, flip) * width, width), width)


def times(block, line_op, to, of):
    return lax.dot_general(
        block, line_op[to, of], (((1,), (1,)), ((), ())), preferred_element_type=jnp.float32
    )


def blocks_of(stay, across, joined):
    return ((0, stay, 0), (2, across, 0), (1, joined, 0), (3, joined, 1))


def own_kernel(own_y, line_op, after, out_y):
    width = own_y.shape[1]
    for start in range(0, line_op.shape[0], width):
        place = pl.ds(start, width)
        out_y[:, place] = times(own_y[...], line_op, place, cells("py", 0, width))


def main_kernel(planes, flux_x, across, joined, line_op, out):
    width = across.shape[2]
    own = flux_x[:, pl.ds(partner("px", 0) * planes, planes)].reshape(-1, width)
    for start in range(0, line_op.shape[0], width):
        place = pl.ds(start, width)
        total = times(own, line_op, place, cells("px", 0, width))
        for flip, ref, index in blocks_of(None, across, joined)[1:]:
            total = total + times(ref[index], line_op, place, cells("px", flip, width))
        out[:, place] = total


def add_kernel(across, joined, stay, products, after, out):
    width = stay.shape[2]
    for flip, ref, index in blocks_of(stay, across, joined):
        place = cells("px", flip, width)
        out[:, place] = (products[:, place] + ref[index].astype(jnp.float32)).astype(jnp.bfloat16)


def step_kernel(flip, block, before, line_op, out):
    place = pl.ds(0, out.shape[1])
    out[...] = before[...] + times(block[...], line_op, place, cells("py", flip, block.shape[1]))


def ordered_step_kernel(flip, block, before, after, line_op, out):
    step_kernel(flip, block, before, line_op, out)


def late_kernel(flip, early, block, line_op, out, held, sems):
    width = block.shape[1]
    rows = out.shape[1]
    copies = []
    for start in range(0, out.shape[2], width):
        place = pl.ds(start, width)
        total = early[:, place] + times(block[...], line_op, place, cells("py", flip, width))
        held[:, :, place] = total.reshape(-1, rows, width).astype(jnp.bfloat16)
        copy = pltpu.make_async_copy(
            held.at[:, :, place], out.at[:, :, place], sems.at[len(copies)]
        )
        copy.start()
        copies.append(copy)
    for copy in copies:
        copy.wait()


def local(flux_x, flux_y, flux_z, line_op):
    variables, slab, lines, x_width = flux_x.shape
    x_count, y_count = lax.axis_size("px"), lax.axis_size("py")
    planes = slab // x_count
    x_lines, y_width = flux_y.shape[2:]
    rows = x_lines // y_count
    line = line_op.shape[0]
    gathered = variables * slab * rows
    lines_x = variables * planes * lines
    bf16 = jnp.bfloat16

    def like(*shape, kind=bf16):
        return jax.ShapeDtypeStruct(shape, kind)

    rows_y = flux_y.reshape(-1, y_width)
    chunk_y = like(gathered, y_width)
    pair_x = like(2, variables, planes, lines, x_width)
    sent_2, sent_1, held_y, faces, across_x = call(
        functools.partial(first_kernel, rows, y_count, (2, 1), planes),
        [
            chunk_y,
            chunk_y,
            like(*rows_y.shape),
            like(variables, 2 * WIDTH, lines, x_width),
            pair_x,
        ],
        rows_y,
        flux_x,
        flux_z,
        far=(0, 1, 2),
        limit=8,
        scratch=[pltpu.SemaphoreType.DMA((5,))],
    )
    got_2 = swap(sent_2, "py", 2)
    faces = swap(faces, "gz", 1)
    across_x = swap(across_x, "px", 2)
    sent_3, own_y = call(
        functools.partial(second_kernel, rows, y_count, (3, 0)),
        [chunk_y] * 2,
        held_y,
        limit=8,
        flops=STAGE,
    )
    got_1 = swap(sent_1, "py", 1)
    got_3 = swap(sent_3, "py", 3)

    across_z, stay_z = call(
        functools.partial(stencil_kernel, planes),
        [pair_x, pair_x],
        flux_z,
        faces,
        limit=8,
        flops=STAGE,
        scratch=[pltpu.VMEM(flux_z.shape, bf16)],
    )
    joined_x = call(
        functools.partial(join_x_kernel, planes),
        pair_x,
        stay_z,
        flux_x,
        across_x,
        limit=8,
        flops=STAGE // 2,
    )
    flat = (2, lines_x, x_width)
    products_like = like(lines_x, line, kind=jnp.float32)
    sums_like = like(gathered, line, kind=jnp.float32)
    own_sum = call(
        own_kernel,
        sums_like,
        own_y,
        line_op,
        joined_x,
        limit=16,
        flops=STAGE,
    )
    joined_x = swap(joined_x, "px", 1)
    products = call(
        functools.partial(main_kernel, planes),
        products_like,
        flux_x,
        across_x.reshape(flat),
        joined_x.reshape(flat),
        line_op,
        limit=16,
        flops=STAGE,
    )
    across_z = swap(across_z, "px", 2)
    joined_z = swap(
        call(join_kernel, pair_x, stay_z, across_z, products, limit=8, flops=STAGE), "px", 1
    )
    block_flops = 2 * gathered * y_width * line
    sum_2 = call(
        functools.partial(step_kernel, 2),
        sums_like,
        got_2,
        own_sum,
        line_op,
        limit=16,
        flops=STAGE,
    )
    xz_part = call(
        add_kernel,
        like(lines_x, line),
        *(a.reshape(flat) for a in (across_z, joined_z, stay_z)),
        products,
        sum_2,
        limit=8,
    )
    sum_1 = call(
        functools.partial(ordered_step_kernel, 1),
        sums_like,
        got_1,
        sum_2,
        xz_part,
        line_op,
        far=(2,),
        limit=16,
        flops=block_flops,
    )
    y_like = like(variables * slab, rows, line)
    y_part = call(
        functools.partial(late_kernel, 3),
        y_like,
        sum_1,
        got_3,
        line_op,
        far_out=True,
        limit=16,
        flops=block_flops,
        scratch=[
            pltpu.VMEM(y_like.shape, bf16),
            pltpu.SemaphoreType.DMA((line // y_width,)),
        ],
    )
    y_part, xz_part = lax.optimization_barrier((y_part, xz_part))
    return (
        xz_part.reshape(variables, planes, lines, line),
        y_part.reshape(variables, slab, rows, line),
    )


def solution(mesh):
    fits = mesh.shape["py"] == 4 and mesh.shape["px"] == 4 and mesh.shape["gz"] == 2
    return jax.shard_map(
        local if fits else plain,
        mesh=mesh,
        in_specs=(
            P(None, "gz", "py", "px"),
            P(None, "gz", "px", "py"),
            P(None, "gz", "py", "px"),
            P(),
        ),
        out_specs=(P(None, ("gz", "px"), "py", None), P(None, "gz", ("px", "py"), None)),
        check_vma=False,
    )
```

```python
import functools

import jax
import jax.numpy as jnp
from jax import lax
from jax.experimental import pallas as pl
from jax.experimental.pallas import tpu as pltpu
from jax.sharding import PartitionSpec as P

STENCIL_COEFS = (0.8, -0.2, 4.0 / 105.0, -1.0 / 280.0)
WIDTH = 4
GROUP = 256
STAGE = 3 * 10**9
MIB = 1 << 20
VMEM = pl.BlockSpec(memory_space=pltpu.VMEM)
FAR = pl.BlockSpec(memory_space=pltpu.HBM)


def with_halo(block, sides, width):
    for axis, dim in sides:
        count = lax.axis_size(axis)
        forward = [(i, i + 1) for i in range(count - 1)]
        forward.append((count - 1, 0))
        backward = [(target, source) for source, target in forward]
        low = lax.ppermute(
            lax.slice_in_dim(block, block.shape[dim] - width, None, axis=dim), axis, forward
        )
        high = lax.ppermute(lax.slice_in_dim(block, 0, width, axis=dim), axis, backward)
        block = jnp.concatenate([low, block, high], axis=dim)
    return block


def line_product(block, line_op):
    return lax.dot_general(
        block, line_op, (((3,), (1,)), ((), ())), preferred_element_type=jnp.float32
    )


def z_stencil(padded, planes):
    widened = padded.astype(jnp.float32)
    total = jnp.zeros((widened.shape[0], planes) + widened.shape[2:], jnp.float32)
    for offset in range(WIDTH):
        reach = offset + 1
        upper = widened[:, WIDTH + reach : WIDTH + reach + planes]
        lower = widened[:, WIDTH - reach : WIDTH - reach + planes]
        total = total + STENCIL_COEFS[offset] * (upper - lower)
    return total.astype(jnp.bfloat16)


def plain(flux_x, flux_y, flux_z, line_op):
    planes = flux_z.shape[1]
    z_deriv = z_stencil(with_halo(flux_z, (("gz", 1),), WIDTH), planes)
    y_part = line_product(
        lax.all_to_all(flux_y, "py", split_axis=2, concat_axis=3, tiled=True), line_op
    ).astype(jnp.bfloat16)
    products = line_product(
        lax.all_to_all(flux_x, "px", split_axis=1, concat_axis=3, tiled=True), line_op
    )
    moved = lax.all_to_all(z_deriv, "px", split_axis=1, concat_axis=3, tiled=True)
    xz_part = (products + moved.astype(jnp.float32)).astype(jnp.bfloat16)
    return (xz_part, y_part)


def partner(axis, flip):
    return lax.axis_index(axis) ^ flip


def swap(block, axis, flip):
    pairs = [(i, i ^ flip) for i in range(lax.axis_size(axis))]
    return lax.ppermute(block, axis, pairs)


def call(kernel, out_shape, *operands, limit, flops=0, scratch=(), far=(), far_out=False):
    moved = sum(a.size * a.dtype.itemsize for a in (*operands, *jax.tree.leaves(out_shape)))
    operands = [
        pltpu.with_memory_space_constraint(a, pltpu.HBM) if index in far else a
        for index, a in enumerate(operands)
    ]
    return pl.pallas_call(
        kernel,
        out_shape=out_shape,
        in_specs=[FAR if index in far else VMEM for index in range(len(operands))],
        out_specs=jax.tree.map(lambda _: FAR if far_out else VMEM, out_shape),
        scratch_shapes=scratch,
        compiler_params=pltpu.CompilerParams(vmem_limit_bytes=limit * MIB),
        cost_estimate=pl.CostEstimate(flops=flops, bytes_accessed=moved, transcendentals=0),
    )(*operands)


def pick_rows(lines, rows, count, flip, out):
    kept = GROUP // count
    line = lax.broadcasted_iota(jnp.int32, (kept, GROUP), 0)
    source = lax.broadcasted_iota(jnp.int32, (kept, GROUP), 1)
    wanted = (line // rows) * (count * rows) + partner("py", flip) * rows + line % rows
    chosen = (source == wanted).astype(jnp.bfloat16)
    for part in range(lines.shape[0] // GROUP):
        picked = jnp.dot(
            chosen,
            lines[part * GROUP : (part + 1) * GROUP, :],
            preferred_element_type=jnp.float32,
        )
        out[part * kept : (part + 1) * kept, :] = picked.astype(jnp.bfloat16)


def first_kernel(rows, count, flips, planes, flux_y, flux_x, flux_z, *refs):
    sent_y, (held_y, faces, across, sems) = refs[: len(flips)], refs[len(flips) :]
    last = flux_z.shape[1] - WIDTH
    moves = [(flux_y, held_y)]
    moves += [(flux_z.at[:, pl.ds(last, WIDTH)], faces.at[:, :WIDTH])]
    moves += [(flux_z.at[:, :WIDTH], faces.at[:, WIDTH:])]
    for flip, place in ((2, across.at[0]), (3, across.at[1])):
        moves.append((flux_x.at[:, pl.ds(partner("px", flip) * planes, planes)], place))
    copies = [pltpu.make_async_copy(a, b, sems.at[i]) for i, (a, b) in enumerate(moves)]
    for copy in copies:
        copy.start()
    copies[0].wait()
    for flip, out in zip(flips, sent_y):
        pick_rows(held_y, rows, count, flip, out)
    for copy in copies[1:]:
        copy.wait()


def second_kernel(rows, count, flips, flux_y, *outs):
    for flip, out in zip(flips, outs):
        pick_rows(flux_y, rows, count, flip, out)


def join_x_kernel(planes, after, flux_x, got, out):
    out[0] = flux_x[:, pl.ds(partner("px", 1) * planes, planes)]
    out[1] = got[1]


def join_kernel(stay, got, *refs):
    out = refs[-1]
    out[0] = stay[1]
    out[1] = got[1]


def stencil_kernel(planes, flux_z, faces, across, stay, held):
    own = flux_z.shape[1]

    def plane(variable, index):
        if index < 0:
            return faces[variable, WIDTH + index].astype(jnp.float32)
        if index >= own:
            return faces[variable, WIDTH + index - own].astype(jnp.float32)
        return flux_z[variable, index].astype(jnp.float32)

    for variable in range(flux_z.shape[0]):
        for index in range(own):
            total = jnp.zeros(flux_z.shape[2:], jnp.float32)
            for offset in range(WIDTH):
                upper = plane(variable, index + offset + 1)
                lower = plane(variable, index - offset - 1)
                total = total + STENCIL_COEFS[offset] * (upper - lower)
            held[variable, index] = total.astype(jnp.bfloat16)
    for flip, place in ((2, across.at[0]), (3, across.at[1]), (0, stay.at[0]), (1, stay.at[1])):
        place[...] = held[:, pl.ds(partner("px", flip) * planes, planes)]


def cells(axis, flip, width):
    return pl.ds(pl.multiple_of(partner(axis, flip) * width, width), width)


def times(block, line_op, to, of):
    return lax.dot_general(
        block, line_op[to, of], (((1,), (1,)), ((), ())), preferred_element_type=jnp.float32
    )


def blocks_of(stay, across, joined):
    return ((0, stay, 0), (2, across, 0), (1, joined, 0), (3, joined, 1))


def own_kernel(own_y, line_op, after, out_y):
    width = own_y.shape[1]
    for start in range(0, line_op.shape[0], width):
        place = pl.ds(start, width)
        out_y[:, place] = times(own_y[...], line_op, place, cells("py", 0, width))


def main_kernel(planes, flux_x, across, joined, line_op, out):
    width = across.shape[2]
    own = flux_x[:, pl.ds(partner("px", 0) * planes, planes)].reshape(-1, width)
    for start in range(0, line_op.shape[0], width):
        place = pl.ds(start, width)
        total = times(own, line_op, place, cells("px", 0, width))
        for flip, ref, index in blocks_of(None, across, joined)[1:]:
            total = total + times(ref[index], line_op, place, cells("px", flip, width))
        out[:, place] = total


def add_kernel(across, joined, stay, products, after, out):
    width = stay.shape[2]
    for flip, ref, index in blocks_of(stay, across, joined):
        place = cells("px", flip, width)
        out[:, place] = (products[:, place] + ref[index].astype(jnp.float32)).astype(jnp.bfloat16)


def step_kernel(flip, block, before, line_op, out):
    place = pl.ds(0, out.shape[1])
    out[...] = before[...] + times(block[...], line_op, place, cells("py", flip, block.shape[1]))


def ordered_step_kernel(flip, before, block, after, line_op, out):
    step_kernel(flip, block, before, line_op, out)


def late_kernel(flip, early, block, line_op, out, held, sems):
    width = block.shape[1]
    rows = out.shape[1]
    copies = []
    for start in range(0, out.shape[2], width):
        place = pl.ds(start, width)
        total = early[:, place] + times(block[...], line_op, place, cells("py", flip, width))
        held[:, :, place] = total.reshape(-1, rows, width).astype(jnp.bfloat16)
        copy = pltpu.make_async_copy(
            held.at[:, :, place], out.at[:, :, place], sems.at[len(copies)]
        )
        copy.start()
        copies.append(copy)
    for copy in copies:
        copy.wait()


def local(flux_x, flux_y, flux_z, line_op):
    variables, slab, lines, x_width = flux_x.shape
    x_count, y_count = lax.axis_size("px"), lax.axis_size("py")
    planes = slab // x_count
    x_lines, y_width = flux_y.shape[2:]
    rows = x_lines // y_count
    line = line_op.shape[0]
    gathered = variables * slab * rows
    lines_x = variables * planes * lines
    bf16 = jnp.bfloat16

    def like(*shape, kind=bf16):
        return jax.ShapeDtypeStruct(shape, kind)

    rows_y = flux_y.reshape(-1, y_width)
    chunk_y = like(gathered, y_width)
    pair_x = like(2, variables, planes, lines, x_width)
    sent_2, sent_1, held_y, faces, across_x = call(
        functools.partial(first_kernel, rows, y_count, (2, 1), planes),
        [
            chunk_y,
            chunk_y,
            like(*rows_y.shape),
            like(variables, 2 * WIDTH, lines, x_width),
            pair_x,
        ],
        rows_y,
        flux_x,
        flux_z,
        far=(0, 1, 2),
        limit=8,
        scratch=[pltpu.SemaphoreType.DMA((5,))],
    )
    got_2 = swap(sent_2, "py", 2)
    faces = swap(faces, "gz", 1)
    across_x = swap(across_x, "px", 2)
    sent_3, own_y = call(
        functools.partial(second_kernel, rows, y_count, (3, 0)),
        [chunk_y] * 2,
        held_y,
        limit=8,
        flops=STAGE,
    )
    got_1 = swap(sent_1, "py", 1)
    got_3 = swap(sent_3, "py", 3)

    across_z, stay_z = call(
        functools.partial(stencil_kernel, planes),
        [pair_x, pair_x],
        flux_z,
        faces,
        limit=8,
        flops=STAGE,
        scratch=[pltpu.VMEM(flux_z.shape, bf16)],
    )
    joined_x = call(
        functools.partial(join_x_kernel, planes),
        pair_x,
        stay_z,
        flux_x,
        across_x,
        limit=8,
        flops=STAGE // 2,
    )
    flat = (2, lines_x, x_width)
    products_like = like(lines_x, line, kind=jnp.float32)
    sums_like = like(gathered, line, kind=jnp.float32)
    own_sum = call(
        own_kernel,
        sums_like,
        own_y,
        line_op,
        joined_x,
        limit=16,
        flops=STAGE,
    )
    joined_x = swap(joined_x, "px", 1)
    products = call(
        functools.partial(main_kernel, planes),
        products_like,
        flux_x,
        across_x.reshape(flat),
        joined_x.reshape(flat),
        line_op,
        limit=16,
        flops=STAGE,
    )
    across_z = swap(across_z, "px", 2)
    joined_z = swap(
        call(join_kernel, pair_x, stay_z, across_z, products, limit=8, flops=STAGE), "px", 1
    )
    block_flops = 2 * gathered * y_width * line
    sum_2 = call(
        functools.partial(step_kernel, 2),
        sums_like,
        got_2,
        own_sum,
        line_op,
        limit=16,
        flops=STAGE,
    )
    xz_part = call(
        add_kernel,
        like(lines_x, line),
        *(a.reshape(flat) for a in (across_z, joined_z, stay_z)),
        products,
        sum_2,
        limit=8,
    )
    sum_1 = call(
        functools.partial(ordered_step_kernel, 1),
        sums_like,
        sum_2,
        got_1,
        xz_part,
        line_op,
        far=(2,),
        limit=16,
        flops=block_flops,
    )
    y_like = like(variables * slab, rows, line)
    y_part = call(
        functools.partial(late_kernel, 3),
        y_like,
        sum_1,
        got_3,
        line_op,
        far_out=True,
        limit=16,
        flops=block_flops,
        scratch=[
            pltpu.VMEM(y_like.shape, bf16),
            pltpu.SemaphoreType.DMA((line // y_width,)),
        ],
    )
    y_part, xz_part = lax.optimization_barrier((y_part, xz_part))
    return (
        xz_part.reshape(variables, planes, lines, line),
        y_part.reshape(variables, slab, rows, line),
    )


def solution(mesh):
    fits = mesh.shape["py"] == 4 and mesh.shape["px"] == 4 and mesh.shape["gz"] == 2
    return jax.shard_map(
        local if fits else plain,
        mesh=mesh,
        in_specs=(
            P(None, "gz", "py", "px"),
            P(None, "gz", "px", "py"),
            P(None, "gz", "py", "px"),
            P(),
        ),
        out_specs=(P(None, ("gz", "px"), "py", None), P(None, "gz", ("px", "py"), None)),
        check_vma=False,
    )
```

```python
import functools

import jax
import jax.numpy as jnp
from jax import lax
from jax.experimental import pallas as pl
from jax.experimental.pallas import tpu as pltpu
from jax.sharding import PartitionSpec as P

STENCIL_COEFS = (0.8, -0.2, 4.0 / 105.0, -1.0 / 280.0)
WIDTH = 4
GROUP = 256
STAGE = 3 * 10**9
MIB = 1 << 20
VMEM = pl.BlockSpec(memory_space=pltpu.VMEM)
ALL = slice(None)
FAR = pl.BlockSpec(memory_space=pltpu.HBM)


def with_halo(block, sides, width):
    for axis, dim in sides:
        count = lax.axis_size(axis)
        forward = [(i, i + 1) for i in range(count - 1)]
        forward.append((count - 1, 0))
        backward = [(target, source) for source, target in forward]
        low = lax.ppermute(
            lax.slice_in_dim(block, block.shape[dim] - width, None, axis=dim), axis, forward
        )
        high = lax.ppermute(lax.slice_in_dim(block, 0, width, axis=dim), axis, backward)
        block = jnp.concatenate([low, block, high], axis=dim)
    return block


def line_product(block, line_op):
    return lax.dot_general(
        block, line_op, (((3,), (1,)), ((), ())), preferred_element_type=jnp.float32
    )


def z_stencil(padded, planes):
    widened = padded.astype(jnp.float32)
    total = jnp.zeros((widened.shape[0], planes) + widened.shape[2:], jnp.float32)
    for offset in range(WIDTH):
        reach = offset + 1
        upper = widened[:, WIDTH + reach : WIDTH + reach + planes]
        lower = widened[:, WIDTH - reach : WIDTH - reach + planes]
        total = total + STENCIL_COEFS[offset] * (upper - lower)
    return total.astype(jnp.bfloat16)


def plain(flux_x, flux_y, flux_z, line_op):
    planes = flux_z.shape[1]
    z_deriv = z_stencil(with_halo(flux_z, (("gz", 1),), WIDTH), planes)
    y_part = line_product(
        lax.all_to_all(flux_y, "py", split_axis=2, concat_axis=3, tiled=True), line_op
    ).astype(jnp.bfloat16)
    products = line_product(
        lax.all_to_all(flux_x, "px", split_axis=1, concat_axis=3, tiled=True), line_op
    )
    moved = lax.all_to_all(z_deriv, "px", split_axis=1, concat_axis=3, tiled=True)
    xz_part = (products + moved.astype(jnp.float32)).astype(jnp.bfloat16)
    return (xz_part, y_part)


def partner(axis, flip):
    return lax.axis_index(axis) ^ flip


def swap(block, axis, flip):
    pairs = [(i, i ^ flip) for i in range(lax.axis_size(axis))]
    return lax.ppermute(block, axis, pairs)


def call(kernel, out_shape, *operands, limit, flops=0, scratch=(), far=(), far_out=False):
    moved = sum(a.size * a.dtype.itemsize for a in (*operands, *jax.tree.leaves(out_shape)))
    operands = [
        pltpu.with_memory_space_constraint(a, pltpu.HBM) if index in far else a
        for index, a in enumerate(operands)
    ]
    return pl.pallas_call(
        kernel,
        out_shape=out_shape,
        in_specs=[FAR if index in far else VMEM for index in range(len(operands))],
        out_specs=jax.tree.map(lambda _: FAR if far_out else VMEM, out_shape),
        scratch_shapes=scratch,
        compiler_params=pltpu.CompilerParams(vmem_limit_bytes=limit * MIB),
        cost_estimate=pl.CostEstimate(flops=flops, bytes_accessed=moved, transcendentals=0),
    )(*operands)


def pick_rows(lines, rows, count, flip, out):
    kept = GROUP // count
    line = lax.broadcasted_iota(jnp.int32, (kept, GROUP), 0)
    source = lax.broadcasted_iota(jnp.int32, (kept, GROUP), 1)
    wanted = (line // rows) * (count * rows) + partner("py", flip) * rows + line % rows
    chosen = (source == wanted).astype(jnp.bfloat16)
    for part in range(lines.shape[0] // GROUP):
        picked = jnp.dot(
            chosen,
            lines[part * GROUP : (part + 1) * GROUP, :],
            preferred_element_type=jnp.float32,
        )
        out[part * kept : (part + 1) * kept, :] = picked.astype(jnp.bfloat16)


def first_kernel(rows, count, flips, planes, flux_y, flux_x, flux_z, *refs):
    sent_y, (held_y, faces, across, sems) = refs[: len(flips)], refs[len(flips) :]
    last = flux_z.shape[1] - WIDTH
    moves = [(flux_y, held_y)]
    moves += [(flux_z.at[:, pl.ds(last, WIDTH)], faces.at[:, :WIDTH])]
    moves += [(flux_z.at[:, :WIDTH], faces.at[:, WIDTH:])]
    for flip, place in ((2, across.at[0]), (3, across.at[1])):
        moves.append((flux_x.at[:, pl.ds(partner("px", flip) * planes, planes)], place))
    copies = [pltpu.make_async_copy(a, b, sems.at[i]) for i, (a, b) in enumerate(moves)]
    for copy in copies:
        copy.start()
    copies[0].wait()
    for flip, out in zip(flips, sent_y):
        pick_rows(held_y, rows, count, flip, out)
    for copy in copies[1:]:
        copy.wait()


def second_kernel(rows, count, flips, flux_y, *outs):
    for flip, out in zip(flips, outs):
        pick_rows(flux_y, rows, count, flip, out)


def join_x_kernel(planes, after, flux_x, got, out):
    out[0] = flux_x[:, pl.ds(partner("px", 1) * planes, planes)]
    out[1] = got[1]


def join_kernel(stay, got, *refs):
    out = refs[-1]
    out[0] = stay[1]
    out[1] = got[1]


def stencil_kernel(planes, flux_z, faces, across, stay, held):
    own = flux_z.shape[1]

    def plane(variable, index):
        if index < 0:
            return faces[variable, WIDTH + index].astype(jnp.float32)
        if index >= own:
            return faces[variable, WIDTH + index - own].astype(jnp.float32)
        return flux_z[variable, index].astype(jnp.float32)

    for variable in range(flux_z.shape[0]):
        for index in range(own):
            total = jnp.zeros(flux_z.shape[2:], jnp.float32)
            for offset in range(WIDTH):
                upper = plane(variable, index + offset + 1)
                lower = plane(variable, index - offset - 1)
                total = total + STENCIL_COEFS[offset] * (upper - lower)
            held[variable, index] = total.astype(jnp.bfloat16)
    for flip, place in ((2, across.at[0]), (3, across.at[1]), (0, stay.at[0]), (1, stay.at[1])):
        place[...] = held[:, pl.ds(partner("px", flip) * planes, planes)]


def times(block, line_op, to, of):
    return lax.dot_general(
        block, line_op[to, of], (((1,), (1,)), ((), ())), preferred_element_type=jnp.float32
    )


def blocks_of(stay, across, joined):
    return ((0, stay, 0), (2, across, 0), (1, joined, 0), (3, joined, 1))


def at_block(axis, flip, count, body):
    held = partner(axis, flip)
    for index in range(count):
        pl.when(held == index)(functools.partial(body, index))


def in_order(stay, across, joined, held):
    for flip, ref, index in blocks_of(stay, across, joined):
        held[partner("px", flip)] = stay if ref is stay and stay.ndim == 2 else ref[index]


def own_kernel(own_y, line_op, after, out):
    width = own_y.shape[1]

    def body(index):
        out[...] = times(own_y[...], line_op, ALL, pl.ds(index * width, width))

    at_block("py", 0, line_op.shape[1] // width, body)


def main_kernel(planes, flux_x, across, joined, line_op, out, held):
    width = across.shape[2]
    own = flux_x[:, pl.ds(partner("px", 0) * planes, planes)].reshape(-1, width)
    in_order(own, across, joined, held)
    for start in range(0, line_op.shape[0], width):
        place = pl.ds(start, width)
        total = None
        for index in range(held.shape[0]):
            part = times(held[index], line_op, place, pl.ds(index * width, width))
            total = part if total is None else total + part
        out[:, place] = total


def add_kernel(across, joined, stay, products, after, out, held):
    width = stay.shape[2]
    in_order(stay, across, joined, held)
    for index in range(held.shape[0]):
        place = pl.ds(index * width, width)
        out[:, place] = (products[:, place] + held[index].astype(jnp.float32)).astype(jnp.bfloat16)


def step_kernel(flip, block, before, line_op, out):
    width = block.shape[1]

    def body(index):
        part = times(block[...], line_op, ALL, pl.ds(index * width, width))
        out[...] = before[...] + part

    at_block("py", flip, line_op.shape[1] // width, body)


def ordered_step_kernel(flip, before, block, after, line_op, out):
    step_kernel(flip, block, before, line_op, out)


def late_kernel(flip, early, block, line_op, out, held, sems):
    width = block.shape[1]
    rows = out.shape[1]
    places = [pl.ds(start, width) for start in range(0, out.shape[2], width)]
    copies = [
        pltpu.make_async_copy(held.at[:, :, place], out.at[:, :, place], sems.at[i])
        for i, place in enumerate(places)
    ]

    def body(index):
        for place, copy in zip(places, copies):
            part = times(block[...], line_op, place, pl.ds(index * width, width))
            total = early[:, place] + part
            held[:, :, place] = total.reshape(-1, rows, width).astype(jnp.bfloat16)
            copy.start()

    at_block("py", flip, line_op.shape[1] // width, body)
    for copy in copies:
        copy.wait()


def local(flux_x, flux_y, flux_z, line_op):
    variables, slab, lines, x_width = flux_x.shape
    x_count, y_count = lax.axis_size("px"), lax.axis_size("py")
    planes = slab // x_count
    x_lines, y_width = flux_y.shape[2:]
    rows = x_lines // y_count
    line = line_op.shape[0]
    gathered = variables * slab * rows
    lines_x = variables * planes * lines
    bf16 = jnp.bfloat16

    def like(*shape, kind=bf16):
        return jax.ShapeDtypeStruct(shape, kind)

    rows_y = flux_y.reshape(-1, y_width)
    chunk_y = like(gathered, y_width)
    pair_x = like(2, variables, planes, lines, x_width)
    sent_2, sent_1, held_y, faces, across_x = call(
        functools.partial(first_kernel, rows, y_count, (2, 1), planes),
        [
            chunk_y,
            chunk_y,
            like(*rows_y.shape),
            like(variables, 2 * WIDTH, lines, x_width),
            pair_x,
        ],
        rows_y,
        flux_x,
        flux_z,
        far=(0, 1, 2),
        limit=8,
        scratch=[pltpu.SemaphoreType.DMA((5,))],
    )
    got_2 = swap(sent_2, "py", 2)
    faces = swap(faces, "gz", 1)
    across_x = swap(across_x, "px", 2)
    sent_3, own_y = call(
        functools.partial(second_kernel, rows, y_count, (3, 0)),
        [chunk_y] * 2,
        held_y,
        limit=8,
        flops=STAGE,
    )
    got_1 = swap(sent_1, "py", 1)
    got_3 = swap(sent_3, "py", 3)

    across_z, stay_z = call(
        functools.partial(stencil_kernel, planes),
        [pair_x, pair_x],
        flux_z,
        faces,
        limit=8,
        flops=STAGE,
        scratch=[pltpu.VMEM(flux_z.shape, bf16)],
    )
    joined_x = call(
        functools.partial(join_x_kernel, planes),
        pair_x,
        stay_z,
        flux_x,
        across_x,
        limit=8,
        flops=STAGE // 2,
    )
    flat = (2, lines_x, x_width)
    products_like = like(lines_x, line, kind=jnp.float32)
    sums_like = like(gathered, line, kind=jnp.float32)
    by_cell = pltpu.VMEM((x_count, lines_x, x_width), bf16)
    own_sum = call(
        own_kernel,
        sums_like,
        own_y,
        line_op,
        joined_x,
        limit=16,
        flops=STAGE,
    )
    joined_x = swap(joined_x, "px", 1)
    products = call(
        functools.partial(main_kernel, planes),
        products_like,
        flux_x,
        across_x.reshape(flat),
        joined_x.reshape(flat),
        line_op,
        limit=16,
        flops=STAGE,
        scratch=[by_cell],
    )
    across_z = swap(across_z, "px", 2)
    joined_z = swap(
        call(join_kernel, pair_x, stay_z, across_z, products, limit=8, flops=STAGE), "px", 1
    )
    block_flops = 2 * gathered * y_width * line
    sum_2 = call(
        functools.partial(step_kernel, 2),
        sums_like,
        got_2,
        own_sum,
        line_op,
        limit=16,
        flops=STAGE,
    )
    xz_part = call(
        add_kernel,
        like(lines_x, line),
        *(a.reshape(flat) for a in (across_z, joined_z, stay_z)),
        products,
        sum_2,
        limit=8,
        scratch=[by_cell],
    )
    sum_1 = call(
        functools.partial(ordered_step_kernel, 1),
        sums_like,
        sum_2,
        got_1,
        xz_part,
        line_op,
        far=(2,),
        limit=16,
        flops=block_flops,
    )
    y_like = like(variables * slab, rows, line)
    y_part = call(
        functools.partial(late_kernel, 3),
        y_like,
        sum_1,
        got_3,
        line_op,
        far_out=True,
        limit=16,
        flops=block_flops,
        scratch=[
            pltpu.VMEM(y_like.shape, bf16),
            pltpu.SemaphoreType.DMA((line // y_width,)),
        ],
    )
    y_part, xz_part = lax.optimization_barrier((y_part, xz_part))
    return (
        xz_part.reshape(variables, planes, lines, line),
        y_part.reshape(variables, slab, rows, line),
    )


def solution(mesh):
    fits = mesh.shape["py"] == 4 and mesh.shape["px"] == 4 and mesh.shape["gz"] == 2
    return jax.shard_map(
        local if fits else plain,
        mesh=mesh,
        in_specs=(
            P(None, "gz", "py", "px"),
            P(None, "gz", "px", "py"),
            P(None, "gz", "py", "px"),
            P(),
        ),
        out_specs=(P(None, ("gz", "px"), "py", None), P(None, "gz", ("px", "py"), None)),
        check_vma=False,
    )
```

```python
import functools

import jax
import jax.numpy as jnp
from jax import lax
from jax.experimental import pallas as pl
from jax.experimental.pallas import tpu as pltpu
from jax.sharding import PartitionSpec as P

STENCIL_COEFS = (0.8, -0.2, 4.0 / 105.0, -1.0 / 280.0)
WIDTH = 4
GROUP = 256
STAGE = 3 * 10**9
MIB = 1 << 20
VMEM = pl.BlockSpec(memory_space=pltpu.VMEM)
FAR = pl.BlockSpec(memory_space=pltpu.HBM)


def with_halo(block, sides, width):
    for axis, dim in sides:
        count = lax.axis_size(axis)
        forward = [(i, i + 1) for i in range(count - 1)]
        forward.append((count - 1, 0))
        backward = [(target, source) for source, target in forward]
        low = lax.ppermute(
            lax.slice_in_dim(block, block.shape[dim] - width, None, axis=dim), axis, forward
        )
        high = lax.ppermute(lax.slice_in_dim(block, 0, width, axis=dim), axis, backward)
        block = jnp.concatenate([low, block, high], axis=dim)
    return block


def line_product(block, line_op):
    return lax.dot_general(
        block, line_op, (((3,), (1,)), ((), ())), preferred_element_type=jnp.float32
    )


def z_stencil(padded, planes):
    widened = padded.astype(jnp.float32)
    total = jnp.zeros((widened.shape[0], planes) + widened.shape[2:], jnp.float32)
    for offset in range(WIDTH):
        reach = offset + 1
        upper = widened[:, WIDTH + reach : WIDTH + reach + planes]
        lower = widened[:, WIDTH - reach : WIDTH - reach + planes]
        total = total + STENCIL_COEFS[offset] * (upper - lower)
    return total.astype(jnp.bfloat16)


def plain(flux_x, flux_y, flux_z, line_op):
    planes = flux_z.shape[1]
    z_deriv = z_stencil(with_halo(flux_z, (("gz", 1),), WIDTH), planes)
    y_part = line_product(
        lax.all_to_all(flux_y, "py", split_axis=2, concat_axis=3, tiled=True), line_op
    ).astype(jnp.bfloat16)
    products = line_product(
        lax.all_to_all(flux_x, "px", split_axis=1, concat_axis=3, tiled=True), line_op
    )
    moved = lax.all_to_all(z_deriv, "px", split_axis=1, concat_axis=3, tiled=True)
    xz_part = (products + moved.astype(jnp.float32)).astype(jnp.bfloat16)
    return (xz_part, y_part)


def partner(axis, flip):
    return lax.axis_index(axis) ^ flip


def swap(block, axis, flip):
    pairs = [(i, i ^ flip) for i in range(lax.axis_size(axis))]
    return lax.ppermute(block, axis, pairs)


def call(kernel, out_shape, *operands, limit, flops=0, scratch=(), far=(), far_out=()):
    single = not isinstance(out_shape, list)
    out_shape = [out_shape] if single else out_shape
    moved = sum(a.size * a.dtype.itemsize for a in (*operands, *jax.tree.leaves(out_shape)))
    operands = [
        pltpu.with_memory_space_constraint(a, pltpu.HBM) if index in far else a
        for index, a in enumerate(operands)
    ]
    results = pl.pallas_call(
        kernel,
        out_shape=out_shape,
        in_specs=[FAR if index in far else VMEM for index in range(len(operands))],
        out_specs=[FAR if index in far_out else VMEM for index in range(len(out_shape))],
        scratch_shapes=scratch,
        compiler_params=pltpu.CompilerParams(vmem_limit_bytes=limit * MIB),
        cost_estimate=pl.CostEstimate(flops=flops, bytes_accessed=moved, transcendentals=0),
    )(*operands)
    return results[0] if single else results


def pick_rows(lines, rows, count, flip, out):
    kept = GROUP // count
    line = lax.broadcasted_iota(jnp.int32, (kept, GROUP), 0)
    source = lax.broadcasted_iota(jnp.int32, (kept, GROUP), 1)
    wanted = (line // rows) * (count * rows) + partner("py", flip) * rows + line % rows
    chosen = (source == wanted).astype(jnp.bfloat16)
    for part in range(lines.shape[0] // GROUP):
        picked = jnp.dot(
            chosen,
            lines[part * GROUP : (part + 1) * GROUP, :],
            preferred_element_type=jnp.float32,
        )
        out[part * kept : (part + 1) * kept, :] = picked.astype(jnp.bfloat16)


def first_kernel(rows, count, flips, planes, flux_y, flux_x, flux_z, *refs):
    sent_y, (held_y, faces, across, sems) = refs[: len(flips)], refs[len(flips) :]
    last = flux_z.shape[1] - WIDTH
    moves = [(flux_y, held_y)]
    moves += [(flux_z.at[:, pl.ds(last, WIDTH)], faces.at[:, :WIDTH])]
    moves += [(flux_z.at[:, :WIDTH], faces.at[:, WIDTH:])]
    for flip, place in ((2, across.at[0]), (3, across.at[1])):
        moves.append((flux_x.at[:, pl.ds(partner("px", flip) * planes, planes)], place))
    copies = [pltpu.make_async_copy(a, b, sems.at[i]) for i, (a, b) in enumerate(moves)]
    for copy in copies:
        copy.start()
    copies[0].wait()
    for flip, out in zip(flips, sent_y):
        pick_rows(held_y, rows, count, flip, out)
    for copy in copies[1:]:
        copy.wait()


def second_kernel(rows, count, flips, flux_y, *outs):
    for flip, out in zip(flips, outs):
        pick_rows(flux_y, rows, count, flip, out)


def join_x_kernel(planes, after, flux_x, got, out):
    out[0] = flux_x[:, pl.ds(partner("px", 1) * planes, planes)]
    out[1] = got[1]


def join_kernel(stay, got, *refs):
    out = refs[-1]
    out[0] = stay[1]
    out[1] = got[1]


def stencil_kernel(planes, flux_z, faces, across, stay, held):
    own = flux_z.shape[1]

    def plane(variable, index):
        if index < 0:
            return faces[variable, WIDTH + index].astype(jnp.float32)
        if index >= own:
            return faces[variable, WIDTH + index - own].astype(jnp.float32)
        return flux_z[variable, index].astype(jnp.float32)

    for variable in range(flux_z.shape[0]):
        for index in range(own):
            total = jnp.zeros(flux_z.shape[2:], jnp.float32)
            for offset in range(WIDTH):
                upper = plane(variable, index + offset + 1)
                lower = plane(variable, index - offset - 1)
                total = total + STENCIL_COEFS[offset] * (upper - lower)
            held[variable, index] = total.astype(jnp.bfloat16)
    for flip, place in ((2, across.at[0]), (3, across.at[1]), (0, stay.at[0]), (1, stay.at[1])):
        place[...] = held[:, pl.ds(partner("px", flip) * planes, planes)]


def cells(axis, flip, width):
    return pl.ds(pl.multiple_of(partner(axis, flip) * width, width), width)


def times(block, line_op, to, of):
    return lax.dot_general(
        block, line_op[to, of], (((1,), (1,)), ((), ())), preferred_element_type=jnp.float32
    )


def blocks_of(stay, across, joined):
    return ((0, stay, 0), (2, across, 0), (1, joined, 0), (3, joined, 1))


def own_kernel(own_y, line_op, after, out_y):
    width = own_y.shape[1]
    for start in range(0, line_op.shape[0], width):
        place = pl.ds(start, width)
        out_y[:, place] = times(own_y[...], line_op, place, cells("py", 0, width))


def main_kernel(planes, flux_x, across, joined, line_op, out):
    width = across.shape[2]
    own = flux_x[:, pl.ds(partner("px", 0) * planes, planes)].reshape(-1, width)
    for start in range(0, line_op.shape[0], width):
        place = pl.ds(start, width)
        total = times(own, line_op, place, cells("px", 0, width))
        for flip, ref, index in blocks_of(None, across, joined)[1:]:
            total = total + times(ref[index], line_op, place, cells("px", flip, width))
        out[:, place] = total


def add_kernel(flip, across, joined, stay, products, line_op, after, out, turned, held, sem):
    width = stay.shape[2]
    for partner_x, ref, index in blocks_of(stay, across, joined):
        place = cells("px", partner_x, width)
        held[:, place] = (products[:, place] + ref[index].astype(jnp.float32)).astype(jnp.bfloat16)
    copy = pltpu.make_async_copy(held, out, sem)
    copy.start()
    depth = turned.shape[0]
    for start in range(0, line_op.shape[0], depth):
        place = pl.ds(start, depth)
        turned[:, place] = line_op[place, cells("py", flip, depth)].T
    copy.wait()


def step_kernel(flip, block, before, line_op, out):
    place = pl.ds(0, out.shape[1])
    out[...] = before[...] + times(block[...], line_op, place, cells("py", flip, block.shape[1]))


def ordered_step_kernel(flip, before, block, after, line_op, out):
    step_kernel(flip, block, before, line_op, out)


def late_kernel(early, block, turned, out, held, sems):
    width = block.shape[1]
    rows = out.shape[1]
    copies = []
    for start in range(0, out.shape[2], width):
        place = pl.ds(start, width)
        part = jnp.dot(block[...], turned[:, place], preferred_element_type=jnp.float32)
        total = early[:, place] + part
        held[:, :, place] = total.reshape(-1, rows, width).astype(jnp.bfloat16)
        copy = pltpu.make_async_copy(
            held.at[:, :, place], out.at[:, :, place], sems.at[len(copies)]
        )
        copy.start()
        copies.append(copy)
    for copy in copies:
        copy.wait()


def local(flux_x, flux_y, flux_z, line_op):
    variables, slab, lines, x_width = flux_x.shape
    x_count, y_count = lax.axis_size("px"), lax.axis_size("py")
    planes = slab // x_count
    x_lines, y_width = flux_y.shape[2:]
    rows = x_lines // y_count
    line = line_op.shape[0]
    gathered = variables * slab * rows
    lines_x = variables * planes * lines
    bf16 = jnp.bfloat16

    def like(*shape, kind=bf16):
        return jax.ShapeDtypeStruct(shape, kind)

    rows_y = flux_y.reshape(-1, y_width)
    chunk_y = like(gathered, y_width)
    pair_x = like(2, variables, planes, lines, x_width)
    sent_2, sent_1, held_y, faces, across_x = call(
        functools.partial(first_kernel, rows, y_count, (2, 1), planes),
        [
            chunk_y,
            chunk_y,
            like(*rows_y.shape),
            like(variables, 2 * WIDTH, lines, x_width),
            pair_x,
        ],
        rows_y,
        flux_x,
        flux_z,
        far=(0, 1, 2),
        limit=8,
        scratch=[pltpu.SemaphoreType.DMA((5,))],
    )
    got_2 = swap(sent_2, "py", 2)
    faces = swap(faces, "gz", 1)
    across_x = swap(across_x, "px", 2)
    sent_3, own_y = call(
        functools.partial(second_kernel, rows, y_count, (3, 0)),
        [chunk_y] * 2,
        held_y,
        limit=8,
        flops=STAGE,
    )
    got_1 = swap(sent_1, "py", 1)
    got_3 = swap(sent_3, "py", 3)

    across_z, stay_z = call(
        functools.partial(stencil_kernel, planes),
        [pair_x, pair_x],
        flux_z,
        faces,
        limit=8,
        flops=STAGE,
        scratch=[pltpu.VMEM(flux_z.shape, bf16)],
    )
    joined_x = call(
        functools.partial(join_x_kernel, planes),
        pair_x,
        stay_z,
        flux_x,
        across_x,
        limit=8,
        flops=STAGE // 2,
    )
    flat = (2, lines_x, x_width)
    products_like = like(lines_x, line, kind=jnp.float32)
    sums_like = like(gathered, line, kind=jnp.float32)
    own_sum = call(
        own_kernel,
        sums_like,
        own_y,
        line_op,
        joined_x,
        limit=16,
        flops=STAGE,
    )
    joined_x = swap(joined_x, "px", 1)
    products = call(
        functools.partial(main_kernel, planes),
        products_like,
        flux_x,
        across_x.reshape(flat),
        joined_x.reshape(flat),
        line_op,
        limit=16,
        flops=STAGE,
    )
    across_z = swap(across_z, "px", 2)
    joined_z = swap(
        call(join_kernel, pair_x, stay_z, across_z, products, limit=8, flops=STAGE), "px", 1
    )
    block_flops = 2 * gathered * y_width * line
    sum_2 = call(
        functools.partial(step_kernel, 2),
        sums_like,
        got_2,
        own_sum,
        line_op,
        limit=16,
        flops=STAGE,
    )
    xz_part, turned = call(
        functools.partial(add_kernel, 3),
        [like(lines_x, line), like(y_width, line)],
        *(a.reshape(flat) for a in (across_z, joined_z, stay_z)),
        products,
        line_op,
        sum_2,
        far_out=(0,),
        limit=16,
        scratch=[pltpu.VMEM((lines_x, line), bf16), pltpu.SemaphoreType.DMA],
    )
    sum_1 = call(
        functools.partial(ordered_step_kernel, 1),
        sums_like,
        sum_2,
        got_1,
        xz_part,
        line_op,
        far=(2,),
        limit=16,
        flops=block_flops,
    )
    y_like = like(variables * slab, rows, line)
    y_part = call(
        late_kernel,
        y_like,
        sum_1,
        got_3,
        turned,
        far_out=(0,),
        limit=16,
        flops=block_flops,
        scratch=[
            pltpu.VMEM(y_like.shape, bf16),
            pltpu.SemaphoreType.DMA((line // y_width,)),
        ],
    )
    y_part, xz_part = lax.optimization_barrier((y_part, xz_part))
    return (
        xz_part.reshape(variables, planes, lines, line),
        y_part.reshape(variables, slab, rows, line),
    )


def solution(mesh):
    fits = mesh.shape["py"] == 4 and mesh.shape["px"] == 4 and mesh.shape["gz"] == 2
    return jax.shard_map(
        local if fits else plain,
        mesh=mesh,
        in_specs=(
            P(None, "gz", "py", "px"),
            P(None, "gz", "px", "py"),
            P(None, "gz", "py", "px"),
            P(),
        ),
        out_specs=(P(None, ("gz", "px"), "py", None), P(None, "gz", ("px", "py"), None)),
        check_vma=False,
    )
```

```python
import functools

import jax
import jax.numpy as jnp
from jax import lax
from jax.experimental import pallas as pl
from jax.experimental.pallas import tpu as pltpu
from jax.sharding import PartitionSpec as P

STENCIL_COEFS = (0.8, -0.2, 4.0 / 105.0, -1.0 / 280.0)
WIDTH = 4
GROUP = 256
STAGE = 3 * 10**9
MIB = 1 << 20
VMEM = pl.BlockSpec(memory_space=pltpu.VMEM)
FAR = pl.BlockSpec(memory_space=pltpu.HBM)


def with_halo(block, sides, width):
    for axis, dim in sides:
        count = lax.axis_size(axis)
        forward = [(i, i + 1) for i in range(count - 1)]
        forward.append((count - 1, 0))
        backward = [(target, source) for source, target in forward]
        low = lax.ppermute(
            lax.slice_in_dim(block, block.shape[dim] - width, None, axis=dim), axis, forward
        )
        high = lax.ppermute(lax.slice_in_dim(block, 0, width, axis=dim), axis, backward)
        block = jnp.concatenate([low, block, high], axis=dim)
    return block


def line_product(block, line_op):
    return lax.dot_general(
        block, line_op, (((3,), (1,)), ((), ())), preferred_element_type=jnp.float32
    )


def z_stencil(padded, planes):
    widened = padded.astype(jnp.float32)
    total = jnp.zeros((widened.shape[0], planes) + widened.shape[2:], jnp.float32)
    for offset in range(WIDTH):
        reach = offset + 1
        upper = widened[:, WIDTH + reach : WIDTH + reach + planes]
        lower = widened[:, WIDTH - reach : WIDTH - reach + planes]
        total = total + STENCIL_COEFS[offset] * (upper - lower)
    return total.astype(jnp.bfloat16)


def plain(flux_x, flux_y, flux_z, line_op):
    planes = flux_z.shape[1]
    z_deriv = z_stencil(with_halo(flux_z, (("gz", 1),), WIDTH), planes)
    y_part = line_product(
        lax.all_to_all(flux_y, "py", split_axis=2, concat_axis=3, tiled=True), line_op
    ).astype(jnp.bfloat16)
    products = line_product(
        lax.all_to_all(flux_x, "px", split_axis=1, concat_axis=3, tiled=True), line_op
    )
    moved = lax.all_to_all(z_deriv, "px", split_axis=1, concat_axis=3, tiled=True)
    xz_part = (products + moved.astype(jnp.float32)).astype(jnp.bfloat16)
    return (xz_part, y_part)


def partner(axis, flip):
    return lax.axis_index(axis) ^ flip


def swap(block, axis, flip):
    pairs = [(i, i ^ flip) for i in range(lax.axis_size(axis))]
    return lax.ppermute(block, axis, pairs)


def call(kernel, out_shape, *operands, limit, flops=0, scratch=(), far=(), far_out=()):
    single = not isinstance(out_shape, list)
    out_shape = [out_shape] if single else out_shape
    moved = sum(a.size * a.dtype.itemsize for a in (*operands, *jax.tree.leaves(out_shape)))
    operands = [
        pltpu.with_memory_space_constraint(a, pltpu.HBM) if index in far else a
        for index, a in enumerate(operands)
    ]
    results = pl.pallas_call(
        kernel,
        out_shape=out_shape,
        in_specs=[FAR if index in far else VMEM for index in range(len(operands))],
        out_specs=[FAR if index in far_out else VMEM for index in range(len(out_shape))],
        scratch_shapes=scratch,
        compiler_params=pltpu.CompilerParams(vmem_limit_bytes=limit * MIB),
        cost_estimate=pl.CostEstimate(flops=flops, bytes_accessed=moved, transcendentals=0),
    )(*operands)
    return results[0] if single else results


def pick_rows(lines, rows, count, flips, outs):
    kept = GROUP // count
    line = lax.broadcasted_iota(jnp.int32, (kept, GROUP), 0)
    source = lax.broadcasted_iota(jnp.int32, (kept, GROUP), 1)
    first = (line // rows) * (count * rows) + line % rows
    chosen = jnp.concatenate(
        [(source == first + partner("py", flip) * rows).astype(jnp.float32) for flip in flips]
    ).astype(jnp.bfloat16)
    for part in range(lines.shape[0] // GROUP):
        picked = jnp.dot(
            chosen,
            lines[part * GROUP : (part + 1) * GROUP, :],
            preferred_element_type=jnp.float32,
        ).astype(jnp.bfloat16)
        for index, out in enumerate(outs):
            out[part * kept : (part + 1) * kept, :] = picked[index * kept : (index + 1) * kept]


def first_kernel(rows, count, flips, planes, flux_y, flux_x, flux_z, *refs):
    sent_y, (held_y, faces, across, sems) = refs[: len(flips)], refs[len(flips) :]
    last = flux_z.shape[1] - WIDTH
    moves = [(flux_y, held_y)]
    moves += [(flux_z.at[:, pl.ds(last, WIDTH)], faces.at[:, :WIDTH])]
    moves += [(flux_z.at[:, :WIDTH], faces.at[:, WIDTH:])]
    for flip, place in ((2, across.at[0]), (3, across.at[1])):
        moves.append((flux_x.at[:, pl.ds(partner("px", flip) * planes, planes)], place))
    copies = [pltpu.make_async_copy(a, b, sems.at[i]) for i, (a, b) in enumerate(moves)]
    for copy in copies:
        copy.start()
    copies[0].wait()
    pick_rows(held_y, rows, count, flips, sent_y)
    for copy in copies[1:]:
        copy.wait()


def second_kernel(rows, count, flips, flux_y, *outs):
    pick_rows(flux_y, rows, count, flips, outs)


def join_x_kernel(planes, after, flux_x, got, out):
    out[0] = flux_x[:, pl.ds(partner("px", 1) * planes, planes)]
    out[1] = got[1]


def join_kernel(stay, got, *refs):
    out = refs[-1]
    out[0] = stay[1]
    out[1] = got[1]


def stencil_kernel(planes, flux_z, faces, across, stay, held):
    own = flux_z.shape[1]

    def plane(variable, index):
        if index < 0:
            return faces[variable, WIDTH + index].astype(jnp.float32)
        if index >= own:
            return faces[variable, WIDTH + index - own].astype(jnp.float32)
        return flux_z[variable, index].astype(jnp.float32)

    for variable in range(flux_z.shape[0]):
        for index in range(own):
            total = jnp.zeros(flux_z.shape[2:], jnp.float32)
            for offset in range(WIDTH):
                upper = plane(variable, index + offset + 1)
                lower = plane(variable, index - offset - 1)
                total = total + STENCIL_COEFS[offset] * (upper - lower)
            held[variable, index] = total.astype(jnp.bfloat16)
    for flip, place in ((2, across.at[0]), (3, across.at[1]), (0, stay.at[0]), (1, stay.at[1])):
        place[...] = held[:, pl.ds(partner("px", flip) * planes, planes)]


def cells(axis, flip, width):
    return pl.ds(pl.multiple_of(partner(axis, flip) * width, width), width)


def times(block, line_op, to, of):
    return lax.dot_general(
        block, line_op[to, of], (((1,), (1,)), ((), ())), preferred_element_type=jnp.float32
    )


def blocks_of(stay, across, joined):
    return ((0, stay, 0), (2, across, 0), (1, joined, 0), (3, joined, 1))


def own_kernel(own_y, line_op, after, out_y):
    width = own_y.shape[1]
    for start in range(0, line_op.shape[0], width):
        place = pl.ds(start, width)
        out_y[:, place] = times(own_y[...], line_op, place, cells("py", 0, width))


def main_kernel(planes, flux_x, across, joined, line_op, out):
    width = across.shape[2]
    own = flux_x[:, pl.ds(partner("px", 0) * planes, planes)].reshape(-1, width)
    for start in range(0, line_op.shape[0], width):
        place = pl.ds(start, width)
        total = times(own, line_op, place, cells("px", 0, width))
        for flip, ref, index in blocks_of(None, across, joined)[1:]:
            total = total + times(ref[index], line_op, place, cells("px", flip, width))
        out[:, place] = total


def add_kernel(flips, across, joined, stay, products, line_op, after, out, *refs):
    *turned, held, sem = refs
    width = stay.shape[2]
    for partner_x, ref, index in blocks_of(stay, across, joined):
        place = cells("px", partner_x, width)
        held[:, place] = (products[:, place] + ref[index].astype(jnp.float32)).astype(jnp.bfloat16)
    copy = pltpu.make_async_copy(held, out, sem)
    copy.start()
    for flip, block in zip(flips, turned):
        depth = block.shape[0]
        for start in range(0, line_op.shape[0], depth):
            place = pl.ds(start, depth)
            block[:, place] = line_op[place, cells("py", flip, depth)].T
    copy.wait()


def step_kernel(flip, block, before, line_op, out):
    place = pl.ds(0, out.shape[1])
    out[...] = before[...] + times(block[...], line_op, place, cells("py", flip, block.shape[1]))


def turned_step_kernel(before, block, turned, out):
    out[...] = before[...] + jnp.dot(
        block[...], turned[...], preferred_element_type=jnp.float32
    )


def late_kernel(early, block, turned, out, held, sems):
    width = block.shape[1]
    rows = out.shape[1]
    copies = []
    for start in range(0, out.shape[2], width):
        place = pl.ds(start, width)
        part = jnp.dot(block[...], turned[:, place], preferred_element_type=jnp.float32)
        total = early[:, place] + part
        held[:, :, place] = total.reshape(-1, rows, width).astype(jnp.bfloat16)
        copy = pltpu.make_async_copy(
            held.at[:, :, place], out.at[:, :, place], sems.at[len(copies)]
        )
        copy.start()
        copies.append(copy)
    for copy in copies:
        copy.wait()


def local(flux_x, flux_y, flux_z, line_op):
    variables, slab, lines, x_width = flux_x.shape
    x_count, y_count = lax.axis_size("px"), lax.axis_size("py")
    planes = slab // x_count
    x_lines, y_width = flux_y.shape[2:]
    rows = x_lines // y_count
    line = line_op.shape[0]
    gathered = variables * slab * rows
    lines_x = variables * planes * lines
    bf16 = jnp.bfloat16

    def like(*shape, kind=bf16):
        return jax.ShapeDtypeStruct(shape, kind)

    rows_y = flux_y.reshape(-1, y_width)
    chunk_y = like(gathered, y_width)
    pair_x = like(2, variables, planes, lines, x_width)
    sent_2, sent_1, held_y, faces, across_x = call(
        functools.partial(first_kernel, rows, y_count, (2, 1), planes),
        [
            chunk_y,
            chunk_y,
            like(*rows_y.shape),
            like(variables, 2 * WIDTH, lines, x_width),
            pair_x,
        ],
        rows_y,
        flux_x,
        flux_z,
        far=(0, 1, 2),
        limit=8,
        scratch=[pltpu.SemaphoreType.DMA((5,))],
    )
    got_2 = swap(sent_2, "py", 2)
    faces = swap(faces, "gz", 1)
    across_x = swap(across_x, "px", 2)
    sent_3, own_y = call(
        functools.partial(second_kernel, rows, y_count, (3, 0)),
        [chunk_y] * 2,
        held_y,
        limit=8,
        flops=STAGE,
    )
    got_1 = swap(sent_1, "py", 1)
    got_3 = swap(sent_3, "py", 3)

    across_z, stay_z = call(
        functools.partial(stencil_kernel, planes),
        [pair_x, pair_x],
        flux_z,
        faces,
        limit=8,
        flops=STAGE,
        scratch=[pltpu.VMEM(flux_z.shape, bf16)],
    )
    joined_x = call(
        functools.partial(join_x_kernel, planes),
        pair_x,
        stay_z,
        flux_x,
        across_x,
        limit=8,
        flops=STAGE // 2,
    )
    flat = (2, lines_x, x_width)
    products_like = like(lines_x, line, kind=jnp.float32)
    sums_like = like(gathered, line, kind=jnp.float32)
    own_sum = call(
        own_kernel,
        sums_like,
        own_y,
        line_op,
        joined_x,
        limit=16,
        flops=STAGE,
    )
    joined_x = swap(joined_x, "px", 1)
    products = call(
        functools.partial(main_kernel, planes),
        products_like,
        flux_x,
        across_x.reshape(flat),
        joined_x.reshape(flat),
        line_op,
        limit=16,
        flops=STAGE,
    )
    across_z = swap(across_z, "px", 2)
    joined_z = swap(
        call(join_kernel, pair_x, stay_z, across_z, products, limit=8, flops=STAGE), "px", 1
    )
    block_flops = 2 * gathered * y_width * line
    sum_2 = call(
        functools.partial(step_kernel, 2),
        sums_like,
        got_2,
        own_sum,
        line_op,
        limit=16,
        flops=STAGE,
    )
    xz_part, turned_1, turned_3 = call(
        functools.partial(add_kernel, (1, 3)),
        [like(lines_x, line), like(y_width, line), like(y_width, line)],
        *(a.reshape(flat) for a in (across_z, joined_z, stay_z)),
        products,
        line_op,
        sum_2,
        far_out=(0,),
        limit=16,
        scratch=[pltpu.VMEM((lines_x, line), bf16), pltpu.SemaphoreType.DMA],
    )
    sum_1 = call(
        turned_step_kernel,
        sums_like,
        sum_2,
        got_1,
        turned_1,
        limit=16,
        flops=block_flops,
    )
    y_like = like(variables * slab, rows, line)
    y_part = call(
        late_kernel,
        y_like,
        sum_1,
        got_3,
        turned_3,
        far_out=(0,),
        limit=16,
        flops=block_flops,
        scratch=[
            pltpu.VMEM(y_like.shape, bf16),
            pltpu.SemaphoreType.DMA((line // y_width,)),
        ],
    )
    y_part, xz_part = lax.optimization_barrier((y_part, xz_part))
    return (
        xz_part.reshape(variables, planes, lines, line),
        y_part.reshape(variables, slab, rows, line),
    )


def solution(mesh):
    fits = mesh.shape["py"] == 4 and mesh.shape["px"] == 4 and mesh.shape["gz"] == 2
    return jax.shard_map(
        local if fits else plain,
        mesh=mesh,
        in_specs=(
            P(None, "gz", "py", "px"),
            P(None, "gz", "px", "py"),
            P(None, "gz", "py", "px"),
            P(),
        ),
        out_specs=(P(None, ("gz", "px"), "py", None), P(None, "gz", ("px", "py"), None)),
        check_vma=False,
    )
```

```python
import functools

import jax
import jax.numpy as jnp
from jax import lax
from jax.experimental import pallas as pl
from jax.experimental.pallas import tpu as pltpu
from jax.sharding import PartitionSpec as P

STENCIL_COEFS = (0.8, -0.2, 4.0 / 105.0, -1.0 / 280.0)
WIDTH = 4
GROUP = 256
STAGE = 3 * 10**9
MIB = 1 << 20
VMEM = pl.BlockSpec(memory_space=pltpu.VMEM)
ALL = slice(None)
FAR = pl.BlockSpec(memory_space=pltpu.HBM)


def with_halo(block, sides, width):
    for axis, dim in sides:
        count = lax.axis_size(axis)
        forward = [(i, i + 1) for i in range(count - 1)]
        forward.append((count - 1, 0))
        backward = [(target, source) for source, target in forward]
        low = lax.ppermute(
            lax.slice_in_dim(block, block.shape[dim] - width, None, axis=dim), axis, forward
        )
        high = lax.ppermute(lax.slice_in_dim(block, 0, width, axis=dim), axis, backward)
        block = jnp.concatenate([low, block, high], axis=dim)
    return block


def line_product(block, line_op):
    return lax.dot_general(
        block, line_op, (((3,), (1,)), ((), ())), preferred_element_type=jnp.float32
    )


def z_stencil(padded, planes):
    widened = padded.astype(jnp.float32)
    total = jnp.zeros((widened.shape[0], planes) + widened.shape[2:], jnp.float32)
    for offset in range(WIDTH):
        reach = offset + 1
        upper = widened[:, WIDTH + reach : WIDTH + reach + planes]
        lower = widened[:, WIDTH - reach : WIDTH - reach + planes]
        total = total + STENCIL_COEFS[offset] * (upper - lower)
    return total.astype(jnp.bfloat16)


def plain(flux_x, flux_y, flux_z, line_op):
    planes = flux_z.shape[1]
    z_deriv = z_stencil(with_halo(flux_z, (("gz", 1),), WIDTH), planes)
    y_part = line_product(
        lax.all_to_all(flux_y, "py", split_axis=2, concat_axis=3, tiled=True), line_op
    ).astype(jnp.bfloat16)
    products = line_product(
        lax.all_to_all(flux_x, "px", split_axis=1, concat_axis=3, tiled=True), line_op
    )
    moved = lax.all_to_all(z_deriv, "px", split_axis=1, concat_axis=3, tiled=True)
    xz_part = (products + moved.astype(jnp.float32)).astype(jnp.bfloat16)
    return (xz_part, y_part)


def partner(axis, flip):
    return lax.axis_index(axis) ^ flip


def ahead(axis, shift):
    return lax.rem(lax.axis_index(axis) + shift, lax.axis_size(axis))


def behind(axis, shift):
    return ahead(axis, lax.axis_size(axis) - shift)


def rotate(block, axis, shift):
    count = lax.axis_size(axis)
    return lax.ppermute(block, axis, [(i, (i + shift) % count) for i in range(count)])


def swap(block, axis, flip):
    pairs = [(i, i ^ flip) for i in range(lax.axis_size(axis))]
    return lax.ppermute(block, axis, pairs)


def call(kernel, out_shape, *operands, limit, flops=0, scratch=(), far=(), far_out=()):
    single = not isinstance(out_shape, list)
    out_shape = [out_shape] if single else out_shape
    moved = sum(a.size * a.dtype.itemsize for a in (*operands, *jax.tree.leaves(out_shape)))
    operands = [
        pltpu.with_memory_space_constraint(a, pltpu.HBM) if index in far else a
        for index, a in enumerate(operands)
    ]
    results = pl.pallas_call(
        kernel,
        out_shape=out_shape,
        in_specs=[FAR if index in far else VMEM for index in range(len(operands))],
        out_specs=[FAR if index in far_out else VMEM for index in range(len(out_shape))],
        scratch_shapes=scratch,
        compiler_params=pltpu.CompilerParams(vmem_limit_bytes=limit * MIB),
        cost_estimate=pl.CostEstimate(flops=flops, bytes_accessed=moved, transcendentals=0),
    )(*operands)
    return results[0] if single else results


def pick_rows(lines, rows, count, shifts, outs):
    kept = GROUP // count
    line = lax.broadcasted_iota(jnp.int32, (kept, GROUP), 0)
    source = lax.broadcasted_iota(jnp.int32, (kept, GROUP), 1)
    first = (line // rows) * (count * rows) + line % rows
    chosen = jnp.concatenate(
        [(source == first + ahead("py", shift) * rows).astype(jnp.float32) for shift in shifts]
    ).astype(jnp.bfloat16)
    for part in range(lines.shape[0] // GROUP):
        picked = jnp.dot(
            chosen,
            lines[part * GROUP : (part + 1) * GROUP, :],
            preferred_element_type=jnp.float32,
        ).astype(jnp.bfloat16)
        for index, out in enumerate(outs):
            out[part * kept : (part + 1) * kept, :] = picked[index * kept : (index + 1) * kept]


def first_kernel(rows, count, shifts, planes, flux_y, flux_x, flux_z, *refs):
    sent_y, (held_y, faces, across, sems) = refs[: len(shifts)], refs[len(shifts) :]
    last = flux_z.shape[1] - WIDTH
    moves = [(flux_y, held_y)]
    moves += [(flux_z.at[:, pl.ds(last, WIDTH)], faces.at[:, :WIDTH])]
    moves += [(flux_z.at[:, :WIDTH], faces.at[:, WIDTH:])]
    for flip, place in ((2, across.at[0]), (3, across.at[1])):
        moves.append((flux_x.at[:, pl.ds(partner("px", flip) * planes, planes)], place))
    copies = [pltpu.make_async_copy(a, b, sems.at[i]) for i, (a, b) in enumerate(moves)]
    for copy in copies:
        copy.start()
    copies[0].wait()
    pick_rows(held_y, rows, count, shifts, sent_y)
    for copy in copies[1:]:
        copy.wait()


def second_kernel(rows, count, shifts, flux_y, *outs):
    pick_rows(flux_y, rows, count, shifts, outs)


def join_x_kernel(planes, after, flux_x, got, out):
    out[0] = flux_x[:, pl.ds(partner("px", 1) * planes, planes)]
    out[1] = got[1]


def join_kernel(stay, got, *refs):
    out = refs[-1]
    out[0] = stay[1]
    out[1] = got[1]


def stencil_kernel(planes, flux_z, faces, across, stay, held):
    own = flux_z.shape[1]

    def plane(variable, index):
        if index < 0:
            return faces[variable, WIDTH + index].astype(jnp.float32)
        if index >= own:
            return faces[variable, WIDTH + index - own].astype(jnp.float32)
        return flux_z[variable, index].astype(jnp.float32)

    for variable in range(flux_z.shape[0]):
        for index in range(own):
            total = jnp.zeros(flux_z.shape[2:], jnp.float32)
            for offset in range(WIDTH):
                upper = plane(variable, index + offset + 1)
                lower = plane(variable, index - offset - 1)
                total = total + STENCIL_COEFS[offset] * (upper - lower)
            held[variable, index] = total.astype(jnp.bfloat16)
    for flip, place in ((2, across.at[0]), (3, across.at[1]), (0, stay.at[0]), (1, stay.at[1])):
        place[...] = held[:, pl.ds(partner("px", flip) * planes, planes)]


def cells(index, width):
    return pl.ds(pl.multiple_of(index * width, width), width)


def times(block, line_op, to, of):
    return lax.dot_general(
        block, line_op[to, of], (((1,), (1,)), ((), ())), preferred_element_type=jnp.float32
    )


def blocks_of(stay, across, joined):
    return ((0, stay, 0), (2, across, 0), (1, joined, 0), (3, joined, 1))


def turn(line_op, index, out):
    depth = out.shape[0]
    for start in range(0, line_op.shape[0], depth):
        place = pl.ds(start, depth)
        out[:, place] = line_op[place, cells(index, depth)].T


def own_kernel(shift, own_y, line_op, after, out, turned):
    width = own_y.shape[1]
    out[...] = times(own_y[...], line_op, ALL, cells(lax.axis_index("py"), width))
    turn(line_op, behind("py", shift), turned)


def main_kernel(planes, flux_x, across, joined, line_op, out):
    width = across.shape[2]
    own = flux_x[:, pl.ds(partner("px", 0) * planes, planes)].reshape(-1, width)
    for start in range(0, line_op.shape[0], width):
        place = pl.ds(start, width)
        total = times(own, line_op, place, cells(partner("px", 0), width))
        for flip, ref, index in blocks_of(None, across, joined)[1:]:
            total = total + times(ref[index], line_op, place, cells(partner("px", flip), width))
        out[:, place] = total


def add_kernel(across, joined, stay, products, after, out):
    width = stay.shape[2]
    for flip, ref, index in blocks_of(stay, across, joined):
        place = cells(partner("px", flip), width)
        out[:, place] = (products[:, place] + ref[index].astype(jnp.float32)).astype(jnp.bfloat16)


def first_step_kernel(shift, later, block, before, line_op, out, turned):
    part = times(block[...], line_op, ALL, cells(behind("py", shift), block.shape[1]))
    out[...] = before[...] + part
    turn(line_op, behind("py", later), turned)


def next_step_kernel(before, block, turned, after, out):
    out[...] = before[...] + jnp.dot(
        block[...], turned[...], preferred_element_type=jnp.float32
    )


def late_kernel(early, block, turned, out, held, sems):
    width = block.shape[1]
    rows = out.shape[1]
    copies = []
    for start in range(0, out.shape[2], width):
        place = pl.ds(start, width)
        part = jnp.dot(block[...], turned[:, place], preferred_element_type=jnp.float32)
        total = early[:, place] + part
        held[:, :, place] = total.reshape(-1, rows, width).astype(jnp.bfloat16)
        copy = pltpu.make_async_copy(
            held.at[:, :, place], out.at[:, :, place], sems.at[len(copies)]
        )
        copy.start()
        copies.append(copy)
    for copy in copies:
        copy.wait()


def local(flux_x, flux_y, flux_z, line_op):
    variables, slab, lines, x_width = flux_x.shape
    x_count, y_count = lax.axis_size("px"), lax.axis_size("py")
    planes = slab // x_count
    x_lines, y_width = flux_y.shape[2:]
    rows = x_lines // y_count
    line = line_op.shape[0]
    gathered = variables * slab * rows
    lines_x = variables * planes * lines
    bf16 = jnp.bfloat16

    def like(*shape, kind=bf16):
        return jax.ShapeDtypeStruct(shape, kind)

    rows_y = flux_y.reshape(-1, y_width)
    chunk_y = like(gathered, y_width)
    pair_x = like(2, variables, planes, lines, x_width)
    sent_2, sent_1, held_y, faces, across_x = call(
        functools.partial(first_kernel, rows, y_count, (2, 1), planes),
        [
            chunk_y,
            chunk_y,
            like(*rows_y.shape),
            like(variables, 2 * WIDTH, lines, x_width),
            pair_x,
        ],
        rows_y,
        flux_x,
        flux_z,
        far=(0, 1, 2),
        limit=8,
        scratch=[pltpu.SemaphoreType.DMA((5,))],
    )
    got_2 = rotate(sent_2, "py", 2)
    faces = swap(faces, "gz", 1)
    across_x = swap(across_x, "px", 2)
    sent_3, own_y = call(
        functools.partial(second_kernel, rows, y_count, (3, 0)),
        [chunk_y] * 2,
        held_y,
        limit=8,
        flops=STAGE,
    )
    got_1 = rotate(sent_1, "py", 1)
    got_3 = rotate(sent_3, "py", 3)

    across_z, stay_z = call(
        functools.partial(stencil_kernel, planes),
        [pair_x, pair_x],
        flux_z,
        faces,
        limit=8,
        flops=STAGE,
        scratch=[pltpu.VMEM(flux_z.shape, bf16)],
    )
    joined_x = call(
        functools.partial(join_x_kernel, planes),
        pair_x,
        stay_z,
        flux_x,
        across_x,
        limit=8,
        flops=STAGE // 2,
    )
    flat = (2, lines_x, x_width)
    products_like = like(lines_x, line, kind=jnp.float32)
    sums_like = like(gathered, line, kind=jnp.float32)
    turned_like = like(y_width, line)
    own_sum, turned_3 = call(
        functools.partial(own_kernel, 3),
        [sums_like, turned_like],
        own_y,
        line_op,
        joined_x,
        limit=16,
        flops=STAGE,
    )
    joined_x = swap(joined_x, "px", 1)
    products = call(
        functools.partial(main_kernel, planes),
        products_like,
        flux_x,
        across_x.reshape(flat),
        joined_x.reshape(flat),
        line_op,
        limit=16,
        flops=STAGE,
    )
    across_z = swap(across_z, "px", 2)
    joined_z = swap(
        call(join_kernel, pair_x, stay_z, across_z, products, limit=8, flops=STAGE), "px", 1
    )
    block_flops = 2 * gathered * y_width * line
    sum_2, turned_1 = call(
        functools.partial(first_step_kernel, 2, 1),
        [sums_like, turned_like],
        got_2,
        own_sum,
        line_op,
        limit=16,
        flops=STAGE,
    )
    xz_part = call(
        add_kernel,
        like(lines_x, line),
        *(a.reshape(flat) for a in (across_z, joined_z, stay_z)),
        products,
        sum_2,
        limit=8,
    )
    sum_1 = call(
        next_step_kernel,
        sums_like,
        sum_2,
        got_1,
        turned_1,
        xz_part,
        far=(3,),
        limit=16,
        flops=block_flops,
    )
    y_like = like(variables * slab, rows, line)
    y_part = call(
        late_kernel,
        y_like,
        sum_1,
        got_3,
        turned_3,
        far_out=(0,),
        limit=16,
        flops=block_flops,
        scratch=[
            pltpu.VMEM(y_like.shape, bf16),
            pltpu.SemaphoreType.DMA((line // y_width,)),
        ],
    )
    y_part, xz_part = lax.optimization_barrier((y_part, xz_part))
    return (
        xz_part.reshape(variables, planes, lines, line),
        y_part.reshape(variables, slab, rows, line),
    )


def solution(mesh):
    fits = mesh.shape["py"] == 4 and mesh.shape["px"] == 4 and mesh.shape["gz"] == 2
    return jax.shard_map(
        local if fits else plain,
        mesh=mesh,
        in_specs=(
            P(None, "gz", "py", "px"),
            P(None, "gz", "px", "py"),
            P(None, "gz", "py", "px"),
            P(),
        ),
        out_specs=(P(None, ("gz", "px"), "py", None), P(None, "gz", ("px", "py"), None)),
        check_vma=False,
    )
```

```python
import functools

import jax
import jax.numpy as jnp
from jax import lax
from jax.experimental import pallas as pl
from jax.experimental.pallas import tpu as pltpu
from jax.sharding import PartitionSpec as P

STENCIL_COEFS = (0.8, -0.2, 4.0 / 105.0, -1.0 / 280.0)
WIDTH = 4
GROUP = 256
STAGE = 3 * 10**9
MIB = 1 << 20
VMEM = pl.BlockSpec(memory_space=pltpu.VMEM)
ALL = slice(None)
FAR = pl.BlockSpec(memory_space=pltpu.HBM)


def with_halo(block, sides, width):
    for axis, dim in sides:
        count = lax.axis_size(axis)
        forward = [(i, i + 1) for i in range(count - 1)]
        forward.append((count - 1, 0))
        backward = [(target, source) for source, target in forward]
        low = lax.ppermute(
            lax.slice_in_dim(block, block.shape[dim] - width, None, axis=dim), axis, forward
        )
        high = lax.ppermute(lax.slice_in_dim(block, 0, width, axis=dim), axis, backward)
        block = jnp.concatenate([low, block, high], axis=dim)
    return block


def line_product(block, line_op):
    return lax.dot_general(
        block, line_op, (((3,), (1,)), ((), ())), preferred_element_type=jnp.float32
    )


def z_stencil(padded, planes):
    widened = padded.astype(jnp.float32)
    total = jnp.zeros((widened.shape[0], planes) + widened.shape[2:], jnp.float32)
    for offset in range(WIDTH):
        reach = offset + 1
        upper = widened[:, WIDTH + reach : WIDTH + reach + planes]
        lower = widened[:, WIDTH - reach : WIDTH - reach + planes]
        total = total + STENCIL_COEFS[offset] * (upper - lower)
    return total.astype(jnp.bfloat16)


def plain(flux_x, flux_y, flux_z, line_op):
    planes = flux_z.shape[1]
    z_deriv = z_stencil(with_halo(flux_z, (("gz", 1),), WIDTH), planes)
    y_part = line_product(
        lax.all_to_all(flux_y, "py", split_axis=2, concat_axis=3, tiled=True), line_op
    ).astype(jnp.bfloat16)
    products = line_product(
        lax.all_to_all(flux_x, "px", split_axis=1, concat_axis=3, tiled=True), line_op
    )
    moved = lax.all_to_all(z_deriv, "px", split_axis=1, concat_axis=3, tiled=True)
    xz_part = (products + moved.astype(jnp.float32)).astype(jnp.bfloat16)
    return (xz_part, y_part)


def partner(axis, flip):
    return lax.axis_index(axis) ^ flip


def swap(block, axis, flip):
    pairs = [(i, i ^ flip) for i in range(lax.axis_size(axis))]
    return lax.ppermute(block, axis, pairs)


def call(kernel, out_shape, *operands, limit, flops=0, scratch=(), far=(), far_out=()):
    single = not isinstance(out_shape, list)
    out_shape = [out_shape] if single else out_shape
    moved = sum(a.size * a.dtype.itemsize for a in (*operands, *jax.tree.leaves(out_shape)))
    operands = [
        pltpu.with_memory_space_constraint(a, pltpu.HBM) if index in far else a
        for index, a in enumerate(operands)
    ]
    results = pl.pallas_call(
        kernel,
        out_shape=out_shape,
        in_specs=[FAR if index in far else VMEM for index in range(len(operands))],
        out_specs=[FAR if index in far_out else VMEM for index in range(len(out_shape))],
        scratch_shapes=scratch,
        compiler_params=pltpu.CompilerParams(vmem_limit_bytes=limit * MIB),
        cost_estimate=pl.CostEstimate(flops=flops, bytes_accessed=moved, transcendentals=0),
    )(*operands)
    return results[0] if single else results


def pick_rows(lines, rows, count, flips, outs):
    kept = GROUP // count
    line = lax.broadcasted_iota(jnp.int32, (kept, GROUP), 0)
    source = lax.broadcasted_iota(jnp.int32, (kept, GROUP), 1)
    first = (line // rows) * (count * rows) + line % rows
    chosen = jnp.concatenate(
        [(source == first + partner("py", flip) * rows).astype(jnp.float32) for flip in flips]
    ).astype(jnp.bfloat16)
    for part in range(lines.shape[0] // GROUP):
        picked = jnp.dot(
            chosen,
            lines[part * GROUP : (part + 1) * GROUP, :],
            preferred_element_type=jnp.float32,
        ).astype(jnp.bfloat16)
        for index, out in enumerate(outs):
            out[part * kept : (part + 1) * kept, :] = picked[index * kept : (index + 1) * kept]


def first_kernel(rows, count, flips, planes, flux_y, flux_x, flux_z, *refs):
    sent_y, (held_y, faces, across, sems) = refs[: len(flips)], refs[len(flips) :]
    last = flux_z.shape[1] - WIDTH
    moves = [(flux_y, held_y)]
    moves += [(flux_z.at[:, pl.ds(last, WIDTH)], faces.at[:, :WIDTH])]
    moves += [(flux_z.at[:, :WIDTH], faces.at[:, WIDTH:])]
    for flip, place in ((2, across.at[0]), (3, across.at[1])):
        moves.append((flux_x.at[:, pl.ds(partner("px", flip) * planes, planes)], place))
    copies = [pltpu.make_async_copy(a, b, sems.at[i]) for i, (a, b) in enumerate(moves)]
    for copy in copies:
        copy.start()
    copies[0].wait()
    pick_rows(held_y, rows, count, flips, sent_y)
    for copy in copies[1:]:
        copy.wait()


def second_kernel(rows, count, flips, flux_y, *outs):
    pick_rows(flux_y, rows, count, flips, outs)


def join_x_kernel(planes, after, flux_x, got, out):
    out[0] = flux_x[:, pl.ds(partner("px", 1) * planes, planes)]
    out[1] = got[1]


def join_kernel(stay, got, *refs):
    out = refs[-1]
    out[0] = stay[1]
    out[1] = got[1]


def stencil_kernel(planes, flux_z, faces, across, stay, held):
    own = flux_z.shape[1]

    def plane(variable, index):
        if index < 0:
            return faces[variable, WIDTH + index].astype(jnp.float32)
        if index >= own:
            return faces[variable, WIDTH + index - own].astype(jnp.float32)
        return flux_z[variable, index].astype(jnp.float32)

    for variable in range(flux_z.shape[0]):
        for index in range(own):
            total = jnp.zeros(flux_z.shape[2:], jnp.float32)
            for offset in range(WIDTH):
                upper = plane(variable, index + offset + 1)
                lower = plane(variable, index - offset - 1)
                total = total + STENCIL_COEFS[offset] * (upper - lower)
            held[variable, index] = total.astype(jnp.bfloat16)
    for flip, place in ((2, across.at[0]), (3, across.at[1]), (0, stay.at[0]), (1, stay.at[1])):
        place[...] = held[:, pl.ds(partner("px", flip) * planes, planes)]


def cells(index, width):
    return pl.ds(pl.multiple_of(index * width, width), width)


def times(block, line_op, to, of):
    return lax.dot_general(
        block, line_op[to, of], (((1,), (1,)), ((), ())), preferred_element_type=jnp.float32
    )


def blocks_of(stay, across, joined):
    return ((0, stay, 0), (2, across, 0), (1, joined, 0), (3, joined, 1))


def turn(line_op, index, out):
    depth = out.shape[0]
    for start in range(0, line_op.shape[0], depth):
        place = pl.ds(start, depth)
        out[:, place] = line_op[place, cells(index, depth)].T


def own_kernel(flip, own_y, line_op, after, out, turned):
    width = own_y.shape[1]
    out[...] = times(own_y[...], line_op, ALL, cells(lax.axis_index("py"), width))
    turn(line_op, partner("py", flip), turned)


def main_kernel(planes, flux_x, across, joined, line_op, out):
    width = across.shape[2]
    own = flux_x[:, pl.ds(partner("px", 0) * planes, planes)].reshape(-1, width)
    for start in range(0, line_op.shape[0], width):
        place = pl.ds(start, width)
        total = times(own, line_op, place, cells(partner("px", 0), width))
        for flip, ref, index in blocks_of(None, across, joined)[1:]:
            total = total + times(ref[index], line_op, place, cells(partner("px", flip), width))
        out[:, place] = total


def add_kernel(across, joined, stay, products, after, out):
    width = stay.shape[2]
    for flip, ref, index in blocks_of(stay, across, joined):
        place = cells(partner("px", flip), width)
        out[:, place] = (products[:, place] + ref[index].astype(jnp.float32)).astype(jnp.bfloat16)


def first_step_kernel(flip, later, block, before, line_op, out, turned):
    part = times(block[...], line_op, ALL, cells(partner("py", flip), block.shape[1]))
    out[...] = before[...] + part
    turn(line_op, partner("py", later), turned)


def next_step_kernel(after_y, after_z, block, before, turned, after, out):
    out[...] = before[...] + jnp.dot(
        block[...], turned[...], preferred_element_type=jnp.float32
    )


def late_kernel(early, block, turned, out, held, sems):
    width = block.shape[1]
    rows = out.shape[1]
    copies = []
    for start in range(0, out.shape[2], width):
        place = pl.ds(start, width)
        part = jnp.dot(block[...], turned[:, place], preferred_element_type=jnp.float32)
        total = early[:, place] + part
        held[:, :, place] = total.reshape(-1, rows, width).astype(jnp.bfloat16)
        copy = pltpu.make_async_copy(
            held.at[:, :, place], out.at[:, :, place], sems.at[len(copies)]
        )
        copy.start()
        copies.append(copy)
    for copy in copies:
        copy.wait()


def local(flux_x, flux_y, flux_z, line_op):
    variables, slab, lines, x_width = flux_x.shape
    x_count, y_count = lax.axis_size("px"), lax.axis_size("py")
    planes = slab // x_count
    x_lines, y_width = flux_y.shape[2:]
    rows = x_lines // y_count
    line = line_op.shape[0]
    gathered = variables * slab * rows
    lines_x = variables * planes * lines
    bf16 = jnp.bfloat16

    def like(*shape, kind=bf16):
        return jax.ShapeDtypeStruct(shape, kind)

    rows_y = flux_y.reshape(-1, y_width)
    chunk_y = like(gathered, y_width)
    pair_x = like(2, variables, planes, lines, x_width)
    sent_2, sent_1, held_y, faces, across_x = call(
        functools.partial(first_kernel, rows, y_count, (2, 1), planes),
        [
            chunk_y,
            chunk_y,
            like(*rows_y.shape),
            like(variables, 2 * WIDTH, lines, x_width),
            pair_x,
        ],
        rows_y,
        flux_x,
        flux_z,
        far=(0, 1, 2),
        limit=8,
        scratch=[pltpu.SemaphoreType.DMA((5,))],
    )
    got_2 = swap(sent_2, "py", 2)
    faces = swap(faces, "gz", 1)
    across_x = swap(across_x, "px", 2)
    sent_3, own_y = call(
        functools.partial(second_kernel, rows, y_count, (3, 0)),
        [chunk_y] * 2,
        held_y,
        limit=8,
        flops=STAGE,
    )
    got_1 = swap(sent_1, "py", 1)
    got_3 = swap(sent_3, "py", 3)

    across_z, stay_z = call(
        functools.partial(stencil_kernel, planes),
        [pair_x, pair_x],
        flux_z,
        faces,
        limit=8,
        flops=STAGE,
        scratch=[pltpu.VMEM(flux_z.shape, bf16)],
    )
    joined_x = call(
        functools.partial(join_x_kernel, planes),
        pair_x,
        stay_z,
        flux_x,
        across_x,
        limit=8,
        flops=STAGE // 2,
    )
    flat = (2, lines_x, x_width)
    products_like = like(lines_x, line, kind=jnp.float32)
    sums_like = like(gathered, line, kind=jnp.float32)
    turned_like = like(y_width, line)
    own_sum, turned_3 = call(
        functools.partial(own_kernel, 3),
        [sums_like, turned_like],
        own_y,
        line_op,
        joined_x,
        limit=16,
        flops=STAGE,
    )
    joined_x = swap(joined_x, "px", 1)
    products = call(
        functools.partial(main_kernel, planes),
        products_like,
        flux_x,
        across_x.reshape(flat),
        joined_x.reshape(flat),
        line_op,
        limit=16,
        flops=STAGE,
    )
    across_z = swap(across_z, "px", 2)
    joined_z = swap(
        call(join_kernel, pair_x, stay_z, across_z, products, limit=8, flops=STAGE), "px", 1
    )
    block_flops = 2 * gathered * y_width * line
    sum_2, turned_1 = call(
        functools.partial(first_step_kernel, 2, 1),
        [sums_like, turned_like],
        got_2,
        own_sum,
        line_op,
        limit=16,
        flops=STAGE,
    )
    xz_part = call(
        add_kernel,
        like(lines_x, line),
        *(a.reshape(flat) for a in (across_z, joined_z, stay_z)),
        products,
        sum_2,
        limit=8,
    )
    sum_1 = call(
        next_step_kernel,
        sums_like,
        got_2,
        stay_z,
        got_1,
        sum_2,
        turned_1,
        xz_part,
        far=(5,),
        limit=16,
        flops=block_flops,
    )
    y_like = like(variables * slab, rows, line)
    y_part = call(
        late_kernel,
        y_like,
        sum_1,
        got_3,
        turned_3,
        far_out=(0,),
        limit=16,
        flops=block_flops,
        scratch=[
            pltpu.VMEM(y_like.shape, bf16),
            pltpu.SemaphoreType.DMA((line // y_width,)),
        ],
    )
    y_part, xz_part = lax.optimization_barrier((y_part, xz_part))
    return (
        xz_part.reshape(variables, planes, lines, line),
        y_part.reshape(variables, slab, rows, line),
    )


def solution(mesh):
    fits = mesh.shape["py"] == 4 and mesh.shape["px"] == 4 and mesh.shape["gz"] == 2
    return jax.shard_map(
        local if fits else plain,
        mesh=mesh,
        in_specs=(
            P(None, "gz", "py", "px"),
            P(None, "gz", "px", "py"),
            P(None, "gz", "py", "px"),
            P(),
        ),
        out_specs=(P(None, ("gz", "px"), "py", None), P(None, "gz", ("px", "py"), None)),
        check_vma=False,
    )
```

```python
import functools

import jax
import jax.numpy as jnp
from jax import lax
from jax.experimental import pallas as pl
from jax.experimental.pallas import tpu as pltpu
from jax.sharding import PartitionSpec as P

STENCIL_COEFS = (0.8, -0.2, 4.0 / 105.0, -1.0 / 280.0)
WIDTH = 4
GROUP = 256
STAGE = 3 * 10**9
MIB = 1 << 20
VMEM = pl.BlockSpec(memory_space=pltpu.VMEM)
ALL = slice(None)
FAR = pl.BlockSpec(memory_space=pltpu.HBM)


def with_halo(block, sides, width):
    for axis, dim in sides:
        count = lax.axis_size(axis)
        forward = [(i, i + 1) for i in range(count - 1)]
        forward.append((count - 1, 0))
        backward = [(target, source) for source, target in forward]
        low = lax.ppermute(
            lax.slice_in_dim(block, block.shape[dim] - width, None, axis=dim), axis, forward
        )
        high = lax.ppermute(lax.slice_in_dim(block, 0, width, axis=dim), axis, backward)
        block = jnp.concatenate([low, block, high], axis=dim)
    return block


def line_product(block, line_op):
    return lax.dot_general(
        block, line_op, (((3,), (1,)), ((), ())), preferred_element_type=jnp.float32
    )


def z_stencil(padded, planes):
    widened = padded.astype(jnp.float32)
    total = jnp.zeros((widened.shape[0], planes) + widened.shape[2:], jnp.float32)
    for offset in range(WIDTH):
        reach = offset + 1
        upper = widened[:, WIDTH + reach : WIDTH + reach + planes]
        lower = widened[:, WIDTH - reach : WIDTH - reach + planes]
        total = total + STENCIL_COEFS[offset] * (upper - lower)
    return total.astype(jnp.bfloat16)


def plain(flux_x, flux_y, flux_z, line_op):
    planes = flux_z.shape[1]
    z_deriv = z_stencil(with_halo(flux_z, (("gz", 1),), WIDTH), planes)
    y_part = line_product(
        lax.all_to_all(flux_y, "py", split_axis=2, concat_axis=3, tiled=True), line_op
    ).astype(jnp.bfloat16)
    products = line_product(
        lax.all_to_all(flux_x, "px", split_axis=1, concat_axis=3, tiled=True), line_op
    )
    moved = lax.all_to_all(z_deriv, "px", split_axis=1, concat_axis=3, tiled=True)
    xz_part = (products + moved.astype(jnp.float32)).astype(jnp.bfloat16)
    return (xz_part, y_part)


def partner(axis, flip):
    return lax.axis_index(axis) ^ flip


def swap(block, axis, flip):
    pairs = [(i, i ^ flip) for i in range(lax.axis_size(axis))]
    return lax.ppermute(block, axis, pairs)


def call(kernel, out_shape, *operands, limit, flops=0, scratch=(), far=(), far_out=()):
    single = not isinstance(out_shape, list)
    out_shape = [out_shape] if single else out_shape
    moved = sum(a.size * a.dtype.itemsize for a in (*operands, *jax.tree.leaves(out_shape)))
    operands = [
        pltpu.with_memory_space_constraint(a, pltpu.HBM) if index in far else a
        for index, a in enumerate(operands)
    ]
    results = pl.pallas_call(
        kernel,
        out_shape=out_shape,
        in_specs=[FAR if index in far else VMEM for index in range(len(operands))],
        out_specs=[FAR if index in far_out else VMEM for index in range(len(out_shape))],
        scratch_shapes=scratch,
        compiler_params=pltpu.CompilerParams(vmem_limit_bytes=limit * MIB),
        cost_estimate=pl.CostEstimate(flops=flops, bytes_accessed=moved, transcendentals=0),
    )(*operands)
    return results[0] if single else results


def pick_rows(lines, rows, count, flips, outs):
    kept = GROUP // count
    line = lax.broadcasted_iota(jnp.int32, (kept, GROUP), 0)
    source = lax.broadcasted_iota(jnp.int32, (kept, GROUP), 1)
    first = (line // rows) * (count * rows) + line % rows
    chosen = jnp.concatenate(
        [(source == first + partner("py", flip) * rows).astype(jnp.float32) for flip in flips]
    ).astype(jnp.bfloat16)
    for part in range(lines.shape[0] // GROUP):
        picked = jnp.dot(
            chosen,
            lines[part * GROUP : (part + 1) * GROUP, :],
            preferred_element_type=jnp.float32,
        ).astype(jnp.bfloat16)
        for index, out in enumerate(outs):
            out[part * kept : (part + 1) * kept, :] = picked[index * kept : (index + 1) * kept]


def first_kernel(rows, count, flips, planes, flux_y, flux_x, flux_z, *refs):
    sent_y, (held_y, faces, across, sems) = refs[: len(flips)], refs[len(flips) :]
    last = flux_z.shape[1] - WIDTH
    moves = [(flux_y, held_y)]
    moves += [(flux_z.at[:, pl.ds(last, WIDTH)], faces.at[:, :WIDTH])]
    moves += [(flux_z.at[:, :WIDTH], faces.at[:, WIDTH:])]
    for flip, place in ((2, across.at[0]), (3, across.at[1])):
        moves.append((flux_x.at[:, pl.ds(partner("px", flip) * planes, planes)], place))
    copies = [pltpu.make_async_copy(a, b, sems.at[i]) for i, (a, b) in enumerate(moves)]
    for copy in copies:
        copy.start()
    copies[0].wait()
    pick_rows(held_y, rows, count, flips, sent_y)
    for copy in copies[1:]:
        copy.wait()


def second_kernel(rows, count, flips, flux_y, *outs):
    pick_rows(flux_y, rows, count, flips, outs)


def join_x_kernel(planes, after, flux_x, got, after_own, out):
    out[0] = flux_x[:, pl.ds(partner("px", 1) * planes, planes)]
    out[1] = got[1]


def join_kernel(stay, got, *refs):
    out = refs[-1]
    out[0] = stay[1]
    out[1] = got[1]


def stencil_kernel(planes, flux_z, faces, across, stay, held):
    own = flux_z.shape[1]

    def plane(variable, index):
        if index < 0:
            return faces[variable, WIDTH + index].astype(jnp.float32)
        if index >= own:
            return faces[variable, WIDTH + index - own].astype(jnp.float32)
        return flux_z[variable, index].astype(jnp.float32)

    for variable in range(flux_z.shape[0]):
        for index in range(own):
            total = jnp.zeros(flux_z.shape[2:], jnp.float32)
            for offset in range(WIDTH):
                upper = plane(variable, index + offset + 1)
                lower = plane(variable, index - offset - 1)
                total = total + STENCIL_COEFS[offset] * (upper - lower)
            held[variable, index] = total.astype(jnp.bfloat16)
    for flip, place in ((2, across.at[0]), (3, across.at[1]), (0, stay.at[0]), (1, stay.at[1])):
        place[...] = held[:, pl.ds(partner("px", flip) * planes, planes)]


def cells(index, width):
    return pl.ds(pl.multiple_of(index * width, width), width)


def times(block, line_op, to, of):
    return lax.dot_general(
        block, line_op[to, of], (((1,), (1,)), ((), ())), preferred_element_type=jnp.float32
    )


def blocks_of(stay, across, joined):
    return ((0, stay, 0), (2, across, 0), (1, joined, 0), (3, joined, 1))


def turn(line_op, index, out):
    depth = out.shape[0]
    for start in range(0, line_op.shape[0], depth):
        place = pl.ds(start, depth)
        out[:, place] = line_op[place, cells(index, depth)].T


def turn_kernel(flips, line_op, after, *outs):
    for flip, out in zip(flips, outs):
        turn(line_op, partner("py", flip), out)


def own_kernel(own_y, line_op, after, out):
    place = cells(lax.axis_index("py"), own_y.shape[1])
    out[...] = times(own_y[...], line_op, ALL, place)


def main_kernel(planes, flux_x, across, joined, line_op, after, out):
    width = across.shape[2]
    own = flux_x[:, pl.ds(partner("px", 0) * planes, planes)].reshape(-1, width)
    for start in range(0, line_op.shape[0], width):
        place = pl.ds(start, width)
        total = times(own, line_op, place, cells(partner("px", 0), width))
        for flip, ref, index in blocks_of(None, across, joined)[1:]:
            total = total + times(ref[index], line_op, place, cells(partner("px", flip), width))
        out[:, place] = total


def add_kernel(across, joined, stay, products, after, out):
    width = stay.shape[2]
    for flip, ref, index in blocks_of(stay, across, joined):
        place = cells(partner("px", flip), width)
        out[:, place] = (products[:, place] + ref[index].astype(jnp.float32)).astype(jnp.bfloat16)


def first_step_kernel(flip, block, before, line_op, out):
    place = cells(partner("py", flip), block.shape[1])
    out[...] = before[...] + times(block[...], line_op, ALL, place)


def next_step_kernel(after_y, after_z, block, before, turned, after, out):
    out[...] = before[...] + jnp.dot(
        block[...], turned[...], preferred_element_type=jnp.float32
    )


def late_kernel(early, block, turned, out, held, sems):
    width = block.shape[1]
    rows = out.shape[1]
    copies = []
    for start in range(0, out.shape[2], width):
        place = pl.ds(start, width)
        part = jnp.dot(block[...], turned[:, place], preferred_element_type=jnp.float32)
        total = early[:, place] + part
        held[:, :, place] = total.reshape(-1, rows, width).astype(jnp.bfloat16)
        copy = pltpu.make_async_copy(
            held.at[:, :, place], out.at[:, :, place], sems.at[len(copies)]
        )
        copy.start()
        copies.append(copy)
    for copy in copies:
        copy.wait()


def local(flux_x, flux_y, flux_z, line_op):
    variables, slab, lines, x_width = flux_x.shape
    x_count, y_count = lax.axis_size("px"), lax.axis_size("py")
    planes = slab // x_count
    x_lines, y_width = flux_y.shape[2:]
    rows = x_lines // y_count
    line = line_op.shape[0]
    gathered = variables * slab * rows
    lines_x = variables * planes * lines
    bf16 = jnp.bfloat16

    def like(*shape, kind=bf16):
        return jax.ShapeDtypeStruct(shape, kind)

    rows_y = flux_y.reshape(-1, y_width)
    chunk_y = like(gathered, y_width)
    pair_x = like(2, variables, planes, lines, x_width)
    sent_2, sent_1, held_y, faces, across_x = call(
        functools.partial(first_kernel, rows, y_count, (2, 1), planes),
        [
            chunk_y,
            chunk_y,
            like(*rows_y.shape),
            like(variables, 2 * WIDTH, lines, x_width),
            pair_x,
        ],
        rows_y,
        flux_x,
        flux_z,
        far=(0, 1, 2),
        limit=8,
        scratch=[pltpu.SemaphoreType.DMA((5,))],
    )
    got_2 = swap(sent_2, "py", 2)
    faces = swap(faces, "gz", 1)
    across_x = swap(across_x, "px", 2)
    sent_3, own_y = call(
        functools.partial(second_kernel, rows, y_count, (3, 0)),
        [chunk_y] * 2,
        held_y,
        limit=8,
        flops=STAGE,
    )
    got_1 = swap(sent_1, "py", 1)
    got_3 = swap(sent_3, "py", 3)

    across_z, stay_z = call(
        functools.partial(stencil_kernel, planes),
        [pair_x, pair_x],
        flux_z,
        faces,
        limit=8,
        flops=STAGE,
        scratch=[pltpu.VMEM(flux_z.shape, bf16)],
    )
    sums_like = like(gathered, line, kind=jnp.float32)
    own_sum = call(
        own_kernel, sums_like, own_y, line_op, stay_z, limit=16, flops=STAGE
    )
    joined_x = call(
        functools.partial(join_x_kernel, planes),
        pair_x,
        stay_z,
        flux_x,
        across_x,
        own_sum,
        limit=8,
        flops=STAGE // 2,
    )
    flat = (2, lines_x, x_width)
    products_like = like(lines_x, line, kind=jnp.float32)
    turned_like = like(y_width, line)
    turned_1, turned_3 = call(
        functools.partial(turn_kernel, (1, 3)),
        [turned_like, turned_like],
        line_op,
        joined_x,
        limit=16,
        flops=STAGE,
    )
    joined_x = swap(joined_x, "px", 1)
    products = call(
        functools.partial(main_kernel, planes),
        products_like,
        flux_x,
        across_x.reshape(flat),
        joined_x.reshape(flat),
        line_op,
        turned_3,
        limit=16,
        flops=STAGE,
    )
    across_z = swap(across_z, "px", 2)
    joined_z = swap(
        call(join_kernel, pair_x, stay_z, across_z, products, limit=8, flops=STAGE), "px", 1
    )
    block_flops = 2 * gathered * y_width * line
    sum_2 = call(
        functools.partial(first_step_kernel, 2),
        sums_like,
        got_2,
        own_sum,
        line_op,
        limit=16,
        flops=STAGE,
    )
    xz_part = call(
        add_kernel,
        like(lines_x, line),
        *(a.reshape(flat) for a in (across_z, joined_z, stay_z)),
        products,
        sum_2,
        limit=8,
    )
    sum_1 = call(
        next_step_kernel,
        sums_like,
        got_2,
        stay_z,
        got_1,
        sum_2,
        turned_1,
        xz_part,
        far=(5,),
        limit=16,
        flops=block_flops,
    )
    y_like = like(variables * slab, rows, line)
    y_part = call(
        late_kernel,
        y_like,
        sum_1,
        got_3,
        turned_3,
        far_out=(0,),
        limit=16,
        flops=block_flops,
        scratch=[
            pltpu.VMEM(y_like.shape, bf16),
            pltpu.SemaphoreType.DMA((line // y_width,)),
        ],
    )
    y_part, xz_part = lax.optimization_barrier((y_part, xz_part))
    return (
        xz_part.reshape(variables, planes, lines, line),
        y_part.reshape(variables, slab, rows, line),
    )


def solution(mesh):
    fits = mesh.shape["py"] == 4 and mesh.shape["px"] == 4 and mesh.shape["gz"] == 2
    return jax.shard_map(
        local if fits else plain,
        mesh=mesh,
        in_specs=(
            P(None, "gz", "py", "px"),
            P(None, "gz", "px", "py"),
            P(None, "gz", "py", "px"),
            P(),
        ),
        out_specs=(P(None, ("gz", "px"), "py", None), P(None, "gz", ("px", "py"), None)),
        check_vma=False,
    )
```

```python
import functools

import jax
import jax.numpy as jnp
from jax import lax
from jax.experimental import pallas as pl
from jax.experimental.pallas import tpu as pltpu
from jax.sharding import PartitionSpec as P

STENCIL_COEFS = (0.8, -0.2, 4.0 / 105.0, -1.0 / 280.0)
WIDTH = 4
GROUP = 256
STAGE = 3 * 10**9
MIB = 1 << 20
VMEM = pl.BlockSpec(memory_space=pltpu.VMEM)
ALL = slice(None)
FAR = pl.BlockSpec(memory_space=pltpu.HBM)


def with_halo(block, sides, width):
    for axis, dim in sides:
        count = lax.axis_size(axis)
        forward = [(i, i + 1) for i in range(count - 1)]
        forward.append((count - 1, 0))
        backward = [(target, source) for source, target in forward]
        low = lax.ppermute(
            lax.slice_in_dim(block, block.shape[dim] - width, None, axis=dim), axis, forward
        )
        high = lax.ppermute(lax.slice_in_dim(block, 0, width, axis=dim), axis, backward)
        block = jnp.concatenate([low, block, high], axis=dim)
    return block


def line_product(block, line_op):
    return lax.dot_general(
        block, line_op, (((3,), (1,)), ((), ())), preferred_element_type=jnp.float32
    )


def z_stencil(padded, planes):
    widened = padded.astype(jnp.float32)
    total = jnp.zeros((widened.shape[0], planes) + widened.shape[2:], jnp.float32)
    for offset in range(WIDTH):
        reach = offset + 1
        upper = widened[:, WIDTH + reach : WIDTH + reach + planes]
        lower = widened[:, WIDTH - reach : WIDTH - reach + planes]
        total = total + STENCIL_COEFS[offset] * (upper - lower)
    return total.astype(jnp.bfloat16)


def plain(flux_x, flux_y, flux_z, line_op):
    planes = flux_z.shape[1]
    z_deriv = z_stencil(with_halo(flux_z, (("gz", 1),), WIDTH), planes)
    y_part = line_product(
        lax.all_to_all(flux_y, "py", split_axis=2, concat_axis=3, tiled=True), line_op
    ).astype(jnp.bfloat16)
    products = line_product(
        lax.all_to_all(flux_x, "px", split_axis=1, concat_axis=3, tiled=True), line_op
    )
    moved = lax.all_to_all(z_deriv, "px", split_axis=1, concat_axis=3, tiled=True)
    xz_part = (products + moved.astype(jnp.float32)).astype(jnp.bfloat16)
    return (xz_part, y_part)


def partner(axis, flip):
    return lax.axis_index(axis) ^ flip


def swap(block, axis, flip):
    pairs = [(i, i ^ flip) for i in range(lax.axis_size(axis))]
    return lax.ppermute(block, axis, pairs)


def call(kernel, out_shape, *operands, limit, flops=0, scratch=(), far=(), far_out=()):
    single = not isinstance(out_shape, list)
    out_shape = [out_shape] if single else out_shape
    moved = sum(a.size * a.dtype.itemsize for a in (*operands, *jax.tree.leaves(out_shape)))
    operands = [
        pltpu.with_memory_space_constraint(a, pltpu.HBM) if index in far else a
        for index, a in enumerate(operands)
    ]
    results = pl.pallas_call(
        kernel,
        out_shape=out_shape,
        in_specs=[FAR if index in far else VMEM for index in range(len(operands))],
        out_specs=[FAR if index in far_out else VMEM for index in range(len(out_shape))],
        scratch_shapes=scratch,
        compiler_params=pltpu.CompilerParams(vmem_limit_bytes=limit * MIB),
        cost_estimate=pl.CostEstimate(flops=flops, bytes_accessed=moved, transcendentals=0),
    )(*operands)
    return results[0] if single else results


def pick_rows(lines, rows, count, flips, outs):
    kept = GROUP // count
    line = lax.broadcasted_iota(jnp.int32, (kept, GROUP), 0)
    source = lax.broadcasted_iota(jnp.int32, (kept, GROUP), 1)
    first = (line // rows) * (count * rows) + line % rows
    chosen = jnp.concatenate(
        [(source == first + partner("py", flip) * rows).astype(jnp.float32) for flip in flips]
    ).astype(jnp.bfloat16)
    for part in range(lines.shape[0] // GROUP):
        picked = jnp.dot(
            chosen,
            lines[part * GROUP : (part + 1) * GROUP, :],
            preferred_element_type=jnp.float32,
        ).astype(jnp.bfloat16)
        for index, out in enumerate(outs):
            out[part * kept : (part + 1) * kept, :] = picked[index * kept : (index + 1) * kept]


def first_kernel(rows, count, flips, planes, flux_y, flux_x, flux_z, *refs):
    sent_y, (held_y, faces, across, sems) = refs[: len(flips)], refs[len(flips) :]
    last = flux_z.shape[1] - WIDTH
    moves = [(flux_y, held_y)]
    moves += [(flux_z.at[:, pl.ds(last, WIDTH)], faces.at[:, :WIDTH])]
    moves += [(flux_z.at[:, :WIDTH], faces.at[:, WIDTH:])]
    for flip, place in ((2, across.at[0]), (3, across.at[1])):
        moves.append((flux_x.at[:, pl.ds(partner("px", flip) * planes, planes)], place))
    copies = [pltpu.make_async_copy(a, b, sems.at[i]) for i, (a, b) in enumerate(moves)]
    for copy in copies:
        copy.start()
    copies[0].wait()
    pick_rows(held_y, rows, count, flips, sent_y)
    for copy in copies[1:]:
        copy.wait()


def second_kernel(rows, count, flips, flux_y, *outs):
    pick_rows(flux_y, rows, count, flips, outs)


def join_x_kernel(planes, after, flux_x, got, out):
    out[0] = flux_x[:, pl.ds(partner("px", 1) * planes, planes)]
    out[1] = got[1]


def join_kernel(stay, got, *refs):
    out = refs[-1]
    out[0] = stay[1]
    out[1] = got[1]


def stencil_kernel(planes, flux_z, faces, across, stay, held):
    own = flux_z.shape[1]

    def plane(variable, index):
        if index < 0:
            return faces[variable, WIDTH + index].astype(jnp.float32)
        if index >= own:
            return faces[variable, WIDTH + index - own].astype(jnp.float32)
        return flux_z[variable, index].astype(jnp.float32)

    for variable in range(flux_z.shape[0]):
        for index in range(own):
            total = jnp.zeros(flux_z.shape[2:], jnp.float32)
            for offset in range(WIDTH):
                upper = plane(variable, index + offset + 1)
                lower = plane(variable, index - offset - 1)
                total = total + STENCIL_COEFS[offset] * (upper - lower)
            held[variable, index] = total.astype(jnp.bfloat16)
    for flip, place in ((2, across.at[0]), (3, across.at[1]), (0, stay.at[0]), (1, stay.at[1])):
        place[...] = held[:, pl.ds(partner("px", flip) * planes, planes)]


def cells(index, width):
    return pl.ds(pl.multiple_of(index * width, width), width)


def times(block, line_op, to, of):
    return lax.dot_general(
        block, line_op[to, of], (((1,), (1,)), ((), ())), preferred_element_type=jnp.float32
    )


def blocks_of(stay, across, joined):
    return ((0, stay, 0), (2, across, 0), (1, joined, 0), (3, joined, 1))


def turn(line_op, index, out):
    depth = out.shape[0]
    for start in range(0, line_op.shape[0], depth):
        place = pl.ds(start, depth)
        out[:, place] = line_op[place, cells(index, depth)].T


def own_kernel(flip, own_y, line_op, after, out, turned):
    width = own_y.shape[1]
    out[...] = times(own_y[...], line_op, ALL, cells(lax.axis_index("py"), width))
    turn(line_op, partner("py", flip), turned)


def main_kernel(planes, flux_x, across, joined, line_op, out):
    width = across.shape[2]
    own = flux_x[:, pl.ds(partner("px", 0) * planes, planes)].reshape(-1, width)
    for start in range(0, line_op.shape[0], width):
        place = pl.ds(start, width)
        total = times(own, line_op, place, cells(partner("px", 0), width))
        for flip, ref, index in blocks_of(None, across, joined)[1:]:
            total = total + times(ref[index], line_op, place, cells(partner("px", flip), width))
        out[:, place] = total


def add_kernel(across, joined, stay, products, after, out):
    width = stay.shape[2]
    for flip, ref, index in blocks_of(stay, across, joined):
        place = cells(partner("px", flip), width)
        out[:, place] = (products[:, place] + ref[index].astype(jnp.float32)).astype(jnp.bfloat16)


def first_step_kernel(flip, later, block, before, line_op, out, turned):
    part = times(block[...], line_op, ALL, cells(partner("py", flip), block.shape[1]))
    out[...] = before[...] + part
    turn(line_op, partner("py", later), turned)


def next_step_kernel(before, block, turned, after, out):
    out[...] = before[...] + jnp.dot(
        block[...], turned[...], preferred_element_type=jnp.float32
    )


def late_kernel(early, block, turned, out, held, sems):
    width = block.shape[1]
    rows = out.shape[1]
    copies = []
    for start in range(0, out.shape[2], width):
        place = pl.ds(start, width)
        part = jnp.dot(block[...], turned[:, place], preferred_element_type=jnp.float32)
        total = early[:, place] + part
        held[:, :, place] = total.astype(jnp.bfloat16).reshape(-1, rows, width)
        copy = pltpu.make_async_copy(
            held.at[:, :, place], out.at[:, :, place], sems.at[len(copies)]
        )
        copy.start()
        copies.append(copy)
    for copy in copies:
        copy.wait()


def local(flux_x, flux_y, flux_z, line_op):
    variables, slab, lines, x_width = flux_x.shape
    x_count, y_count = lax.axis_size("px"), lax.axis_size("py")
    planes = slab // x_count
    x_lines, y_width = flux_y.shape[2:]
    rows = x_lines // y_count
    line = line_op.shape[0]
    gathered = variables * slab * rows
    lines_x = variables * planes * lines
    bf16 = jnp.bfloat16

    def like(*shape, kind=bf16):
        return jax.ShapeDtypeStruct(shape, kind)

    rows_y = flux_y.reshape(-1, y_width)
    chunk_y = like(gathered, y_width)
    pair_x = like(2, variables, planes, lines, x_width)
    sent_2, sent_1, held_y, faces, across_x = call(
        functools.partial(first_kernel, rows, y_count, (2, 1), planes),
        [
            chunk_y,
            chunk_y,
            like(*rows_y.shape),
            like(variables, 2 * WIDTH, lines, x_width),
            pair_x,
        ],
        rows_y,
        flux_x,
        flux_z,
        far=(0, 1, 2),
        limit=8,
        scratch=[pltpu.SemaphoreType.DMA((5,))],
    )
    got_2 = swap(sent_2, "py", 2)
    faces = swap(faces, "gz", 1)
    across_x = swap(across_x, "px", 2)
    sent_3, own_y = call(
        functools.partial(second_kernel, rows, y_count, (3, 0)),
        [chunk_y] * 2,
        held_y,
        limit=8,
        flops=STAGE,
    )
    got_1 = swap(sent_1, "py", 1)
    got_3 = swap(sent_3, "py", 3)

    across_z, stay_z = call(
        functools.partial(stencil_kernel, planes),
        [pair_x, pair_x],
        flux_z,
        faces,
        limit=8,
        flops=STAGE,
        scratch=[pltpu.VMEM(flux_z.shape, bf16)],
    )
    joined_x = call(
        functools.partial(join_x_kernel, planes),
        pair_x,
        stay_z,
        flux_x,
        across_x,
        limit=8,
        flops=STAGE // 2,
    )
    flat = (2, lines_x, x_width)
    products_like = like(lines_x, line, kind=jnp.float32)
    sums_like = like(gathered, line, kind=jnp.float32)
    turned_like = like(y_width, line)
    own_sum, turned_3 = call(
        functools.partial(own_kernel, 3),
        [sums_like, turned_like],
        own_y,
        line_op,
        joined_x,
        limit=16,
        flops=STAGE,
    )
    joined_x = swap(joined_x, "px", 1)
    products = call(
        functools.partial(main_kernel, planes),
        products_like,
        flux_x,
        across_x.reshape(flat),
        joined_x.reshape(flat),
        line_op,
        limit=16,
        flops=STAGE,
    )
    across_z = swap(across_z, "px", 2)
    joined_z = swap(
        call(join_kernel, pair_x, stay_z, across_z, products, limit=8, flops=STAGE), "px", 1
    )
    block_flops = 2 * gathered * y_width * line
    sum_2, turned_1 = call(
        functools.partial(first_step_kernel, 2, 1),
        [sums_like, turned_like],
        got_2,
        own_sum,
        line_op,
        limit=16,
        flops=STAGE,
    )
    xz_part = call(
        add_kernel,
        like(lines_x, line),
        *(a.reshape(flat) for a in (across_z, joined_z, stay_z)),
        products,
        sum_2,
        limit=8,
    )
    sum_1 = call(
        next_step_kernel,
        sums_like,
        sum_2,
        got_1,
        turned_1,
        xz_part,
        far=(3,),
        limit=16,
        flops=block_flops,
    )
    y_like = like(variables * slab, rows, line)
    y_part = call(
        late_kernel,
        y_like,
        sum_1,
        got_3,
        turned_3,
        far_out=(0,),
        limit=16,
        flops=block_flops,
        scratch=[
            pltpu.VMEM(y_like.shape, bf16),
            pltpu.SemaphoreType.DMA((line // y_width,)),
        ],
    )
    y_part, xz_part = lax.optimization_barrier((y_part, xz_part))
    return (
        xz_part.reshape(variables, planes, lines, line),
        y_part.reshape(variables, slab, rows, line),
    )


def solution(mesh):
    fits = mesh.shape["py"] == 4 and mesh.shape["px"] == 4 and mesh.shape["gz"] == 2
    return jax.shard_map(
        local if fits else plain,
        mesh=mesh,
        in_specs=(
            P(None, "gz", "py", "px"),
            P(None, "gz", "px", "py"),
            P(None, "gz", "py", "px"),
            P(),
        ),
        out_specs=(P(None, ("gz", "px"), "py", None), P(None, "gz", ("px", "py"), None)),
        check_vma=False,
    )
```

```python
import functools

import jax
import jax.numpy as jnp
from jax import lax
from jax.experimental import pallas as pl
from jax.experimental.pallas import tpu as pltpu
from jax.sharding import PartitionSpec as P

STENCIL_COEFS = (0.8, -0.2, 4.0 / 105.0, -1.0 / 280.0)
WIDTH = 4
GROUP = 256
STAGE = 3 * 10**9
MIB = 1 << 20
VMEM = pl.BlockSpec(memory_space=pltpu.VMEM)
ALL = slice(None)
FAR = pl.BlockSpec(memory_space=pltpu.HBM)


def with_halo(block, sides, width):
    for axis, dim in sides:
        count = lax.axis_size(axis)
        forward = [(i, i + 1) for i in range(count - 1)]
        forward.append((count - 1, 0))
        backward = [(target, source) for source, target in forward]
        low = lax.ppermute(
            lax.slice_in_dim(block, block.shape[dim] - width, None, axis=dim), axis, forward
        )
        high = lax.ppermute(lax.slice_in_dim(block, 0, width, axis=dim), axis, backward)
        block = jnp.concatenate([low, block, high], axis=dim)
    return block


def line_product(block, line_op):
    return lax.dot_general(
        block, line_op, (((3,), (1,)), ((), ())), preferred_element_type=jnp.float32
    )


def z_stencil(padded, planes):
    widened = padded.astype(jnp.float32)
    total = jnp.zeros((widened.shape[0], planes) + widened.shape[2:], jnp.float32)
    for offset in range(WIDTH):
        reach = offset + 1
        upper = widened[:, WIDTH + reach : WIDTH + reach + planes]
        lower = widened[:, WIDTH - reach : WIDTH - reach + planes]
        total = total + STENCIL_COEFS[offset] * (upper - lower)
    return total.astype(jnp.bfloat16)


def plain(flux_x, flux_y, flux_z, line_op):
    planes = flux_z.shape[1]
    z_deriv = z_stencil(with_halo(flux_z, (("gz", 1),), WIDTH), planes)
    y_part = line_product(
        lax.all_to_all(flux_y, "py", split_axis=2, concat_axis=3, tiled=True), line_op
    ).astype(jnp.bfloat16)
    products = line_product(
        lax.all_to_all(flux_x, "px", split_axis=1, concat_axis=3, tiled=True), line_op
    )
    moved = lax.all_to_all(z_deriv, "px", split_axis=1, concat_axis=3, tiled=True)
    xz_part = (products + moved.astype(jnp.float32)).astype(jnp.bfloat16)
    return (xz_part, y_part)


def partner(axis, flip):
    return lax.axis_index(axis) ^ flip


def swap(block, axis, flip):
    pairs = [(i, i ^ flip) for i in range(lax.axis_size(axis))]
    return lax.ppermute(block, axis, pairs)


def call(kernel, out_shape, *operands, limit, flops=0, scratch=(), far=(), far_out=()):
    single = not isinstance(out_shape, list)
    out_shape = [out_shape] if single else out_shape
    moved = sum(a.size * a.dtype.itemsize for a in (*operands, *jax.tree.leaves(out_shape)))
    operands = [
        pltpu.with_memory_space_constraint(a, pltpu.HBM) if index in far else a
        for index, a in enumerate(operands)
    ]
    results = pl.pallas_call(
        kernel,
        out_shape=out_shape,
        in_specs=[FAR if index in far else VMEM for index in range(len(operands))],
        out_specs=[FAR if index in far_out else VMEM for index in range(len(out_shape))],
        scratch_shapes=scratch,
        compiler_params=pltpu.CompilerParams(vmem_limit_bytes=limit * MIB),
        cost_estimate=pl.CostEstimate(flops=flops, bytes_accessed=moved, transcendentals=0),
    )(*operands)
    return results[0] if single else results


def pick_rows(lines, rows, count, flips, outs):
    kept = GROUP // count
    line = lax.broadcasted_iota(jnp.int32, (kept, GROUP), 0)
    source = lax.broadcasted_iota(jnp.int32, (kept, GROUP), 1)
    first = (line // rows) * (count * rows) + line % rows
    chosen = jnp.concatenate(
        [(source == first + partner("py", flip) * rows).astype(jnp.float32) for flip in flips]
    ).astype(jnp.bfloat16)
    for part in range(lines.shape[0] // GROUP):
        picked = jnp.dot(
            chosen,
            lines[part * GROUP : (part + 1) * GROUP, :],
            preferred_element_type=jnp.float32,
        ).astype(jnp.bfloat16)
        for index, out in enumerate(outs):
            out[part * kept : (part + 1) * kept, :] = picked[index * kept : (index + 1) * kept]


def first_kernel(rows, count, flips, planes, flux_y, flux_x, flux_z, *refs):
    sent_y, (held_y, faces, across, sems) = refs[: len(flips)], refs[len(flips) :]
    last = flux_z.shape[1] - WIDTH
    moves = [(flux_y, held_y)]
    moves += [(flux_z.at[:, pl.ds(last, WIDTH)], faces.at[:, :WIDTH])]
    moves += [(flux_z.at[:, :WIDTH], faces.at[:, WIDTH:])]
    for flip, place in ((2, across.at[0]), (3, across.at[1])):
        moves.append((flux_x.at[:, pl.ds(partner("px", flip) * planes, planes)], place))
    copies = [pltpu.make_async_copy(a, b, sems.at[i]) for i, (a, b) in enumerate(moves)]
    for copy in copies:
        copy.start()
    copies[0].wait()
    pick_rows(held_y, rows, count, flips, sent_y)
    for copy in copies[1:]:
        copy.wait()


def second_kernel(rows, count, flips, flux_y, *outs):
    pick_rows(flux_y, rows, count, flips, outs)


def join_x_kernel(planes, after, flux_x, got, out):
    out[0] = flux_x[:, pl.ds(partner("px", 1) * planes, planes)]
    out[1] = got[1]


def join_kernel(stay, got, *refs):
    out = refs[-1]
    out[0] = stay[1]
    out[1] = got[1]


def stencil_kernel(planes, flux_z, faces, across, stay, held):
    own = flux_z.shape[1]

    def plane(variable, index):
        if index < 0:
            return faces[variable, WIDTH + index].astype(jnp.float32)
        if index >= own:
            return faces[variable, WIDTH + index - own].astype(jnp.float32)
        return flux_z[variable, index].astype(jnp.float32)

    for variable in range(flux_z.shape[0]):
        for index in range(own):
            total = jnp.zeros(flux_z.shape[2:], jnp.float32)
            for offset in range(WIDTH):
                upper = plane(variable, index + offset + 1)
                lower = plane(variable, index - offset - 1)
                total = total + STENCIL_COEFS[offset] * (upper - lower)
            held[variable, index] = total.astype(jnp.bfloat16)
    for flip, place in ((2, across.at[0]), (3, across.at[1]), (0, stay.at[0]), (1, stay.at[1])):
        place[...] = held[:, pl.ds(partner("px", flip) * planes, planes)]


def cells(index, width):
    return pl.ds(pl.multiple_of(index * width, width), width)


def times(block, line_op, to, of):
    return lax.dot_general(
        block, line_op[to, of], (((1,), (1,)), ((), ())), preferred_element_type=jnp.float32
    )


def blocks_of(stay, across, joined):
    return ((0, stay, 0), (2, across, 0), (1, joined, 0), (3, joined, 1))


def turn(line_op, index, out):
    depth = out.shape[0]
    for start in range(0, line_op.shape[0], depth):
        place = pl.ds(start, depth)
        out[:, place] = line_op[place, cells(index, depth)].T


def own_kernel(flip, own_y, line_op, after, out, turned):
    width = own_y.shape[1]
    out[...] = times(own_y[...], line_op, ALL, cells(lax.axis_index("py"), width))
    turn(line_op, partner("py", flip), turned)


def main_kernel(planes, flux_x, across, joined, line_op, out):
    width = across.shape[2]
    own = flux_x[:, pl.ds(partner("px", 0) * planes, planes)].reshape(-1, width)
    for start in range(0, line_op.shape[0], width):
        place = pl.ds(start, width)
        total = times(own, line_op, place, cells(partner("px", 0), width))
        for flip, ref, index in blocks_of(None, across, joined)[1:]:
            total = total + times(ref[index], line_op, place, cells(partner("px", flip), width))
        out[:, place] = total


def add_kernel(across, joined, stay, products, after, out):
    width = stay.shape[2]
    for flip, ref, index in blocks_of(stay, across, joined):
        place = cells(partner("px", flip), width)
        out[:, place] = (products[:, place] + ref[index].astype(jnp.float32)).astype(jnp.bfloat16)


def first_step_kernel(flip, later, block, before, line_op, out, turned):
    part = times(block[...], line_op, ALL, cells(partner("py", flip), block.shape[1]))
    out[...] = before[...] + part
    turn(line_op, partner("py", later), turned)


def next_step_kernel(after_y, block, before, turned, after, out):
    out[...] = before[...] + jnp.dot(
        block[...], turned[...], preferred_element_type=jnp.float32
    )


def late_kernel(early, block, turned, out, held, sems):
    width = block.shape[1]
    rows = out.shape[1]
    copies = []
    for start in range(0, out.shape[2], width):
        place = pl.ds(start, width)
        part = jnp.dot(block[...], turned[:, place], preferred_element_type=jnp.float32)
        total = early[:, place] + part
        held[:, :, place] = total.astype(jnp.bfloat16).reshape(-1, rows, width)
        copy = pltpu.make_async_copy(
            held.at[:, :, place], out.at[:, :, place], sems.at[len(copies)]
        )
        copy.start()
        copies.append(copy)
    for copy in copies:
        copy.wait()


def local(flux_x, flux_y, flux_z, line_op):
    variables, slab, lines, x_width = flux_x.shape
    x_count, y_count = lax.axis_size("px"), lax.axis_size("py")
    planes = slab // x_count
    x_lines, y_width = flux_y.shape[2:]
    rows = x_lines // y_count
    line = line_op.shape[0]
    gathered = variables * slab * rows
    lines_x = variables * planes * lines
    bf16 = jnp.bfloat16

    def like(*shape, kind=bf16):
        return jax.ShapeDtypeStruct(shape, kind)

    rows_y = flux_y.reshape(-1, y_width)
    chunk_y = like(gathered, y_width)
    pair_x = like(2, variables, planes, lines, x_width)
    sent_2, sent_1, held_y, faces, across_x = call(
        functools.partial(first_kernel, rows, y_count, (2, 1), planes),
        [
            chunk_y,
            chunk_y,
            like(*rows_y.shape),
            like(variables, 2 * WIDTH, lines, x_width),
            pair_x,
        ],
        rows_y,
        flux_x,
        flux_z,
        far=(0, 1, 2),
        limit=8,
        scratch=[pltpu.SemaphoreType.DMA((5,))],
    )
    got_2 = swap(sent_2, "py", 2)
    faces = swap(faces, "gz", 1)
    across_x = swap(across_x, "px", 2)
    sent_3, own_y = call(
        functools.partial(second_kernel, rows, y_count, (3, 0)),
        [chunk_y] * 2,
        held_y,
        limit=8,
        flops=STAGE,
    )
    got_1 = swap(sent_1, "py", 1)
    got_3 = swap(sent_3, "py", 3)

    across_z, stay_z = call(
        functools.partial(stencil_kernel, planes),
        [pair_x, pair_x],
        flux_z,
        faces,
        limit=8,
        flops=STAGE,
        scratch=[pltpu.VMEM(flux_z.shape, bf16)],
    )
    joined_x = call(
        functools.partial(join_x_kernel, planes),
        pair_x,
        stay_z,
        flux_x,
        across_x,
        limit=8,
        flops=STAGE // 2,
    )
    flat = (2, lines_x, x_width)
    products_like = like(lines_x, line, kind=jnp.float32)
    sums_like = like(gathered, line, kind=jnp.float32)
    turned_like = like(y_width, line)
    own_sum, turned_3 = call(
        functools.partial(own_kernel, 3),
        [sums_like, turned_like],
        own_y,
        line_op,
        joined_x,
        limit=16,
        flops=STAGE,
    )
    joined_x = swap(joined_x, "px", 1)
    products = call(
        functools.partial(main_kernel, planes),
        products_like,
        flux_x,
        across_x.reshape(flat),
        joined_x.reshape(flat),
        line_op,
        limit=16,
        flops=STAGE,
    )
    across_z = swap(across_z, "px", 2)
    joined_z = swap(
        call(join_kernel, pair_x, stay_z, across_z, products, limit=8, flops=STAGE), "px", 1
    )
    block_flops = 2 * gathered * y_width * line
    sum_2, turned_1 = call(
        functools.partial(first_step_kernel, 2, 1),
        [sums_like, turned_like],
        got_2,
        own_sum,
        line_op,
        limit=16,
        flops=STAGE,
    )
    xz_part = call(
        add_kernel,
        like(lines_x, line),
        *(a.reshape(flat) for a in (across_z, joined_z, stay_z)),
        products,
        sum_2,
        limit=8,
    )
    sum_1 = call(
        next_step_kernel,
        sums_like,
        got_2,
        got_1,
        sum_2,
        turned_1,
        xz_part,
        far=(4,),
        limit=16,
        flops=block_flops,
    )
    y_like = like(variables * slab, rows, line)
    y_part = call(
        late_kernel,
        y_like,
        sum_1,
        got_3,
        turned_3,
        far_out=(0,),
        limit=16,
        flops=block_flops,
        scratch=[
            pltpu.VMEM(y_like.shape, bf16),
            pltpu.SemaphoreType.DMA((line // y_width,)),
        ],
    )
    y_part, xz_part = lax.optimization_barrier((y_part, xz_part))
    return (
        xz_part.reshape(variables, planes, lines, line),
        y_part.reshape(variables, slab, rows, line),
    )


def solution(mesh):
    fits = mesh.shape["py"] == 4 and mesh.shape["px"] == 4 and mesh.shape["gz"] == 2
    return jax.shard_map(
        local if fits else plain,
        mesh=mesh,
        in_specs=(
            P(None, "gz", "py", "px"),
            P(None, "gz", "px", "py"),
            P(None, "gz", "py", "px"),
            P(),
        ),
        out_specs=(P(None, ("gz", "px"), "py", None), P(None, "gz", ("px", "py"), None)),
        check_vma=False,
    )
```

```python
import functools

import jax
import jax.numpy as jnp
from jax import lax
from jax.experimental import pallas as pl
from jax.experimental.pallas import tpu as pltpu
from jax.sharding import PartitionSpec as P

STENCIL_COEFS = (0.8, -0.2, 4.0 / 105.0, -1.0 / 280.0)
WIDTH = 4
GROUP = 256
STAGE = 3 * 10**9
MIB = 1 << 20
VMEM = pl.BlockSpec(memory_space=pltpu.VMEM)
ALL = slice(None)
FAR = pl.BlockSpec(memory_space=pltpu.HBM)


def with_halo(block, sides, width):
    for axis, dim in sides:
        count = lax.axis_size(axis)
        forward = [(i, i + 1) for i in range(count - 1)]
        forward.append((count - 1, 0))
        backward = [(target, source) for source, target in forward]
        low = lax.ppermute(
            lax.slice_in_dim(block, block.shape[dim] - width, None, axis=dim), axis, forward
        )
        high = lax.ppermute(lax.slice_in_dim(block, 0, width, axis=dim), axis, backward)
        block = jnp.concatenate([low, block, high], axis=dim)
    return block


def line_product(block, line_op):
    return lax.dot_general(
        block, line_op, (((3,), (1,)), ((), ())), preferred_element_type=jnp.float32
    )


def z_stencil(padded, planes):
    widened = padded.astype(jnp.float32)
    total = jnp.zeros((widened.shape[0], planes) + widened.shape[2:], jnp.float32)
    for offset in range(WIDTH):
        reach = offset + 1
        upper = widened[:, WIDTH + reach : WIDTH + reach + planes]
        lower = widened[:, WIDTH - reach : WIDTH - reach + planes]
        total = total + STENCIL_COEFS[offset] * (upper - lower)
    return total.astype(jnp.bfloat16)


def plain(flux_x, flux_y, flux_z, line_op):
    planes = flux_z.shape[1]
    z_deriv = z_stencil(with_halo(flux_z, (("gz", 1),), WIDTH), planes)
    y_part = line_product(
        lax.all_to_all(flux_y, "py", split_axis=2, concat_axis=3, tiled=True), line_op
    ).astype(jnp.bfloat16)
    products = line_product(
        lax.all_to_all(flux_x, "px", split_axis=1, concat_axis=3, tiled=True), line_op
    )
    moved = lax.all_to_all(z_deriv, "px", split_axis=1, concat_axis=3, tiled=True)
    xz_part = (products + moved.astype(jnp.float32)).astype(jnp.bfloat16)
    return (xz_part, y_part)


def partner(axis, flip):
    return lax.axis_index(axis) ^ flip


def swap(block, axis, flip):
    pairs = [(i, i ^ flip) for i in range(lax.axis_size(axis))]
    return lax.ppermute(block, axis, pairs)


def call(kernel, out_shape, *operands, limit, flops=0, scratch=(), far=(), far_out=()):
    single = not isinstance(out_shape, list)
    out_shape = [out_shape] if single else out_shape
    moved = sum(a.size * a.dtype.itemsize for a in (*operands, *jax.tree.leaves(out_shape)))
    operands = [
        pltpu.with_memory_space_constraint(a, pltpu.HBM) if index in far else a
        for index, a in enumerate(operands)
    ]
    results = pl.pallas_call(
        kernel,
        out_shape=out_shape,
        in_specs=[FAR if index in far else VMEM for index in range(len(operands))],
        out_specs=[FAR if index in far_out else VMEM for index in range(len(out_shape))],
        scratch_shapes=scratch,
        compiler_params=pltpu.CompilerParams(vmem_limit_bytes=limit * MIB),
        cost_estimate=pl.CostEstimate(flops=flops, bytes_accessed=moved, transcendentals=0),
    )(*operands)
    return results[0] if single else results


def pick_rows(lines, rows, count, flips, outs):
    kept = GROUP // count
    line = lax.broadcasted_iota(jnp.int32, (kept, GROUP), 0)
    source = lax.broadcasted_iota(jnp.int32, (kept, GROUP), 1)
    first = (line // rows) * (count * rows) + line % rows
    chosen = jnp.concatenate(
        [(source == first + partner("py", flip) * rows).astype(jnp.float32) for flip in flips]
    ).astype(jnp.bfloat16)
    for part in range(lines.shape[0] // GROUP):
        picked = jnp.dot(
            chosen,
            lines[part * GROUP : (part + 1) * GROUP, :],
            preferred_element_type=jnp.float32,
        ).astype(jnp.bfloat16)
        for index, out in enumerate(outs):
            out[part * kept : (part + 1) * kept, :] = picked[index * kept : (index + 1) * kept]


def first_kernel(rows, count, flips, planes, flux_y, flux_x, flux_z, *refs):
    sent_y, (held_y, faces, across, sems) = refs[: len(flips)], refs[len(flips) :]
    last = flux_z.shape[1] - WIDTH
    moves = [(flux_y, held_y)]
    moves += [(flux_z.at[:, pl.ds(last, WIDTH)], faces.at[:, :WIDTH])]
    moves += [(flux_z.at[:, :WIDTH], faces.at[:, WIDTH:])]
    for flip, place in ((2, across.at[0]), (3, across.at[1])):
        moves.append((flux_x.at[:, pl.ds(partner("px", flip) * planes, planes)], place))
    copies = [pltpu.make_async_copy(a, b, sems.at[i]) for i, (a, b) in enumerate(moves)]
    for copy in copies:
        copy.start()
    copies[0].wait()
    pick_rows(held_y, rows, count, flips, sent_y)
    for copy in copies[1:]:
        copy.wait()


def second_kernel(rows, count, flips, flux_y, *outs):
    pick_rows(flux_y, rows, count, flips, outs)


def join_x_kernel(planes, after, flux_x, got, out):
    out[0] = flux_x[:, pl.ds(partner("px", 1) * planes, planes)]
    out[1] = got[1]


def join_kernel(stay, got, *refs):
    out = refs[-1]
    out[0] = stay[1]
    out[1] = got[1]


def stencil_kernel(planes, flux_z, faces, across, stay, held):
    own = flux_z.shape[1]

    def plane(variable, index):
        if index < 0:
            return faces[variable, WIDTH + index].astype(jnp.float32)
        if index >= own:
            return faces[variable, WIDTH + index - own].astype(jnp.float32)
        return flux_z[variable, index].astype(jnp.float32)

    for variable in range(flux_z.shape[0]):
        for index in range(own):
            total = jnp.zeros(flux_z.shape[2:], jnp.float32)
            for offset in range(WIDTH):
                upper = plane(variable, index + offset + 1)
                lower = plane(variable, index - offset - 1)
                total = total + STENCIL_COEFS[offset] * (upper - lower)
            held[variable, index] = total.astype(jnp.bfloat16)
    for flip, place in ((2, across.at[0]), (3, across.at[1]), (0, stay.at[0]), (1, stay.at[1])):
        place[...] = held[:, pl.ds(partner("px", flip) * planes, planes)]


def cells(index, width):
    return pl.ds(pl.multiple_of(index * width, width), width)


def times(block, line_op, to, of):
    return lax.dot_general(
        block, line_op[to, of], (((1,), (1,)), ((), ())), preferred_element_type=jnp.float32
    )


def blocks_of(stay, across, joined):
    return ((0, stay, 0), (2, across, 0), (1, joined, 0), (3, joined, 1))


def turn(line_op, index, out):
    depth = out.shape[0]
    for start in range(0, line_op.shape[0], depth):
        place = pl.ds(start, depth)
        out[:, place] = line_op[place, cells(index, depth)].T


def own_kernel(flip, planes, after, own_y, line_op, flux_x, across, out_y, out_x, turned):
    width = own_y.shape[1]
    out_y[...] = times(own_y[...], line_op, ALL, cells(lax.axis_index("py"), width))
    turn(line_op, partner("py", flip), turned)
    width = across.shape[2]
    own_x = flux_x[:, pl.ds(partner("px", 0) * planes, planes)].reshape(-1, width)
    out_x[...] = times(own_x, line_op, ALL, cells(partner("px", 0), width)) + times(
        across[0], line_op, ALL, cells(partner("px", 2), width)
    )


def main_kernel(before, joined, line_op, out):
    width = joined.shape[2]
    out[...] = (
        before[...]
        + times(joined[0], line_op, ALL, cells(partner("px", 1), width))
        + times(joined[1], line_op, ALL, cells(partner("px", 3), width))
    )


def add_kernel(across, joined, stay, products, after, out):
    width = stay.shape[2]
    for flip, ref, index in blocks_of(stay, across, joined):
        place = cells(partner("px", flip), width)
        out[:, place] = (products[:, place] + ref[index].astype(jnp.float32)).astype(jnp.bfloat16)


def first_step_kernel(flip, later, block, before, line_op, out, turned):
    part = times(block[...], line_op, ALL, cells(partner("py", flip), block.shape[1]))
    out[...] = before[...] + part
    turn(line_op, partner("py", later), turned)


def next_step_kernel(after, block, before, turned, out):
    out[...] = before[...] + jnp.dot(
        block[...], turned[...], preferred_element_type=jnp.float32
    )


def late_kernel(early, block, turned, after, out, held, sems):
    width = block.shape[1]
    rows = out.shape[1]
    copies = []
    last = out.shape[2] - width
    for place in (pl.ds(0, last), pl.ds(last, width)):
        part = jnp.dot(block[...], turned[:, place], preferred_element_type=jnp.float32)
        total = early[:, place] + part
        held[:, :, place] = total.astype(jnp.bfloat16).reshape(-1, rows, place.size)
        copy = pltpu.make_async_copy(
            held.at[:, :, place], out.at[:, :, place], sems.at[len(copies)]
        )
        copy.start()
        copies.append(copy)
    for copy in copies:
        copy.wait()


def local(flux_x, flux_y, flux_z, line_op):
    variables, slab, lines, x_width = flux_x.shape
    x_count, y_count = lax.axis_size("px"), lax.axis_size("py")
    planes = slab // x_count
    x_lines, y_width = flux_y.shape[2:]
    rows = x_lines // y_count
    line = line_op.shape[0]
    gathered = variables * slab * rows
    lines_x = variables * planes * lines
    bf16 = jnp.bfloat16

    def like(*shape, kind=bf16):
        return jax.ShapeDtypeStruct(shape, kind)

    rows_y = flux_y.reshape(-1, y_width)
    chunk_y = like(gathered, y_width)
    pair_x = like(2, variables, planes, lines, x_width)
    sent_2, sent_1, held_y, faces, across_x = call(
        functools.partial(first_kernel, rows, y_count, (2, 1), planes),
        [
            chunk_y,
            chunk_y,
            like(*rows_y.shape),
            like(variables, 2 * WIDTH, lines, x_width),
            pair_x,
        ],
        rows_y,
        flux_x,
        flux_z,
        far=(0, 1, 2),
        limit=8,
        scratch=[pltpu.SemaphoreType.DMA((5,))],
    )
    got_2 = swap(sent_2, "py", 2)
    faces = swap(faces, "gz", 1)
    across_x = swap(across_x, "px", 2)
    sent_3, own_y = call(
        functools.partial(second_kernel, rows, y_count, (3, 0)),
        [chunk_y] * 2,
        held_y,
        limit=8,
        flops=STAGE,
    )
    got_1 = swap(sent_1, "py", 1)
    got_3 = swap(sent_3, "py", 3)

    across_z, stay_z = call(
        functools.partial(stencil_kernel, planes),
        [pair_x, pair_x],
        flux_z,
        faces,
        limit=8,
        flops=STAGE,
        scratch=[pltpu.VMEM(flux_z.shape, bf16)],
    )
    joined_x = call(
        functools.partial(join_x_kernel, planes),
        pair_x,
        stay_z,
        flux_x,
        across_x,
        limit=8,
        flops=STAGE // 2,
    )
    flat = (2, lines_x, x_width)
    products_like = like(lines_x, line, kind=jnp.float32)
    sums_like = like(gathered, line, kind=jnp.float32)
    turned_like = like(y_width, line)
    own_sum, half_products, turned_3 = call(
        functools.partial(own_kernel, 3, planes),
        [sums_like, products_like, turned_like],
        joined_x,
        own_y,
        line_op,
        flux_x,
        across_x.reshape(flat),
        limit=16,
        flops=STAGE,
    )
    joined_x = swap(joined_x, "px", 1)
    products = call(
        main_kernel,
        products_like,
        half_products,
        joined_x.reshape(flat),
        line_op,
        limit=16,
        flops=STAGE,
    )
    across_z = swap(across_z, "px", 2)
    joined_z = swap(
        call(join_kernel, pair_x, stay_z, across_z, products, limit=8, flops=STAGE), "px", 1
    )
    block_flops = 2 * gathered * y_width * line
    sum_2, turned_1 = call(
        functools.partial(first_step_kernel, 2, 1),
        [sums_like, turned_like],
        got_2,
        own_sum,
        line_op,
        limit=16,
        flops=STAGE,
    )
    sum_1 = call(
        next_step_kernel,
        sums_like,
        got_2,
        got_1,
        sum_2,
        turned_1,
        limit=16,
        flops=block_flops,
    )
    xz_part = call(
        add_kernel,
        like(lines_x, line),
        *(a.reshape(flat) for a in (across_z, joined_z, stay_z)),
        products,
        sum_1,
        limit=8,
    )
    y_like = like(variables * slab, rows, line)
    y_part = call(
        late_kernel,
        y_like,
        sum_1,
        got_3,
        turned_3,
        xz_part,
        far=(3,),
        far_out=(0,),
        limit=16,
        flops=block_flops,
        scratch=[
            pltpu.VMEM(y_like.shape, bf16),
            pltpu.SemaphoreType.DMA((2,)),
        ],
    )
    y_part, xz_part = lax.optimization_barrier((y_part, xz_part))
    return (
        xz_part.reshape(variables, planes, lines, line),
        y_part.reshape(variables, slab, rows, line),
    )


def solution(mesh):
    fits = mesh.shape["py"] == 4 and mesh.shape["px"] == 4 and mesh.shape["gz"] == 2
    return jax.shard_map(
        local if fits else plain,
        mesh=mesh,
        in_specs=(
            P(None, "gz", "py", "px"),
            P(None, "gz", "px", "py"),
            P(None, "gz", "py", "px"),
            P(),
        ),
        out_specs=(P(None, ("gz", "px"), "py", None), P(None, "gz", ("px", "py"), None)),
        check_vma=False,
    )
```

```python
import functools

import jax
import jax.numpy as jnp
from jax import lax
from jax.experimental import pallas as pl
from jax.experimental.pallas import tpu as pltpu
from jax.sharding import PartitionSpec as P

STENCIL_COEFS = (0.8, -0.2, 4.0 / 105.0, -1.0 / 280.0)
WIDTH = 4
GROUP = 256
COLUMNS = 256
STAGE = 3 * 10**9
MIB = 1 << 20
VMEM = pl.BlockSpec(memory_space=pltpu.VMEM)
ALL = slice(None)
FAR = pl.BlockSpec(memory_space=pltpu.HBM)


def with_halo(block, sides, width):
    for axis, dim in sides:
        count = lax.axis_size(axis)
        forward = [(i, i + 1) for i in range(count - 1)]
        forward.append((count - 1, 0))
        backward = [(target, source) for source, target in forward]
        low = lax.ppermute(
            lax.slice_in_dim(block, block.shape[dim] - width, None, axis=dim), axis, forward
        )
        high = lax.ppermute(lax.slice_in_dim(block, 0, width, axis=dim), axis, backward)
        block = jnp.concatenate([low, block, high], axis=dim)
    return block


def line_product(block, line_op):
    return lax.dot_general(
        block, line_op, (((3,), (1,)), ((), ())), preferred_element_type=jnp.float32
    )


def z_stencil(padded, planes):
    widened = padded.astype(jnp.float32)
    total = jnp.zeros((widened.shape[0], planes) + widened.shape[2:], jnp.float32)
    for offset in range(WIDTH):
        reach = offset + 1
        upper = widened[:, WIDTH + reach : WIDTH + reach + planes]
        lower = widened[:, WIDTH - reach : WIDTH - reach + planes]
        total = total + STENCIL_COEFS[offset] * (upper - lower)
    return total.astype(jnp.bfloat16)


def plain(flux_x, flux_y, flux_z, line_op):
    planes = flux_z.shape[1]
    z_deriv = z_stencil(with_halo(flux_z, (("gz", 1),), WIDTH), planes)
    y_part = line_product(
        lax.all_to_all(flux_y, "py", split_axis=2, concat_axis=3, tiled=True), line_op
    ).astype(jnp.bfloat16)
    products = line_product(
        lax.all_to_all(flux_x, "px", split_axis=1, concat_axis=3, tiled=True), line_op
    )
    moved = lax.all_to_all(z_deriv, "px", split_axis=1, concat_axis=3, tiled=True)
    xz_part = (products + moved.astype(jnp.float32)).astype(jnp.bfloat16)
    return (xz_part, y_part)


def partner(axis, flip):
    return lax.axis_index(axis) ^ flip


def swap(block, axis, flip):
    pairs = [(i, i ^ flip) for i in range(lax.axis_size(axis))]
    return lax.ppermute(block, axis, pairs)


def call(kernel, out_shape, *operands, limit, flops=0, scratch=(), far=(), far_out=()):
    single = not isinstance(out_shape, list)
    out_shape = [out_shape] if single else out_shape
    moved = sum(a.size * a.dtype.itemsize for a in (*operands, *jax.tree.leaves(out_shape)))
    operands = [
        pltpu.with_memory_space_constraint(a, pltpu.HBM) if index in far else a
        for index, a in enumerate(operands)
    ]
    results = pl.pallas_call(
        kernel,
        out_shape=out_shape,
        in_specs=[FAR if index in far else VMEM for index in range(len(operands))],
        out_specs=[FAR if index in far_out else VMEM for index in range(len(out_shape))],
        scratch_shapes=scratch,
        compiler_params=pltpu.CompilerParams(vmem_limit_bytes=limit * MIB),
        cost_estimate=pl.CostEstimate(flops=flops, bytes_accessed=moved, transcendentals=0),
    )(*operands)
    return results[0] if single else results


def pick_rows(lines, rows, count, flips, outs):
    kept = GROUP // count
    line = lax.broadcasted_iota(jnp.int32, (kept, GROUP), 0)
    source = lax.broadcasted_iota(jnp.int32, (kept, GROUP), 1)
    first = (line // rows) * (count * rows) + line % rows
    chosen = jnp.concatenate(
        [(source == first + partner("py", flip) * rows).astype(jnp.float32) for flip in flips]
    ).astype(jnp.bfloat16)
    for part in range(lines.shape[0] // GROUP):
        picked = jnp.dot(
            chosen,
            lines[part * GROUP : (part + 1) * GROUP, :],
            preferred_element_type=jnp.float32,
        ).astype(jnp.bfloat16)
        for index, out in enumerate(outs):
            out[part * kept : (part + 1) * kept, :] = picked[index * kept : (index + 1) * kept]


def first_kernel(rows, count, flips, planes, flux_y, flux_x, flux_z, *refs):
    sent_y, (held_y, faces, across, sems) = refs[: len(flips)], refs[len(flips) :]
    last = flux_z.shape[1] - WIDTH
    moves = [(flux_y, held_y)]
    moves += [(flux_z.at[:, pl.ds(last, WIDTH)], faces.at[:, :WIDTH])]
    moves += [(flux_z.at[:, :WIDTH], faces.at[:, WIDTH:])]
    for flip, place in ((2, across.at[0]), (3, across.at[1])):
        moves.append((flux_x.at[:, pl.ds(partner("px", flip) * planes, planes)], place))
    copies = [pltpu.make_async_copy(a, b, sems.at[i]) for i, (a, b) in enumerate(moves)]
    for copy in copies:
        copy.start()
    copies[0].wait()
    pick_rows(held_y, rows, count, flips, sent_y)
    for copy in copies[1:]:
        copy.wait()


def second_kernel(rows, count, flips, flux_y, *outs):
    pick_rows(flux_y, rows, count, flips, outs)


def join_x_kernel(planes, after, flux_x, got, out):
    out[0] = flux_x[:, pl.ds(partner("px", 1) * planes, planes)]
    out[1] = got[1]


def join_kernel(stay, got, *refs):
    out = refs[-1]
    out[0] = stay[1]
    out[1] = got[1]


def stencil_kernel(planes, flux_z, faces, across, stay, held):
    own = flux_z.shape[1]

    def plane(variable, index):
        if index < 0:
            return faces[variable, WIDTH + index].astype(jnp.float32)
        if index >= own:
            return faces[variable, WIDTH + index - own].astype(jnp.float32)
        return flux_z[variable, index].astype(jnp.float32)

    for variable in range(flux_z.shape[0]):
        for index in range(own):
            total = jnp.zeros(flux_z.shape[2:], jnp.float32)
            for offset in range(WIDTH):
                upper = plane(variable, index + offset + 1)
                lower = plane(variable, index - offset - 1)
                total = total + STENCIL_COEFS[offset] * (upper - lower)
            held[variable, index] = total.astype(jnp.bfloat16)
    for flip, place in ((2, across.at[0]), (3, across.at[1]), (0, stay.at[0]), (1, stay.at[1])):
        place[...] = held[:, pl.ds(partner("px", flip) * planes, planes)]


def cells(index, width):
    return pl.ds(pl.multiple_of(index * width, width), width)


def times(block, line_op, to, of):
    return lax.dot_general(
        block, line_op[to, of], (((1,), (1,)), ((), ())), preferred_element_type=jnp.float32
    )


def blocks_of(stay, across, joined):
    return ((0, stay, 0), (2, across, 0), (1, joined, 0), (3, joined, 1))


def turn(line_op, index, out):
    depth = out.shape[0]
    for start in range(0, line_op.shape[0], depth):
        place = pl.ds(start, depth)
        out[:, place] = line_op[place, cells(index, depth)].T


def own_kernel(flip, planes, after, own_y, line_op, flux_x, across, out_y, out_x, turned):
    width = own_y.shape[1]
    out_y[...] = times(own_y[...], line_op, ALL, cells(lax.axis_index("py"), width))
    turn(line_op, partner("py", flip), turned)
    width = across.shape[2]
    own_x = flux_x[:, pl.ds(partner("px", 0) * planes, planes)].reshape(-1, width)
    out_x[...] = times(own_x, line_op, ALL, cells(partner("px", 0), width)) + times(
        across[0], line_op, ALL, cells(partner("px", 2), width)
    )


def main_kernel(before, joined, line_op, out):
    width = joined.shape[2]
    out[...] = (
        before[...]
        + times(joined[0], line_op, ALL, cells(partner("px", 1), width))
        + times(joined[1], line_op, ALL, cells(partner("px", 3), width))
    )


def add_kernel(across, joined, stay, products, after, out):
    width = stay.shape[2]
    for flip, ref, index in blocks_of(stay, across, joined):
        place = cells(partner("px", flip), width)
        out[:, place] = (products[:, place] + ref[index].astype(jnp.float32)).astype(jnp.bfloat16)


def first_step_kernel(flip, later, block, before, line_op, out, turned):
    part = times(block[...], line_op, ALL, cells(partner("py", flip), block.shape[1]))
    out[...] = before[...] + part
    turn(line_op, partner("py", later), turned)


def next_step_kernel(after, block, before, turned, out):
    out[...] = before[...] + jnp.dot(
        block[...], turned[...], preferred_element_type=jnp.float32
    )


def late_kernel(early, block, turned, after, out, held, sems):
    rows = out.shape[1]
    copies = []
    for start in range(0, out.shape[2], COLUMNS):
        place = pl.ds(start, COLUMNS)
        part = jnp.dot(block[...], turned[:, place], preferred_element_type=jnp.float32)
        total = early[:, place] + part
        held[:, :, place] = total.astype(jnp.bfloat16).reshape(-1, rows, COLUMNS)
        copy = pltpu.make_async_copy(
            held.at[:, :, place], out.at[:, :, place], sems.at[len(copies)]
        )
        copy.start()
        copies.append(copy)
    for copy in copies:
        copy.wait()


def local(flux_x, flux_y, flux_z, line_op):
    variables, slab, lines, x_width = flux_x.shape
    x_count, y_count = lax.axis_size("px"), lax.axis_size("py")
    planes = slab // x_count
    x_lines, y_width = flux_y.shape[2:]
    rows = x_lines // y_count
    line = line_op.shape[0]
    gathered = variables * slab * rows
    lines_x = variables * planes * lines
    bf16 = jnp.bfloat16

    def like(*shape, kind=bf16):
        return jax.ShapeDtypeStruct(shape, kind)

    rows_y = flux_y.reshape(-1, y_width)
    chunk_y = like(gathered, y_width)
    pair_x = like(2, variables, planes, lines, x_width)
    sent_2, sent_1, held_y, faces, across_x = call(
        functools.partial(first_kernel, rows, y_count, (2, 1), planes),
        [
            chunk_y,
            chunk_y,
            like(*rows_y.shape),
            like(variables, 2 * WIDTH, lines, x_width),
            pair_x,
        ],
        rows_y,
        flux_x,
        flux_z,
        far=(0, 1, 2),
        limit=8,
        scratch=[pltpu.SemaphoreType.DMA((5,))],
    )
    got_2 = swap(sent_2, "py", 2)
    faces = swap(faces, "gz", 1)
    across_x = swap(across_x, "px", 2)
    sent_3, own_y = call(
        functools.partial(second_kernel, rows, y_count, (3, 0)),
        [chunk_y] * 2,
        held_y,
        limit=8,
        flops=STAGE,
    )
    got_1 = swap(sent_1, "py", 1)
    got_3 = swap(sent_3, "py", 3)

    across_z, stay_z = call(
        functools.partial(stencil_kernel, planes),
        [pair_x, pair_x],
        flux_z,
        faces,
        limit=8,
        flops=STAGE,
        scratch=[pltpu.VMEM(flux_z.shape, bf16)],
    )
    joined_x = call(
        functools.partial(join_x_kernel, planes),
        pair_x,
        stay_z,
        flux_x,
        across_x,
        limit=8,
        flops=STAGE // 2,
    )
    flat = (2, lines_x, x_width)
    products_like = like(lines_x, line, kind=jnp.float32)
    sums_like = like(gathered, line, kind=jnp.float32)
    turned_like = like(y_width, line)
    own_sum, half_products, turned_3 = call(
        functools.partial(own_kernel, 3, planes),
        [sums_like, products_like, turned_like],
        joined_x,
        own_y,
        line_op,
        flux_x,
        across_x.reshape(flat),
        limit=16,
        flops=STAGE,
    )
    joined_x = swap(joined_x, "px", 1)
    products = call(
        main_kernel,
        products_like,
        half_products,
        joined_x.reshape(flat),
        line_op,
        limit=16,
        flops=STAGE,
    )
    across_z = swap(across_z, "px", 2)
    joined_z = swap(
        call(join_kernel, pair_x, stay_z, across_z, products, limit=8, flops=STAGE), "px", 1
    )
    block_flops = 2 * gathered * y_width * line
    sum_2, turned_1 = call(
        functools.partial(first_step_kernel, 2, 1),
        [sums_like, turned_like],
        got_2,
        own_sum,
        line_op,
        limit=16,
        flops=STAGE,
    )
    sum_1 = call(
        next_step_kernel,
        sums_like,
        got_2,
        got_1,
        sum_2,
        turned_1,
        limit=16,
        flops=block_flops,
    )
    xz_part = call(
        add_kernel,
        like(lines_x, line),
        *(a.reshape(flat) for a in (across_z, joined_z, stay_z)),
        products,
        sum_1,
        limit=8,
    )
    y_like = like(variables * slab, rows, line)
    y_part = call(
        late_kernel,
        y_like,
        sum_1,
        got_3,
        turned_3,
        xz_part,
        far=(3,),
        far_out=(0,),
        limit=16,
        flops=block_flops,
        scratch=[
            pltpu.VMEM(y_like.shape, bf16),
            pltpu.SemaphoreType.DMA((line // COLUMNS,)),
        ],
    )
    y_part, xz_part = lax.optimization_barrier((y_part, xz_part))
    return (
        xz_part.reshape(variables, planes, lines, line),
        y_part.reshape(variables, slab, rows, line),
    )


def solution(mesh):
    fits = mesh.shape["py"] == 4 and mesh.shape["px"] == 4 and mesh.shape["gz"] == 2
    return jax.shard_map(
        local if fits else plain,
        mesh=mesh,
        in_specs=(
            P(None, "gz", "py", "px"),
            P(None, "gz", "px", "py"),
            P(None, "gz", "py", "px"),
            P(),
        ),
        out_specs=(P(None, ("gz", "px"), "py", None), P(None, "gz", ("px", "py"), None)),
        check_vma=False,
    )
```

```python
import functools
import math

import jax
import jax.numpy as jnp
from jax import lax
from jax.experimental import pallas as pl
from jax.experimental.pallas import tpu as pltpu
from jax.sharding import PartitionSpec as P

STENCIL_COEFS = (0.8, -0.2, 4.0 / 105.0, -1.0 / 280.0)
WIDTH = 4
GROUP = 256
COLUMNS = 512
STAGE = 3 * 10**9
MIB = 1 << 20
VMEM = pl.BlockSpec(memory_space=pltpu.VMEM)
ALL = slice(None)
FAR = pl.BlockSpec(memory_space=pltpu.HBM)


def with_halo(block, sides, width):
    for axis, dim in sides:
        count = lax.axis_size(axis)
        forward = [(i, i + 1) for i in range(count - 1)]
        forward.append((count - 1, 0))
        backward = [(target, source) for source, target in forward]
        low = lax.ppermute(
            lax.slice_in_dim(block, block.shape[dim] - width, None, axis=dim), axis, forward
        )
        high = lax.ppermute(lax.slice_in_dim(block, 0, width, axis=dim), axis, backward)
        block = jnp.concatenate([low, block, high], axis=dim)
    return block


def line_product(block, line_op):
    return lax.dot_general(
        block, line_op, (((3,), (1,)), ((), ())), preferred_element_type=jnp.float32
    )


def z_stencil(padded, planes):
    widened = padded.astype(jnp.float32)
    total = jnp.zeros((widened.shape[0], planes) + widened.shape[2:], jnp.float32)
    for offset in range(WIDTH):
        reach = offset + 1
        upper = widened[:, WIDTH + reach : WIDTH + reach + planes]
        lower = widened[:, WIDTH - reach : WIDTH - reach + planes]
        total = total + STENCIL_COEFS[offset] * (upper - lower)
    return total.astype(jnp.bfloat16)


def plain(flux_x, flux_y, flux_z, line_op):
    planes = flux_z.shape[1]
    z_deriv = z_stencil(with_halo(flux_z, (("gz", 1),), WIDTH), planes)
    y_part = line_product(
        lax.all_to_all(flux_y, "py", split_axis=2, concat_axis=3, tiled=True), line_op
    ).astype(jnp.bfloat16)
    products = line_product(
        lax.all_to_all(flux_x, "px", split_axis=1, concat_axis=3, tiled=True), line_op
    )
    moved = lax.all_to_all(z_deriv, "px", split_axis=1, concat_axis=3, tiled=True)
    xz_part = (products + moved.astype(jnp.float32)).astype(jnp.bfloat16)
    return (xz_part, y_part)


def partner(axis, flip):
    return lax.axis_index(axis) ^ flip


def swap(block, axis, flip):
    pairs = [(i, i ^ flip) for i in range(lax.axis_size(axis))]
    return lax.ppermute(block, axis, pairs)


def call(kernel, out_shape, *operands, limit, flops=0, scratch=(), far=(), far_out=()):
    single = not isinstance(out_shape, list)
    out_shape = [out_shape] if single else out_shape
    moved = sum(a.size * a.dtype.itemsize for a in (*operands, *jax.tree.leaves(out_shape)))
    operands = [
        pltpu.with_memory_space_constraint(a, pltpu.HBM) if index in far else a
        for index, a in enumerate(operands)
    ]
    results = pl.pallas_call(
        kernel,
        out_shape=out_shape,
        in_specs=[FAR if index in far else VMEM for index in range(len(operands))],
        out_specs=[FAR if index in far_out else VMEM for index in range(len(out_shape))],
        scratch_shapes=scratch,
        compiler_params=pltpu.CompilerParams(vmem_limit_bytes=limit * MIB),
        cost_estimate=pl.CostEstimate(flops=flops, bytes_accessed=moved, transcendentals=0),
    )(*operands)
    return results[0] if single else results


def pick_rows(lines, rows, count, flips, outs):
    kept = GROUP // count
    line = lax.broadcasted_iota(jnp.int32, (kept, GROUP), 0)
    source = lax.broadcasted_iota(jnp.int32, (kept, GROUP), 1)
    first = (line // rows) * (count * rows) + line % rows
    chosen = jnp.concatenate(
        [(source == first + partner("py", flip) * rows).astype(jnp.float32) for flip in flips]
    ).astype(jnp.bfloat16)
    for part in range(lines.shape[0] // GROUP):
        picked = jnp.dot(
            chosen,
            lines[part * GROUP : (part + 1) * GROUP, :],
            preferred_element_type=jnp.float32,
        ).astype(jnp.bfloat16)
        for index, out in enumerate(outs):
            out[part * kept : (part + 1) * kept, :] = picked[index * kept : (index + 1) * kept]


def first_kernel(rows, count, flips, planes, flux_y, flux_x, flux_z, *refs):
    sent_y, (held_y, faces, across, sems) = refs[: len(flips)], refs[len(flips) :]
    last = flux_z.shape[1] - WIDTH
    moves = [(flux_y, held_y)]
    moves += [(flux_z.at[:, pl.ds(last, WIDTH)], faces.at[:, :WIDTH])]
    moves += [(flux_z.at[:, :WIDTH], faces.at[:, WIDTH:])]
    for flip, place in ((2, across.at[0]), (3, across.at[1])):
        moves.append((flux_x.at[:, pl.ds(partner("px", flip) * planes, planes)], place))
    copies = [pltpu.make_async_copy(a, b, sems.at[i]) for i, (a, b) in enumerate(moves)]
    for copy in copies:
        copy.start()
    copies[0].wait()
    pick_rows(held_y, rows, count, flips, sent_y)
    for copy in copies[1:]:
        copy.wait()


def second_kernel(rows, count, flips, flux_y, *outs):
    pick_rows(flux_y, rows, count, flips, outs)


def join_x_kernel(planes, after, flux_x, got, out):
    out[0] = flux_x[:, pl.ds(partner("px", 1) * planes, planes)]
    out[1] = got[1]


def join_kernel(stay, got, *refs):
    out = refs[-1]
    out[0] = stay[1]
    out[1] = got[1]


def stencil_kernel(planes, flux_z, faces, across, stay, held):
    own = flux_z.shape[1]

    def plane(variable, index):
        if index < 0:
            return faces[variable, WIDTH + index].astype(jnp.float32)
        if index >= own:
            return faces[variable, WIDTH + index - own].astype(jnp.float32)
        return flux_z[variable, index].astype(jnp.float32)

    for variable in range(flux_z.shape[0]):
        for index in range(own):
            total = jnp.zeros(flux_z.shape[2:], jnp.float32)
            for offset in range(WIDTH):
                upper = plane(variable, index + offset + 1)
                lower = plane(variable, index - offset - 1)
                total = total + STENCIL_COEFS[offset] * (upper - lower)
            held[variable, index] = total.astype(jnp.bfloat16)
    for flip, place in ((2, across.at[0]), (3, across.at[1]), (0, stay.at[0]), (1, stay.at[1])):
        place[...] = held[:, pl.ds(partner("px", flip) * planes, planes)]


def cells(index, width):
    return pl.ds(pl.multiple_of(index * width, width), width)


def times(block, line_op, to, of):
    return lax.dot_general(
        block, line_op[to, of], (((1,), (1,)), ((), ())), preferred_element_type=jnp.float32
    )


def blocks_of(stay, across, joined):
    return ((0, stay, 0), (2, across, 0), (1, joined, 0), (3, joined, 1))


def turn(line_op, index, out):
    depth = out.shape[0]
    for start in range(0, line_op.shape[0], depth):
        place = pl.ds(start, depth)
        out[:, place] = line_op[place, cells(index, depth)].T


def own_kernel(flip, planes, after, own_y, line_op, flux_x, across, out_y, out_x, turned):
    width = own_y.shape[1]
    out_y[...] = times(own_y[...], line_op, ALL, cells(lax.axis_index("py"), width))
    turn(line_op, partner("py", flip), turned)
    width = across.shape[2]
    own_x = flux_x[:, pl.ds(partner("px", 0) * planes, planes)].reshape(-1, width)
    out_x[...] = times(own_x, line_op, ALL, cells(partner("px", 0), width)) + times(
        across[0], line_op, ALL, cells(partner("px", 2), width)
    )


def main_kernel(before, joined, line_op, out):
    width = joined.shape[2]
    out[...] = (
        before[...]
        + times(joined[0], line_op, ALL, cells(partner("px", 1), width))
        + times(joined[1], line_op, ALL, cells(partner("px", 3), width))
    )


def add_kernel(across, joined, stay, products, after, out):
    width = stay.shape[2]
    for flip, ref, index in blocks_of(stay, across, joined):
        place = cells(partner("px", flip), width)
        out[:, place] = (products[:, place] + ref[index].astype(jnp.float32)).astype(jnp.bfloat16)


def first_step_kernel(flip, later, block, before, line_op, out, turned):
    part = times(block[...], line_op, ALL, cells(partner("py", flip), block.shape[1]))
    out[...] = before[...] + part
    turn(line_op, partner("py", later), turned)


def next_step_kernel(after, block, before, turned, out):
    out[...] = before[...] + jnp.dot(
        block[...], turned[...], preferred_element_type=jnp.float32
    )


def late_kernel(early, block, turned, after, out, held, sems):
    rows = out.shape[1]
    copies = []
    for start in range(0, out.shape[2], COLUMNS):
        place = pl.ds(start, COLUMNS)
        part = jnp.dot(block[...], turned[:, place], preferred_element_type=jnp.float32)
        total = early[:, place] + part
        held[:, :, place] = total.astype(jnp.bfloat16).reshape(-1, rows, COLUMNS)
        copy = pltpu.make_async_copy(
            held.at[:, :, place], out.at[:, :, place], sems.at[len(copies)]
        )
        copy.start()
        copies.append(copy)
    for copy in copies:
        copy.wait()


def exchanged(flux_x, flux_y, flux_z, line_op):
    variables, slab, lines, x_width = flux_x.shape
    x_count, y_count = lax.axis_size("px"), lax.axis_size("py")
    planes = slab // x_count
    x_lines, y_width = flux_y.shape[2:]
    rows = x_lines // y_count
    line = line_op.shape[0]
    gathered = variables * slab * rows
    lines_x = variables * planes * lines
    bf16 = jnp.bfloat16

    def like(*shape, kind=bf16):
        return jax.ShapeDtypeStruct(shape, kind)

    rows_y = flux_y.reshape(-1, y_width)
    chunk_y = like(gathered, y_width)
    pair_x = like(2, variables, planes, lines, x_width)
    sent_2, sent_1, held_y, faces, across_x = call(
        functools.partial(first_kernel, rows, y_count, (2, 1), planes),
        [
            chunk_y,
            chunk_y,
            like(*rows_y.shape),
            like(variables, 2 * WIDTH, lines, x_width),
            pair_x,
        ],
        rows_y,
        flux_x,
        flux_z,
        far=(0, 1, 2),
        limit=8,
        scratch=[pltpu.SemaphoreType.DMA((5,))],
    )
    got_2 = swap(sent_2, "py", 2)
    faces = swap(faces, "gz", 1)
    across_x = swap(across_x, "px", 2)
    sent_3, own_y = call(
        functools.partial(second_kernel, rows, y_count, (3, 0)),
        [chunk_y] * 2,
        held_y,
        limit=8,
        flops=STAGE,
    )
    got_1 = swap(sent_1, "py", 1)
    got_3 = swap(sent_3, "py", 3)

    across_z, stay_z = call(
        functools.partial(stencil_kernel, planes),
        [pair_x, pair_x],
        flux_z,
        faces,
        limit=8,
        flops=STAGE,
        scratch=[pltpu.VMEM(flux_z.shape, bf16)],
    )
    joined_x = call(
        functools.partial(join_x_kernel, planes),
        pair_x,
        stay_z,
        flux_x,
        across_x,
        limit=8,
        flops=STAGE // 2,
    )
    flat = (2, lines_x, x_width)
    products_like = like(lines_x, line, kind=jnp.float32)
    sums_like = like(gathered, line, kind=jnp.float32)
    turned_like = like(y_width, line)
    own_sum, half_products, turned_3 = call(
        functools.partial(own_kernel, 3, planes),
        [sums_like, products_like, turned_like],
        joined_x,
        own_y,
        line_op,
        flux_x,
        across_x.reshape(flat),
        limit=16,
        flops=STAGE,
    )
    joined_x = swap(joined_x, "px", 1)
    products = call(
        main_kernel,
        products_like,
        half_products,
        joined_x.reshape(flat),
        line_op,
        limit=16,
        flops=STAGE,
    )
    across_z = swap(across_z, "px", 2)
    joined_z = swap(
        call(join_kernel, pair_x, stay_z, across_z, products, limit=8, flops=STAGE), "px", 1
    )
    block_flops = 2 * gathered * y_width * line
    sum_2, turned_1 = call(
        functools.partial(first_step_kernel, 2, 1),
        [sums_like, turned_like],
        got_2,
        own_sum,
        line_op,
        limit=16,
        flops=STAGE,
    )
    sum_1 = call(
        next_step_kernel,
        sums_like,
        got_2,
        got_1,
        sum_2,
        turned_1,
        limit=16,
        flops=block_flops,
    )
    xz_part = call(
        add_kernel,
        like(lines_x, line),
        *(a.reshape(flat) for a in (across_z, joined_z, stay_z)),
        products,
        sum_1,
        limit=8,
    )
    y_like = like(variables * slab, rows, line)
    y_part = call(
        late_kernel,
        y_like,
        sum_1,
        got_3,
        turned_3,
        xz_part,
        far=(3,),
        far_out=(0,),
        limit=16,
        flops=block_flops,
        scratch=[
            pltpu.VMEM(y_like.shape, bf16),
            pltpu.SemaphoreType.DMA((line // COLUMNS,)),
        ],
    )
    y_part, xz_part = lax.optimization_barrier((y_part, xz_part))
    return (
        xz_part.reshape(variables, planes, lines, line),
        y_part.reshape(variables, slab, rows, line),
    )


def local(flux_x, flux_y, flux_z, line_op):
    counts = tuple(lax.axis_size(axis) for axis in ("gz", "px", "py"))
    lines_y = math.prod(flux_y.shape[:3])
    widths = (flux_x.shape[3], flux_y.shape[3], COLUMNS)
    fits = (
        counts == (2, 4, 4)
        and flux_x.shape == flux_z.shape
        and lines_y % GROUP == 0
        and GROUP % flux_y.shape[2] == 0
        and flux_x.shape[2] % 8 == 0
        and flux_z.shape[1] >= 2 * WIDTH
        and all(line_op.shape[0] % width == 0 and width % 128 == 0 for width in widths)
    )
    return (exchanged if fits else plain)(flux_x, flux_y, flux_z, line_op)


def solution(mesh):
    return jax.shard_map(
        local,
        mesh=mesh,
        in_specs=(
            P(None, "gz", "py", "px"),
            P(None, "gz", "px", "py"),
            P(None, "gz", "py", "px"),
            P(),
        ),
        out_specs=(P(None, ("gz", "px"), "py", None), P(None, "gz", ("px", "py"), None)),
        check_vma=False,
    )
```

```python
import functools
import math

import jax
import jax.numpy as jnp
from jax import lax
from jax.experimental import pallas as pl
from jax.experimental.pallas import tpu as pltpu
from jax.sharding import PartitionSpec as P

STENCIL_COEFS = (0.8, -0.2, 4.0 / 105.0, -1.0 / 280.0)
WIDTH = 4
GROUP = 256
COLUMNS = 512
STAGE = 3 * 10**9
MIB = 1 << 20
VMEM = pl.BlockSpec(memory_space=pltpu.VMEM)
ALL = slice(None)
FAR = pl.BlockSpec(memory_space=pltpu.HBM)


def with_halo(block, sides, width):
    for axis, dim in sides:
        count = lax.axis_size(axis)
        forward = [(i, i + 1) for i in range(count - 1)]
        forward.append((count - 1, 0))
        backward = [(target, source) for source, target in forward]
        low = lax.ppermute(
            lax.slice_in_dim(block, block.shape[dim] - width, None, axis=dim), axis, forward
        )
        high = lax.ppermute(lax.slice_in_dim(block, 0, width, axis=dim), axis, backward)
        block = jnp.concatenate([low, block, high], axis=dim)
    return block


def line_product(block, line_op):
    return lax.dot_general(
        block, line_op, (((3,), (1,)), ((), ())), preferred_element_type=jnp.float32
    )


def z_stencil(padded, planes):
    widened = padded.astype(jnp.float32)
    total = jnp.zeros((widened.shape[0], planes) + widened.shape[2:], jnp.float32)
    for offset in range(WIDTH):
        reach = offset + 1
        upper = widened[:, WIDTH + reach : WIDTH + reach + planes]
        lower = widened[:, WIDTH - reach : WIDTH - reach + planes]
        total = total + STENCIL_COEFS[offset] * (upper - lower)
    return total.astype(jnp.bfloat16)


def plain(flux_x, flux_y, flux_z, line_op):
    planes = flux_z.shape[1]
    z_deriv = z_stencil(with_halo(flux_z, (("gz", 1),), WIDTH), planes)
    y_part = line_product(
        lax.all_to_all(flux_y, "py", split_axis=2, concat_axis=3, tiled=True), line_op
    ).astype(jnp.bfloat16)
    products = line_product(
        lax.all_to_all(flux_x, "px", split_axis=1, concat_axis=3, tiled=True), line_op
    )
    moved = lax.all_to_all(z_deriv, "px", split_axis=1, concat_axis=3, tiled=True)
    xz_part = (products + moved.astype(jnp.float32)).astype(jnp.bfloat16)
    return (xz_part, y_part)


def partner(axis, flip):
    return lax.axis_index(axis) ^ flip


def swap(block, axis, flip):
    pairs = [(i, i ^ flip) for i in range(lax.axis_size(axis))]
    return lax.ppermute(block, axis, pairs)


def call(kernel, out_shape, *operands, limit, flops=0, scratch=(), far=(), far_out=()):
    single = not isinstance(out_shape, list)
    out_shape = [out_shape] if single else out_shape
    moved = sum(a.size * a.dtype.itemsize for a in (*operands, *jax.tree.leaves(out_shape)))
    operands = [
        pltpu.with_memory_space_constraint(a, pltpu.HBM) if index in far else a
        for index, a in enumerate(operands)
    ]
    results = pl.pallas_call(
        kernel,
        out_shape=out_shape,
        in_specs=[FAR if index in far else VMEM for index in range(len(operands))],
        out_specs=[FAR if index in far_out else VMEM for index in range(len(out_shape))],
        scratch_shapes=scratch,
        compiler_params=pltpu.CompilerParams(vmem_limit_bytes=limit * MIB),
        cost_estimate=pl.CostEstimate(flops=flops, bytes_accessed=moved, transcendentals=0),
    )(*operands)
    return results[0] if single else results


def pick_rows(lines, rows, count, flips, outs):
    kept = GROUP // count
    line = lax.broadcasted_iota(jnp.int32, (kept, GROUP), 0)
    source = lax.broadcasted_iota(jnp.int32, (kept, GROUP), 1)
    first = (line // rows) * (count * rows) + line % rows
    chosen = jnp.concatenate(
        [(source == first + partner("py", flip) * rows).astype(jnp.float32) for flip in flips]
    ).astype(jnp.bfloat16)
    for part in range(lines.shape[0] // GROUP):
        picked = jnp.dot(
            chosen,
            lines[part * GROUP : (part + 1) * GROUP, :],
            preferred_element_type=jnp.float32,
        ).astype(jnp.bfloat16)
        for index, out in enumerate(outs):
            out[part * kept : (part + 1) * kept, :] = picked[index * kept : (index + 1) * kept]


def first_kernel(rows, count, flips, planes, flux_y, flux_x, flux_z, *refs):
    sent_y, (held_y, faces, across, sems) = refs[: len(flips)], refs[len(flips) :]
    last = flux_z.shape[1] - WIDTH
    moves = [(flux_y, held_y)]
    moves += [(flux_z.at[:, pl.ds(last, WIDTH)], faces.at[:, :WIDTH])]
    moves += [(flux_z.at[:, :WIDTH], faces.at[:, WIDTH:])]
    for flip, place in ((2, across.at[0]), (3, across.at[1])):
        moves.append((flux_x.at[:, pl.ds(partner("px", flip) * planes, planes)], place))
    copies = [pltpu.make_async_copy(a, b, sems.at[i]) for i, (a, b) in enumerate(moves)]
    for copy in copies:
        copy.start()
    copies[0].wait()
    pick_rows(held_y, rows, count, flips, sent_y)
    for copy in copies[1:]:
        copy.wait()


def second_kernel(rows, count, flips, flux_y, *outs):
    pick_rows(flux_y, rows, count, flips, outs)


def join_x_kernel(planes, after, flux_x, got, out):
    out[0] = flux_x[:, pl.ds(partner("px", 1) * planes, planes)]
    out[1] = got[1]


def join_kernel(stay, got, *refs):
    out = refs[-1]
    out[0] = stay[1]
    out[1] = got[1]


def stencil_kernel(planes, flux_z, faces, across, stay, held):
    own = flux_z.shape[1]

    def plane(variable, index):
        if index < 0:
            return faces[variable, WIDTH + index].astype(jnp.float32)
        if index >= own:
            return faces[variable, WIDTH + index - own].astype(jnp.float32)
        return flux_z[variable, index].astype(jnp.float32)

    for variable in range(flux_z.shape[0]):
        for index in range(own):
            total = jnp.zeros(flux_z.shape[2:], jnp.float32)
            for offset in range(WIDTH):
                upper = plane(variable, index + offset + 1)
                lower = plane(variable, index - offset - 1)
                total = total + STENCIL_COEFS[offset] * (upper - lower)
            held[variable, index] = total.astype(jnp.bfloat16)
    for flip, place in ((2, across.at[0]), (3, across.at[1]), (0, stay.at[0]), (1, stay.at[1])):
        place[...] = held[:, pl.ds(partner("px", flip) * planes, planes)]


def cells(index, width):
    return pl.ds(pl.multiple_of(index * width, width), width)


def times(block, line_op, to, of):
    return lax.dot_general(
        block, line_op[to, of], (((1,), (1,)), ((), ())), preferred_element_type=jnp.float32
    )


def blocks_of(stay, across, joined):
    return ((0, stay, 0), (2, across, 0), (1, joined, 0), (3, joined, 1))


def turn(line_op, index, out):
    depth = out.shape[0]
    for start in range(0, line_op.shape[0], depth):
        place = pl.ds(start, depth)
        out[:, place] = line_op[place, cells(index, depth)].T


def own_kernel(flip, planes, after, own_y, line_op, flux_x, across, out_y, out_x, turned):
    width = own_y.shape[1]
    out_y[...] = times(own_y[...], line_op, ALL, cells(lax.axis_index("py"), width))
    turn(line_op, partner("py", flip), turned)
    width = across.shape[2]
    own_x = flux_x[:, pl.ds(partner("px", 0) * planes, planes)].reshape(-1, width)
    out_x[...] = times(own_x, line_op, ALL, cells(partner("px", 0), width)) + times(
        across[0], line_op, ALL, cells(partner("px", 2), width)
    )


def main_kernel(before, joined, line_op, out):
    width = joined.shape[2]
    out[...] = (
        before[...]
        + times(joined[0], line_op, ALL, cells(partner("px", 1), width))
        + times(joined[1], line_op, ALL, cells(partner("px", 3), width))
    )


def add_kernel(across, joined, stay, products, after, out):
    width = stay.shape[2]
    for flip, ref, index in blocks_of(stay, across, joined):
        place = cells(partner("px", flip), width)
        out[:, place] = (products[:, place] + ref[index].astype(jnp.float32)).astype(jnp.bfloat16)


def first_step_kernel(flip, later, block, before, line_op, out, turned):
    part = times(block[...], line_op, ALL, cells(partner("py", flip), block.shape[1]))
    out[...] = before[...] + part
    turn(line_op, partner("py", later), turned)


def next_step_kernel(after, block, before, turned, out):
    out[...] = before[...] + jnp.dot(
        block[...], turned[...], preferred_element_type=jnp.float32
    )


def late_kernel(early, block, turned, after, out, held, sems):
    rows = out.shape[1]
    copies = []
    for start in range(0, out.shape[2], COLUMNS):
        place = pl.ds(start, COLUMNS)
        part = jnp.dot(block[...], turned[:, place], preferred_element_type=jnp.float32)
        total = early[:, place] + part
        held[:, :, place] = total.astype(jnp.bfloat16).reshape(-1, rows, COLUMNS)
        copy = pltpu.make_async_copy(
            held.at[:, :, place], out.at[:, :, place], sems.at[len(copies)]
        )
        copy.start()
        copies.append(copy)
    for copy in copies:
        copy.wait()


def exchanged(flux_x, flux_y, flux_z, line_op):
    variables, slab, lines, x_width = flux_x.shape
    x_count, y_count = lax.axis_size("px"), lax.axis_size("py")
    planes = slab // x_count
    x_lines, y_width = flux_y.shape[2:]
    rows = x_lines // y_count
    line = line_op.shape[0]
    gathered = variables * slab * rows
    lines_x = variables * planes * lines
    bf16 = jnp.bfloat16

    def like(*shape, kind=bf16):
        return jax.ShapeDtypeStruct(shape, kind)

    rows_y = flux_y.reshape(-1, y_width)
    chunk_y = like(gathered, y_width)
    pair_x = like(2, variables, planes, lines, x_width)
    sent_2, sent_1, sent_3, held_y, faces, across_x = call(
        functools.partial(first_kernel, rows, y_count, (2, 1, 3), planes),
        [
            chunk_y,
            chunk_y,
            chunk_y,
            like(*rows_y.shape),
            like(variables, 2 * WIDTH, lines, x_width),
            pair_x,
        ],
        rows_y,
        flux_x,
        flux_z,
        far=(0, 1, 2),
        limit=8,
        scratch=[pltpu.SemaphoreType.DMA((5,))],
    )
    got_2 = swap(sent_2, "py", 2)
    faces = swap(faces, "gz", 1)
    across_x = swap(across_x, "px", 2)
    (own_y,) = call(
        functools.partial(second_kernel, rows, y_count, (0,)),
        [chunk_y],
        held_y,
        limit=8,
        flops=STAGE,
    )
    got_1 = swap(sent_1, "py", 1)
    got_3 = swap(sent_3, "py", 3)

    across_z, stay_z = call(
        functools.partial(stencil_kernel, planes),
        [pair_x, pair_x],
        flux_z,
        faces,
        limit=8,
        flops=STAGE,
        scratch=[pltpu.VMEM(flux_z.shape, bf16)],
    )
    joined_x = call(
        functools.partial(join_x_kernel, planes),
        pair_x,
        stay_z,
        flux_x,
        across_x,
        limit=8,
        flops=STAGE // 2,
    )
    flat = (2, lines_x, x_width)
    products_like = like(lines_x, line, kind=jnp.float32)
    sums_like = like(gathered, line, kind=jnp.float32)
    turned_like = like(y_width, line)
    own_sum, half_products, turned_3 = call(
        functools.partial(own_kernel, 3, planes),
        [sums_like, products_like, turned_like],
        joined_x,
        own_y,
        line_op,
        flux_x,
        across_x.reshape(flat),
        limit=16,
        flops=STAGE,
    )
    joined_x = swap(joined_x, "px", 1)
    products = call(
        main_kernel,
        products_like,
        half_products,
        joined_x.reshape(flat),
        line_op,
        limit=16,
        flops=STAGE,
    )
    across_z = swap(across_z, "px", 2)
    joined_z = swap(
        call(join_kernel, pair_x, stay_z, across_z, products, limit=8, flops=STAGE), "px", 1
    )
    block_flops = 2 * gathered * y_width * line
    sum_2, turned_1 = call(
        functools.partial(first_step_kernel, 2, 1),
        [sums_like, turned_like],
        got_2,
        own_sum,
        line_op,
        limit=16,
        flops=STAGE,
    )
    sum_1 = call(
        next_step_kernel,
        sums_like,
        got_2,
        got_1,
        sum_2,
        turned_1,
        limit=16,
        flops=block_flops,
    )
    xz_part = call(
        add_kernel,
        like(lines_x, line),
        *(a.reshape(flat) for a in (across_z, joined_z, stay_z)),
        products,
        sum_1,
        limit=8,
    )
    y_like = like(variables * slab, rows, line)
    y_part = call(
        late_kernel,
        y_like,
        sum_1,
        got_3,
        turned_3,
        xz_part,
        far=(3,),
        far_out=(0,),
        limit=16,
        flops=block_flops,
        scratch=[
            pltpu.VMEM(y_like.shape, bf16),
            pltpu.SemaphoreType.DMA((line // COLUMNS,)),
        ],
    )
    y_part, xz_part = lax.optimization_barrier((y_part, xz_part))
    return (
        xz_part.reshape(variables, planes, lines, line),
        y_part.reshape(variables, slab, rows, line),
    )


def local(flux_x, flux_y, flux_z, line_op):
    counts = tuple(lax.axis_size(axis) for axis in ("gz", "px", "py"))
    lines_y = math.prod(flux_y.shape[:3])
    widths = (flux_x.shape[3], flux_y.shape[3], COLUMNS)
    fits = (
        counts == (2, 4, 4)
        and flux_x.shape == flux_z.shape
        and lines_y % GROUP == 0
        and GROUP % flux_y.shape[2] == 0
        and flux_x.shape[2] % 8 == 0
        and flux_z.shape[1] >= 2 * WIDTH
        and all(line_op.shape[0] % width == 0 and width % 128 == 0 for width in widths)
    )
    return (exchanged if fits else plain)(flux_x, flux_y, flux_z, line_op)


def solution(mesh):
    return jax.shard_map(
        local,
        mesh=mesh,
        in_specs=(
            P(None, "gz", "py", "px"),
            P(None, "gz", "px", "py"),
            P(None, "gz", "py", "px"),
            P(),
        ),
        out_specs=(P(None, ("gz", "px"), "py", None), P(None, "gz", ("px", "py"), None)),
        check_vma=False,
    )
```

```python
import functools
import math

import jax
import jax.numpy as jnp
from jax import lax
from jax.experimental import pallas as pl
from jax.experimental.pallas import tpu as pltpu
from jax.sharding import PartitionSpec as P

STENCIL_COEFS = (0.8, -0.2, 4.0 / 105.0, -1.0 / 280.0)
WIDTH = 4
GROUP = 256
COLUMNS = 512
STAGE = 3 * 10**9
MIB = 1 << 20
VMEM = pl.BlockSpec(memory_space=pltpu.VMEM)
ALL = slice(None)
FAR = pl.BlockSpec(memory_space=pltpu.HBM)


def with_halo(block, sides, width):
    for axis, dim in sides:
        count = lax.axis_size(axis)
        forward = [(i, i + 1) for i in range(count - 1)]
        forward.append((count - 1, 0))
        backward = [(target, source) for source, target in forward]
        low = lax.ppermute(
            lax.slice_in_dim(block, block.shape[dim] - width, None, axis=dim), axis, forward
        )
        high = lax.ppermute(lax.slice_in_dim(block, 0, width, axis=dim), axis, backward)
        block = jnp.concatenate([low, block, high], axis=dim)
    return block


def line_product(block, line_op):
    return lax.dot_general(
        block, line_op, (((3,), (1,)), ((), ())), preferred_element_type=jnp.float32
    )


def z_stencil(padded, planes):
    widened = padded.astype(jnp.float32)
    total = jnp.zeros((widened.shape[0], planes) + widened.shape[2:], jnp.float32)
    for offset in range(WIDTH):
        reach = offset + 1
        upper = widened[:, WIDTH + reach : WIDTH + reach + planes]
        lower = widened[:, WIDTH - reach : WIDTH - reach + planes]
        total = total + STENCIL_COEFS[offset] * (upper - lower)
    return total.astype(jnp.bfloat16)


def plain(flux_x, flux_y, flux_z, line_op):
    planes = flux_z.shape[1]
    z_deriv = z_stencil(with_halo(flux_z, (("gz", 1),), WIDTH), planes)
    y_part = line_product(
        lax.all_to_all(flux_y, "py", split_axis=2, concat_axis=3, tiled=True), line_op
    ).astype(jnp.bfloat16)
    products = line_product(
        lax.all_to_all(flux_x, "px", split_axis=1, concat_axis=3, tiled=True), line_op
    )
    moved = lax.all_to_all(z_deriv, "px", split_axis=1, concat_axis=3, tiled=True)
    xz_part = (products + moved.astype(jnp.float32)).astype(jnp.bfloat16)
    return (xz_part, y_part)


def partner(axis, flip):
    return lax.axis_index(axis) ^ flip


def swap(block, axis, flip):
    pairs = [(i, i ^ flip) for i in range(lax.axis_size(axis))]
    return lax.ppermute(block, axis, pairs)


def call(kernel, out_shape, *operands, limit, flops=0, scratch=(), far=(), far_out=()):
    single = not isinstance(out_shape, list)
    out_shape = [out_shape] if single else out_shape
    moved = sum(a.size * a.dtype.itemsize for a in (*operands, *jax.tree.leaves(out_shape)))
    operands = [
        pltpu.with_memory_space_constraint(a, pltpu.HBM) if index in far else a
        for index, a in enumerate(operands)
    ]
    results = pl.pallas_call(
        kernel,
        out_shape=out_shape,
        in_specs=[FAR if index in far else VMEM for index in range(len(operands))],
        out_specs=[FAR if index in far_out else VMEM for index in range(len(out_shape))],
        scratch_shapes=scratch,
        compiler_params=pltpu.CompilerParams(vmem_limit_bytes=limit * MIB),
        cost_estimate=pl.CostEstimate(flops=flops, bytes_accessed=moved, transcendentals=0),
    )(*operands)
    return results[0] if single else results


def pick_rows(lines, rows, count, flips, outs):
    kept = GROUP // count
    line = lax.broadcasted_iota(jnp.int32, (kept, GROUP), 0)
    source = lax.broadcasted_iota(jnp.int32, (kept, GROUP), 1)
    first = (line // rows) * (count * rows) + line % rows
    chosen = jnp.concatenate(
        [(source == first + partner("py", flip) * rows).astype(jnp.float32) for flip in flips]
    ).astype(jnp.bfloat16)
    for part in range(lines.shape[0] // GROUP):
        picked = jnp.dot(
            chosen,
            lines[part * GROUP : (part + 1) * GROUP, :],
            preferred_element_type=jnp.float32,
        ).astype(jnp.bfloat16)
        for index, out in enumerate(outs):
            out[part * kept : (part + 1) * kept, :] = picked[index * kept : (index + 1) * kept]


def first_kernel(rows, count, flips, planes, flux_y, flux_x, flux_z, *refs):
    sent_y, (held_y, faces, across, sems) = refs[: len(flips)], refs[len(flips) :]
    last = flux_z.shape[1] - WIDTH
    moves = [(flux_y, held_y)]
    moves += [(flux_z.at[:, pl.ds(last, WIDTH)], faces.at[:, :WIDTH])]
    moves += [(flux_z.at[:, :WIDTH], faces.at[:, WIDTH:])]
    for flip, place in ((2, across.at[0]), (3, across.at[1])):
        moves.append((flux_x.at[:, pl.ds(partner("px", flip) * planes, planes)], place))
    copies = [pltpu.make_async_copy(a, b, sems.at[i]) for i, (a, b) in enumerate(moves)]
    for copy in copies:
        copy.start()
    copies[0].wait()
    pick_rows(held_y, rows, count, flips, sent_y)
    for copy in copies[1:]:
        copy.wait()


def second_kernel(rows, count, flips, flux_y, *outs):
    pick_rows(flux_y, rows, count, flips, outs)


def join_x_kernel(planes, after, flux_x, got, out):
    out[0] = flux_x[:, pl.ds(partner("px", 1) * planes, planes)]
    out[1] = got[1]


def join_kernel(stay, got, *refs):
    out = refs[-1]
    out[0] = stay[1]
    out[1] = got[1]


def stencil_kernel(planes, flux_z, faces, across, stay, held):
    own = flux_z.shape[1]

    def plane(variable, index):
        if index < 0:
            return faces[variable, WIDTH + index].astype(jnp.float32)
        if index >= own:
            return faces[variable, WIDTH + index - own].astype(jnp.float32)
        return flux_z[variable, index].astype(jnp.float32)

    for variable in range(flux_z.shape[0]):
        for index in range(own):
            total = jnp.zeros(flux_z.shape[2:], jnp.float32)
            for offset in range(WIDTH):
                upper = plane(variable, index + offset + 1)
                lower = plane(variable, index - offset - 1)
                total = total + STENCIL_COEFS[offset] * (upper - lower)
            held[variable, index] = total.astype(jnp.bfloat16)
    for flip, place in ((2, across.at[0]), (3, across.at[1]), (0, stay.at[0]), (1, stay.at[1])):
        place[...] = held[:, pl.ds(partner("px", flip) * planes, planes)]


def cells(index, width):
    return pl.ds(pl.multiple_of(index * width, width), width)


def times(block, line_op, to, of):
    return lax.dot_general(
        block, line_op[to, of], (((1,), (1,)), ((), ())), preferred_element_type=jnp.float32
    )


def blocks_of(stay, across, joined):
    return ((0, stay, 0), (2, across, 0), (1, joined, 0), (3, joined, 1))


def turn(line_op, index, out):
    depth = out.shape[0]
    for start in range(0, line_op.shape[0], depth):
        place = pl.ds(start, depth)
        out[:, place] = line_op[place, cells(index, depth)].T


def own_kernel(flip, planes, after, own_y, line_op, flux_x, across, out_y, out_x, turned):
    width = own_y.shape[1]
    out_y[...] = times(own_y[...], line_op, ALL, cells(lax.axis_index("py"), width))
    turn(line_op, partner("py", flip), turned)
    width = across.shape[2]
    own_x = flux_x[:, pl.ds(partner("px", 0) * planes, planes)].reshape(-1, width)
    out_x[...] = times(own_x, line_op, ALL, cells(partner("px", 0), width)) + times(
        across[0], line_op, ALL, cells(partner("px", 2), width)
    )


def main_kernel(before, joined, line_op, out):
    width = joined.shape[2]
    out[...] = (
        before[...]
        + times(joined[0], line_op, ALL, cells(partner("px", 1), width))
        + times(joined[1], line_op, ALL, cells(partner("px", 3), width))
    )


def add_kernel(across, joined, stay, products, after, out):
    width = stay.shape[2]
    for flip, ref, index in blocks_of(stay, across, joined):
        place = cells(partner("px", flip), width)
        out[:, place] = (products[:, place] + ref[index].astype(jnp.float32)).astype(jnp.bfloat16)


def first_step_kernel(flip, later, block, before, line_op, out, turned):
    part = times(block[...], line_op, ALL, cells(partner("py", flip), block.shape[1]))
    out[...] = before[...] + part
    turn(line_op, partner("py", later), turned)


def next_step_kernel(after, block, before, turned, out):
    out[...] = before[...] + jnp.dot(
        block[...], turned[...], preferred_element_type=jnp.float32
    )


def column_blocks(columns):
    count, half = columns // COLUMNS, COLUMNS // 2
    inner = [(COLUMNS * index + half, COLUMNS) for index in range(1, count - 1)]
    return [(0, COLUMNS + half), *inner, (columns - half, half)]


def late_kernel(early, block, turned, after, out, held, sems):
    rows = out.shape[1]
    copies = []
    for start, size in column_blocks(out.shape[2]):
        place = pl.ds(start, size)
        part = jnp.dot(block[...], turned[:, place], preferred_element_type=jnp.float32)
        total = early[:, place] + part
        held[:, :, place] = total.astype(jnp.bfloat16).reshape(-1, rows, size)
        copy = pltpu.make_async_copy(
            held.at[:, :, place], out.at[:, :, place], sems.at[len(copies)]
        )
        copy.start()
        copies.append(copy)
    for copy in copies:
        copy.wait()


def exchanged(flux_x, flux_y, flux_z, line_op):
    variables, slab, lines, x_width = flux_x.shape
    x_count, y_count = lax.axis_size("px"), lax.axis_size("py")
    planes = slab // x_count
    x_lines, y_width = flux_y.shape[2:]
    rows = x_lines // y_count
    line = line_op.shape[0]
    gathered = variables * slab * rows
    lines_x = variables * planes * lines
    bf16 = jnp.bfloat16

    def like(*shape, kind=bf16):
        return jax.ShapeDtypeStruct(shape, kind)

    rows_y = flux_y.reshape(-1, y_width)
    chunk_y = like(gathered, y_width)
    pair_x = like(2, variables, planes, lines, x_width)
    sent_2, sent_1, sent_3, held_y, faces, across_x = call(
        functools.partial(first_kernel, rows, y_count, (2, 1, 3), planes),
        [
            chunk_y,
            chunk_y,
            chunk_y,
            like(*rows_y.shape),
            like(variables, 2 * WIDTH, lines, x_width),
            pair_x,
        ],
        rows_y,
        flux_x,
        flux_z,
        far=(0, 1, 2),
        limit=8,
        scratch=[pltpu.SemaphoreType.DMA((5,))],
    )
    got_2 = swap(sent_2, "py", 2)
    faces = swap(faces, "gz", 1)
    across_x = swap(across_x, "px", 2)
    (own_y,) = call(
        functools.partial(second_kernel, rows, y_count, (0,)),
        [chunk_y],
        held_y,
        limit=8,
        flops=STAGE,
    )
    got_1 = swap(sent_1, "py", 1)
    got_3 = swap(sent_3, "py", 3)

    across_z, stay_z = call(
        functools.partial(stencil_kernel, planes),
        [pair_x, pair_x],
        flux_z,
        faces,
        limit=8,
        flops=STAGE,
        scratch=[pltpu.VMEM(flux_z.shape, bf16)],
    )
    joined_x = call(
        functools.partial(join_x_kernel, planes),
        pair_x,
        stay_z,
        flux_x,
        across_x,
        limit=8,
        flops=STAGE // 2,
    )
    flat = (2, lines_x, x_width)
    products_like = like(lines_x, line, kind=jnp.float32)
    sums_like = like(gathered, line, kind=jnp.float32)
    turned_like = like(y_width, line)
    own_sum, half_products, turned_3 = call(
        functools.partial(own_kernel, 3, planes),
        [sums_like, products_like, turned_like],
        joined_x,
        own_y,
        line_op,
        flux_x,
        across_x.reshape(flat),
        limit=16,
        flops=STAGE,
    )
    joined_x = swap(joined_x, "px", 1)
    products = call(
        main_kernel,
        products_like,
        half_products,
        joined_x.reshape(flat),
        line_op,
        limit=16,
        flops=STAGE,
    )
    across_z = swap(across_z, "px", 2)
    joined_z = swap(
        call(join_kernel, pair_x, stay_z, across_z, products, limit=8, flops=STAGE), "px", 1
    )
    block_flops = 2 * gathered * y_width * line
    sum_2, turned_1 = call(
        functools.partial(first_step_kernel, 2, 1),
        [sums_like, turned_like],
        got_2,
        own_sum,
        line_op,
        limit=16,
        flops=STAGE,
    )
    sum_1 = call(
        next_step_kernel,
        sums_like,
        got_2,
        got_1,
        sum_2,
        turned_1,
        limit=16,
        flops=block_flops,
    )
    xz_part = call(
        add_kernel,
        like(lines_x, line),
        *(a.reshape(flat) for a in (across_z, joined_z, stay_z)),
        products,
        sum_1,
        limit=8,
    )
    y_like = like(variables * slab, rows, line)
    y_part = call(
        late_kernel,
        y_like,
        sum_1,
        got_3,
        turned_3,
        xz_part,
        far=(3,),
        far_out=(0,),
        limit=16,
        flops=block_flops,
        scratch=[
            pltpu.VMEM(y_like.shape, bf16),
            pltpu.SemaphoreType.DMA((line // COLUMNS,)),
        ],
    )
    y_part, xz_part = lax.optimization_barrier((y_part, xz_part))
    return (
        xz_part.reshape(variables, planes, lines, line),
        y_part.reshape(variables, slab, rows, line),
    )


def local(flux_x, flux_y, flux_z, line_op):
    counts = tuple(lax.axis_size(axis) for axis in ("gz", "px", "py"))
    lines_y = math.prod(flux_y.shape[:3])
    widths = (flux_x.shape[3], flux_y.shape[3], COLUMNS)
    fits = (
        counts == (2, 4, 4)
        and flux_x.shape == flux_z.shape
        and lines_y % GROUP == 0
        and GROUP % flux_y.shape[2] == 0
        and flux_x.shape[2] % 8 == 0
        and flux_z.shape[1] >= 2 * WIDTH
        and all(line_op.shape[0] % width == 0 and width % 128 == 0 for width in widths)
    )
    return (exchanged if fits else plain)(flux_x, flux_y, flux_z, line_op)


def solution(mesh):
    return jax.shard_map(
        local,
        mesh=mesh,
        in_specs=(
            P(None, "gz", "py", "px"),
            P(None, "gz", "px", "py"),
            P(None, "gz", "py", "px"),
            P(),
        ),
        out_specs=(P(None, ("gz", "px"), "py", None), P(None, "gz", ("px", "py"), None)),
        check_vma=False,
    )
```

```python
import functools
import math

import jax
import jax.numpy as jnp
from jax import lax
from jax.experimental import pallas as pl
from jax.experimental.pallas import tpu as pltpu
from jax.sharding import PartitionSpec as P

STENCIL_COEFS = (0.8, -0.2, 4.0 / 105.0, -1.0 / 280.0)
WIDTH = 4
GROUP = 256
COLUMNS = 512
STAGE = 3 * 10**9
MIB = 1 << 20
VMEM = pl.BlockSpec(memory_space=pltpu.VMEM)
ALL = slice(None)
FAR = pl.BlockSpec(memory_space=pltpu.HBM)


def with_halo(block, sides, width):
    for axis, dim in sides:
        count = lax.axis_size(axis)
        forward = [(i, i + 1) for i in range(count - 1)]
        forward.append((count - 1, 0))
        backward = [(target, source) for source, target in forward]
        low = lax.ppermute(
            lax.slice_in_dim(block, block.shape[dim] - width, None, axis=dim), axis, forward
        )
        high = lax.ppermute(lax.slice_in_dim(block, 0, width, axis=dim), axis, backward)
        block = jnp.concatenate([low, block, high], axis=dim)
    return block


def line_product(block, line_op):
    return lax.dot_general(
        block, line_op, (((3,), (1,)), ((), ())), preferred_element_type=jnp.float32
    )


def z_stencil(padded, planes):
    widened = padded.astype(jnp.float32)
    total = jnp.zeros((widened.shape[0], planes) + widened.shape[2:], jnp.float32)
    for offset in range(WIDTH):
        reach = offset + 1
        upper = widened[:, WIDTH + reach : WIDTH + reach + planes]
        lower = widened[:, WIDTH - reach : WIDTH - reach + planes]
        total = total + STENCIL_COEFS[offset] * (upper - lower)
    return total.astype(jnp.bfloat16)


def plain(flux_x, flux_y, flux_z, line_op):
    planes = flux_z.shape[1]
    z_deriv = z_stencil(with_halo(flux_z, (("gz", 1),), WIDTH), planes)
    y_part = line_product(
        lax.all_to_all(flux_y, "py", split_axis=2, concat_axis=3, tiled=True), line_op
    ).astype(jnp.bfloat16)
    products = line_product(
        lax.all_to_all(flux_x, "px", split_axis=1, concat_axis=3, tiled=True), line_op
    )
    moved = lax.all_to_all(z_deriv, "px", split_axis=1, concat_axis=3, tiled=True)
    xz_part = (products + moved.astype(jnp.float32)).astype(jnp.bfloat16)
    return (xz_part, y_part)


def partner(axis, flip):
    return lax.axis_index(axis) ^ flip


def swap(block, axis, flip):
    pairs = [(i, i ^ flip) for i in range(lax.axis_size(axis))]
    return lax.ppermute(block, axis, pairs)


def call(kernel, out_shape, *operands, limit, flops=0, scratch=(), far=(), far_out=()):
    single = not isinstance(out_shape, list)
    out_shape = [out_shape] if single else out_shape
    moved = sum(a.size * a.dtype.itemsize for a in (*operands, *jax.tree.leaves(out_shape)))
    operands = [
        pltpu.with_memory_space_constraint(a, pltpu.HBM) if index in far else a
        for index, a in enumerate(operands)
    ]
    results = pl.pallas_call(
        kernel,
        out_shape=out_shape,
        in_specs=[FAR if index in far else VMEM for index in range(len(operands))],
        out_specs=[FAR if index in far_out else VMEM for index in range(len(out_shape))],
        scratch_shapes=scratch,
        compiler_params=pltpu.CompilerParams(vmem_limit_bytes=limit * MIB),
        cost_estimate=pl.CostEstimate(flops=flops, bytes_accessed=moved, transcendentals=0),
    )(*operands)
    return results[0] if single else results


def choice(rows, count, flips):
    kept = GROUP // count
    line = lax.broadcasted_iota(jnp.int32, (kept, GROUP), 0)
    source = lax.broadcasted_iota(jnp.int32, (kept, GROUP), 1)
    first = (line // rows) * (count * rows) + line % rows
    return jnp.concatenate(
        [(source == first + partner("py", flip) * rows).astype(jnp.float32) for flip in flips]
    ).astype(jnp.bfloat16)


def pick_rows(chosen, lines, outs):
    kept = chosen.shape[0] // len(outs)
    for part in range(lines.shape[0] // GROUP):
        picked = jnp.dot(
            chosen,
            lines[part * GROUP : (part + 1) * GROUP, :],
            preferred_element_type=jnp.float32,
        ).astype(jnp.bfloat16)
        for index, out in enumerate(outs):
            out[part * kept : (part + 1) * kept, :] = picked[index * kept : (index + 1) * kept]


def first_kernel(rows, count, flips, planes, flux_y, flux_x, flux_z, *refs):
    sent_y, (held_y, faces, across, sems) = refs[: len(flips)], refs[len(flips) :]
    last = flux_z.shape[1] - WIDTH
    moves = [(flux_y, held_y)]
    moves += [(flux_z.at[:, pl.ds(last, WIDTH)], faces.at[:, :WIDTH])]
    moves += [(flux_z.at[:, :WIDTH], faces.at[:, WIDTH:])]
    for flip, place in ((2, across.at[0]), (3, across.at[1])):
        moves.append((flux_x.at[:, pl.ds(partner("px", flip) * planes, planes)], place))
    copies = [pltpu.make_async_copy(a, b, sems.at[i]) for i, (a, b) in enumerate(moves)]
    for copy in copies:
        copy.start()
    chosen = choice(rows, count, flips)
    copies[0].wait()
    pick_rows(chosen, held_y, sent_y)
    for copy in copies[1:]:
        copy.wait()


def second_kernel(rows, count, flips, flux_y, *outs):
    pick_rows(choice(rows, count, flips), flux_y, outs)


def join_x_kernel(planes, after, flux_x, got, out):
    out[0] = flux_x[:, pl.ds(partner("px", 1) * planes, planes)]
    out[1] = got[1]


def join_kernel(stay, got, *refs):
    out = refs[-1]
    out[0] = stay[1]
    out[1] = got[1]


def stencil_kernel(planes, flux_z, faces, across, stay, held):
    own = flux_z.shape[1]

    def plane(variable, index):
        if index < 0:
            return faces[variable, WIDTH + index].astype(jnp.float32)
        if index >= own:
            return faces[variable, WIDTH + index - own].astype(jnp.float32)
        return flux_z[variable, index].astype(jnp.float32)

    for variable in range(flux_z.shape[0]):
        for index in range(own):
            total = jnp.zeros(flux_z.shape[2:], jnp.float32)
            for offset in range(WIDTH):
                upper = plane(variable, index + offset + 1)
                lower = plane(variable, index - offset - 1)
                total = total + STENCIL_COEFS[offset] * (upper - lower)
            held[variable, index] = total.astype(jnp.bfloat16)
    for flip, place in ((2, across.at[0]), (3, across.at[1]), (0, stay.at[0]), (1, stay.at[1])):
        place[...] = held[:, pl.ds(partner("px", flip) * planes, planes)]


def cells(index, width):
    return pl.ds(pl.multiple_of(index * width, width), width)


def times(block, line_op, to, of):
    return lax.dot_general(
        block, line_op[to, of], (((1,), (1,)), ((), ())), preferred_element_type=jnp.float32
    )


def blocks_of(stay, across, joined):
    return ((0, stay, 0), (2, across, 0), (1, joined, 0), (3, joined, 1))


def turn(line_op, index, out):
    depth = out.shape[0]
    for start in range(0, line_op.shape[0], depth):
        place = pl.ds(start, depth)
        out[:, place] = line_op[place, cells(index, depth)].T


def own_kernel(flip, planes, after, own_y, line_op, flux_x, across, out_y, out_x, turned):
    width = own_y.shape[1]
    out_y[...] = times(own_y[...], line_op, ALL, cells(lax.axis_index("py"), width))
    turn(line_op, partner("py", flip), turned)
    width = across.shape[2]
    own_x = flux_x[:, pl.ds(partner("px", 0) * planes, planes)].reshape(-1, width)
    out_x[...] = times(own_x, line_op, ALL, cells(partner("px", 0), width)) + times(
        across[0], line_op, ALL, cells(partner("px", 2), width)
    )


def main_kernel(before, joined, line_op, out):
    width = joined.shape[2]
    out[...] = (
        before[...]
        + times(joined[0], line_op, ALL, cells(partner("px", 1), width))
        + times(joined[1], line_op, ALL, cells(partner("px", 3), width))
    )


def add_kernel(across, joined, stay, products, after, out):
    width = stay.shape[2]
    for flip, ref, index in blocks_of(stay, across, joined):
        place = cells(partner("px", flip), width)
        out[:, place] = (products[:, place] + ref[index].astype(jnp.float32)).astype(jnp.bfloat16)


def first_step_kernel(flip, later, block, before, line_op, out, turned):
    part = times(block[...], line_op, ALL, cells(partner("py", flip), block.shape[1]))
    out[...] = before[...] + part
    turn(line_op, partner("py", later), turned)


def next_step_kernel(after, block, before, turned, out):
    out[...] = before[...] + jnp.dot(
        block[...], turned[...], preferred_element_type=jnp.float32
    )


def late_kernel(early, block, turned, after, out, held, sems):
    rows = out.shape[1]
    copies = []
    for start in range(0, out.shape[2], COLUMNS):
        place = pl.ds(start, COLUMNS)
        part = jnp.dot(block[...], turned[:, place], preferred_element_type=jnp.float32)
        total = early[:, place] + part
        held[:, :, place] = total.astype(jnp.bfloat16).reshape(-1, rows, COLUMNS)
        copy = pltpu.make_async_copy(
            held.at[:, :, place], out.at[:, :, place], sems.at[len(copies)]
        )
        copy.start()
        copies.append(copy)
    for copy in copies:
        copy.wait()


def exchanged(flux_x, flux_y, flux_z, line_op):
    variables, slab, lines, x_width = flux_x.shape
    x_count, y_count = lax.axis_size("px"), lax.axis_size("py")
    planes = slab // x_count
    x_lines, y_width = flux_y.shape[2:]
    rows = x_lines // y_count
    line = line_op.shape[0]
    gathered = variables * slab * rows
    lines_x = variables * planes * lines
    bf16 = jnp.bfloat16

    def like(*shape, kind=bf16):
        return jax.ShapeDtypeStruct(shape, kind)

    rows_y = flux_y.reshape(-1, y_width)
    chunk_y = like(gathered, y_width)
    pair_x = like(2, variables, planes, lines, x_width)
    sent_2, sent_1, sent_3, held_y, faces, across_x = call(
        functools.partial(first_kernel, rows, y_count, (2, 1, 3), planes),
        [
            chunk_y,
            chunk_y,
            chunk_y,
            like(*rows_y.shape),
            like(variables, 2 * WIDTH, lines, x_width),
            pair_x,
        ],
        rows_y,
        flux_x,
        flux_z,
        far=(0, 1, 2),
        limit=8,
        scratch=[pltpu.SemaphoreType.DMA((5,))],
    )
    got_2 = swap(sent_2, "py", 2)
    faces = swap(faces, "gz", 1)
    across_x = swap(across_x, "px", 2)
    (own_y,) = call(
        functools.partial(second_kernel, rows, y_count, (0,)),
        [chunk_y],
        held_y,
        limit=8,
        flops=STAGE,
    )
    got_1 = swap(sent_1, "py", 1)
    got_3 = swap(sent_3, "py", 3)

    across_z, stay_z = call(
        functools.partial(stencil_kernel, planes),
        [pair_x, pair_x],
        flux_z,
        faces,
        limit=8,
        flops=STAGE,
        scratch=[pltpu.VMEM(flux_z.shape, bf16)],
    )
    joined_x = call(
        functools.partial(join_x_kernel, planes),
        pair_x,
        stay_z,
        flux_x,
        across_x,
        limit=8,
        flops=STAGE // 2,
    )
    flat = (2, lines_x, x_width)
    products_like = like(lines_x, line, kind=jnp.float32)
    sums_like = like(gathered, line, kind=jnp.float32)
    turned_like = like(y_width, line)
    own_sum, half_products, turned_3 = call(
        functools.partial(own_kernel, 3, planes),
        [sums_like, products_like, turned_like],
        joined_x,
        own_y,
        line_op,
        flux_x,
        across_x.reshape(flat),
        limit=16,
        flops=STAGE,
    )
    joined_x = swap(joined_x, "px", 1)
    products = call(
        main_kernel,
        products_like,
        half_products,
        joined_x.reshape(flat),
        line_op,
        limit=16,
        flops=STAGE,
    )
    across_z = swap(across_z, "px", 2)
    joined_z = swap(
        call(join_kernel, pair_x, stay_z, across_z, products, limit=8, flops=STAGE), "px", 1
    )
    block_flops = 2 * gathered * y_width * line
    sum_2, turned_1 = call(
        functools.partial(first_step_kernel, 2, 1),
        [sums_like, turned_like],
        got_2,
        own_sum,
        line_op,
        limit=16,
        flops=STAGE,
    )
    sum_1 = call(
        next_step_kernel,
        sums_like,
        got_2,
        got_1,
        sum_2,
        turned_1,
        limit=16,
        flops=block_flops,
    )
    xz_part = call(
        add_kernel,
        like(lines_x, line),
        *(a.reshape(flat) for a in (across_z, joined_z, stay_z)),
        products,
        sum_1,
        limit=8,
    )
    y_like = like(variables * slab, rows, line)
    y_part = call(
        late_kernel,
        y_like,
        sum_1,
        got_3,
        turned_3,
        xz_part,
        far=(3,),
        far_out=(0,),
        limit=16,
        flops=block_flops,
        scratch=[
            pltpu.VMEM(y_like.shape, bf16),
            pltpu.SemaphoreType.DMA((line // COLUMNS,)),
        ],
    )
    y_part, xz_part = lax.optimization_barrier((y_part, xz_part))
    return (
        xz_part.reshape(variables, planes, lines, line),
        y_part.reshape(variables, slab, rows, line),
    )


def local(flux_x, flux_y, flux_z, line_op):
    counts = tuple(lax.axis_size(axis) for axis in ("gz", "px", "py"))
    lines_y = math.prod(flux_y.shape[:3])
    widths = (flux_x.shape[3], flux_y.shape[3], COLUMNS)
    fits = (
        counts == (2, 4, 4)
        and flux_x.shape == flux_z.shape
        and lines_y % GROUP == 0
        and GROUP % flux_y.shape[2] == 0
        and flux_x.shape[2] % 8 == 0
        and flux_z.shape[1] >= 2 * WIDTH
        and all(line_op.shape[0] % width == 0 and width % 128 == 0 for width in widths)
    )
    return (exchanged if fits else plain)(flux_x, flux_y, flux_z, line_op)


def solution(mesh):
    return jax.shard_map(
        local,
        mesh=mesh,
        in_specs=(
            P(None, "gz", "py", "px"),
            P(None, "gz", "px", "py"),
            P(None, "gz", "py", "px"),
            P(),
        ),
        out_specs=(P(None, ("gz", "px"), "py", None), P(None, "gz", ("px", "py"), None)),
        check_vma=False,
    )
```

```python
import functools
import math

import jax
import jax.numpy as jnp
from jax import lax
from jax.experimental import pallas as pl
from jax.experimental.pallas import tpu as pltpu
from jax.sharding import PartitionSpec as P

STENCIL_COEFS = (0.8, -0.2, 4.0 / 105.0, -1.0 / 280.0)
WIDTH = 4
GROUP = 256
COLUMNS = 512
STAGE = 3 * 10**9
MIB = 1 << 20
VMEM = pl.BlockSpec(memory_space=pltpu.VMEM)
ALL = slice(None)
FAR = pl.BlockSpec(memory_space=pltpu.HBM)


def with_halo(block, sides, width):
    for axis, dim in sides:
        count = lax.axis_size(axis)
        forward = [(i, i + 1) for i in range(count - 1)]
        forward.append((count - 1, 0))
        backward = [(target, source) for source, target in forward]
        low = lax.ppermute(
            lax.slice_in_dim(block, block.shape[dim] - width, None, axis=dim), axis, forward
        )
        high = lax.ppermute(lax.slice_in_dim(block, 0, width, axis=dim), axis, backward)
        block = jnp.concatenate([low, block, high], axis=dim)
    return block


def line_product(block, line_op):
    return lax.dot_general(
        block, line_op, (((3,), (1,)), ((), ())), preferred_element_type=jnp.float32
    )


def z_stencil(padded, planes):
    widened = padded.astype(jnp.float32)
    total = jnp.zeros((widened.shape[0], planes) + widened.shape[2:], jnp.float32)
    for offset in range(WIDTH):
        reach = offset + 1
        upper = widened[:, WIDTH + reach : WIDTH + reach + planes]
        lower = widened[:, WIDTH - reach : WIDTH - reach + planes]
        total = total + STENCIL_COEFS[offset] * (upper - lower)
    return total.astype(jnp.bfloat16)


def plain(flux_x, flux_y, flux_z, line_op):
    planes = flux_z.shape[1]
    z_deriv = z_stencil(with_halo(flux_z, (("gz", 1),), WIDTH), planes)
    y_part = line_product(
        lax.all_to_all(flux_y, "py", split_axis=2, concat_axis=3, tiled=True), line_op
    ).astype(jnp.bfloat16)
    products = line_product(
        lax.all_to_all(flux_x, "px", split_axis=1, concat_axis=3, tiled=True), line_op
    )
    moved = lax.all_to_all(z_deriv, "px", split_axis=1, concat_axis=3, tiled=True)
    xz_part = (products + moved.astype(jnp.float32)).astype(jnp.bfloat16)
    return (xz_part, y_part)


def partner(axis, flip):
    return lax.axis_index(axis) ^ flip


def swap(block, axis, flip):
    pairs = [(i, i ^ flip) for i in range(lax.axis_size(axis))]
    return lax.ppermute(block, axis, pairs)


def call(kernel, out_shape, *operands, limit, flops=0, scratch=(), far=(), far_out=()):
    single = not isinstance(out_shape, list)
    out_shape = [out_shape] if single else out_shape
    moved = sum(a.size * a.dtype.itemsize for a in (*operands, *jax.tree.leaves(out_shape)))
    operands = [
        pltpu.with_memory_space_constraint(a, pltpu.HBM) if index in far else a
        for index, a in enumerate(operands)
    ]
    results = pl.pallas_call(
        kernel,
        out_shape=out_shape,
        in_specs=[FAR if index in far else VMEM for index in range(len(operands))],
        out_specs=[FAR if index in far_out else VMEM for index in range(len(out_shape))],
        scratch_shapes=scratch,
        compiler_params=pltpu.CompilerParams(vmem_limit_bytes=limit * MIB),
        cost_estimate=pl.CostEstimate(flops=flops, bytes_accessed=moved, transcendentals=0),
    )(*operands)
    return results[0] if single else results


def pick_rows(lines, rows, count, flips, outs):
    kept = GROUP // count
    line = lax.broadcasted_iota(jnp.int32, (kept, GROUP), 0)
    source = lax.broadcasted_iota(jnp.int32, (kept, GROUP), 1)
    first = (line // rows) * (count * rows) + line % rows
    chosen = jnp.concatenate(
        [(source == first + partner("py", flip) * rows).astype(jnp.float32) for flip in flips]
    ).astype(jnp.bfloat16)
    for part in range(lines.shape[0] // GROUP):
        picked = jnp.dot(
            chosen,
            lines[part * GROUP : (part + 1) * GROUP, :],
            preferred_element_type=jnp.float32,
        ).astype(jnp.bfloat16)
        for index, out in enumerate(outs):
            out[part * kept : (part + 1) * kept, :] = picked[index * kept : (index + 1) * kept]


def first_kernel(rows, count, flips, planes, flux_y, flux_x, flux_z, *refs):
    sent_y, (held_y, faces, across, sems) = refs[: len(flips)], refs[len(flips) :]
    last = flux_z.shape[1] - WIDTH
    moves = [(flux_y, held_y)]
    moves += [(flux_z.at[:, pl.ds(last, WIDTH)], faces.at[:, :WIDTH])]
    moves += [(flux_z.at[:, :WIDTH], faces.at[:, WIDTH:])]
    for flip, place in ((2, across.at[0]), (3, across.at[1])):
        moves.append((flux_x.at[:, pl.ds(partner("px", flip) * planes, planes)], place))
    copies = [pltpu.make_async_copy(a, b, sems.at[i]) for i, (a, b) in enumerate(moves)]
    for copy in copies:
        copy.start()
    copies[0].wait()
    pick_rows(held_y, rows, count, flips, sent_y)
    for copy in copies[1:]:
        copy.wait()


def second_kernel(rows, count, flips, flux_y, *outs):
    pick_rows(flux_y, rows, count, flips, outs)


def join_x_kernel(planes, after, flux_x, got, out):
    out[0] = flux_x[:, pl.ds(partner("px", 1) * planes, planes)]
    out[1] = got[1]


def join_kernel(stay, got, *refs):
    out = refs[-1]
    out[0] = stay[1]
    out[1] = got[1]


def stencil_kernel(planes, flux_z, faces, across, stay, held):
    own = flux_z.shape[1]

    def plane(variable, index):
        if index < 0:
            return faces[variable, WIDTH + index].astype(jnp.float32)
        if index >= own:
            return faces[variable, WIDTH + index - own].astype(jnp.float32)
        return flux_z[variable, index].astype(jnp.float32)

    for variable in range(flux_z.shape[0]):
        for index in range(own):
            total = jnp.zeros(flux_z.shape[2:], jnp.float32)
            for offset in range(WIDTH):
                upper = plane(variable, index + offset + 1)
                lower = plane(variable, index - offset - 1)
                total = total + STENCIL_COEFS[offset] * (upper - lower)
            held[variable, index] = total.astype(jnp.bfloat16)
    for flip, place in ((2, across.at[0]), (3, across.at[1]), (0, stay.at[0]), (1, stay.at[1])):
        place[...] = held[:, pl.ds(partner("px", flip) * planes, planes)]


def cells(index, width):
    return pl.ds(pl.multiple_of(index * width, width), width)


def times(block, line_op, to, of):
    return lax.dot_general(
        block, line_op[to, of], (((1,), (1,)), ((), ())), preferred_element_type=jnp.float32
    )


def blocks_of(stay, across, joined):
    return ((0, stay, 0), (2, across, 0), (1, joined, 0), (3, joined, 1))


def turn(line_op, index, out):
    depth = out.shape[0]
    for start in range(0, line_op.shape[0], depth):
        place = pl.ds(start, depth)
        out[:, place] = line_op[place, cells(index, depth)].T


def own_kernel(flip, planes, after, own_y, line_op, flux_x, across, out_y, out_x, turned):
    width = own_y.shape[1]
    out_y[...] = times(own_y[...], line_op, ALL, cells(lax.axis_index("py"), width))
    turn(line_op, partner("py", flip), turned)
    width = across.shape[2]
    own_x = flux_x[:, pl.ds(partner("px", 0) * planes, planes)].reshape(-1, width)
    out_x[...] = times(own_x, line_op, ALL, cells(partner("px", 0), width)) + times(
        across[0], line_op, ALL, cells(partner("px", 2), width)
    )


def main_kernel(flips, before, joined, line_op, out, *turned):
    width = joined.shape[2]
    out[...] = (
        before[...]
        + times(joined[0], line_op, ALL, cells(partner("px", 1), width))
        + times(joined[1], line_op, ALL, cells(partner("px", 3), width))
    )
    for flip, block in zip(flips, turned):
        turn(line_op, partner("py", flip), block)


def add_kernel(across, joined, stay, products, after, out):
    width = stay.shape[2]
    for flip, ref, index in blocks_of(stay, across, joined):
        place = cells(partner("px", flip), width)
        out[:, place] = (products[:, place] + ref[index].astype(jnp.float32)).astype(jnp.bfloat16)


def first_step_kernel(block, before, turned, out):
    out[...] = before[...] + jnp.dot(
        block[...], turned[...], preferred_element_type=jnp.float32
    )


def next_step_kernel(after, block, before, turned, out):
    out[...] = before[...] + jnp.dot(
        block[...], turned[...], preferred_element_type=jnp.float32
    )


def late_kernel(early, block, turned, after, out, held, sems):
    rows = out.shape[1]
    copies = []
    for start in range(0, out.shape[2], COLUMNS):
        place = pl.ds(start, COLUMNS)
        part = jnp.dot(block[...], turned[:, place], preferred_element_type=jnp.float32)
        total = early[:, place] + part
        held[:, :, place] = total.astype(jnp.bfloat16).reshape(-1, rows, COLUMNS)
        copy = pltpu.make_async_copy(
            held.at[:, :, place], out.at[:, :, place], sems.at[len(copies)]
        )
        copy.start()
        copies.append(copy)
    for copy in copies:
        copy.wait()


def exchanged(flux_x, flux_y, flux_z, line_op):
    variables, slab, lines, x_width = flux_x.shape
    x_count, y_count = lax.axis_size("px"), lax.axis_size("py")
    planes = slab // x_count
    x_lines, y_width = flux_y.shape[2:]
    rows = x_lines // y_count
    line = line_op.shape[0]
    gathered = variables * slab * rows
    lines_x = variables * planes * lines
    bf16 = jnp.bfloat16

    def like(*shape, kind=bf16):
        return jax.ShapeDtypeStruct(shape, kind)

    rows_y = flux_y.reshape(-1, y_width)
    chunk_y = like(gathered, y_width)
    pair_x = like(2, variables, planes, lines, x_width)
    sent_2, sent_1, sent_3, held_y, faces, across_x = call(
        functools.partial(first_kernel, rows, y_count, (2, 1, 3), planes),
        [
            chunk_y,
            chunk_y,
            chunk_y,
            like(*rows_y.shape),
            like(variables, 2 * WIDTH, lines, x_width),
            pair_x,
        ],
        rows_y,
        flux_x,
        flux_z,
        far=(0, 1, 2),
        limit=8,
        scratch=[pltpu.SemaphoreType.DMA((5,))],
    )
    got_2 = swap(sent_2, "py", 2)
    faces = swap(faces, "gz", 1)
    across_x = swap(across_x, "px", 2)
    (own_y,) = call(
        functools.partial(second_kernel, rows, y_count, (0,)),
        [chunk_y],
        held_y,
        limit=8,
        flops=STAGE,
    )
    got_1 = swap(sent_1, "py", 1)
    got_3 = swap(sent_3, "py", 3)

    across_z, stay_z = call(
        functools.partial(stencil_kernel, planes),
        [pair_x, pair_x],
        flux_z,
        faces,
        limit=8,
        flops=STAGE,
        scratch=[pltpu.VMEM(flux_z.shape, bf16)],
    )
    joined_x = call(
        functools.partial(join_x_kernel, planes),
        pair_x,
        stay_z,
        flux_x,
        across_x,
        limit=8,
        flops=STAGE // 2,
    )
    flat = (2, lines_x, x_width)
    products_like = like(lines_x, line, kind=jnp.float32)
    sums_like = like(gathered, line, kind=jnp.float32)
    turned_like = like(y_width, line)
    own_sum, half_products, turned_3 = call(
        functools.partial(own_kernel, 3, planes),
        [sums_like, products_like, turned_like],
        joined_x,
        own_y,
        line_op,
        flux_x,
        across_x.reshape(flat),
        limit=16,
        flops=STAGE,
    )
    joined_x = swap(joined_x, "px", 1)
    products, turned_2, turned_1 = call(
        functools.partial(main_kernel, (2, 1)),
        [products_like, turned_like, turned_like],
        half_products,
        joined_x.reshape(flat),
        line_op,
        limit=16,
        flops=STAGE,
    )
    across_z = swap(across_z, "px", 2)
    joined_z = swap(
        call(join_kernel, pair_x, stay_z, across_z, products, limit=8, flops=STAGE), "px", 1
    )
    block_flops = 2 * gathered * y_width * line
    sum_2 = call(
        first_step_kernel,
        sums_like,
        got_2,
        own_sum,
        turned_2,
        limit=16,
        flops=STAGE,
    )
    sum_1 = call(
        next_step_kernel,
        sums_like,
        got_2,
        got_1,
        sum_2,
        turned_1,
        limit=16,
        flops=block_flops,
    )
    xz_part = call(
        add_kernel,
        like(lines_x, line),
        *(a.reshape(flat) for a in (across_z, joined_z, stay_z)),
        products,
        sum_1,
        limit=8,
    )
    y_like = like(variables * slab, rows, line)
    y_part = call(
        late_kernel,
        y_like,
        sum_1,
        got_3,
        turned_3,
        xz_part,
        far=(3,),
        far_out=(0,),
        limit=16,
        flops=block_flops,
        scratch=[
            pltpu.VMEM(y_like.shape, bf16),
            pltpu.SemaphoreType.DMA((line // COLUMNS,)),
        ],
    )
    y_part, xz_part = lax.optimization_barrier((y_part, xz_part))
    return (
        xz_part.reshape(variables, planes, lines, line),
        y_part.reshape(variables, slab, rows, line),
    )


def local(flux_x, flux_y, flux_z, line_op):
    counts = tuple(lax.axis_size(axis) for axis in ("gz", "px", "py"))
    lines_y = math.prod(flux_y.shape[:3])
    widths = (flux_x.shape[3], flux_y.shape[3], COLUMNS)
    fits = (
        counts == (2, 4, 4)
        and flux_x.shape == flux_z.shape
        and lines_y % GROUP == 0
        and GROUP % flux_y.shape[2] == 0
        and flux_x.shape[2] % 8 == 0
        and flux_z.shape[1] >= 2 * WIDTH
        and all(line_op.shape[0] % width == 0 and width % 128 == 0 for width in widths)
    )
    return (exchanged if fits else plain)(flux_x, flux_y, flux_z, line_op)


def solution(mesh):
    return jax.shard_map(
        local,
        mesh=mesh,
        in_specs=(
            P(None, "gz", "py", "px"),
            P(None, "gz", "px", "py"),
            P(None, "gz", "py", "px"),
            P(),
        ),
        out_specs=(P(None, ("gz", "px"), "py", None), P(None, "gz", ("px", "py"), None)),
        check_vma=False,
    )
```

```python
import functools
import math

import jax
import jax.numpy as jnp
from jax import lax
from jax.experimental import pallas as pl
from jax.experimental.pallas import tpu as pltpu
from jax.sharding import PartitionSpec as P

STENCIL_COEFS = (0.8, -0.2, 4.0 / 105.0, -1.0 / 280.0)
WIDTH = 4
GROUP = 256
COLUMNS = 512
STAGE = 3 * 10**9
MIB = 1 << 20
VMEM = pl.BlockSpec(memory_space=pltpu.VMEM)
ALL = slice(None)
FAR = pl.BlockSpec(memory_space=pltpu.HBM)


def with_halo(block, sides, width):
    for axis, dim in sides:
        count = lax.axis_size(axis)
        forward = [(i, i + 1) for i in range(count - 1)]
        forward.append((count - 1, 0))
        backward = [(target, source) for source, target in forward]
        low = lax.ppermute(
            lax.slice_in_dim(block, block.shape[dim] - width, None, axis=dim), axis, forward
        )
        high = lax.ppermute(lax.slice_in_dim(block, 0, width, axis=dim), axis, backward)
        block = jnp.concatenate([low, block, high], axis=dim)
    return block


def line_product(block, line_op):
    return lax.dot_general(
        block, line_op, (((3,), (1,)), ((), ())), preferred_element_type=jnp.float32
    )


def z_stencil(padded, planes):
    widened = padded.astype(jnp.float32)
    total = jnp.zeros((widened.shape[0], planes) + widened.shape[2:], jnp.float32)
    for offset in range(WIDTH):
        reach = offset + 1
        upper = widened[:, WIDTH + reach : WIDTH + reach + planes]
        lower = widened[:, WIDTH - reach : WIDTH - reach + planes]
        total = total + STENCIL_COEFS[offset] * (upper - lower)
    return total.astype(jnp.bfloat16)


def plain(flux_x, flux_y, flux_z, line_op):
    planes = flux_z.shape[1]
    z_deriv = z_stencil(with_halo(flux_z, (("gz", 1),), WIDTH), planes)
    y_part = line_product(
        lax.all_to_all(flux_y, "py", split_axis=2, concat_axis=3, tiled=True), line_op
    ).astype(jnp.bfloat16)
    products = line_product(
        lax.all_to_all(flux_x, "px", split_axis=1, concat_axis=3, tiled=True), line_op
    )
    moved = lax.all_to_all(z_deriv, "px", split_axis=1, concat_axis=3, tiled=True)
    xz_part = (products + moved.astype(jnp.float32)).astype(jnp.bfloat16)
    return (xz_part, y_part)


def partner(axis, flip):
    return lax.axis_index(axis) ^ flip


def swap(block, axis, flip):
    pairs = [(i, i ^ flip) for i in range(lax.axis_size(axis))]
    return lax.ppermute(block, axis, pairs)


def call(kernel, out_shape, *operands, limit, flops=0, scratch=(), far=(), far_out=()):
    single = not isinstance(out_shape, list)
    out_shape = [out_shape] if single else out_shape
    moved = sum(a.size * a.dtype.itemsize for a in (*operands, *jax.tree.leaves(out_shape)))
    operands = [
        pltpu.with_memory_space_constraint(a, pltpu.HBM) if index in far else a
        for index, a in enumerate(operands)
    ]
    results = pl.pallas_call(
        kernel,
        out_shape=out_shape,
        in_specs=[FAR if index in far else VMEM for index in range(len(operands))],
        out_specs=[FAR if index in far_out else VMEM for index in range(len(out_shape))],
        scratch_shapes=scratch,
        compiler_params=pltpu.CompilerParams(vmem_limit_bytes=limit * MIB),
        cost_estimate=pl.CostEstimate(flops=flops, bytes_accessed=moved, transcendentals=0),
    )(*operands)
    return results[0] if single else results


def pick_rows(lines, rows, count, flips, outs):
    kept = GROUP // count
    line = lax.broadcasted_iota(jnp.int32, (kept, GROUP), 0)
    source = lax.broadcasted_iota(jnp.int32, (kept, GROUP), 1)
    first = (line // rows) * (count * rows) + line % rows
    chosen = jnp.concatenate(
        [(source == first + partner("py", flip) * rows).astype(jnp.float32) for flip in flips]
    ).astype(jnp.bfloat16)
    for part in range(lines.shape[0] // GROUP):
        picked = jnp.dot(
            chosen,
            lines[part * GROUP : (part + 1) * GROUP, :],
            preferred_element_type=jnp.float32,
        ).astype(jnp.bfloat16)
        for index, out in enumerate(outs):
            out[part * kept : (part + 1) * kept, :] = picked[index * kept : (index + 1) * kept]


def first_kernel(rows, count, flips, planes, flux_y, flux_x, flux_z, *refs):
    sent_y, (held_y, faces, across, sems) = refs[: len(flips)], refs[len(flips) :]
    last = flux_z.shape[1] - WIDTH
    moves = [(flux_y, held_y)]
    moves += [(flux_z.at[:, pl.ds(last, WIDTH)], faces.at[:, :WIDTH])]
    moves += [(flux_z.at[:, :WIDTH], faces.at[:, WIDTH:])]
    for flip, place in ((2, across.at[0]), (3, across.at[1])):
        moves.append((flux_x.at[:, pl.ds(partner("px", flip) * planes, planes)], place))
    copies = [pltpu.make_async_copy(a, b, sems.at[i]) for i, (a, b) in enumerate(moves)]
    copies[0].start(priority=1)
    for copy in copies[1:]:
        copy.start()
    copies[0].wait()
    pick_rows(held_y, rows, count, flips, sent_y)
    for copy in copies[1:]:
        copy.wait()


def second_kernel(rows, count, flips, flux_y, *outs):
    pick_rows(flux_y, rows, count, flips, outs)


def join_x_kernel(planes, after, flux_x, got, out):
    out[0] = flux_x[:, pl.ds(partner("px", 1) * planes, planes)]
    out[1] = got[1]


def join_kernel(stay, got, *refs):
    out = refs[-1]
    out[0] = stay[1]
    out[1] = got[1]


def stencil_kernel(planes, flux_z, faces, across, stay, held):
    own = flux_z.shape[1]

    def plane(variable, index):
        if index < 0:
            return faces[variable, WIDTH + index].astype(jnp.float32)
        if index >= own:
            return faces[variable, WIDTH + index - own].astype(jnp.float32)
        return flux_z[variable, index].astype(jnp.float32)

    for variable in range(flux_z.shape[0]):
        for index in range(own):
            total = jnp.zeros(flux_z.shape[2:], jnp.float32)
            for offset in range(WIDTH):
                upper = plane(variable, index + offset + 1)
                lower = plane(variable, index - offset - 1)
                total = total + STENCIL_COEFS[offset] * (upper - lower)
            held[variable, index] = total.astype(jnp.bfloat16)
    for flip, place in ((2, across.at[0]), (3, across.at[1]), (0, stay.at[0]), (1, stay.at[1])):
        place[...] = held[:, pl.ds(partner("px", flip) * planes, planes)]


def cells(index, width):
    return pl.ds(pl.multiple_of(index * width, width), width)


def times(block, line_op, to, of):
    return lax.dot_general(
        block, line_op[to, of], (((1,), (1,)), ((), ())), preferred_element_type=jnp.float32
    )


def blocks_of(stay, across, joined):
    return ((0, stay, 0), (2, across, 0), (1, joined, 0), (3, joined, 1))


def turn(line_op, index, out):
    depth = out.shape[0]
    for start in range(0, line_op.shape[0], depth):
        place = pl.ds(start, depth)
        out[:, place] = line_op[place, cells(index, depth)].T


def own_kernel(flip, planes, after, own_y, line_op, flux_x, across, out_y, out_x, turned):
    width = own_y.shape[1]
    out_y[...] = times(own_y[...], line_op, ALL, cells(lax.axis_index("py"), width))
    turn(line_op, partner("py", flip), turned)
    width = across.shape[2]
    own_x = flux_x[:, pl.ds(partner("px", 0) * planes, planes)].reshape(-1, width)
    out_x[...] = times(own_x, line_op, ALL, cells(partner("px", 0), width)) + times(
        across[0], line_op, ALL, cells(partner("px", 2), width)
    )


def main_kernel(before, joined, line_op, out):
    width = joined.shape[2]
    out[...] = (
        before[...]
        + times(joined[0], line_op, ALL, cells(partner("px", 1), width))
        + times(joined[1], line_op, ALL, cells(partner("px", 3), width))
    )


def add_kernel(across, joined, stay, products, after, out):
    width = stay.shape[2]
    for flip, ref, index in blocks_of(stay, across, joined):
        place = cells(partner("px", flip), width)
        out[:, place] = (products[:, place] + ref[index].astype(jnp.float32)).astype(jnp.bfloat16)


def first_step_kernel(flip, later, block, before, line_op, out, turned):
    part = times(block[...], line_op, ALL, cells(partner("py", flip), block.shape[1]))
    out[...] = before[...] + part
    turn(line_op, partner("py", later), turned)


def next_step_kernel(after, block, before, turned, out):
    out[...] = before[...] + jnp.dot(
        block[...], turned[...], preferred_element_type=jnp.float32
    )


def late_kernel(early, block, turned, after, out, held, sems):
    rows = out.shape[1]
    copies = []
    for start in range(0, out.shape[2], COLUMNS):
        place = pl.ds(start, COLUMNS)
        part = jnp.dot(block[...], turned[:, place], preferred_element_type=jnp.float32)
        total = early[:, place] + part
        held[:, :, place] = total.astype(jnp.bfloat16).reshape(-1, rows, COLUMNS)
        copy = pltpu.make_async_copy(
            held.at[:, :, place], out.at[:, :, place], sems.at[len(copies)]
        )
        copy.start()
        copies.append(copy)
    for copy in copies:
        copy.wait()


def exchanged(flux_x, flux_y, flux_z, line_op):
    variables, slab, lines, x_width = flux_x.shape
    x_count, y_count = lax.axis_size("px"), lax.axis_size("py")
    planes = slab // x_count
    x_lines, y_width = flux_y.shape[2:]
    rows = x_lines // y_count
    line = line_op.shape[0]
    gathered = variables * slab * rows
    lines_x = variables * planes * lines
    bf16 = jnp.bfloat16

    def like(*shape, kind=bf16):
        return jax.ShapeDtypeStruct(shape, kind)

    rows_y = flux_y.reshape(-1, y_width)
    chunk_y = like(gathered, y_width)
    pair_x = like(2, variables, planes, lines, x_width)
    sent_2, sent_1, sent_3, held_y, faces, across_x = call(
        functools.partial(first_kernel, rows, y_count, (2, 1, 3), planes),
        [
            chunk_y,
            chunk_y,
            chunk_y,
            like(*rows_y.shape),
            like(variables, 2 * WIDTH, lines, x_width),
            pair_x,
        ],
        rows_y,
        flux_x,
        flux_z,
        far=(0, 1, 2),
        limit=8,
        scratch=[pltpu.SemaphoreType.DMA((5,))],
    )
    got_2 = swap(sent_2, "py", 2)
    faces = swap(faces, "gz", 1)
    across_x = swap(across_x, "px", 2)
    (own_y,) = call(
        functools.partial(second_kernel, rows, y_count, (0,)),
        [chunk_y],
        held_y,
        limit=8,
        flops=STAGE,
    )
    got_1 = swap(sent_1, "py", 1)
    got_3 = swap(sent_3, "py", 3)

    across_z, stay_z = call(
        functools.partial(stencil_kernel, planes),
        [pair_x, pair_x],
        flux_z,
        faces,
        limit=8,
        flops=STAGE,
        scratch=[pltpu.VMEM(flux_z.shape, bf16)],
    )
    joined_x = call(
        functools.partial(join_x_kernel, planes),
        pair_x,
        stay_z,
        flux_x,
        across_x,
        limit=8,
        flops=STAGE // 2,
    )
    flat = (2, lines_x, x_width)
    products_like = like(lines_x, line, kind=jnp.float32)
    sums_like = like(gathered, line, kind=jnp.float32)
    turned_like = like(y_width, line)
    own_sum, half_products, turned_3 = call(
        functools.partial(own_kernel, 3, planes),
        [sums_like, products_like, turned_like],
        joined_x,
        own_y,
        line_op,
        flux_x,
        across_x.reshape(flat),
        limit=16,
        flops=STAGE,
    )
    joined_x = swap(joined_x, "px", 1)
    products = call(
        main_kernel,
        products_like,
        half_products,
        joined_x.reshape(flat),
        line_op,
        limit=16,
        flops=STAGE,
    )
    across_z = swap(across_z, "px", 2)
    joined_z = swap(
        call(join_kernel, pair_x, stay_z, across_z, products, limit=8, flops=STAGE), "px", 1
    )
    block_flops = 2 * gathered * y_width * line
    sum_2, turned_1 = call(
        functools.partial(first_step_kernel, 2, 1),
        [sums_like, turned_like],
        got_2,
        own_sum,
        line_op,
        limit=16,
        flops=STAGE,
    )
    sum_1 = call(
        next_step_kernel,
        sums_like,
        got_2,
        got_1,
        sum_2,
        turned_1,
        limit=16,
        flops=block_flops,
    )
    xz_part = call(
        add_kernel,
        like(lines_x, line),
        *(a.reshape(flat) for a in (across_z, joined_z, stay_z)),
        products,
        sum_1,
        limit=8,
    )
    y_like = like(variables * slab, rows, line)
    y_part = call(
        late_kernel,
        y_like,
        sum_1,
        got_3,
        turned_3,
        xz_part,
        far=(3,),
        far_out=(0,),
        limit=16,
        flops=block_flops,
        scratch=[
            pltpu.VMEM(y_like.shape, bf16),
            pltpu.SemaphoreType.DMA((line // COLUMNS,)),
        ],
    )
    y_part, xz_part = lax.optimization_barrier((y_part, xz_part))
    return (
        xz_part.reshape(variables, planes, lines, line),
        y_part.reshape(variables, slab, rows, line),
    )


def local(flux_x, flux_y, flux_z, line_op):
    counts = tuple(lax.axis_size(axis) for axis in ("gz", "px", "py"))
    lines_y = math.prod(flux_y.shape[:3])
    widths = (flux_x.shape[3], flux_y.shape[3], COLUMNS)
    fits = (
        counts == (2, 4, 4)
        and flux_x.shape == flux_z.shape
        and lines_y % GROUP == 0
        and GROUP % flux_y.shape[2] == 0
        and flux_x.shape[2] % 8 == 0
        and flux_z.shape[1] >= 2 * WIDTH
        and all(line_op.shape[0] % width == 0 and width % 128 == 0 for width in widths)
    )
    return (exchanged if fits else plain)(flux_x, flux_y, flux_z, line_op)


def solution(mesh):
    return jax.shard_map(
        local,
        mesh=mesh,
        in_specs=(
            P(None, "gz", "py", "px"),
            P(None, "gz", "px", "py"),
            P(None, "gz", "py", "px"),
            P(),
        ),
        out_specs=(P(None, ("gz", "px"), "py", None), P(None, "gz", ("px", "py"), None)),
        check_vma=False,
    )
```
